32 devices in a mesh: wide: 16 (over z, x, core), narrow: 2 (over y).
Axes of the slice: x: 2, y: 2, z: 4, core: 2. Of those that a mesh axis runs over, the one named last changes fastest.
Arguments:
- images: bfloat16 [64, 16, 14, 1024], P('wide', 'narrow')
- crop: int32 [64], replicated, may hold values from 96 to 224, as said below
- micro: int32 [64], replicated, may hold values from 0 to 1, as said below
- first_reduce: bfloat16 [1024, 512], replicated, may hold values from -0.1875 to 0.1875
- first_reduce_gain: bfloat16 [512], replicated, may hold values from 0.099609375 to 1.8984375
- first_reduce_bias: bfloat16 [512], replicated, may hold values from -2.5 to 2.5
- first_spatial: bfloat16 [3, 3, 512, 512], replicated, may hold values from -0.09375 to 0.09375
- first_spatial_gain: bfloat16 [512], replicated, may hold values from 0.099609375 to 1.8984375
- first_spatial_bias: bfloat16 [512], replicated, may hold values from -2.5 to 2.5
- first_expand: bfloat16 [512, 2048], replicated, may hold values from -0.25 to 0.25
- first_expand_gain: bfloat16 [2048], replicated, may hold values from 0.099609375 to 1.8984375
- first_expand_bias: bfloat16 [2048], replicated, may hold values from -2.5 to 2.5
- first_project: bfloat16 [1024, 2048], replicated, may hold values from -0.1875 to 0.1875
- first_project_gain: bfloat16 [2048], replicated, may hold values from 0.099609375 to 1.8984375
- first_project_bias: bfloat16 [2048], replicated, may hold values from -2.5 to 2.5
- first_squeeze: bfloat16 [2048, 128], replicated, may hold values from -0.25 to 0.25
- first_squeeze_bias: bfloat16 [128], replicated, may hold values from -2.5 to 2.5
- first_excite: bfloat16 [128, 2048], replicated, may hold values from -0.5 to 0.5
- first_excite_bias: bfloat16 [2048], replicated, may hold values from -2.5 to 2.5
- second_reduce: bfloat16 [2048, 512], P('narrow'), may hold values from -0.125 to 0.125
- second_reduce_gain: bfloat16 [512], replicated, may hold values from 0.099609375 to 1.8984375
- second_reduce_bias: bfloat16 [512], replicated, may hold values from -2.5 to 2.5
- second_spatial: bfloat16 [3, 3, 512, 512], P(None, None, None, 'narrow'), may hold values from -0.09375 to 0.09375
- second_spatial_gain: bfloat16 [512], P('narrow'), may hold values from 0.099609375 to 1.8984375
- second_spatial_bias: bfloat16 [512], P('narrow'), may hold values from -2.5 to 2.5
- second_expand: bfloat16 [512, 2048], P('narrow'), may hold values from -0.25 to 0.25
- second_expand_gain: bfloat16 [2048], P('narrow'), may hold values from 0.099609375 to 1.8984375
- second_expand_bias: bfloat16 [2048], P('narrow'), may hold values from -2.5 to 2.5
- second_squeeze: bfloat16 [2048, 128], P('narrow'), may hold values from -0.25 to 0.25
- second_squeeze_bias: bfloat16 [128], replicated, may hold values from -2.5 to 2.5
- second_excite: bfloat16 [128, 2048], P(None, 'narrow'), may hold values from -0.5 to 0.5
- second_excite_bias: bfloat16 [2048], P('narrow'), may hold values from -2.5 to 2.5
- out_grad: bfloat16 [64, 8, 7, 2048], P('wide', None, None, 'narrow'), may hold values from -6 to 6
Outputs:
- result: bfloat16 [64, 8, 7, 2048], P('wide', None, None, 'narrow')
- grad_images: float32 [64, 16, 14, 1024], P('wide', 'narrow')
- grad_first_reduce: float32 [1024, 512], P('wide', 'narrow')
- grad_first_reduce_gain: float32 [512], replicated
- grad_first_reduce_bias: float32 [512], replicated
- grad_first_spatial: float32 [3, 3, 512, 512], P(None, None, 'wide', 'narrow')
- grad_first_spatial_gain: float32 [512], replicated
- grad_first_spatial_bias: float32 [512], replicated
- grad_first_expand: float32 [512, 2048], P('wide', 'narrow')
- grad_first_expand_gain: float32 [2048], replicated
- grad_first_expand_bias: float32 [2048], replicated
- grad_first_project: float32 [1024, 2048], P('wide', 'narrow')
- grad_first_project_gain: float32 [2048], replicated
- grad_first_project_bias: float32 [2048], replicated
- grad_first_squeeze: float32 [2048, 128], P('narrow', 'wide')
- grad_first_squeeze_bias: float32 [128], replicated
- grad_first_excite: float32 [128, 2048], P('wide', 'narrow')
- grad_first_excite_bias: float32 [2048], replicated
- grad_second_reduce: float32 [2048, 512], P('narrow', 'wide')
- grad_second_reduce_gain: float32 [512], replicated
- grad_second_reduce_bias: float32 [512], replicated
- grad_second_spatial: float32 [3, 3, 512, 512], P(None, None, 'wide', 'narrow')
- grad_second_spatial_gain: float32 [512], P('narrow')
- grad_second_spatial_bias: float32 [512], P('narrow')
- grad_second_expand: float32 [512, 2048], P('narrow', 'wide')
- grad_second_expand_gain: float32 [2048], P('narrow')
- grad_second_expand_bias: float32 [2048], P('narrow')
- grad_second_squeeze: float32 [2048, 128], P('narrow', 'wide')
- grad_second_squeeze_bias: float32 [128], replicated
- grad_second_excite: float32 [128, 2048], P('wide', 'narrow')
- grad_second_excite_bias: float32 [2048], P('narrow')
- norms: float32 [5], replicated
The draws below stay inside these ranges and needn't reach their ends.
Inputs may be any that keep to these rules, and one draw needn't show every extreme that they name: Each image's crop is 96 or 224 pixels; at least one image of the batch is 224. Each micro-batch holds exactly 32 images.
All inputs are finite; a program needn't handle non-finite values.
Results may differ from the reference program's by a relative error of at most 0.025.
Values may be sent and summed in bfloat16 or wider, within the bound.
No kernel may reach another device: no remote copies, remote signals or barrier semaphores. Data moves between devices by JAX's collectives and lax.ppermute only.
A program may use at most 192 MiB of HBM per device.

```python
import jax
import jax.numpy as jnp
from jax import lax

C_IN = 1024
MID = 512
C_OUT = 2048
SQUEEZE = 128
MICRO = 2
ROWS_IN = 16
COLS_IN = 14
ROWS_OUT = 8
COLS_OUT = 7
IMAGES = 64


def draw_images(key, part):
    key = jax.random.fold_in(key, 13)
    base_key, channel_key, image_key = jax.random.split(key, 3)
    shape = (IMAGES, ROWS_IN, COLS_IN, C_IN)
    base = jax.random.normal(base_key, shape, jnp.float32)
    spread = 2.0
    channel = jnp.exp(jax.random.uniform(channel_key, (C_IN,), jnp.float32, -1.0, 1.0) * jnp.log(spread))
    rising = jnp.exp(jnp.log(3.0) * jnp.arange(IMAGES, dtype=jnp.float32) / max(IMAGES - 1, 1))
    jitter = jnp.exp(jax.random.uniform(image_key, (IMAGES,), jnp.float32, -0.3, 0.3))
    return (base * channel * (rising * jitter)[:, None, None, None]).astype(jnp.bfloat16)


def draw_crop(key, part):
    key = jax.random.fold_in(key, 11)
    coin_key, pick_key = jax.random.split(key)
    coins = jax.random.randint(coin_key, (IMAGES,), 0, 2).astype(jnp.int32)
    chosen = jax.random.randint(pick_key, (), 0, IMAGES).astype(jnp.int32)
    places = jnp.arange(IMAGES, dtype=jnp.int32)
    forced = (places == chosen).astype(jnp.int32)
    larger = jnp.maximum(coins, forced)
    return (96 + 128 * larger).astype(jnp.int32)


def draw_micro(key, part):
    key = jax.random.fold_in(key, 12)
    ordering = jax.random.permutation(key, IMAGES).astype(jnp.int32)
    return (ordering % MICRO).astype(jnp.int32)


def steps_of(own_key, dims, cuts, least, top_value):
    def one(axis_at, shards_of):
        draws = jax.random.uniform(jax.random.fold_in(jax.random.fold_in(own_key, 6), axis_at), (shards_of,), jnp.float32, least / len(cuts), top_value / len(cuts))
        return jnp.repeat(jnp.exp(draws), dims[axis_at] // shards_of).reshape((-1,) + (1,) * (len(dims) - axis_at - 1))

    factor_of = one(*cuts[0])
    for cut in cuts[1:]:
        factor_of = factor_of * one(*cut)
    return factor_of


def normal_values(rng, dims, deviation, limit, cuts=(), held_as=jnp.bfloat16):
    result = deviation * jax.random.normal(rng, dims, jnp.float32)
    if cuts:
        result = result * steps_of(rng, dims, cuts, -0.22, 0.18)
    return jnp.clip(result, -limit, limit).astype(held_as)


def setup_inputs(seed: int = 0) -> dict:
    key_of = jax.random.split(jax.random.key(seed), 34)
    images = draw_images(jax.random.fold_in(key_of[33], 71), 0)
    crop = draw_crop(jax.random.fold_in(key_of[33], 71), 0)
    micro = draw_micro(jax.random.fold_in(key_of[33], 71), 0)
    first_reduce = normal_values(key_of[3], (C_IN, MID), C_IN ** -0.5, 0.1875)
    first_reduce_gain = jnp.clip(1.0 + 0.18 * jax.random.normal(key_of[4], (MID,), jnp.float32), 0.099609375, 1.8984375).astype(jnp.bfloat16)
    first_reduce_bias = normal_values(key_of[5], (MID,), 0.5, 2.5)
    first_spatial = normal_values(key_of[6], (3, 3, MID, MID), (9 * MID) ** -0.5, 0.09375)
    first_spatial_gain = jnp.clip(1.0 + 0.18 * jax.random.normal(key_of[7], (MID,), jnp.float32), 0.099609375, 1.8984375).astype(jnp.bfloat16)
    first_spatial_bias = normal_values(key_of[8], (MID,), 0.5, 2.5)
    first_expand = normal_values(key_of[9], (MID, C_OUT), MID ** -0.5, 0.25)
    first_expand_gain = jnp.clip(1.0 + 0.18 * jax.random.normal(key_of[10], (C_OUT,), jnp.float32), 0.099609375, 1.8984375).astype(jnp.bfloat16)
    first_expand_bias = normal_values(key_of[11], (C_OUT,), 0.5, 2.5)
    first_project = normal_values(key_of[12], (C_IN, C_OUT), C_IN ** -0.5, 0.1875)
    first_project_gain = jnp.clip(1.0 + 0.18 * jax.random.normal(key_of[13], (C_OUT,), jnp.float32), 0.099609375, 1.8984375).astype(jnp.bfloat16)
    first_project_bias = normal_values(key_of[14], (C_OUT,), 0.5, 2.5)
    first_squeeze = normal_values(key_of[15], (C_OUT, SQUEEZE), (C_OUT // 4) ** -0.5, 0.25)
    first_squeeze_bias = normal_values(key_of[16], (SQUEEZE,), 0.5, 2.5)
    first_excite = normal_values(key_of[17], (SQUEEZE, C_OUT), SQUEEZE ** -0.5, 0.5)
    first_excite_bias = normal_values(key_of[18], (C_OUT,), 0.5, 2.5)
    second_reduce = normal_values(key_of[19], (C_OUT, MID), C_OUT ** -0.5, 0.125, ((0, 2),))
    second_reduce_gain = jnp.clip(1.0 + 0.18 * jax.random.normal(key_of[20], (MID,), jnp.float32), 0.099609375, 1.8984375).astype(jnp.bfloat16)
    second_reduce_bias = normal_values(key_of[21], (MID,), 0.5, 2.5)
    second_spatial = normal_values(key_of[22], (3, 3, MID, MID), (9 * MID) ** -0.5, 0.09375, ((3, 2),))
    second_spatial_gain = jnp.clip(1.0 + 0.18 * jax.random.normal(key_of[23], (MID,), jnp.float32), 0.099609375, 1.8984375).astype(jnp.bfloat16)
    second_spatial_bias = normal_values(key_of[24], (MID,), 0.5, 2.5, ((0, 2),))
    second_expand = normal_values(key_of[25], (MID, C_OUT), MID ** -0.5, 0.25, ((0, 2),))
    second_expand_gain = jnp.clip(1.0 + 0.18 * jax.random.normal(key_of[26], (C_OUT,), jnp.float32), 0.099609375, 1.8984375).astype(jnp.bfloat16)
    second_expand_bias = normal_values(key_of[27], (C_OUT,), 0.5, 2.5, ((0, 2),))
    second_squeeze = normal_values(key_of[28], (C_OUT, SQUEEZE), (C_OUT // 4) ** -0.5, 0.25, ((0, 2),))
    second_squeeze_bias = normal_values(key_of[29], (SQUEEZE,), 0.5, 2.5)
    second_excite = normal_values(key_of[30], (SQUEEZE, C_OUT), SQUEEZE ** -0.5, 0.5, ((1, 2),))
    second_excite_bias = normal_values(key_of[31], (C_OUT,), 0.5, 2.5, ((0, 2),))
    out_grad = normal_values(key_of[32], (IMAGES, ROWS_OUT, COLS_OUT, C_OUT), 1.0, 6.0, ((0, 16), (3, 2)))
    return dict(images=images, crop=crop, micro=micro, first_reduce=first_reduce, first_reduce_gain=first_reduce_gain, first_reduce_bias=first_reduce_bias, first_spatial=first_spatial, first_spatial_gain=first_spatial_gain, first_spatial_bias=first_spatial_bias, first_expand=first_expand, first_expand_gain=first_expand_gain, first_expand_bias=first_expand_bias, first_project=first_project, first_project_gain=first_project_gain, first_project_bias=first_project_bias, first_squeeze=first_squeeze, first_squeeze_bias=first_squeeze_bias, first_excite=first_excite, first_excite_bias=first_excite_bias, second_reduce=second_reduce, second_reduce_gain=second_reduce_gain, second_reduce_bias=second_reduce_bias, second_spatial=second_spatial, second_spatial_gain=second_spatial_gain, second_spatial_bias=second_spatial_bias, second_expand=second_expand, second_expand_gain=second_expand_gain, second_expand_bias=second_expand_bias, second_squeeze=second_squeeze, second_squeeze_bias=second_squeeze_bias, second_excite=second_excite, second_excite_bias=second_excite_bias, out_grad=out_grad)


EPSILON = 1e-05
HIGHEST = lax.Precision.HIGHEST

@jax.custom_vjp
def low(v):
    return lax.optimization_barrier(v.astype(jnp.bfloat16)).astype(jnp.float32)

@jax.custom_vjp
def low_back(v):
    return v

def low_keep(v):
    return (low(v), None)

def low_pass(kept, grad):
    return (grad,)

def back_keep(v):
    return (v, None)

def back_low(kept, grad):
    return (low(grad),)
low.defvjp(low_keep, low_pass)
low_back.defvjp(back_keep, back_low)

def cell_mask(side_len, row_count, col_count):
    row_ids = jnp.arange(row_count, dtype=jnp.int32)
    col_ids = jnp.arange(col_count, dtype=jnp.int32)
    inside = (row_ids[None, :, None] < side_len[:, None, None]) & (col_ids[None, None, :] < side_len[:, None, None])
    return inside.astype(jnp.float32)[..., None]

def pointwise(values, weights):
    return jnp.einsum('brci,io->brco', values, weights, precision=HIGHEST)

def conv_down(values, weights):
    return lax.conv_general_dilated(values, weights, (2, 2), ((1, 0), (1, 0)), dimension_numbers=('NHWC', 'HWIO', 'NHWC'), precision=HIGHEST)

def conv_same(values, weights):
    return lax.conv_general_dilated(values, weights, (1, 1), ((1, 1), (1, 1)), dimension_numbers=('NHWC', 'HWIO', 'NHWC'), precision=HIGHEST)

def batch_norm(values, keep_mask, onehot, counts, gain_vector, bias_vector):
    masked = values * keep_mask
    mean_value = jnp.dot(onehot.T, lax.optimization_barrier(jnp.sum(masked, axis=(1, 2))), precision=HIGHEST) / counts[:, None]
    square_value = jnp.dot(onehot.T, lax.optimization_barrier(jnp.sum(masked * values, axis=(1, 2))), precision=HIGHEST) / counts[:, None]
    scale_value = lax.rsqrt(square_value - mean_value * mean_value + EPSILON)
    mean_rows = jnp.dot(onehot, mean_value, precision=HIGHEST)[:, None, None, :]
    scale_rows = jnp.dot(onehot, scale_value, precision=HIGHEST)[:, None, None, :]
    return (values - mean_rows) * scale_rows * gain_vector + bias_vector

def excite_gate(unit_value, cell_counts, squeeze, squeeze_bias, excite, excite_bias):
    pooled = lax.optimization_barrier(jnp.sum(unit_value, axis=(1, 2))) / cell_counts[:, None]
    squeezed = jax.nn.silu(jnp.dot(pooled, squeeze, precision=HIGHEST) + squeeze_bias)
    return jax.nn.sigmoid(jnp.dot(squeezed, excite, precision=HIGHEST) + excite_bias)

def reference(images, crop, micro, first_reduce, first_reduce_gain, first_reduce_bias, first_spatial, first_spatial_gain, first_spatial_bias, first_expand, first_expand_gain, first_expand_bias, first_project, first_project_gain, first_project_bias, first_squeeze, first_squeeze_bias, first_excite, first_excite_bias, second_reduce, second_reduce_gain, second_reduce_bias, second_spatial, second_spatial_gain, second_spatial_bias, second_expand, second_expand_gain, second_expand_bias, second_squeeze, second_squeeze_bias, second_excite, second_excite_bias, out_grad):
    side_in = crop // 16
    side_out = crop // 32
    keep_in = cell_mask(side_in, ROWS_IN, COLS_IN)
    keep_out = cell_mask(side_out, ROWS_OUT, COLS_OUT)
    onehot = (micro[:, None] == jnp.arange(MICRO, dtype=jnp.int32)[None, :]).astype(jnp.float32)
    count_in = lax.optimization_barrier(jnp.sum(onehot * (side_in * side_in).astype(jnp.float32)[:, None], axis=0))
    count_out = lax.optimization_barrier(jnp.sum(onehot * (side_out * side_out).astype(jnp.float32)[:, None], axis=0))
    cell_counts = (side_out * side_out).astype(jnp.float32)
    initials = [first_reduce, first_reduce_gain, first_reduce_bias, first_spatial, first_spatial_gain, first_spatial_bias, first_expand, first_expand_gain, first_expand_bias, first_project, first_project_gain, first_project_bias, first_squeeze, first_squeeze_bias, first_excite, first_excite_bias, second_reduce, second_reduce_gain, second_reduce_bias, second_spatial, second_spatial_gain, second_spatial_bias, second_expand, second_expand_gain, second_expand_bias, second_squeeze, second_squeeze_bias, second_excite, second_excite_bias]
    params_in = [member.astype(jnp.float32) for member in initials]

    def forward(pixels_in, params):
        one_reduce, one_reduce_gain, one_reduce_bias, one_spatial, one_spatial_gain, one_spatial_bias, one_expand, one_expand_gain, one_expand_bias, one_project, one_project_gain, one_project_bias, one_squeeze, one_squeeze_bias, one_excite, one_excite_bias, two_reduce, two_reduce_gain, two_reduce_bias, two_spatial, two_spatial_gain, two_spatial_bias, two_expand, two_expand_gain, two_expand_bias, two_squeeze, two_squeeze_bias, two_excite, two_excite_bias = params
        pixels = pixels_in * keep_in
        pre_one = low_back(pointwise(pixels, one_reduce))
        hidden_one = low(jax.nn.silu(batch_norm(pre_one, keep_in, onehot, count_in, one_reduce_gain, one_reduce_bias)) * keep_in)
        pre_two = low_back(conv_down(hidden_one, one_spatial))
        hidden_two = low(jax.nn.silu(batch_norm(pre_two, keep_out, onehot, count_out, one_spatial_gain, one_spatial_bias)) * keep_out)
        pre_three = low_back(pointwise(hidden_two, one_expand))
        unit_one = batch_norm(pre_three, keep_out, onehot, count_out, one_expand_gain, one_expand_bias) * keep_out
        pre_proj = low_back(pointwise(pixels[:, ::2, ::2, :], one_project))
        short_one = batch_norm(pre_proj, keep_out, onehot, count_out, one_project_gain, one_project_bias) * keep_out
        gate_one = excite_gate(unit_one, cell_counts, one_squeeze, one_squeeze_bias, one_excite, one_excite_bias)
        branch_one = unit_one * gate_one[:, None, None, :]
        stream_one = jax.nn.silu(branch_one + short_one) * keep_out
        stream_low = low_back(low(stream_one))
        pre_four = low_back(pointwise(stream_low, two_reduce))
        hidden_four = low(jax.nn.silu(batch_norm(pre_four, keep_out, onehot, count_out, two_reduce_gain, two_reduce_bias)) * keep_out)
        pre_five = low_back(conv_same(hidden_four, two_spatial))
        hidden_five = low(jax.nn.silu(batch_norm(pre_five, keep_out, onehot, count_out, two_spatial_gain, two_spatial_bias)) * keep_out)
        pre_six = low_back(pointwise(hidden_five, two_expand))
        unit_two = batch_norm(pre_six, keep_out, onehot, count_out, two_expand_gain, two_expand_bias) * keep_out
        gate_two = excite_gate(unit_two, cell_counts, two_squeeze, two_squeeze_bias, two_excite, two_excite_bias)
        branch_two = unit_two * gate_two[:, None, None, :]
        stream_two = jax.nn.silu(branch_two + stream_low) * keep_out
        squares = jnp.stack([jnp.sum(stream_one * stream_one), jnp.sum(branch_one * branch_one), jnp.sum(short_one * short_one), jnp.sum(branch_two * branch_two), jnp.sum(stream_two * stream_two)])
        norms = jnp.sqrt(squares / (jnp.sum(count_out) * C_OUT))
        return (stream_two, norms)
    stream_two, pullback, norms = jax.vjp(forward, images.astype(jnp.float32), params_in, has_aux=True)
    grad_images, grads = pullback(out_grad.astype(jnp.float32))
    return (stream_two.astype(jnp.bfloat16), grad_images, grads[0], grads[1], grads[2], grads[3], grads[4], grads[5], grads[6], grads[7], grads[8], grads[9], grads[10], grads[11], grads[12], grads[13], grads[14], grads[15], grads[16], grads[17], grads[18], grads[19], grads[20], grads[21], grads[22], grads[23], grads[24], grads[25], grads[26], grads[27], grads[28], norms)
```

```python
import functools

import numpy as np
import jax
import jax.numpy as jnp
from jax import lax
from jax.experimental import pallas as pl
from jax.experimental.pallas import tpu as pltpu
from jax.sharding import PartitionSpec as P

EPSILON = 1e-05
BF = jnp.bfloat16
F32 = jnp.float32
B = 4
POS = 56
LIMIT = 24
M = B * POS
HALF = 112
HROWS = B * HALF
VMEM = pl.BlockSpec(memory_space=pltpu.VMEM)
SMEM = pl.BlockSpec(memory_space=pltpu.SMEM)
ANY = pl.BlockSpec(memory_space=pl.ANY)
INV_IN, INV_OUT, CELLS, MICRO, INV_ALL = 0, 2, 4, 8, 12
NARROW, CORE, DEST = 0, 1, 2
W6_AT, EX_AT, SQ_AT, VEC_AT, PACK_ROWS = 2304, 3328, 3584, 3840, 3856


def mm(a, b):
    return lax.dot_general(a, b, (((1,), (0,)), ((), ())), preferred_element_type=F32)


def mm_nt(a, b):
    return lax.dot_general(a, b, (((1,), (1,)), ((), ())), preferred_element_type=F32)


def mm_tn(a, b):
    return lax.dot_general(a, b, (((0,), (0,)), ((), ())), preferred_element_type=F32)


def f32(v):
    return v.astype(F32)


def low(v):
    return v.astype(BF)


def split2(v):
    a = low(v)
    return a, low(v - f32(a))


def split3(v):
    a = low(v)
    r = v - f32(a)
    b = low(r)
    return a, b, low(r - f32(b))


def dot3(v, w):
    return sum(mm(p, w) for p in split3(v))


def dot3_nt(v, w):
    return sum(mm_nt(p, w) for p in split3(v))


def outer(a, b):
    a1, a2 = split2(a)
    b1, b2 = split2(b)
    return mm_tn(a1, b1) + mm_tn(a1, b2) + mm_tn(a2, b1)


def sigmoid(v):
    return 1.0 / (1.0 + jnp.exp(-v))


def slope(v):
    s = sigmoid(v)
    return s * (1.0 + v * (1.0 - s))


def cols(c, size=256):
    return pl.ds(pl.multiple_of(c * size, size), size)


def expand(rows):
    return jnp.concatenate([jnp.broadcast_to(r, (POS, r.shape[1])) for r in rows], axis=0)


def pick(r0, r1, fs):
    return expand([r0 * (1.0 - fs[MICRO + b]) + r1 * fs[MICRO + b] for b in range(B)])


def image_sums(v):
    return [jnp.sum(v[b * POS : (b + 1) * POS], axis=0, keepdims=True) for b in range(B)]


def grouped(sums, fs, reps=1):
    zero = one = 0.0
    for b in range(B):
        zero = zero + sums[b] * (1.0 - fs[MICRO + b])
        one = one + sums[b] * fs[MICRO + b]
    return [zero, one]


def group_sums(v, fs):
    return grouped(image_sums(v), fs)


def put(ref, at, rows, sl):
    for k, r in enumerate(rows):
        ref[at + k : at + k + 1, sl] = r


def add_parts(parts, tot):
    t = parts[0]
    for k in range(1, parts.shape[0]):
        t = t + parts[k]
    tot[...] = t


def coefs(tot, at, sl, fs, inv):
    i0, i1 = fs[inv], fs[inv + 1]
    m0, m1 = tot[at : at + 1, sl] * i0, tot[at + 1 : at + 2, sl] * i1
    q0 = lax.rsqrt(tot[at + 2 : at + 3, sl] * i0 - m0 * m0 + EPSILON)
    q1 = lax.rsqrt(tot[at + 3 : at + 4, sl] * i1 - m1 * m1 + EPSILON)
    return pick(m0, m1, fs), pick(q0, q1, fs)


def means(tot, at, sl, fs, inv):
    i0, i1 = fs[inv], fs[inv + 1]
    a = pick(tot[at : at + 1, sl] * i0, tot[at + 1 : at + 2, sl] * i1, fs)
    b = pick(tot[at + 2 : at + 3, sl] * i0, tot[at + 3 : at + 4, sl] * i1, fs)
    return a, b


def stat_rows(v, keep, fs):
    kept = v * keep
    return group_sums(kept, fs) + group_sums(kept * v, fs)


def back_rows(d, x, fs):
    return group_sums(d, fs) + group_sums(d * x, fs)


def loop(count, body):
    lax.fori_loop(0, count, lambda c, _: (body(c), 0)[1], 0)


def copy_all(pairs, sems):
    copies = [pltpu.make_async_copy(s, d, sems.at[k]) for k, (s, d) in enumerate(pairs)]
    for c in copies:
        c.start()
    return copies


def wait_all(copies):
    for c in copies:
        c.wait()


def at_rows(start, size):
    return pl.ds(pl.multiple_of(start, 16), size)


def flip(p):
    return (p & 1) * 8 + (p & 2) * 2 + (p & 4) // 2 + (p & 8) // 8


def setup_kernel(exact, crop, micro, fs, isc, keep, keep1, keep_half):
    n = lax.axis_index("narrow").astype(jnp.int32)
    w = lax.axis_index("wide").astype(jnp.int32)
    isc[NARROW] = n
    isc[CORE] = w & 1
    for p in range(16):
        isc[DEST + p] = (w ^ flip(p)) if exact else jnp.int32(p)

    def count(k, sums):
        c, one = crop[k], micro[k]
        a, b = (c >> 4) * (c >> 4), (c >> 5) * (c >> 5)
        return (
            sums[0] + a * (1 - one), sums[1] + a * one, sums[2] + b * (1 - one), sums[3] + b * one,
        )

    zero = jnp.int32(0)
    sums = lax.fori_loop(0, crop.shape[0], count, (zero, zero, zero, zero))
    for k in range(4):
        fs[k] = 1.0 / sums[k].astype(F32)
    fs[INV_ALL] = 1.0 / ((sums[2] + sums[3]).astype(F32) * 2048.0)
    at = lax.broadcasted_iota(jnp.int32, (POS, 1), 0)
    i8, j7 = at & 7, at >> 3
    at = lax.broadcasted_iota(jnp.int32, (HALF, 1), 0)
    r8, c14 = n * 8 + (at & 7), at >> 3

    def inside(r, c, side):
        return jnp.where((r < side) & (c < side), 1.0, 0.0).astype(F32)

    for b in range(B):
        c = crop[w * B + b]
        side_in, side_out = c >> 4, c >> 5
        fs[CELLS + b] = 1.0 / (side_out * side_out).astype(F32)
        fs[MICRO + b] = micro[w * B + b].astype(F32)
        keep[b * POS : (b + 1) * POS, :] = inside(i8, j7, side_out)
        for k in range(4):
            keep1[k, b * POS : (b + 1) * POS, :] = inside(2 * i8 + k // 2, 2 * j7 + k % 2, side_in)
        keep_half[b * HALF : (b + 1) * HALF, :] = inside(r8, c14, side_in)


def one_half_kernel(fs, x, keep, w1, st):
    def body(c):
        sl = cols(c)
        v = mm(x[...], w1[:, sl]) * keep[...]
        sums = [jnp.sum(v[b * HALF : (b + 1) * HALF], axis=0, keepdims=True) for b in range(B)]
        v2 = v * v
        sq = [jnp.sum(v2[b * HALF : (b + 1) * HALF], axis=0, keepdims=True) for b in range(B)]
        put(st, 0, grouped(sums, fs) + grouped(sq, fs), sl)

    loop(2, body)


TAPS = [(p, q) for p in range(3) for q in range(3)]


def stage_two_kernel(
    fs, isc, own, other, part, part_other, perm, keep1, keep, w1, ws, gb, sh,
    xp, strided, x1, col, pre2, st, tot1, xs, tmp, hid, tot, sems,
):
    n = isc[NARROW]
    copies = copy_all([(own, xs.at[n]), (other, xs.at[1 - n])], sems)
    tot[...] = part[...] + part_other[...]
    tot1[...] = tot[...]
    wait_all(copies)

    def permute(c):
        sl = cols(c)
        for b in range(B):
            r = mm(perm[0], xs[0, b, :, sl]) + mm(perm[1], xs[1, b, :, sl])
            for k in range(4):
                tmp[k, b * POS : (b + 1) * POS, :] = r[k * POS : (k + 1) * POS]
        for k in range(4):
            xp[k, :, sl] = low(tmp[k] * keep1[k])
        strided[:, sl] = xp[0, :, sl]

    loop(4, permute)

    def first(c):
        k, sl = c // 2, cols(c % 2)
        v = mm(xp[k], w1[:, sl])
        mean, scale = coefs(tot, 0, sl, fs, INV_IN)
        x = (v - mean) * scale
        x1[k, :, sl] = x
        o = x * gb[0:1, sl] + gb[1:2, sl]
        hid[k, :, sl] = low(o * sigmoid(o) * keep1[k])

    loop(8, first)
    for t, (p, q) in enumerate(TAPS):
        h = hid[2 * (p != 1) + (q != 1)]
        if p == 0 or q == 0:
            h = low(mm(sh[3 * (0 if p == 0 else 1) + (0 if q == 0 else 1)], h))
        col[t] = h

    def second(c):
        sl = cols(c)
        v = mm(col[0], ws[0, :, sl])
        for t in range(1, 9):
            v = v + mm(col[t], ws[t, :, sl])
        pre2[:, sl] = v
        put(st, 0, stat_rows(v, keep[...], fs), sl)

    loop(2, second)


def project_kernel(fs, x, keep, wp, prep, st):
    def body(c):
        sl = cols(c)
        v = mm(x[...], wp[:, sl])
        prep[:, sl] = v
        put(st, 0, stat_rows(v, keep[...], fs), sl)

    loop(8, body)


def stage_three_kernel(fs, parts, pre2, stp, keep, w3, gb, h2, pre3, st, tot2, tot):
    add_parts(parts, tot)
    tot2[...] = tot[...]
    sl = slice(0, 512)
    mean, scale = coefs(tot, 0, sl, fs, INV_OUT)
    o = (pre2[...] - mean) * scale * gb[2:3, :] + gb[3:4, :]
    h2[...] = low(o * sigmoid(o) * keep[...])
    st[4:8, :] = stp[...]

    def body(c):
        sl = cols(c)
        v = mm(h2[...], w3[:, sl])
        pre3[:, sl] = v
        put(st, 0, stat_rows(v, keep[...], fs), sl)

    loop(8, body)


def stage_four_kernel(
    fs, isc, parts, pre3, prep, keep, vec, sqb, sq, ex, w4own, r1, r2,
    lows, pre4, st, tot3, gate, sp, pooled, squares, unit, short, w4, acc, tot, sems,
):
    n, core = isc[NARROW], isc[CORE]
    away = (1 - n) * 1024
    copies = copy_all(
        [
            (w4own, w4.at[at_rows(n * 1024, 1024)]),
            (r1, w4.at[at_rows(away + core * 512, 512)]),
            (r2, w4.at[at_rows(away + (1 - core) * 512, 512)]),
        ],
        sems,
    )
    add_parts(parts, tot)
    tot3[...] = tot[...]
    pooled[...] = jnp.zeros((8, 2048), F32)

    def units(c):
        sl = cols(c)
        mean, scale = coefs(tot, 0, sl, fs, INV_OUT)
        u = ((pre3[:, sl] - mean) * scale * vec[0:1, sl] + vec[1:2, sl]) * keep[...]
        unit[:, sl] = u
        for b, r in enumerate(image_sums(u)):
            pooled[b : b + 1, sl] = r * fs[CELLS + b]
        mean, scale = coefs(tot, 4, sl, fs, INV_OUT)
        s = ((prep[:, sl] - mean) * scale * vec[2:3, sl] + vec[3:4, sl]) * keep[...]
        short[:, sl] = s

    loop(8, units)
    sp[...] = dot3(pooled[...], sq[...]) + sqb[0:1, :]
    squeezed = sp[...] * sigmoid(sp[...])
    gate[...] = sigmoid(dot3(squeezed, ex[...]) + vec[4:5, :])
    squares[...] = jnp.zeros((8, 256), F32)
    acc[...] = jnp.zeros((M, 512), F32)
    wait_all(copies)

    def streams(c):
        sl = cols(c)
        branch = unit[:, sl] * expand([gate[b : b + 1, sl] for b in range(B)])
        s = short[:, sl]
        join = branch + s
        stream = join * sigmoid(join) * keep[...]
        for k, v in enumerate((stream, branch, s)):
            squares[k : k + 1, :] += jnp.sum(v * v, axis=0, keepdims=True)
        lo = low(stream)
        lows[:, sl] = lo
        acc[...] += mm(lo, w4[cols(c), :])

    loop(8, streams)
    pre4[...] = acc[...]
    put(st, 0, stat_rows(acc[...], keep[...], fs), slice(0, 512))


def w5_copies(isc, own, r1, r2, w5):
    n, core = isc[NARROW], isc[CORE]
    return [
        (own, w5.at[n]),
        (r1.at[0:2304], w5.at[1 - n, at_rows(core * 2304, 2304)]),
        (r2.at[0:2304], w5.at[1 - n, at_rows((1 - core) * 2304, 2304)]),
    ]


def stage_five_kernel(
    fs, isc, parts, pre4, keep, gb, sh, vown, w5own, r1, r2,
    col, pre5, st, tot4, gain5, vec2, w5, tot, vaway, sems,
):
    n = isc[NARROW]
    pairs = w5_copies(isc, w5own, r1, r2, w5) + [(r1.at[VEC_AT:PACK_ROWS], vaway)]
    copies = copy_all(pairs, sems)
    add_parts(parts, tot)
    tot4[...] = tot[...]
    mean, scale = coefs(tot, 0, slice(0, 512), fs, INV_OUT)
    o = (pre4[...] - mean) * scale * gb[4:5, :] + gb[5:6, :]
    h = low(o * sigmoid(o) * keep[...])
    for t in range(9):
        col[t] = h if t == 4 else low(mm(sh[t], h))
    wait_all(copies)
    for side, v in ((n, f32(vown[...])), (1 - n, f32(vaway[...]))):
        for k in range(2):
            gain5[k : k + 1, cols(side)] = v[k : k + 1]
        for k in range(3):
            for c in range(4):
                at = 2 + 4 * k + c
                vec2[k : k + 1, cols(side * 4 + c)] = v[at : at + 1]

    def body(c):
        v = 0.0
        for t in range(9):
            v = v + mm(col[t], w5[c, t * 512 : (t + 1) * 512, :])
        pre5[:, cols(c)] = v
        put(st, 0, stat_rows(v, keep[...], fs), cols(c))

    loop(2, body)


def w6_copies(isc, own, r1, r2, w6):
    n, core = isc[NARROW], isc[CORE]
    pairs = [(own, w6.at[at_rows(n * 256, 256)])]
    for r, h in ((r1, core), (r2, 1 - core)):
        for c in range(8):
            pairs.append(
                (
                    r.at[W6_AT + c * 128 : W6_AT + (c + 1) * 128],
                    w6.at[at_rows((1 - n) * 256 + h * 128, 128), c * 256 : (c + 1) * 256],
                )
            )
    return pairs


def stage_six_kernel(
    fs, isc, parts, pre5, keep, gain5, w6own, r1, r2, h5, pre6, st, tot5, w6, tot, sems
):
    copies = copy_all(w6_copies(isc, w6own, r1, r2, w6), sems)
    add_parts(parts, tot)
    tot5[...] = tot[...]
    mean, scale = coefs(tot, 0, slice(0, 512), fs, INV_OUT)
    o = (pre5[...] - mean) * scale * gain5[0:1, :] + gain5[1:2, :]
    h5[...] = low(o * sigmoid(o) * keep[...])
    wait_all(copies)

    def body(c):
        sl = cols(c)
        v = mm(h5[...], w6[:, sl])
        pre6[:, sl] = v
        put(st, 0, stat_rows(v, keep[...], fs), sl)

    loop(8, body)


def turn_kernel(
    fs, isc, parts, pre6, keep, lows, vec, sqb, sq1s, sqown, exown, r1, r2, ogown, ogother,
    result, dj2, pay, extra, tot6, gate, dp, pooled, de, ds, squeezed,
    unit, og, res, sq, ex, tot, sp, sems,
):
    n, core = isc[NARROW], isc[CORE]
    pairs = [
        (sqown, sq.at[at_rows(n * 1024, 1024)]),
        (exown, ex.at[n]),
        (ogown, og.at[n]),
        (ogother, og.at[1 - n]),
    ]
    for r, h in ((r1, core), (r2, 1 - core)):
        for k in range(2):
            pairs.append(
                (
                    r.at[SQ_AT : SQ_AT + 256, k * 128 : (k + 1) * 128],
                    sq.at[at_rows((1 - n) * 1024 + h * 512 + k * 256, 256)],
                )
            )
        for c in range(4):
            pairs.append(
                (
                    r.at[EX_AT + c * 64 : EX_AT + (c + 1) * 64],
                    ex.at[1 - n, at_rows(h * 64, 64), c * 256 : (c + 1) * 256],
                )
            )
    copies = copy_all(pairs, sems)
    add_parts(parts, tot)
    tot6[...] = tot[...]
    pooled[...] = jnp.zeros((8, 2048), F32)
    de[...] = jnp.zeros((8, 2048), F32)

    def units(c):
        sl = cols(c)
        mean, scale = coefs(tot, 0, sl, fs, INV_OUT)
        u = ((pre6[:, sl] - mean) * scale * vec[0:1, sl] + vec[1:2, sl]) * keep[...]
        unit[:, sl] = u
        for b, r in enumerate(image_sums(u)):
            pooled[b : b + 1, sl] = r * fs[CELLS + b]

    loop(8, units)
    wait_all(copies)
    sp[...] = dot3(pooled[...], sq[...]) + sqb[1:2, :]
    squeezed[...] = sp[...] * sigmoid(sp[...])
    for h in range(2):
        sl = slice(h * 1024, (h + 1) * 1024)
        gate[:, sl] = sigmoid(dot3(squeezed[...], ex[h]) + vec[2:3, sl])
    extra[...] = jnp.zeros((8, 512), F32)
    for k in range(3):
        extra[5 + k // 2 : 6 + k // 2, (k % 2) * 256 : (k % 2) * 256 + 256] = sq1s[k : k + 1, :]

    def streams(c):
        sl = cols(c)
        h, part = c // 4, cols(c % 4)
        u = unit[:, sl]
        branch = u * expand([gate[b : b + 1, sl] for b in range(B)])
        join = branch + f32(lows[:, sl])
        s = sigmoid(join)
        stream = join * s * keep[...]
        res[h, :, part] = low(stream)
        d = f32(og[h, :, part]) * keep[...] * (s * (1.0 + join * (1.0 - s)))
        dj2[:, sl] = d
        for b, r in enumerate(image_sums(d * u)):
            de[b : b + 1, sl] = r
        extra[6:7, 256:512] += jnp.sum(branch * branch, axis=0, keepdims=True)
        extra[7:8, 0:256] += jnp.sum(stream * stream, axis=0, keepdims=True)

    loop(8, streams)
    result[...] = res[n]
    de[...] = de[...] * gate[...] * (1.0 - gate[...])
    back = 0.0
    for h in range(2):
        back = back + dot3_nt(de[:, h * 1024 : (h + 1) * 1024], ex[h])
    ds[...] = back * slope(sp[...])
    dp[...] = dot3_nt(ds[...], sq[...])
    for b in range(B):
        dp[b : b + 1, :] = dp[b : b + 1, :] * fs[CELLS + b]
    total = jnp.sum(de[...], axis=0, keepdims=True)
    for k in range(4):
        extra[k : k + 1, :] = total[:, k * 512 : (k + 1) * 512]
    extra[4:5, 0:128] = jnp.sum(ds[...], axis=0, keepdims=True)

    def tops(c):
        sl = cols(c)
        mean, scale = coefs(tot, 0, sl, fs, INV_OUT)
        x = (pre6[:, sl] - mean) * scale
        du = (
            dj2[:, sl] * expand([gate[b : b + 1, sl] for b in range(B)])
            + expand([dp[b : b + 1, sl] for b in range(B)])
        ) * keep[...]
        put(pay, 0, back_rows(du, x, fs), sl)

    loop(8, tops)


def whole_gain(tot, at, gain, bias):
    gain[...] = (tot[at + 2 : at + 3, :] + tot[at + 3 : at + 4, :]).reshape(gain.shape)
    bias[...] = (tot[at : at + 1, :] + tot[at + 1 : at + 2, :]).reshape(bias.shape)


def half_gain(tot, n, gain, bias):
    sl = cols(n, gain.shape[0])
    gain[...] = (tot[2:3, sl] + tot[3:4, sl]).reshape(gain.shape)
    bias[...] = (tot[0:1, sl] + tot[1:2, sl]).reshape(bias.shape)


def back_six_kernel(
    fs, isc, parts, tot6, pre6, dj2, gate, dp, pre5, tot5, extra, keep, vec, gain5, w6own, r1, r2,
    d6, do5, st, dgain, dbias, w6, tot, acc, sems,
):
    copies = copy_all(w6_copies(isc, w6own, r1, r2, w6), sems)
    add_parts(parts, tot)
    half_gain(tot, isc[NARROW], dgain, dbias)
    acc[...] = jnp.zeros((M, 512), F32)
    wait_all(copies)

    def body(c):
        sl = cols(c)
        mean, scale = coefs(tot6, 0, sl, fs, INV_OUT)
        x = (pre6[:, sl] - mean) * scale
        du = (
            dj2[:, sl] * expand([gate[b : b + 1, sl] for b in range(B)])
            + expand([dp[b : b + 1, sl] for b in range(B)])
        ) * keep[...]
        a, bb = means(tot, 0, sl, fs, INV_OUT)
        d = low((du - a - x * bb) * (scale * vec[0:1, sl]) * keep[...])
        d6[:, sl] = d
        acc[...] += mm_nt(d, w6[:, sl])

    loop(8, body)
    mean, scale = coefs(tot5, 0, slice(0, 512), fs, INV_OUT)
    x = (pre5[...] - mean) * scale
    o = x * gain5[0:1, :] + gain5[1:2, :]
    d = acc[...] * keep[...] * slope(o)
    do5[...] = d
    put(st, 0, back_rows(d, x, fs), slice(0, 512))
    st[4:12, :] = extra[...]


def back_five_kernel(
    fs, isc, parts, tot5, pre5, do5, pre4, tot4, keep, gb, gain5, sh, w5own, r1, r2,
    d5, do4, st, dgain, dbias, debias, dsbias, norms, w5, tot, sems,
):
    n = isc[NARROW]
    copies = copy_all(w5_copies(isc, w5own, r1, r2, w5), sems)
    add_parts(parts, tot)
    half_gain(tot, n, dgain, dbias)
    excite = jnp.concatenate([tot[pl.ds(4 + 2 * n, 1), :], tot[pl.ds(5 + 2 * n, 1), :]], axis=1)
    debias[...] = excite.reshape(1024)
    dsbias[...] = tot[8:9, 0:128].reshape(128)
    for k in range(5):
        v = tot[9 + k // 2 : 10 + k // 2, (k % 2) * 256 : (k % 2) * 256 + 256]
        norms[k] = jnp.sqrt(jnp.sum(v, axis=1, keepdims=True) * fs[INV_ALL])[0, 0]
    sl = slice(0, 512)
    mean, scale = coefs(tot5, 0, sl, fs, INV_OUT)
    x = (pre5[...] - mean) * scale
    a, bb = means(tot, 0, sl, fs, INV_OUT)
    d = low((do5[...] - a - x * bb) * (scale * gain5[0:1, :]) * keep[...])
    d5[...] = d
    wait_all(copies)
    acc = 0.0
    for t in range(9):
        dc = d if t == 4 else low(mm(sh[8 - t], d))
        for h in range(2):
            acc = acc + mm_nt(dc[:, h * 256 : (h + 1) * 256], w5[h, t * 512 : (t + 1) * 512, :])
    mean, scale = coefs(tot4, 0, sl, fs, INV_OUT)
    x = (pre4[...] - mean) * scale
    o = x * gb[4:5, :] + gb[5:6, :]
    d = acc * keep[...] * slope(o)
    do4[...] = d
    put(st, 0, back_rows(d, x, fs), sl)


def back_four_kernel(
    fs, isc, parts, tot4, pre4, do4, dj2, tot3, pre3, prep, gate, sp, keep, gb, vec, sq, ex,
    w4own, r1, r2,
    d4, dj1, st, dgain, dbias, dp, de, ds, bias, w4, tot, sems,
):
    n, core = isc[NARROW], isc[CORE]
    away = (1 - n) * 1024
    copies = copy_all(
        [
            (w4own, w4.at[at_rows(n * 1024, 1024)]),
            (r1, w4.at[at_rows(away + core * 512, 512)]),
            (r2, w4.at[at_rows(away + (1 - core) * 512, 512)]),
        ],
        sems,
    )
    add_parts(parts, tot)
    whole_gain(tot, 0, dgain, dbias)
    de[...] = jnp.zeros((8, 2048), F32)
    mean, scale = coefs(tot4, 0, slice(0, 512), fs, INV_OUT)
    x = (pre4[...] - mean) * scale
    a, bb = means(tot, 0, slice(0, 512), fs, INV_OUT)
    d4[...] = low((do4[...] - a - x * bb) * (scale * gb[4:5, :]) * keep[...])
    wait_all(copies)

    def joins(c):
        sl = cols(c)
        back = dj2[:, sl] + mm_nt(d4[...], w4[cols(c), :])
        mean, scale = coefs(tot3, 0, sl, fs, INV_OUT)
        u = ((pre3[:, sl] - mean) * scale * vec[0:1, sl] + vec[1:2, sl]) * keep[...]
        mean, scale = coefs(tot3, 4, sl, fs, INV_OUT)
        s = ((prep[:, sl] - mean) * scale * vec[2:3, sl] + vec[3:4, sl]) * keep[...]
        join = u * expand([gate[b : b + 1, sl] for b in range(B)]) + s
        d = f32(low(back)) * keep[...] * slope(join)
        dj1[:, sl] = d
        for b, r in enumerate(image_sums(d * u)):
            de[b : b + 1, sl] = r

    loop(8, joins)
    de[...] = de[...] * gate[...] * (1.0 - gate[...])
    ds[...] = dot3_nt(de[...], ex[...]) * slope(sp[...])
    dp[...] = dot3_nt(ds[...], sq[...])
    for b in range(B):
        dp[b : b + 1, :] = dp[b : b + 1, :] * fs[CELLS + b]
    total = jnp.sum(de[...], axis=0, keepdims=True)
    bias[...] = jnp.zeros((8, 512), F32)
    for k in range(4):
        bias[k : k + 1, :] = total[:, k * 512 : (k + 1) * 512]
    bias[4:5, 0:128] = jnp.sum(ds[...], axis=0, keepdims=True)

    def tops(c):
        sl = cols(c)
        d = dj1[:, sl]
        mean, scale = coefs(tot3, 0, sl, fs, INV_OUT)
        x = (pre3[:, sl] - mean) * scale
        du = (
            d * expand([gate[b : b + 1, sl] for b in range(B)])
            + expand([dp[b : b + 1, sl] for b in range(B)])
        ) * keep[...]
        put(st, 0, back_rows(du, x, fs), sl)
        mean, scale = coefs(tot3, 4, sl, fs, INV_OUT)
        put(st, 4, back_rows(d, (prep[:, sl] - mean) * scale, fs), sl)

    loop(8, tops)


def back_three_kernel(
    fs, parts, tot3, pre3, prep, dj1, gate, dp, bias, pre2, tot2, keep, vec, gb, w3,
    d3, dproj, do2, st, dgain, dbias, dgainp, dbiasp, tot, acc,
):
    add_parts(parts, tot)
    whole_gain(tot, 0, dgain, dbias)
    whole_gain(tot, 4, dgainp, dbiasp)
    acc[...] = jnp.zeros((M, 512), F32)

    def body(c):
        sl = cols(c)
        mean, scale = coefs(tot3, 0, sl, fs, INV_OUT)
        x = (pre3[:, sl] - mean) * scale
        dj = dj1[:, sl]
        du = (
            dj * expand([gate[b : b + 1, sl] for b in range(B)])
            + expand([dp[b : b + 1, sl] for b in range(B)])
        ) * keep[...]
        a, bb = means(tot, 0, sl, fs, INV_OUT)
        d = low((du - a - x * bb) * (scale * vec[0:1, sl]) * keep[...])
        d3[:, sl] = d
        acc[...] += mm_nt(d, w3[:, sl])
        mean, scale = coefs(tot3, 4, sl, fs, INV_OUT)
        x = (prep[:, sl] - mean) * scale
        a, bb = means(tot, 4, sl, fs, INV_OUT)
        dproj[:, sl] = low((dj - a - x * bb) * (scale * vec[2:3, sl]) * keep[...])

    loop(8, body)
    sl = slice(0, 512)
    mean, scale = coefs(tot2, 0, sl, fs, INV_OUT)
    x = (pre2[...] - mean) * scale
    o = x * gb[2:3, :] + gb[3:4, :]
    d = acc[...] * keep[...] * slope(o)
    do2[...] = d
    put(st, 0, back_rows(d, x, fs), sl)
    st[4:12, :] = bias[...]


def back_two_kernel(
    fs, parts, tot2, pre2, do2, x1, keep1, keep, gb, sh, ws,
    d2, do1, st, dgain, dbias, debias, dsbias, tot, dcol,
):
    add_parts(parts, tot)
    whole_gain(tot, 0, dgain, dbias)
    debias[...] = jnp.concatenate([tot[k : k + 1, :] for k in range(4, 8)], axis=1).reshape(2048)
    dsbias[...] = tot[8:9, 0:128].reshape(128)
    sl = slice(0, 512)
    mean, scale = coefs(tot2, 0, sl, fs, INV_OUT)
    x = (pre2[...] - mean) * scale
    a, bb = means(tot, 0, sl, fs, INV_OUT)
    d = low((do2[...] - a - x * bb) * (scale * gb[2:3, :]) * keep[...])
    d2[...] = d
    dcol[0] = d
    dcol[1] = low(mm(sh[5], d))
    dcol[2] = low(mm(sh[7], d))
    dcol[3] = low(mm(sh[8], d))
    terms = (
        ((0, 4),),
        ((0, 5), (1, 3)),
        ((0, 7), (2, 1)),
        ((0, 8), (1, 6), (2, 2), (3, 0)),
    )
    st[...] = jnp.zeros((4, 512), F32)
    for k in range(4):
        acc = 0.0
        for which, t in terms[k]:
            acc = acc + mm_nt(dcol[which], ws[t])
        x = x1[k]
        o = x * gb[0:1, :] + gb[1:2, :]
        d = acc * keep1[k] * slope(o)
        do1[k] = d
        rows = back_rows(d, x, fs)
        for r in range(4):
            st[r : r + 1, :] += rows[r]


def deal(isc, full, rows, keep, send, at):
    for p in range(16):
        tile = full[pl.ds(pl.multiple_of(isc[DEST + p] * rows, rows), rows), :]
        (keep if p < 8 else send)[p % 8, at_rows(at, rows), :] = tile


def back_one_kernel(
    fs, isc, parts, tot1, x1, do1, xp, keep1, gb, d1, gkeep, gsend, dgain, dbias, tot, dn, full
):
    n = isc[NARROW]
    add_parts(parts, tot)
    whole_gain(tot, 0, dgain, dbias)
    sl = slice(0, 512)
    scale = coefs(tot1, 0, sl, fs, INV_IN)[1] * gb[0:1, :]
    a, bb = means(tot, 0, sl, fs, INV_IN)
    planes = []
    for k in range(4):
        d = (do1[k] - a - x1[k] * bb) * scale * keep1[k]
        planes.append(d)
        dn[k] = low(d)
    for b in range(B):
        d1[b] = low(jnp.concatenate([d[b * POS : (b + 1) * POS] for d in planes], axis=0))

    def body(c):
        g = 0.0
        for k in range(4):
            g = g + mm_tn(xp[k, :, cols(c)], dn[k, :, cols(n)])
        full[cols(c), :] = low(g)

    loop(4, body)
    deal(isc, full, 64, gkeep, gsend, 0)


def image_kernel(own, pick_own, spread, d1, dproj, keep, w1, wp, out, dc, cc):
    for b in range(B):
        dc[b * HALF : (b + 1) * HALF, :] = low(mm(own[...], d1[b]))
    cc[...] = low(mm(pick_own[...], dproj[...]))

    def body(c):
        sl = cols(c)
        hi, lo = split2(mm_nt(cc[...], wp[sl, :]))
        v = mm_nt(dc[...], w1[sl, :]) + mm(spread[...], hi) + mm(spread[...], lo)
        out[:, sl] = v * keep[...]

    loop(4, body)


def grads_a_kernel(isc, h5, d6, col4, d5, gkeep, gsend, wider, full):
    n = isc[NARROW]

    def expand2(c):
        wider[:, cols(c)] = low(mm_tn(h5[:, cols(n)], d6[:, cols(c)]))

    loop(8, expand2)
    for p in range(16):
        sl = cols(isc[DEST + p], 128)
        for k in range(2):
            (gkeep if p < 8 else gsend)[p % 8, 0:128, k * 128 : (k + 1) * 128] = wider[
                k * 128 : (k + 1) * 128, sl
            ]

    def spatial(t):
        full[...] = low(mm_tn(col4[t], d5[:, cols(n)]))
        deal(isc, full, 32, gkeep, gsend, 128 + t * 32)

    loop(9, spatial)


def gate_grads(isc, n, c, at, squeezed, pooled, de, ds, gkeep, gsend, q, e):
    sl = cols(n * 4 + c)
    q[...] = outer(ds[...], pooled[:, sl])
    e[...] = outer(squeezed[...], de[:, sl])
    for p in range(16):
        rows = pl.ds(pl.multiple_of(isc[DEST + p] * 8, 8), 8)
        both = jnp.concatenate([q[rows, :], e[rows, :]], axis=0)
        (gkeep if p < 8 else gsend)[p % 8, at_rows(at + c * 16, 16), :] = low(both)


def grads_b_kernel(isc, d4, lows, squeezed, pooled, de, ds, gkeep, gsend, full, q, e):
    n = isc[NARROW]

    def body(c):
        full[...] = low(mm_tn(d4[...], lows[:, cols(n * 4 + c)]))
        deal(isc, full, 32, gkeep, gsend, c * 32)
        gate_grads(isc, n, c, 128, squeezed, pooled, de, ds, gkeep, gsend, q, e)

    loop(4, body)


def grads_c_kernel(
    isc, h2, d3, strided, dproj, sp, pooled, de, ds, gkeep, gsend, full, taller, q, e, squeezed
):
    n = isc[NARROW]
    squeezed[...] = sp[...] * sigmoid(sp[...])

    def body(c):
        sl = cols(n * 4 + c)
        full[...] = low(mm_tn(h2[...], d3[:, sl]))
        deal(isc, full, 32, gkeep, gsend, c * 32)
        taller[...] = low(mm_tn(strided[...], dproj[:, sl]))
        deal(isc, taller, 64, gkeep, gsend, 128 + c * 64)
        gate_grads(isc, n, c, 384, squeezed, pooled, de, ds, gkeep, gsend, q, e)

    loop(4, body)


def grads_d_kernel(isc, col1, d2, gkeep, gsend, full):
    n = isc[NARROW]

    def spatial(t):
        full[...] = low(mm_tn(col1[t], d2[:, cols(n)]))
        deal(isc, full, 32, gkeep, gsend, t * 32)

    loop(9, spatial)


def joined(v, out, at, rows):
    for c in range(4):
        out[:, c * 256 : (c + 1) * 256] = v[at + c * rows : at + (c + 1) * rows, :]


def unpack_gates(v, at, squeeze, excite):
    for c in range(4):
        part = v[at + c * 16 : at + (c + 1) * 16, :]
        squeeze[:, c * 256 : (c + 1) * 256] = part[0:8]
        excite[:, c * 256 : (c + 1) * 256] = part[8:16]


def unpack_a_kernel(a, b, expand2, spatial2):
    v = f32(a[0]) + f32(b[0])
    expand2[0:128, :] = v[0:128, 0:128]
    expand2[128:256, :] = v[0:128, 128:256]
    spatial2[...] = v[128:416, :]


def unpack_b_kernel(a, b, reduce2, squeeze2, excite2):
    v = f32(a[0]) + f32(b[0])
    joined(v, reduce2, 0, 32)
    unpack_gates(v, 128, squeeze2, excite2)


def unpack_c_kernel(a, b, expand1, project1, squeeze1, excite1):
    v = f32(a[0]) + f32(b[0])
    joined(v, expand1, 0, 32)
    joined(v, project1, 128, 64)
    unpack_gates(v, 384, squeeze1, excite1)


def unpack_d_kernel(a, b, spatial1):
    spatial1[...] = f32(a[0]) + f32(b[0])


REST = PACK_ROWS - W6_AT


def pack_kernel(
    isc, w5, w4, w6, ex, sq,
    g1, b1, g2, b2, g4, b4, g3, b3, gp, bp, eb1, sqb1, sqb2, g5, b5, g6, b6, eb2,
    out, w4_half, gb, vec1, sqb, vown, rest, rows, sems,
):
    core = isc[CORE]
    copies = copy_all(
        [
            (w4.at[at_rows(core * 512, 512)], w4_half),
            (w5.at[at_rows(core * 2304, 2304)], out.at[0:W6_AT]),
        ],
        sems,
    )

    def row(v):
        return f32(v[...]).reshape(1, v.shape[0])

    for k, v in enumerate((g1, b1, g2, b2, g4, b4)):
        gb[k : k + 1, :] = row(v)
    for k, v in enumerate((g3, b3, gp, bp, eb1)):
        vec1[k : k + 1, :] = row(v)
    for k, v in enumerate((sqb1, sqb2)):
        sqb[k : k + 1, :] = row(v)
    rows[...] = jnp.zeros((16, 256), F32)
    at = 0
    for v in (g5, b5, g6, b6, eb2):
        r = row(v)
        for c in range(v.shape[0] // 256):
            rows[at : at + 1, :] = r[:, c * 256 : (c + 1) * 256]
            at += 1
    vown[...] = low(rows[...])
    for c in range(8):
        rest[c * 128 : (c + 1) * 128, :] = w6[at_rows(core * 128, 128), c * 256 : (c + 1) * 256]
    for c in range(4):
        start = EX_AT - W6_AT + c * 64
        rest[start : start + 64, :] = ex[at_rows(core * 64, 64), c * 256 : (c + 1) * 256]
    for k in range(2):
        rest[SQ_AT - W6_AT : SQ_AT - W6_AT + 256, k * 128 : (k + 1) * 128] = sq[
            at_rows(core * 512 + k * 256, 256), :
        ]
    rest[VEC_AT - W6_AT : REST, :] = vown[...]
    last = pltpu.make_async_copy(rest, out.at[W6_AT:PACK_ROWS], sems.at[2])
    last.start()
    last.wait()
    wait_all(copies)


def call(body, outs, args, scratch=(), flops=1e8, size=5e6, name=None, vmem=LIMIT):
    specs, values = [], []
    for a in args:
        kind, v = a if isinstance(a, tuple) else (VMEM, a)
        specs.append(kind)
        values.append(v)
    return pl.pallas_call(
        body,
        out_shape=tuple(jax.ShapeDtypeStruct(o[0], o[1]) for o in outs),
        in_specs=specs,
        out_specs=tuple(o[2] if len(o) > 2 else VMEM for o in outs),
        scratch_shapes=list(scratch),
        compiler_params=pltpu.CompilerParams(vmem_limit_bytes=vmem * 2**20),
        cost_estimate=pl.CostEstimate(
            flops=int(flops), bytes_accessed=int(size), transcendentals=0
        ),
        name=name,
    )(*values)


def constants():
    perm = np.zeros((2, M, HALF), np.float32)
    for r in range(16):
        for c in range(14):
            place = (2 * (r % 2) + c % 2) * POS + (c // 2) * 8 + r // 2
            perm[r // 8, place, c * 8 + r % 8] = 1
    shift = np.zeros((9, M, M), np.float32)
    for di in range(3):
        for dj in range(3):
            for b in range(B):
                for i in range(8):
                    for j in range(7):
                        si, sj = i + di - 1, j + dj - 1
                        if 0 <= si < 8 and 0 <= sj < 7:
                            shift[3 * di + dj, b * POS + j * 8 + i, b * POS + sj * 8 + si] = 1
    pick_own = np.zeros((2, HALF, M), np.float32)
    spread = np.zeros((HROWS, HALF), np.float32)
    for b in range(B):
        for j in range(7):
            for i in range(4):
                for n in range(2):
                    pick_own[n, b * 28 + j * 4 + i, b * POS + j * 8 + n * 4 + i] = 1
                spread[b * HALF + 2 * j * 8 + 2 * i, b * 28 + j * 4 + i] = 1
    return perm, shift, pick_own, spread


def swap(v, axis, pairs):
    return lax.ppermute(v, axis, pairs)


def after(v, *others):
    return lax.optimization_barrier((v,) + others)[0]


def local(
    images, crop, micro,
    first_reduce, first_reduce_gain, first_reduce_bias,
    first_spatial, first_spatial_gain, first_spatial_bias,
    first_expand, first_expand_gain, first_expand_bias,
    first_project, first_project_gain, first_project_bias,
    first_squeeze, first_squeeze_bias, first_excite, first_excite_bias,
    second_reduce, second_reduce_gain, second_reduce_bias,
    second_spatial, second_spatial_gain, second_spatial_bias,
    second_expand, second_expand_gain, second_expand_bias,
    second_squeeze, second_squeeze_bias, second_excite, second_excite_bias,
    out_grad,
):
    wide = lax.axis_size("wide")
    n = lax.axis_index("narrow")
    exact = wide == 16
    near = [(i, i ^ 1) for i in range(wide)]
    pair = [(0, 1), (1, 0)]
    groups = [list(range(k, wide, 2)) for k in range(2)]
    V = pltpu.VMEM
    D = pltpu.SemaphoreType.DMA
    f = lambda *shape: (shape, F32)
    h = lambda *shape: (shape, BF)

    def across(x):
        x = x + swap(x, "wide", near)
        sent = jnp.broadcast_to(x[None], (wide // 2,) + x.shape)
        got = lax.all_to_all(sent, "wide", 0, 0, axis_index_groups=groups, tiled=True)
        return got if exact else jnp.sum(got, axis=0, keepdims=True)

    def steps(x):
        step = 1
        while step < wide:
            x = x + swap(x, "wide", [(i, i ^ step) for i in range(wide)])
            step *= 2
        return x[None]

    perm_np, shift_np, pick_np, spread_np = constants()
    perm, sh = jnp.asarray(perm_np, BF), jnp.asarray(shift_np, BF)

    own_px = images.transpose(0, 2, 1, 3).reshape(B, HALF, 1024)
    other_px = swap(own_px, "narrow", pair)

    fs_, isc_, keep, keep1, keep_half = call(
        functools.partial(setup_kernel, exact),
        [((13,), F32, SMEM), ((18,), jnp.int32, SMEM), f(M, 1), f(4, M, 1), f(HROWS, 1)],
        [(SMEM, crop), (SMEM, micro)], name="setup",
    )
    fs, isc = (SMEM, fs_), (SMEM, isc_)
    st1 = call(
        one_half_kernel, [f(4, 512)], [fs, own_px.reshape(HROWS, 1024), keep_half, first_reduce],
        flops=5e8, name="one_half",
    )[0]
    part = jnp.sum(across(st1), axis=0)
    part_other = swap(part, "narrow", pair)

    w5_own = second_spatial.reshape(9 * 512, 256)
    pack, w4_half, gb, vec1, sqb, vown = call(
        pack_kernel,
        [
            ((PACK_ROWS, 256), BF, ANY), ((512, 512), BF, ANY), f(8, 512), f(8, 2048), f(8, 128), h(16, 256),
        ],
        [
            (SMEM, after(isc_, st1)), (ANY, w5_own), (ANY, second_reduce), second_expand, second_excite, second_squeeze,
            first_reduce_gain, first_reduce_bias, first_spatial_gain, first_spatial_bias,
            second_reduce_gain, second_reduce_bias, first_expand_gain, first_expand_bias,
            first_project_gain, first_project_bias, first_excite_bias,
            first_squeeze_bias, second_squeeze_bias,
            second_spatial_gain, second_spatial_bias, second_expand_gain, second_expand_bias, second_excite_bias,
        ],
        [V((REST, 256), BF), V((16, 256), F32), D((3,))],
        size=1e7, name="pack",
    )
    w4_r1 = swap(after(w4_half, other_px, part_other), "narrow", pair)
    pk1 = swap(after(pack, other_px, part_other), "narrow", pair)
    og_own = out_grad.transpose(0, 2, 1, 3).reshape(M, 1024)
    ws = first_spatial.reshape(9, 512, 512)

    xp, strided, x1, col1, pre2, st2, tot1 = call(
        stage_two_kernel,
        [h(4, M, 1024), h(M, 1024), f(4, M, 512), h(9, M, 512), f(M, 512), f(4, 512), f(4, 512)],
        [
            fs, isc, (ANY, own_px), (ANY, other_px), part, part_other, perm, keep1, keep,
            first_reduce, ws, gb, sh,
        ],
        [V((2, B, HALF, 1024), BF), V((4, M, 256), F32), V((4, M, 512), BF), V((4, 512), F32), D((2,))],
        flops=4e9, size=2e7, name="stage_two",
    )
    parts2 = across(st2)
    w4_r2 = swap(after(w4_r1, st2), "wide", near)
    w4_refs = [(ANY, second_reduce), (ANY, w4_r1), (ANY, w4_r2)]
    prep, stp = call(
        project_kernel, [f(M, 2048), f(4, 2048)], [fs, after(strided, w4_r1), keep, first_project],
        flops=1e9, size=8e6, name="project",
    )
    h2, pre3, st3, tot2 = call(
        stage_three_kernel, [h(M, 512), f(M, 2048), f(8, 2048), f(4, 512)],
        [fs, parts2, pre2, stp, keep, first_expand, gb], [V((4, 512), F32)],
        flops=1e9, size=6e6, name="stage_three",
    )
    parts3 = steps(st3)
    lows, pre4, st4, tot3, gate1, sp1, pooled1, squares = call(
        stage_four_kernel,
        [
            h(M, 2048), f(M, 512), f(4, 512), f(8, 2048), f(8, 2048), f(8, 128), f(8, 2048), f(8, 256),
        ],
        [fs, isc, parts3, pre3, prep, keep, vec1, sqb, first_squeeze, first_excite] + w4_refs,
        [V((M, 2048), F32), V((M, 2048), F32), V((2048, 512), BF), V((M, 512), F32), V((8, 2048), F32), D((3,))],
        flops=1e9, size=1e7, name="stage_four",
    )
    parts4 = across(st4)
    pk2 = swap(after(pk1, st4), "wide", near)
    og_other = swap(after(og_own, pk1, st4), "narrow", pair)
    w5_refs = [(ANY, w5_own), (ANY, pk1), (ANY, pk2)]
    w6_refs = [(ANY, second_expand), (ANY, pk1), (ANY, pk2)]
    col4, pre5, st5, tot4, gain5, vec2 = call(
        stage_five_kernel,
        [h(9, M, 512), f(M, 512), f(4, 512), f(4, 512), f(2, 512), f(3, 2048)],
        [fs, isc, parts4, pre4, keep, gb, sh, vown] + w5_refs,
        [V((2, 4608, 256), BF), V((4, 512), F32), V((16, 256), BF), D((4,))],
        flops=2e9, size=1e7, name="stage_five",
    )
    parts5 = across(st5)
    h5, pre6, st6, tot5 = call(
        stage_six_kernel, [h(M, 512), f(M, 2048), f(4, 2048), f(4, 512)],
        [fs, isc, parts5, pre5, keep, gain5] + w6_refs,
        [V((512, 2048), BF), V((4, 512), F32), D((17,))],
        flops=1e9, size=6e6, name="stage_six",
    )
    parts6 = across(st6)
    result, dj2, pay6, extra6, tot6, gate2, dp2, pooled2, de2, ds2, sq2 = call(
        turn_kernel,
        [
            h(M, 1024), f(M, 2048), f(4, 2048), f(8, 512), f(4, 2048), f(8, 2048),
            f(8, 2048), f(8, 2048), f(8, 2048), f(8, 128), f(8, 128),
        ],
        [
            fs, isc, parts6, pre6, keep, lows, vec2, sqb, squares,
            (ANY, second_squeeze), (ANY, second_excite), (ANY, pk1), (ANY, pk2), (ANY, og_own), (ANY, og_other),
        ],
        [
            V((M, 2048), F32), V((2, M, 1024), BF), V((2, M, 1024), BF), V((2048, 128), BF),
            V((2, 128, 1024), BF), V((4, 2048), F32), V((8, 128), F32), D((16,)),
        ],
        flops=1e9, size=1e7, name="turn",
    )
    back6 = across(pay6)
    d6, do5, bt5, dgain6, dbias6 = call(
        back_six_kernel, [h(M, 2048), f(M, 512), f(12, 512), f(1024), f(1024)],
        [fs, isc, back6, tot6, pre6, dj2, gate2, dp2, pre5, tot5, extra6, keep, vec2, gain5] + w6_refs,
        [V((512, 2048), BF), V((4, 2048), F32), V((M, 512), F32), D((17,))],
        flops=1e9, size=1e7, name="back_six",
    )
    back5 = across(bt5)
    d5, do4, bt4, dgain5, dbias5, debias2, dsbias2, norms = call(
        back_five_kernel,
        [h(M, 512), f(M, 512), f(4, 512), f(256), f(256), f(1024), f(128), ((5,), F32, SMEM)],
        [fs, isc, back5, tot5, pre5, do5, pre4, tot4, keep, gb, gain5, sh] + w5_refs,
        [V((2, 4608, 256), BF), V((12, 512), F32), D((3,))],
        flops=2e9, size=1e7, name="back_five",
    )
    back4 = across(bt4)

    def step(g, k):
        if not exact:
            return g
        partner = [(i, i ^ (1 << k)) for i in range(wide)]
        if k == 0:
            return g[0] + swap(g[1], "wide", partner)
        half = g.shape[0] // 2
        return g[:half] + swap(g[half:], "wide", partner)

    def last_step(g):
        return g[:1], swap(g[1:], "wide", [(i, i ^ 8) for i in range(wide)])

    ga = call(
        grads_a_kernel, [h(8, 416, 256)] * 2, [isc, h5, d6, col4, d5],
        [V((256, 2048), BF), V((512, 256), BF)], flops=2e9, size=1e7, name="grads_a",
    )
    back4, ga = lax.optimization_barrier((back4, ga))
    d4, dj1, bt3, dgain4, dbias4, dp1, de1, ds1, bias1 = call(
        back_four_kernel,
        [
            h(M, 512), f(M, 2048), f(8, 2048), f(512), f(512), f(8, 2048),
            f(8, 2048), f(8, 128), f(8, 512),
        ],
        [
            fs, isc, back4, tot4, pre4, do4, dj2, tot3, pre3, prep, gate1, sp1, keep, gb, vec1,
            first_squeeze, first_excite,
        ] + w4_refs,
        [V((2048, 512), BF), V((4, 512), F32), D((3,))],
        flops=1e9, size=1e7, name="back_four",
    )
    back3 = steps(bt3)
    ga = step(ga, 0)
    gb1 = call(
        grads_b_kernel, [h(8, 192, 256)] * 2, [isc, d4, lows, sq2, pooled2, de2, ds2],
        [V((512, 256), BF), V((128, 256), F32), V((128, 256), F32)],
        flops=1e9, size=4e6, name="grads_b",
    )
    back3, ga, gb1 = lax.optimization_barrier((back3, ga, gb1))
    d3, dproj, do2, bt2, dgain3, dbias3, dgainp, dbiasp = call(
        back_three_kernel,
        [h(M, 2048), h(M, 2048), f(M, 512), f(12, 512), f(2048), f(2048), f(2048), f(2048)],
        [fs, back3, tot3, pre3, prep, dj1, gate1, dp1, bias1, pre2, tot2, keep, vec1, gb, first_expand],
        [V((8, 2048), F32), V((M, 512), F32)],
        flops=1e9, size=1e7, name="back_three",
    )
    back2 = across(bt2)
    ga, gb1 = step(ga, 1), step(gb1, 0)
    gc = call(
        grads_c_kernel, [h(8, 448, 256)] * 2,
        [isc, h2, d3, strided, dproj, sp1, pooled1, de1, ds1],
        [V((512, 256), BF), V((1024, 256), BF), V((128, 256), F32), V((128, 256), F32), V((8, 128), F32)],
        flops=3e9, size=1e7, name="grads_c",
    )
    back2, ga, gb1, gc = lax.optimization_barrier((back2, ga, gb1, gc))
    d2, do1, bt1, dgain2, dbias2, debias1, dsbias1 = call(
        back_two_kernel,
        [h(M, 512), f(4, M, 512), f(4, 512), f(512), f(512), f(2048), f(128)],
        [fs, back2, tot2, pre2, do2, x1, keep1, keep, gb, sh, ws],
        [V((12, 512), F32), V((4, M, 512), BF)],
        flops=2e9, size=1e7, name="back_two",
    )
    back1 = across(bt1)
    ga, gb1, gc = step(ga, 2), step(gb1, 1), step(gc, 0)
    gd = call(
        grads_d_kernel, [h(8, 288, 256)] * 2, [isc, col1, d2], [V((512, 256), BF)],
        flops=2e9, size=6e6, name="grads_d",
    )
    back1, ga, gb1, gc, gd = lax.optimization_barrier((back1, ga, gb1, gc, gd))
    d1, ge_keep, ge_send, dgain1, dbias1 = call(
        back_one_kernel, [h(B, M, 512), h(8, 64, 256), h(8, 64, 256), f(512), f(512)],
        [fs, isc, back1, tot1, x1, do1, xp, keep1, gb],
        [V((4, 512), F32), V((4, M, 512), BF), V((1024, 256), BF)],
        flops=1e9, size=6e6, name="back_one",
    )
    ge = (ge_keep, ge_send)
    dimg = call(
        image_kernel, [f(HROWS, 1024)],
        [
            perm.transpose(0, 2, 1)[n], jnp.asarray(pick_np, BF)[n], jnp.asarray(spread_np, BF),
            d1, dproj, keep_half, first_reduce, first_project,
        ],
        [V((HROWS, 512), BF), V((HALF, 2048), BF)],
        flops=1e9, size=1e7, name="image",
    )[0]

    if exact:
        for k in range(1, 4):
            gb1 = step(gb1, k) if k == 2 else gb1
            gc = step(gc, k) if k < 3 else gc
        gd, ge = step(step(gd, 0), 1), step(ge, 0)
        gd, ge, dimg = lax.optimization_barrier((gd, ge, dimg))
        gd, ge = step(gd, 2), step(step(ge, 1), 2)
        expand2, spatial2 = call(
            unpack_a_kernel, [f(256, 128), f(288, 256)], list(last_step(ga)), name="unpack_a"
        )
        reduce2, squeeze2, excite2 = call(
            unpack_b_kernel, [f(32, 1024), f(8, 1024), f(8, 1024)], list(last_step(gb1)), name="unpack_b"
        )
        expand1, project1, squeeze1, excite1 = call(
            unpack_c_kernel, [f(32, 1024), f(64, 1024), f(8, 1024), f(8, 1024)], list(last_step(gc)),
            name="unpack_c",
        )
        spatial1 = call(unpack_d_kernel, [f(288, 256)], list(last_step(gd)), name="unpack_d")[0]
        reduce1 = call(unpack_d_kernel, [f(64, 256)], list(last_step(ge)), name="unpack_e")[0]
    else:
        finer = wide // 16

        def summed(g):
            return lax.psum_scatter(g, "wide", scatter_dimension=0, tiled=True)

        def blocks(g, start, count, rows):
            p = g[:, start : start + count * rows].reshape(16, count, finer, rows // finer, 256)
            p = summed(p.transpose(0, 2, 1, 3, 4).reshape(wide, count, rows // finer, 256))[0]
            return f32(p).transpose(1, 0, 2).reshape(rows // finer, count * 256)

        def both(g, start):
            p = g[:, start : start + 64].reshape(16, 4, 2, finer, 8 // finer, 256)
            p = f32(summed(p.transpose(0, 3, 1, 2, 4, 5).reshape(wide, 4, 2, -1, 256))[0])
            return [p[:, k].transpose(1, 0, 2).reshape(-1, 1024) for k in range(2)]

        def taps(g, start):
            p = g[:, start : start + 288].reshape(16, 9, finer, 32 // finer, 256)
            return f32(summed(p.transpose(0, 2, 1, 3, 4).reshape(wide, 9, -1, 256))[0]).reshape(-1, 256)

        ga, gb1, gc, gd, ge = (jnp.concatenate(g) for g in (ga, gb1, gc, gd, ge))
        e2 = ga[:, 0:128].reshape(16, 128, 2, finer, 128 // finer).transpose(0, 3, 1, 2, 4)
        e2 = summed(e2.reshape(wide, 1, -1)).reshape(128, 2, -1)
        expand2 = f32(e2.transpose(1, 0, 2).reshape(256, -1))
        spatial2 = taps(ga, 128)
        reduce2 = blocks(gb1, 0, 4, 32)
        squeeze2, excite2 = both(gb1, 128)
        expand1, project1 = blocks(gc, 0, 4, 32), blocks(gc, 128, 4, 64)
        squeeze1, excite1 = both(gc, 384)
        spatial1, reduce1 = taps(gd, 0), blocks(ge, 0, 1, 64)
    return (
        result.reshape(B, 7, 8, 1024).transpose(0, 2, 1, 3),
        dimg.reshape(B, 14, 8, 1024).transpose(0, 2, 1, 3),
        reduce1, dgain1, dbias1,
        spatial1.reshape(3, 3, -1, 256), dgain2, dbias2,
        expand1, dgain3, dbias3,
        project1, dgainp, dbiasp,
        squeeze1.T, dsbias1, excite1, debias1,
        reduce2.T, dgain4, dbias4,
        spatial2.reshape(3, 3, -1, 256), dgain5, dbias5,
        expand2, dgain6, dbias6,
        squeeze2.T, dsbias2, excite2, debias2,
        norms,
    )


def solution(mesh):
    rep, nar = P(), P("narrow")
    return jax.shard_map(
        local,
        mesh=mesh,
        in_specs=(P("wide", "narrow", None, None),) + (rep,) * 18 + (
            P("narrow", None), rep, rep,
            P(None, None, None, "narrow"), nar, nar,
            P("narrow", None), nar, nar,
            P("narrow", None), rep, P(None, "narrow"), nar,
            P("wide", None, None, "narrow"),
        ),
        out_specs=(
            P("wide", None, None, "narrow"), P("wide", "narrow", None, None),
            P("wide", "narrow"), rep, rep,
            P(None, None, "wide", "narrow"), rep, rep,
            P("wide", "narrow"), rep, rep,
            P("wide", "narrow"), rep, rep,
            P("narrow", "wide"), rep, P("wide", "narrow"), rep,
            P("narrow", "wide"), rep, rep,
            P(None, None, "wide", "narrow"), nar, nar,
            P("narrow", "wide"), nar, nar,
            P("narrow", "wide"), rep, P("wide", "narrow"), nar,
            rep,
        ),
        check_vma=False,
    )
```

```python
import functools

import numpy as np
import jax
import jax.numpy as jnp
from jax import lax
from jax.experimental import pallas as pl
from jax.experimental.pallas import tpu as pltpu
from jax.sharding import PartitionSpec as P

EPSILON = 1e-05
BF = jnp.bfloat16
F32 = jnp.float32
B = 4
POS = 56
LIMIT = 14
M = B * POS
HALF = 112
HROWS = B * HALF
VMEM = pl.BlockSpec(memory_space=pltpu.VMEM)
SMEM = pl.BlockSpec(memory_space=pltpu.SMEM)
ANY = pl.BlockSpec(memory_space=pl.ANY)
INV_IN, INV_OUT, CELLS, MICRO, INV_ALL = 0, 2, 4, 8, 12
NARROW, CORE, DEST = 0, 1, 2
W6_AT, EX_AT, SQ_AT, VEC_AT, PACK_ROWS = 2304, 3328, 3584, 3840, 3856


def mm(a, b):
    return lax.dot_general(a, b, (((1,), (0,)), ((), ())), preferred_element_type=F32)


def mm_nt(a, b):
    return lax.dot_general(a, b, (((1,), (1,)), ((), ())), preferred_element_type=F32)


def mm_tn(a, b):
    return lax.dot_general(a, b, (((0,), (0,)), ((), ())), preferred_element_type=F32)


def f32(v):
    return v.astype(F32)


def low(v):
    return v.astype(BF)


def split2(v):
    a = low(v)
    return a, low(v - f32(a))


def split3(v):
    a = low(v)
    r = v - f32(a)
    b = low(r)
    return a, b, low(r - f32(b))


def dot3(v, w):
    return sum(mm(p, w) for p in split3(v))


def dot3_nt(v, w):
    return sum(mm_nt(p, w) for p in split3(v))


def outer(a, b):
    a1, a2 = split2(a)
    b1, b2 = split2(b)
    return mm_tn(a1, b1) + mm_tn(a1, b2) + mm_tn(a2, b1)


def sigmoid(v):
    return 1.0 / (1.0 + jnp.exp(-v))


def slope(v):
    s = sigmoid(v)
    return s * (1.0 + v * (1.0 - s))


def cols(c, size=256):
    return pl.ds(pl.multiple_of(c * size, size), size)


def expand(rows):
    return jnp.concatenate([jnp.broadcast_to(r, (POS, r.shape[1])) for r in rows], axis=0)


def pick(r0, r1, fs):
    return expand([r0 * (1.0 - fs[MICRO + b]) + r1 * fs[MICRO + b] for b in range(B)])


def image_sums(v):
    return [jnp.sum(v[b * POS : (b + 1) * POS], axis=0, keepdims=True) for b in range(B)]


def grouped(sums, fs, reps=1):
    zero = one = 0.0
    for b in range(B):
        zero = zero + sums[b] * (1.0 - fs[MICRO + b])
        one = one + sums[b] * fs[MICRO + b]
    return [zero, one]


def group_sums(v, fs):
    return grouped(image_sums(v), fs)


def put(ref, at, rows, sl):
    for k, r in enumerate(rows):
        ref[at + k : at + k + 1, sl] = r


def add_parts(parts, tot):
    t = parts[0]
    for k in range(1, parts.shape[0]):
        t = t + parts[k]
    tot[...] = t


def coefs(tot, at, sl, fs, inv):
    i0, i1 = fs[inv], fs[inv + 1]
    m0, m1 = tot[at : at + 1, sl] * i0, tot[at + 1 : at + 2, sl] * i1
    q0 = lax.rsqrt(tot[at + 2 : at + 3, sl] * i0 - m0 * m0 + EPSILON)
    q1 = lax.rsqrt(tot[at + 3 : at + 4, sl] * i1 - m1 * m1 + EPSILON)
    return pick(m0, m1, fs), pick(q0, q1, fs)


def means(tot, at, sl, fs, inv):
    i0, i1 = fs[inv], fs[inv + 1]
    a = pick(tot[at : at + 1, sl] * i0, tot[at + 1 : at + 2, sl] * i1, fs)
    b = pick(tot[at + 2 : at + 3, sl] * i0, tot[at + 3 : at + 4, sl] * i1, fs)
    return a, b


def stat_rows(v, keep, fs):
    kept = v * keep
    return group_sums(kept, fs) + group_sums(kept * v, fs)


def back_rows(d, x, fs):
    return group_sums(d, fs) + group_sums(d * x, fs)


def loop(count, body):
    lax.fori_loop(0, count, lambda c, _: (body(c), 0)[1], 0)


def loop_from(first, last, body):
    lax.fori_loop(first, last, lambda c, _: (body(c), 0)[1], 0)


def copy_all(pairs, sems):
    copies = [pltpu.make_async_copy(s, d, sems.at[k]) for k, (s, d) in enumerate(pairs)]
    for c in copies:
        c.start()
    return copies


def wait_all(copies):
    for c in copies:
        c.wait()


def at_rows(start, size):
    return pl.ds(pl.multiple_of(start, 16), size)


def flip(p):
    return (p & 1) * 8 + (p & 2) * 2 + (p & 4) // 2 + (p & 8) // 8


def setup_kernel(exact, crop, micro, fs, isc, keep, keep1, keep_half, sh, perm):
    n = lax.axis_index("narrow").astype(jnp.int32)
    w = lax.axis_index("wide").astype(jnp.int32)
    isc[NARROW] = n
    isc[CORE] = w & 1
    for p in range(16):
        isc[DEST + p] = (w ^ flip(p)) if exact else jnp.int32(p)

    def count(k, sums):
        c, one = crop[k], micro[k]
        a, b = (c >> 4) * (c >> 4), (c >> 5) * (c >> 5)
        return (
            sums[0] + a * (1 - one), sums[1] + a * one, sums[2] + b * (1 - one), sums[3] + b * one,
        )

    zero = jnp.int32(0)
    sums = lax.fori_loop(0, crop.shape[0], count, (zero, zero, zero, zero))
    for k in range(4):
        fs[k] = 1.0 / sums[k].astype(F32)
    fs[INV_ALL] = 1.0 / ((sums[2] + sums[3]).astype(F32) * 2048.0)
    at = lax.broadcasted_iota(jnp.int32, (POS, 1), 0)
    i8, j7 = at & 7, at >> 3
    at = lax.broadcasted_iota(jnp.int32, (HALF, 1), 0)
    r8, c14 = n * 8 + (at & 7), at >> 3

    def inside(r, c, side):
        return jnp.where((r < side) & (c < side), 1.0, 0.0).astype(F32)

    for b in range(B):
        c = crop[w * B + b]
        side_in, side_out = c >> 4, c >> 5
        fs[CELLS + b] = 1.0 / (side_out * side_out).astype(F32)
        fs[MICRO + b] = micro[w * B + b].astype(F32)
        keep[b * POS : (b + 1) * POS, :] = inside(i8, j7, side_out)
        for k in range(4):
            keep1[k, b * POS : (b + 1) * POS, :] = inside(2 * i8 + k // 2, 2 * j7 + k % 2, side_in)
        keep_half[b * HALF : (b + 1) * HALF, :] = inside(r8, c14, side_in)
    place = lax.broadcasted_iota(jnp.int32, (POS, M), 1)
    it = lax.broadcasted_iota(jnp.int32, (POS, M), 0)
    for t in range(9):
        di, dj = t // 3 - 1, t % 3 - 1
        i, j = (it & 7) + di, (it >> 3) + dj
        fits = (i >= 0) & (i < 8) & (j >= 0) & (j < 7)
        sh[t] = low(jnp.concatenate([
            jnp.where(fits & (place == b * POS + j * 8 + i), 1.0, 0.0) for b in range(B)
        ], axis=0))
    place = lax.broadcasted_iota(jnp.int32, (POS, HALF), 1)
    it = lax.broadcasted_iota(jnp.int32, (POS, HALF), 0)
    for half in range(2):
        planes = []
        for k in range(4):
            r, c = 2 * (it & 7) + k // 2, 2 * (it >> 3) + k % 2
            planes.append(
                jnp.where(((r >> 3) == half) & (place == c * 8 + (r & 7)), 1.0, 0.0)
            )
        perm[half] = low(jnp.concatenate(planes, axis=0))


def one_half_kernel(fs, px, keep, w1_far, st, x, w1, flat, sems):
    copies = copy_all([(px, x), (w1_far, w1)], sems)
    copies[0].wait()
    for b in range(B):
        flat[b * HALF : (b + 1) * HALF, :] = x[b]
    copies[1].wait()

    def body(c):
        sl = cols(c)
        v = mm(flat[...], w1[:, sl]) * keep[...]
        sums = [jnp.sum(v[b * HALF : (b + 1) * HALF], axis=0, keepdims=True) for b in range(B)]
        v2 = v * v
        sq = [jnp.sum(v2[b * HALF : (b + 1) * HALF], axis=0, keepdims=True) for b in range(B)]
        put(st, 0, grouped(sums, fs) + grouped(sq, fs), sl)

    loop(2, body)


TAPS = [(p, q) for p in range(3) for q in range(3)]


def stage_two_kernel(
    fs, isc, own, other, part, part_other, perm, keep1, keep, w1, ws, gb, sh,
    xp, strided, x1, col, pre2, st, tot1, tmp, hid, tot,
):
    n = isc[NARROW]
    tot[...] = part[...] + part_other[...]
    tot1[...] = tot[...]

    def permute(c):
        sl = cols(c)
        for b in range(B):
            r = mm(perm[n], own[b, :, sl]) + mm(perm[1 - n], other[b, :, sl])
            for k in range(4):
                tmp[k, b * POS : (b + 1) * POS, :] = r[k * POS : (k + 1) * POS]
        for k in range(4):
            xp[k, :, sl] = low(tmp[k] * keep1[k])
        strided[:, sl] = xp[0, :, sl]

    loop(4, permute)

    def first(c):
        k, sl = c // 2, cols(c % 2)
        v = mm(xp[k], w1[:, sl])
        mean, scale = coefs(tot, 0, sl, fs, INV_IN)
        x = (v - mean) * scale
        x1[k, :, sl] = x
        o = x * gb[0:1, sl] + gb[1:2, sl]
        hid[k, :, sl] = low(o * sigmoid(o) * keep1[k])

    loop(8, first)
    for t, (p, q) in enumerate(TAPS):
        h = hid[2 * (p != 1) + (q != 1)]
        if p == 0 or q == 0:
            h = low(mm(sh[3 * (0 if p == 0 else 1) + (0 if q == 0 else 1)], h))
        col[t] = h

    def second(c):
        sl = cols(c)
        v = mm(col[0], ws[0, :, sl])
        for t in range(1, 9):
            v = v + mm(col[t], ws[t, :, sl])
        pre2[:, sl] = v
        put(st, 0, stat_rows(v, keep[...], fs), sl)

    loop(2, second)


def project_kernel(fs, x, keep, wp_far, w3_far, prep, st, w3, wp, sems):
    copies = []
    for c in range(4):
        sl = slice(c * 512, (c + 1) * 512)
        copies.append(pltpu.make_async_copy(wp_far.at[:, sl], wp.at[:, sl], sems.at[c]))
    copies.append(pltpu.make_async_copy(w3_far, w3, sems.at[4]))
    for c in copies:
        c.start()

    def body(c):
        sl = cols(c)
        v = mm(x[...], wp[:, sl])
        prep[:, sl] = v
        put(st, 0, stat_rows(v, keep[...], fs), sl)

    for c in range(4):
        copies[c].wait()
        loop_from(2 * c, 2 * c + 2, body)
    copies[4].wait()


def stage_three_kernel(fs, parts, pre2, stp, keep, w3, gb, h2, pre3, st, tot2, tot):
    add_parts(parts, tot)
    tot2[...] = tot[...]
    sl = slice(0, 512)
    mean, scale = coefs(tot, 0, sl, fs, INV_OUT)
    o = (pre2[...] - mean) * scale * gb[2:3, :] + gb[3:4, :]
    h2[...] = low(o * sigmoid(o) * keep[...])
    st[4:8, :] = stp[...]

    def body(c):
        sl = cols(c)
        v = mm(h2[...], w3[:, sl])
        pre3[:, sl] = v
        put(st, 0, stat_rows(v, keep[...], fs), sl)

    loop(8, body)


def fetch_four_kernel(isc, own, r1, r2, w4, sems):
    n, core = isc[NARROW], isc[CORE]
    away = (1 - n) * 1024
    wait_all(copy_all(
        [
            (own, w4.at[at_rows(n * 1024, 1024)]),
            (r1, w4.at[at_rows(away + core * 512, 512)]),
            (r2, w4.at[at_rows(away + (1 - core) * 512, 512)]),
        ],
        sems,
    ))


def stage_four_kernel(
    fs, parts, pre3, prep, keep, vec, sqb, sq_far, ex_far, w4,
    lows, pre4, st, tot3, gate, sp, pooled, squares, unit, short, acc, tot, sq, ex, sems,
):
    copies = copy_all([(sq_far, sq), (ex_far, ex)], sems)
    add_parts(parts, tot)
    tot3[...] = tot[...]
    pooled[...] = jnp.zeros((8, 2048), F32)

    def units(c):
        sl = cols(c)
        mean, scale = coefs(tot, 0, sl, fs, INV_OUT)
        u = ((pre3[:, sl] - mean) * scale * vec[0:1, sl] + vec[1:2, sl]) * keep[...]
        unit[:, sl] = u
        for b, r in enumerate(image_sums(u)):
            pooled[b : b + 1, sl] = r * fs[CELLS + b]
        mean, scale = coefs(tot, 4, sl, fs, INV_OUT)
        s = ((prep[:, sl] - mean) * scale * vec[2:3, sl] + vec[3:4, sl]) * keep[...]
        short[:, sl] = s

    loop(8, units)
    wait_all(copies)
    sp[...] = dot3(pooled[...], sq[...]) + sqb[0:1, :]
    squeezed = sp[...] * sigmoid(sp[...])
    gate[...] = sigmoid(dot3(squeezed, ex[...]) + vec[4:5, :])
    squares[...] = jnp.zeros((8, 256), F32)
    acc[...] = jnp.zeros((M, 512), F32)

    def streams(c):
        sl = cols(c)
        branch = unit[:, sl] * expand([gate[b : b + 1, sl] for b in range(B)])
        s = short[:, sl]
        join = branch + s
        stream = join * sigmoid(join) * keep[...]
        for k, v in enumerate((stream, branch, s)):
            squares[k : k + 1, :] += jnp.sum(v * v, axis=0, keepdims=True)
        lo = low(stream)
        lows[:, sl] = lo
        acc[...] += mm(lo, w4[cols(c), :])

    loop(8, streams)
    pre4[...] = acc[...]
    put(st, 0, stat_rows(acc[...], keep[...], fs), slice(0, 512))


def fetch_five_kernel(isc, own, r1, r2, w5, vaway, sems):
    n, core = isc[NARROW], isc[CORE]
    wait_all(copy_all([
        (r1.at[VEC_AT:PACK_ROWS], vaway),
        (own, w5.at[n]),
        (r1.at[0:2304], w5.at[1 - n, at_rows(core * 2304, 2304)]),
        (r2.at[0:2304], w5.at[1 - n, at_rows((1 - core) * 2304, 2304)]),
    ], sems))


def stage_five_kernel(
    fs, isc, parts, pre4, keep, gb, sh, vown, vaway, w5, col, pre5, st, tot4, gain5, vec2, tot,
):
    n = isc[NARROW]
    add_parts(parts, tot)
    tot4[...] = tot[...]
    mean, scale = coefs(tot, 0, slice(0, 512), fs, INV_OUT)
    o = (pre4[...] - mean) * scale * gb[4:5, :] + gb[5:6, :]
    h = low(o * sigmoid(o) * keep[...])
    for t in range(9):
        col[t] = h if t == 4 else low(mm(sh[t], h))
    for side, v in ((n, f32(vown[...])), (1 - n, f32(vaway[...]))):
        for k in range(2):
            gain5[k : k + 1, cols(side)] = v[k : k + 1]
        for k in range(3):
            for c in range(4):
                at = 2 + 4 * k + c
                vec2[k : k + 1, cols(side * 4 + c)] = v[at : at + 1]

    def body(c):
        v = 0.0
        for t in range(9):
            v = v + mm(col[t], w5[c, t * 512 : (t + 1) * 512, :])
        pre5[:, cols(c)] = v
        put(st, 0, stat_rows(v, keep[...], fs), cols(c))

    loop(2, body)


def fetch_six_kernel(isc, own, r1, r2, w6, sems):
    n, core = isc[NARROW], isc[CORE]
    pairs = [(own, w6.at[at_rows(n * 256, 256)])]
    for r, h in ((r1, core), (r2, 1 - core)):
        for c in range(8):
            pairs.append(
                (
                    r.at[W6_AT + c * 128 : W6_AT + (c + 1) * 128],
                    w6.at[at_rows((1 - n) * 256 + h * 128, 128), c * 256 : (c + 1) * 256],
                )
            )
    wait_all(copy_all(pairs, sems))


def stage_six_kernel(
    fs, parts, pre5, keep, gain5, w6, h5, pre6, st, tot5, tot
):
    add_parts(parts, tot)
    tot5[...] = tot[...]
    mean, scale = coefs(tot, 0, slice(0, 512), fs, INV_OUT)
    o = (pre5[...] - mean) * scale * gain5[0:1, :] + gain5[1:2, :]
    h5[...] = low(o * sigmoid(o) * keep[...])

    def body(c):
        sl = cols(c)
        v = mm(h5[...], w6[:, sl])
        pre6[:, sl] = v
        put(st, 0, stat_rows(v, keep[...], fs), sl)

    loop(8, body)


def fetch_turn_kernel(isc, sqown, exown, r1, r2, ogown, ogother, sq, ex, og, sems):
    n, core = isc[NARROW], isc[CORE]
    pairs = [
        (sqown, sq.at[at_rows(n * 1024, 1024)]),
        (exown, ex.at[n]),
        (ogown, og.at[n]),
        (ogother, og.at[1 - n]),
    ]
    for r, h in ((r1, core), (r2, 1 - core)):
        for k in range(2):
            pairs.append(
                (
                    r.at[SQ_AT : SQ_AT + 256, k * 128 : (k + 1) * 128],
                    sq.at[at_rows((1 - n) * 1024 + h * 512 + k * 256, 256)],
                )
            )
        for c in range(4):
            pairs.append(
                (
                    r.at[EX_AT + c * 64 : EX_AT + (c + 1) * 64],
                    ex.at[1 - n, at_rows(h * 64, 64), c * 256 : (c + 1) * 256],
                )
            )
    wait_all(copy_all(pairs, sems))


def turn_kernel(
    fs, isc, parts, pre6, keep, lows, vec, sqb, sq1s, sq, ex, og,
    result, dj2, pay, extra, tot6, gate, dp, pooled, de, ds, squeezed, unit, res, tot, sp,
):
    n = isc[NARROW]
    add_parts(parts, tot)
    tot6[...] = tot[...]
    pooled[...] = jnp.zeros((8, 2048), F32)
    de[...] = jnp.zeros((8, 2048), F32)

    def units(c):
        sl = cols(c)
        mean, scale = coefs(tot, 0, sl, fs, INV_OUT)
        u = ((pre6[:, sl] - mean) * scale * vec[0:1, sl] + vec[1:2, sl]) * keep[...]
        unit[:, sl] = u
        for b, r in enumerate(image_sums(u)):
            pooled[b : b + 1, sl] = r * fs[CELLS + b]

    loop(8, units)
    sp[...] = dot3(pooled[...], sq[...]) + sqb[1:2, :]
    squeezed[...] = sp[...] * sigmoid(sp[...])
    for h in range(2):
        sl = slice(h * 1024, (h + 1) * 1024)
        gate[:, sl] = sigmoid(dot3(squeezed[...], ex[h]) + vec[2:3, sl])
    extra[...] = jnp.zeros((8, 512), F32)
    for k in range(3):
        extra[5 + k // 2 : 6 + k // 2, (k % 2) * 256 : (k % 2) * 256 + 256] = sq1s[k : k + 1, :]

    def streams(c):
        sl = cols(c)
        h, part = c // 4, cols(c % 4)
        u = unit[:, sl]
        branch = u * expand([gate[b : b + 1, sl] for b in range(B)])
        join = branch + f32(lows[:, sl])
        s = sigmoid(join)
        stream = join * s * keep[...]
        res[h, :, part] = low(stream)
        d = f32(og[h, :, part]) * keep[...] * (s * (1.0 + join * (1.0 - s)))
        dj2[:, sl] = d
        for b, r in enumerate(image_sums(d * u)):
            de[b : b + 1, sl] = r
        extra[6:7, 256:512] += jnp.sum(branch * branch, axis=0, keepdims=True)
        extra[7:8, 0:256] += jnp.sum(stream * stream, axis=0, keepdims=True)

    loop(8, streams)
    result[...] = res[n]
    de[...] = de[...] * gate[...] * (1.0 - gate[...])
    back = 0.0
    for h in range(2):
        back = back + dot3_nt(de[:, h * 1024 : (h + 1) * 1024], ex[h])
    ds[...] = back * slope(sp[...])
    dp[...] = dot3_nt(ds[...], sq[...])
    for b in range(B):
        dp[b : b + 1, :] = dp[b : b + 1, :] * fs[CELLS + b]
    total = jnp.sum(de[...], axis=0, keepdims=True)
    for k in range(4):
        extra[k : k + 1, :] = total[:, k * 512 : (k + 1) * 512]
    extra[4:5, 0:128] = jnp.sum(ds[...], axis=0, keepdims=True)

    def tops(c):
        sl = cols(c)
        mean, scale = coefs(tot, 0, sl, fs, INV_OUT)
        x = (pre6[:, sl] - mean) * scale
        du = (
            dj2[:, sl] * expand([gate[b : b + 1, sl] for b in range(B)])
            + expand([dp[b : b + 1, sl] for b in range(B)])
        ) * keep[...]
        put(pay, 0, back_rows(du, x, fs), sl)

    loop(8, tops)


def whole_gain(tot, at, gain, bias):
    gain[...] = (tot[at + 2 : at + 3, :] + tot[at + 3 : at + 4, :]).reshape(gain.shape)
    bias[...] = (tot[at : at + 1, :] + tot[at + 1 : at + 2, :]).reshape(bias.shape)


def half_gain(tot, n, gain, bias):
    sl = cols(n, gain.shape[0])
    gain[...] = (tot[2:3, sl] + tot[3:4, sl]).reshape(gain.shape)
    bias[...] = (tot[0:1, sl] + tot[1:2, sl]).reshape(bias.shape)


def back_six_kernel(
    fs, isc, parts, tot6, pre6, dj2, gate, dp, pre5, tot5, extra, keep, vec, gain5, w6,
    d6, do5, st, dgain, dbias, tot, acc,
):
    add_parts(parts, tot)
    half_gain(tot, isc[NARROW], dgain, dbias)
    acc[...] = jnp.zeros((M, 512), F32)

    def body(c):
        sl = cols(c)
        mean, scale = coefs(tot6, 0, sl, fs, INV_OUT)
        x = (pre6[:, sl] - mean) * scale
        du = (
            dj2[:, sl] * expand([gate[b : b + 1, sl] for b in range(B)])
            + expand([dp[b : b + 1, sl] for b in range(B)])
        ) * keep[...]
        a, bb = means(tot, 0, sl, fs, INV_OUT)
        d = low((du - a - x * bb) * (scale * vec[0:1, sl]) * keep[...])
        d6[:, sl] = d
        acc[...] += mm_nt(d, w6[:, sl])

    loop(8, body)
    mean, scale = coefs(tot5, 0, slice(0, 512), fs, INV_OUT)
    x = (pre5[...] - mean) * scale
    o = x * gain5[0:1, :] + gain5[1:2, :]
    d = acc[...] * keep[...] * slope(o)
    do5[...] = d
    put(st, 0, back_rows(d, x, fs), slice(0, 512))
    st[4:12, :] = extra[...]


def back_five_kernel(
    fs, isc, parts, tot5, pre5, do5, pre4, tot4, keep, gb, gain5, sh, w5,
    d5, do4, st, dgain, dbias, debias, dsbias, norms, tot,
):
    n = isc[NARROW]
    add_parts(parts, tot)
    half_gain(tot, n, dgain, dbias)
    excite = jnp.concatenate([tot[pl.ds(4 + 2 * n, 1), :], tot[pl.ds(5 + 2 * n, 1), :]], axis=1)
    debias[...] = excite.reshape(1024)
    dsbias[...] = tot[8:9, 0:128].reshape(128)
    for k in range(5):
        v = tot[9 + k // 2 : 10 + k // 2, (k % 2) * 256 : (k % 2) * 256 + 256]
        norms[k] = jnp.sqrt(jnp.sum(v, axis=1, keepdims=True) * fs[INV_ALL])[0, 0]
    sl = slice(0, 512)
    mean, scale = coefs(tot5, 0, sl, fs, INV_OUT)
    x = (pre5[...] - mean) * scale
    a, bb = means(tot, 0, sl, fs, INV_OUT)
    d = low((do5[...] - a - x * bb) * (scale * gain5[0:1, :]) * keep[...])
    d5[...] = d
    acc = 0.0
    for t in range(9):
        dc = d if t == 4 else low(mm(sh[8 - t], d))
        for h in range(2):
            acc = acc + mm_nt(dc[:, h * 256 : (h + 1) * 256], w5[h, t * 512 : (t + 1) * 512, :])
    mean, scale = coefs(tot4, 0, sl, fs, INV_OUT)
    x = (pre4[...] - mean) * scale
    o = x * gb[4:5, :] + gb[5:6, :]
    d = acc * keep[...] * slope(o)
    do4[...] = d
    put(st, 0, back_rows(d, x, fs), sl)


def back_four_kernel(
    fs, parts, tot4, pre4, do4, dj2, tot3, pre3, prep, gate, sp, keep, gb, vec, sq_far, ex_far, w4,
    d4, dj1, st, dgain, dbias, dp, de, ds, bias, tot, sq, ex, sems,
):
    copies = copy_all([(sq_far, sq), (ex_far, ex)], sems)
    add_parts(parts, tot)
    whole_gain(tot, 0, dgain, dbias)
    de[...] = jnp.zeros((8, 2048), F32)
    mean, scale = coefs(tot4, 0, slice(0, 512), fs, INV_OUT)
    x = (pre4[...] - mean) * scale
    a, bb = means(tot, 0, slice(0, 512), fs, INV_OUT)
    d4[...] = low((do4[...] - a - x * bb) * (scale * gb[4:5, :]) * keep[...])

    def joins(c):
        sl = cols(c)
        back = dj2[:, sl] + mm_nt(d4[...], w4[cols(c), :])
        mean, scale = coefs(tot3, 0, sl, fs, INV_OUT)
        u = ((pre3[:, sl] - mean) * scale * vec[0:1, sl] + vec[1:2, sl]) * keep[...]
        mean, scale = coefs(tot3, 4, sl, fs, INV_OUT)
        s = ((prep[:, sl] - mean) * scale * vec[2:3, sl] + vec[3:4, sl]) * keep[...]
        join = u * expand([gate[b : b + 1, sl] for b in range(B)]) + s
        d = f32(low(back)) * keep[...] * slope(join)
        dj1[:, sl] = d
        for b, r in enumerate(image_sums(d * u)):
            de[b : b + 1, sl] = r

    loop(8, joins)
    wait_all(copies)
    de[...] = de[...] * gate[...] * (1.0 - gate[...])
    ds[...] = dot3_nt(de[...], ex[...]) * slope(sp[...])
    dp[...] = dot3_nt(ds[...], sq[...])
    for b in range(B):
        dp[b : b + 1, :] = dp[b : b + 1, :] * fs[CELLS + b]
    total = jnp.sum(de[...], axis=0, keepdims=True)
    bias[...] = jnp.zeros((8, 512), F32)
    for k in range(4):
        bias[k : k + 1, :] = total[:, k * 512 : (k + 1) * 512]
    bias[4:5, 0:128] = jnp.sum(ds[...], axis=0, keepdims=True)

    def tops(c):
        sl = cols(c)
        d = dj1[:, sl]
        mean, scale = coefs(tot3, 0, sl, fs, INV_OUT)
        x = (pre3[:, sl] - mean) * scale
        du = (
            d * expand([gate[b : b + 1, sl] for b in range(B)])
            + expand([dp[b : b + 1, sl] for b in range(B)])
        ) * keep[...]
        put(st, 0, back_rows(du, x, fs), sl)
        mean, scale = coefs(tot3, 4, sl, fs, INV_OUT)
        put(st, 4, back_rows(d, (prep[:, sl] - mean) * scale, fs), sl)

    loop(8, tops)


def back_three_kernel(
    fs, parts, tot3, pre3, prep, dj1, gate, dp, bias, pre2, tot2, keep, vec, gb, w3,
    d3, dproj, do2, st, dgain, dbias, dgainp, dbiasp, tot, acc,
):
    add_parts(parts, tot)
    whole_gain(tot, 0, dgain, dbias)
    whole_gain(tot, 4, dgainp, dbiasp)
    acc[...] = jnp.zeros((M, 512), F32)

    def body(c):
        sl = cols(c)
        mean, scale = coefs(tot3, 0, sl, fs, INV_OUT)
        x = (pre3[:, sl] - mean) * scale
        dj = dj1[:, sl]
        du = (
            dj * expand([gate[b : b + 1, sl] for b in range(B)])
            + expand([dp[b : b + 1, sl] for b in range(B)])
        ) * keep[...]
        a, bb = means(tot, 0, sl, fs, INV_OUT)
        d = low((du - a - x * bb) * (scale * vec[0:1, sl]) * keep[...])
        d3[:, sl] = d
        acc[...] += mm_nt(d, w3[:, sl])
        mean, scale = coefs(tot3, 4, sl, fs, INV_OUT)
        x = (prep[:, sl] - mean) * scale
        a, bb = means(tot, 4, sl, fs, INV_OUT)
        dproj[:, sl] = low((dj - a - x * bb) * (scale * vec[2:3, sl]) * keep[...])

    loop(8, body)
    sl = slice(0, 512)
    mean, scale = coefs(tot2, 0, sl, fs, INV_OUT)
    x = (pre2[...] - mean) * scale
    o = x * gb[2:3, :] + gb[3:4, :]
    d = acc[...] * keep[...] * slope(o)
    do2[...] = d
    put(st, 0, back_rows(d, x, fs), sl)
    st[4:12, :] = bias[...]


def fetch_two_kernel(far, ws, sems):
    wait_all(copy_all([(far.at[3 * k : 3 * k + 3], ws.at[3 * k : 3 * k + 3]) for k in range(3)], sems))


def back_two_kernel(
    fs, parts, tot2, pre2, do2, x1, keep1, keep, gb, sh, ws,
    d2, do1, st, dgain, dbias, debias, dsbias, tot, dcol,
):
    add_parts(parts, tot)
    whole_gain(tot, 0, dgain, dbias)
    debias[...] = jnp.concatenate([tot[k : k + 1, :] for k in range(4, 8)], axis=1).reshape(2048)
    dsbias[...] = tot[8:9, 0:128].reshape(128)
    sl = slice(0, 512)
    mean, scale = coefs(tot2, 0, sl, fs, INV_OUT)
    x = (pre2[...] - mean) * scale
    a, bb = means(tot, 0, sl, fs, INV_OUT)
    d = low((do2[...] - a - x * bb) * (scale * gb[2:3, :]) * keep[...])
    d2[...] = d
    dcol[0] = d
    dcol[1] = low(mm(sh[5], d))
    dcol[2] = low(mm(sh[7], d))
    dcol[3] = low(mm(sh[8], d))
    terms = (
        ((0, 4),),
        ((0, 5), (1, 3)),
        ((0, 7), (2, 1)),
        ((0, 8), (1, 6), (2, 2), (3, 0)),
    )
    st[...] = jnp.zeros((4, 512), F32)
    for k in range(4):
        acc = 0.0
        for which, t in terms[k]:
            acc = acc + mm_nt(dcol[which], ws[t])
        x = x1[k]
        o = x * gb[0:1, :] + gb[1:2, :]
        d = acc * keep1[k] * slope(o)
        do1[k] = d
        rows = back_rows(d, x, fs)
        for r in range(4):
            st[r : r + 1, :] += rows[r]


def deal(isc, full, rows, keep, send, at):
    for p in range(16):
        tile = full[pl.ds(pl.multiple_of(isc[DEST + p] * rows, rows), rows), :]
        (keep if p < 8 else send)[p % 8, at_rows(at, rows), :] = tile


def back_one_kernel(
    fs, isc, parts, tot1, x1, do1, xp, keep1, gb, d1, gkeep, gsend, dgain, dbias, tot, dn, full
):
    n = isc[NARROW]
    add_parts(parts, tot)
    whole_gain(tot, 0, dgain, dbias)
    sl = slice(0, 512)
    scale = coefs(tot1, 0, sl, fs, INV_IN)[1] * gb[0:1, :]
    a, bb = means(tot, 0, sl, fs, INV_IN)
    planes = []
    for k in range(4):
        d = (do1[k] - a - x1[k] * bb) * scale * keep1[k]
        planes.append(d)
        dn[k] = low(d)
    for b in range(B):
        d1[b] = low(jnp.concatenate([d[b * POS : (b + 1) * POS] for d in planes], axis=0))

    def body(c):
        g = 0.0
        for k in range(4):
            g = g + mm_tn(xp[k, :, cols(c)], dn[k, :, cols(n)])
        full[cols(c), :] = low(g)

    loop(4, body)
    deal(isc, full, 64, gkeep, gsend, 0)


def image_kernel(isc, perm, d1, dproj, keep, w1, wp_far, out, dc, cc, pick_own, spread, wp, sems):
    n = isc[NARROW]
    copies = [
        pltpu.make_async_copy(wp_far.at[cut], wp.at[cut], sems.at[k])
        for k, cut in enumerate(slice(256 * k, 256 * (k + 1)) for k in range(4))
    ]
    for c in copies:
        c.start()
    for b in range(B):
        dc[b * HALF : (b + 1) * HALF, :] = low(mm_tn(perm[n], d1[b]))
        place = lax.broadcasted_iota(jnp.int32, (32, M), 1)
        it = lax.broadcasted_iota(jnp.int32, (32, M), 0)
        pick_own[b * 32 : (b + 1) * 32, :] = low(jnp.where(
            (place == b * POS + (it >> 2) * 8 + n * 4 + (it & 3)) & (it < 28), 1.0, 0.0
        ))
        place = lax.broadcasted_iota(jnp.int32, (HALF, 128), 1)
        it = lax.broadcasted_iota(jnp.int32, (HALF, 128), 0)
        spread[b * HALF : (b + 1) * HALF, :] = low(jnp.where(
            ((it & 9) == 0) & (place == b * 32 + (it >> 4) * 4 + ((it & 7) >> 1)), 1.0, 0.0
        ))
    cc[...] = low(mm(pick_own[...], dproj[...]))

    def body(c):
        sl = cols(c)
        hi, lo = split2(mm_nt(cc[...], wp[sl, :]))
        v = mm_nt(dc[...], w1[sl, :]) + mm(spread[...], hi) + mm(spread[...], lo)
        out[:, sl] = v * keep[...]

    for c in range(4):
        copies[c].wait()
        body(c)


def grads_a_kernel(isc, h5, d6, col4, d5, gkeep, gsend, wider, full):
    n = isc[NARROW]

    def expand2(c):
        wider[:, cols(c)] = low(mm_tn(h5[:, cols(n)], d6[:, cols(c)]))

    loop(8, expand2)
    for p in range(16):
        sl = cols(isc[DEST + p], 128)
        for k in range(2):
            (gkeep if p < 8 else gsend)[p % 8, 0:128, k * 128 : (k + 1) * 128] = wider[
                k * 128 : (k + 1) * 128, sl
            ]

    def spatial(t):
        full[...] = low(mm_tn(col4[t], d5[:, cols(n)]))
        deal(isc, full, 32, gkeep, gsend, 128 + t * 32)

    loop(9, spatial)


def gate_grads(isc, n, c, at, squeezed, pooled, de, ds, gkeep, gsend, q, e):
    sl = cols(n * 4 + c)
    q[...] = outer(ds[...], pooled[:, sl])
    e[...] = outer(squeezed[...], de[:, sl])
    for p in range(16):
        rows = pl.ds(pl.multiple_of(isc[DEST + p] * 8, 8), 8)
        both = jnp.concatenate([q[rows, :], e[rows, :]], axis=0)
        (gkeep if p < 8 else gsend)[p % 8, at_rows(at + c * 16, 16), :] = low(both)


def grads_b_kernel(isc, d4, lows, squeezed, pooled, de, ds, gkeep, gsend, full, q, e):
    n = isc[NARROW]

    def body(c):
        full[...] = low(mm_tn(d4[...], lows[:, cols(n * 4 + c)]))
        deal(isc, full, 32, gkeep, gsend, c * 32)
        gate_grads(isc, n, c, 128, squeezed, pooled, de, ds, gkeep, gsend, q, e)

    loop(4, body)


def grads_c_kernel(
    isc, h2, d3, strided, dproj, sp, pooled, de, ds, gkeep, gsend, full, taller, q, e, squeezed
):
    n = isc[NARROW]
    squeezed[...] = sp[...] * sigmoid(sp[...])

    def body(c):
        sl = cols(n * 4 + c)
        full[...] = low(mm_tn(h2[...], d3[:, sl]))
        deal(isc, full, 32, gkeep, gsend, c * 32)
        taller[...] = low(mm_tn(strided[...], dproj[:, sl]))
        deal(isc, taller, 64, gkeep, gsend, 128 + c * 64)
        gate_grads(isc, n, c, 384, squeezed, pooled, de, ds, gkeep, gsend, q, e)

    loop(4, body)


def grads_d_kernel(isc, col1, d2, gkeep, gsend, full):
    n = isc[NARROW]

    def spatial(t):
        full[...] = low(mm_tn(col1[t], d2[:, cols(n)]))
        deal(isc, full, 32, gkeep, gsend, t * 32)

    loop(9, spatial)


def joined(v, out, at, rows):
    for c in range(4):
        out[:, c * 256 : (c + 1) * 256] = v[at + c * rows : at + (c + 1) * rows, :]


def unpack_gates(v, at, squeeze, excite):
    for c in range(4):
        part = v[at + c * 16 : at + (c + 1) * 16, :]
        squeeze[:, c * 256 : (c + 1) * 256] = part[0:8]
        excite[:, c * 256 : (c + 1) * 256] = part[8:16]


def unpack_a_kernel(a, b, expand2, spatial2):
    v = f32(a[0]) + f32(b[0])
    expand2[0:128, :] = v[0:128, 0:128]
    expand2[128:256, :] = v[0:128, 128:256]
    spatial2[...] = v[128:416, :]


def unpack_b_kernel(a, b, reduce2, squeeze2, excite2):
    v = f32(a[0]) + f32(b[0])
    joined(v, reduce2, 0, 32)
    unpack_gates(v, 128, squeeze2, excite2)


def unpack_c_kernel(a, b, expand1, project1, squeeze1, excite1):
    v = f32(a[0]) + f32(b[0])
    joined(v, expand1, 0, 32)
    joined(v, project1, 128, 64)
    unpack_gates(v, 384, squeeze1, excite1)


def unpack_d_kernel(a, b, spatial1):
    spatial1[...] = f32(a[0]) + f32(b[0])


VECTORS = (512,) * 6 + (2048,) * 5 + (128,) * 2 + (256,) * 2 + (1024,) * 3


def pack_kernel(isc, w5, w4, w6, ex, sq, ws_far, *refs):
    far, refs = refs[:18], refs[18:]
    out, w4_half, gb, vec1, sqb, vown, ws, w6v, exv, sqv, rows = refs[:11]
    vecs, sems = refs[11:29], refs[29]
    core = isc[CORE]
    pairs = [(f, v) for f, v in zip(far, vecs)] + [
        (w6.at[at_rows(core * 128, 128)], w6v),
        (ex.at[at_rows(core * 64, 64)], exv),
        (sq.at[at_rows(core * 512, 512)], sqv),
        (w4.at[at_rows(core * 512, 512)], w4_half),
        (w5.at[at_rows(core * 2304, 2304)], out.at[0:W6_AT]),
        (ws_far, ws),
    ]
    copies = copy_all(pairs, sems)
    wait_all(copies[:21])

    def row(v):
        return f32(v[...]).reshape(1, v.shape[0])

    for k in range(6):
        gb[k : k + 1, :] = row(vecs[k])
    for k in range(5):
        vec1[k : k + 1, :] = row(vecs[6 + k])
    for k in range(2):
        sqb[k : k + 1, :] = row(vecs[11 + k])
    rows[...] = jnp.zeros((16, 256), F32)
    at = 0
    for v in vecs[13:18]:
        r = row(v)
        for c in range(v.shape[0] // 256):
            rows[at : at + 1, :] = r[:, c * 256 : (c + 1) * 256]
            at += 1
    vown[...] = low(rows[...])
    for c in range(8):
        out[W6_AT + c * 128 : W6_AT + (c + 1) * 128, :] = w6v[:, c * 256 : (c + 1) * 256]
    for c in range(4):
        out[EX_AT + c * 64 : EX_AT + (c + 1) * 64, :] = exv[:, c * 256 : (c + 1) * 256]
    for k in range(2):
        out[SQ_AT : SQ_AT + 256, k * 128 : (k + 1) * 128] = sqv[k * 256 : (k + 1) * 256, :]
    out[VEC_AT:PACK_ROWS, :] = vown[...]
    wait_all(copies[21:])


def call(body, outs, args, scratch=(), flops=1e8, size=5e6, name=None, vmem=LIMIT):
    specs, values = [], []
    for a in args:
        kind, v = a if isinstance(a, tuple) else (VMEM, a)
        specs.append(kind)
        values.append(v)
    return pl.pallas_call(
        body,
        out_shape=tuple(o if hasattr(o, "memory_space") else jax.ShapeDtypeStruct(o[0], o[1]) for o in outs),
        in_specs=specs,
        out_specs=tuple(o[2] if isinstance(o, tuple) and len(o) > 2 else pl.BlockSpec(memory_space=getattr(o, "memory_space", pltpu.VMEM)) for o in outs),
        scratch_shapes=list(scratch),
        compiler_params=pltpu.CompilerParams(vmem_limit_bytes=vmem * 2**20),
        cost_estimate=pl.CostEstimate(
            flops=int(flops), bytes_accessed=int(size), transcendentals=0
        ),
        name=name,
    )(*values)


def swap(v, axis, pairs):
    return lax.ppermute(v, axis, pairs)


def after(v, *others):
    return lax.optimization_barrier((v,) + others)[0]


def local(
    images, crop, micro,
    first_reduce, first_reduce_gain, first_reduce_bias,
    first_spatial, first_spatial_gain, first_spatial_bias,
    first_expand, first_expand_gain, first_expand_bias,
    first_project, first_project_gain, first_project_bias,
    first_squeeze, first_squeeze_bias, first_excite, first_excite_bias,
    second_reduce, second_reduce_gain, second_reduce_bias,
    second_spatial, second_spatial_gain, second_spatial_bias,
    second_expand, second_expand_gain, second_expand_bias,
    second_squeeze, second_squeeze_bias, second_excite, second_excite_bias,
    out_grad,
):
    wide = lax.axis_size("wide")
    exact = wide == 16
    near = [(i, i ^ 1) for i in range(wide)]
    pair = [(0, 1), (1, 0)]
    groups = [list(range(k, wide, 2)) for k in range(2)]
    V = pltpu.VMEM
    D = pltpu.SemaphoreType.DMA
    out = lambda *shape: (shape, F32)
    f = lambda *shape: V(shape, F32)
    h = lambda *shape: V(shape, BF)
    far = lambda v: (ANY, pltpu.with_memory_space_constraint(v, pltpu.HBM))

    def across(x):
        x = x + swap(x, "wide", near)
        sent = jnp.broadcast_to(x[None], (wide // 2,) + x.shape)
        got = lax.all_to_all(sent, "wide", 0, 0, axis_index_groups=groups, tiled=True)
        return got if exact else jnp.sum(got, axis=0, keepdims=True)

    def steps(x):
        step = 1
        while step < wide:
            x = x + swap(x, "wide", [(i, i ^ step) for i in range(wide)])
            step *= 2
        return x[None]

    own_px = images.transpose(0, 2, 1, 3).reshape(B, HALF, 1024)
    other_px = swap(own_px, "narrow", pair)
    ws_far = first_spatial.reshape(9, 512, 512)

    fs_, isc_, keep, keep1, keep_half, sh, perm = call(
        functools.partial(setup_kernel, exact),
        [
            pltpu.SMEM((13,), F32), pltpu.SMEM((18,), jnp.int32), f(M, 1), f(4, M, 1), f(HROWS, 1),
            h(9, M, M), h(2, M, HALF),
        ],
        [(SMEM, far(crop)[1]), (SMEM, far(micro)[1])], name="setup",
    )
    fs, isc = (SMEM, fs_), (SMEM, isc_)
    st1, xown, w1 = call(
        one_half_kernel, [f(4, 512), h(B, HALF, 1024), h(1024, 512)],
        [fs, far(own_px), keep_half, far(first_reduce)],
        [V((HROWS, 1024), BF), D((2,))], flops=5e8, name="one_half",
    )
    part = steps(st1)[0]

    w5_own = second_spatial.reshape(9 * 512, 256)
    vectors = [
        first_reduce_gain, first_reduce_bias, first_spatial_gain, first_spatial_bias,
        second_reduce_gain, second_reduce_bias, first_expand_gain, first_expand_bias,
        first_project_gain, first_project_bias, first_excite_bias,
        first_squeeze_bias, second_squeeze_bias,
        second_spatial_gain, second_spatial_bias, second_expand_gain, second_expand_bias, second_excite_bias,
    ]
    pack, w4_half, gb, vec1, sqb, vown, ws = call(
        pack_kernel,
        [
            ((PACK_ROWS, 256), BF), ((512, 512), BF), f(8, 512), f(8, 2048), f(8, 128), h(16, 256),
            h(9, 512, 512),
        ],
        [
            (SMEM, after(isc_, st1)), far(w5_own), far(second_reduce), far(second_expand), far(second_excite),
            far(second_squeeze), far(ws_far),
        ] + [far(v) for v in vectors],
        [V((128, 2048), BF), V((64, 1024), BF), V((512, 128), BF), V((16, 256), F32)]
        + [V((size,), BF) for size in VECTORS] + [D((24,))],
        size=2e7, name="pack",
    )
    part = after(part, gb)
    part_other = swap(part, "narrow", pair)
    w4_r1 = swap(after(w4_half, other_px, part_other), "narrow", pair)
    og_own = out_grad.transpose(0, 2, 1, 3).reshape(M, 1024)

    xp, strided, x1, col1, pre2, st2, tot1 = call(
        stage_two_kernel,
        [h(4, M, 1024), h(M, 1024), f(4, M, 512), h(9, M, 512), f(M, 512), f(4, 512), f(4, 512)],
        [fs, isc, xown, other_px, part, part_other, perm, keep1, keep, w1, ws, gb, sh],
        [V((4, M, 256), F32), V((4, M, 512), BF), V((4, 512), F32)],
        flops=4e9, size=2e7, name="stage_two",
    )
    parts2 = steps(st2)
    w4_r2 = swap(after(w4_r1, st2), "wide", near)
    pk1 = swap(after(pack, w4_r1, st2), "narrow", pair)
    prep, stp, w3 = call(
        project_kernel, [f(M, 2048), f(4, 2048), h(512, 2048)],
        [fs, after(strided, w4_r1), keep, far(first_project), far(first_expand)],
        [V((1024, 2048), BF), D((5,))], flops=1e9, size=8e6, name="project",
    )
    h2, pre3, st3, tot2 = call(
        stage_three_kernel, [h(M, 512), f(M, 2048), f(8, 2048), f(4, 512)],
        [fs, parts2, pre2, stp, keep, w3, gb], [V((4, 512), F32)],
        flops=1e9, size=6e6, name="stage_three",
    )
    parts3 = steps(st3)
    w4 = call(
        fetch_four_kernel, [h(2048, 512)],
        [(SMEM, after(isc_, st3)), far(second_reduce), far(w4_r1), far(w4_r2)], [D((3,))],
        size=4e6, name="fetch_four",
    )[0]
    lows, pre4, st4, tot3, gate1, sp1, pooled1, squares = call(
        stage_four_kernel,
        [
            h(M, 2048), f(M, 512), f(4, 512), f(8, 2048), f(8, 2048), f(8, 128), f(8, 2048), f(8, 256),
        ],
        [fs, parts3, pre3, prep, keep, vec1, sqb, far(first_squeeze), far(first_excite), w4],
        [
            V((M, 2048), F32), V((M, 2048), F32), V((M, 512), F32), V((8, 2048), F32),
            V((2048, 128), BF), V((128, 2048), BF), D((2,)),
        ],
        flops=1e9, size=1e7, name="stage_four",
    )
    parts4 = steps(st4)
    pk2 = swap(after(pk1, st4), "wide", near)
    og_other = swap(after(og_own, pk1, st4), "narrow", pair)
    pk1, pk2 = far(pk1), far(pk2)
    w5, vaway = call(
        fetch_five_kernel, [h(2, 4608, 256), h(16, 256)],
        [(SMEM, after(isc_, st4)), far(w5_own), pk1, pk2], [D((4,))], size=8e6, name="fetch_five",
    )
    col4, pre5, st5, tot4, gain5, vec2 = call(
        stage_five_kernel,
        [h(9, M, 512), f(M, 512), f(4, 512), f(4, 512), f(2, 512), f(3, 2048)],
        [fs, isc, parts4, pre4, keep, gb, sh, vown, vaway, w5], [V((4, 512), F32)],
        flops=2e9, size=1e7, name="stage_five",
    )
    parts5 = steps(st5)
    w6 = call(
        fetch_six_kernel, [h(512, 2048)],
        [(SMEM, after(isc_, st5)), far(second_expand), pk1, pk2], [D((17,))], size=4e6, name="fetch_six",
    )[0]
    h5, pre6, st6, tot5 = call(
        stage_six_kernel, [h(M, 512), f(M, 2048), f(4, 2048), f(4, 512)],
        [fs, parts5, pre5, keep, gain5, w6], [V((4, 512), F32)],
        flops=1e9, size=6e6, name="stage_six",
    )
    parts6 = steps(st6)
    sq, ex, og = call(
        fetch_turn_kernel, [h(2048, 128), h(2, 128, 1024), h(2, M, 1024)],
        [
            (SMEM, after(isc_, st6)), far(second_squeeze), far(second_excite), pk1, pk2,
            far(og_own), far(og_other),
        ],
        [D((16,))], size=4e6, name="fetch_turn",
    )
    result, dj2, pay6, extra6, tot6, gate2, dp2, pooled2, de2, ds2, sq2 = call(
        turn_kernel,
        [
            ((M, 1024), BF), f(M, 2048), f(4, 2048), f(8, 512), f(4, 2048), f(8, 2048),
            f(8, 2048), f(8, 2048), f(8, 2048), f(8, 128), f(8, 128),
        ],
        [fs, isc, parts6, pre6, keep, lows, vec2, sqb, squares, sq, ex, og],
        [V((M, 2048), F32), V((2, M, 1024), BF), V((4, 2048), F32), V((8, 128), F32)],
        flops=1e9, size=1e7, name="turn",
    )
    back6 = across(pay6)
    d6, do5, bt5, dgain6, dbias6 = call(
        back_six_kernel, [h(M, 2048), f(M, 512), f(12, 512), out(1024), out(1024)],
        [fs, isc, back6, tot6, pre6, dj2, gate2, dp2, pre5, tot5, extra6, keep, vec2, gain5, w6],
        [V((4, 2048), F32), V((M, 512), F32)],
        flops=1e9, size=1e7, name="back_six",
    )
    back5 = across(bt5)
    d5, do4, bt4, dgain5, dbias5, debias2, dsbias2, norms = call(
        back_five_kernel,
        [h(M, 512), f(M, 512), f(4, 512), out(256), out(256), out(1024), out(128), ((5,), F32, SMEM)],
        [fs, isc, back5, tot5, pre5, do5, pre4, tot4, keep, gb, gain5, sh, w5],
        [V((12, 512), F32)],
        flops=2e9, size=1e7, name="back_five",
    )
    back4 = steps(bt4)

    def step(g, k):
        if not exact:
            return g
        kept, sent = g
        got = swap(sent, "wide", [(i, i ^ (1 << k)) for i in range(wide)])
        if k == 3:
            return kept, got
        half = kept.shape[0] // 2
        return kept[:half] + got[:half], kept[half:] + got[half:]

    ga = call(
        grads_a_kernel, [h(8, 416, 256)] * 2, [isc, h5, d6, col4, d5],
        [V((256, 2048), BF), V((512, 256), BF)], flops=2e9, size=1e7, name="grads_a",
    )
    back4, ga = lax.optimization_barrier((back4, ga))
    d4, dj1, bt3, dgain4, dbias4, dp1, de1, ds1, bias1 = call(
        back_four_kernel,
        [
            h(M, 512), f(M, 2048), f(8, 2048), out(512), out(512), f(8, 2048),
            f(8, 2048), f(8, 128), f(8, 512),
        ],
        [
            fs, back4, tot4, pre4, do4, dj2, tot3, pre3, prep, gate1, sp1, keep, gb, vec1,
            far(first_squeeze), far(first_excite), w4,
        ],
        [V((4, 512), F32), V((2048, 128), BF), V((128, 2048), BF), D((2,))],
        flops=1e9, size=1e7, name="back_four",
    )
    back3 = steps(bt3)
    ga = step(ga, 0)
    gb1 = call(
        grads_b_kernel, [h(8, 192, 256)] * 2, [isc, d4, lows, sq2, pooled2, de2, ds2],
        [V((512, 256), BF), V((128, 256), F32), V((128, 256), F32)],
        flops=1e9, size=4e6, name="grads_b",
    )
    back3, ga, gb1 = lax.optimization_barrier((back3, ga, gb1))
    d3, dproj, do2, bt2, dgain3, dbias3, dgainp, dbiasp = call(
        back_three_kernel,
        [h(M, 2048), h(M, 2048), f(M, 512), f(12, 512), out(2048), out(2048), out(2048), out(2048)],
        [fs, back3, tot3, pre3, prep, dj1, gate1, dp1, bias1, pre2, tot2, keep, vec1, gb, w3],
        [V((8, 2048), F32), V((M, 512), F32)],
        flops=1e9, size=1e7, name="back_three",
    )
    back2 = steps(bt2)
    ga, gb1 = step(ga, 1), step(gb1, 0)
    gc = call(
        grads_c_kernel, [h(8, 448, 256)] * 2,
        [isc, h2, d3, strided, dproj, sp1, pooled1, de1, ds1],
        [V((512, 256), BF), V((1024, 256), BF), V((128, 256), F32), V((128, 256), F32), V((8, 128), F32)],
        flops=3e9, size=1e7, name="grads_c",
    )
    gc = step(gc, 0)
    back2, ga, gb1, gc = lax.optimization_barrier((back2, ga, gb1, gc))
    ws_back = call(
        fetch_two_kernel, [h(9, 512, 512)], [far(after(ws_far, bt2))], [D((3,))], size=9e6, name="fetch_two",
    )[0]
    d2, do1, bt1, dgain2, dbias2, debias1, dsbias1 = call(
        back_two_kernel,
        [h(M, 512), f(4, M, 512), f(4, 512), out(512), out(512), out(2048), out(128)],
        [fs, back2, tot2, pre2, do2, x1, keep1, keep, gb, sh, ws_back],
        [V((12, 512), F32), V((4, M, 512), BF)],
        flops=2e9, size=1e7, name="back_two",
    )
    back1 = steps(bt1)
    ga, gb1, gc = step(ga, 2), step(gb1, 1), step(gc, 1)
    gd = call(
        grads_d_kernel, [h(8, 288, 256)] * 2, [isc, col1, d2], [V((512, 256), BF)],
        flops=2e9, size=6e6, name="grads_d",
    )
    gd = step(gd, 0)
    back1, ga, gb1, gc, gd = lax.optimization_barrier((back1, ga, gb1, gc, gd))
    d1, ge_keep, ge_send, dgain1, dbias1 = call(
        back_one_kernel, [h(B, M, 512), h(8, 64, 256), h(8, 64, 256), out(512), out(512)],
        [fs, isc, back1, tot1, x1, do1, xp, keep1, gb],
        [V((4, 512), F32), V((4, M, 512), BF), V((1024, 256), BF)],
        flops=1e9, size=6e6, name="back_one",
    )
    ge = (ge_keep, ge_send)
    dimg = call(
        image_kernel, [out(HROWS, 1024)],
        [isc, perm, d1, dproj, keep_half, w1, far(after(first_project, bt1))],
        [
            V((HROWS, 512), BF), V((128, 2048), BF), V((128, M), BF), V((HROWS, 128), BF),
            V((1024, 2048), BF), D((4,)),
        ],
        flops=1e9, size=1e7, name="image",
    )[0]

    if exact:
        ge, gd = step(ge, 0), step(gd, 1)
        gd, ge, dimg = lax.optimization_barrier((gd, ge, dimg))
        ge = step(step(ge, 1), 2)
        gd, gb1, gc = step(gd, 2), step(gb1, 2), step(gc, 2)
        expand2, spatial2 = call(
            unpack_a_kernel, [out(256, 128), out(288, 256)], list(step(ga, 3)), name="unpack_a"
        )
        reduce2, squeeze2, excite2 = call(
            unpack_b_kernel, [out(32, 1024), out(8, 1024), out(8, 1024)], list(step(gb1, 3)), name="unpack_b"
        )
        expand1, project1, squeeze1, excite1 = call(
            unpack_c_kernel, [out(32, 1024), out(64, 1024), out(8, 1024), out(8, 1024)], list(step(gc, 3)),
            name="unpack_c",
        )
        spatial1 = call(unpack_d_kernel, [out(288, 256)], list(step(gd, 3)), name="unpack_d")[0]
        reduce1 = call(unpack_d_kernel, [out(64, 256)], list(step(ge, 3)), name="unpack_e")[0]
    else:
        finer = wide // 16

        def summed(g):
            return lax.psum_scatter(g, "wide", scatter_dimension=0, tiled=True)

        def blocks(g, start, count, rows):
            p = g[:, start : start + count * rows].reshape(16, count, finer, rows // finer, 256)
            p = summed(p.transpose(0, 2, 1, 3, 4).reshape(wide, count, rows // finer, 256))[0]
            return f32(p).transpose(1, 0, 2).reshape(rows // finer, count * 256)

        def both(g, start):
            p = g[:, start : start + 64].reshape(16, 4, 2, finer, 8 // finer, 256)
            p = f32(summed(p.transpose(0, 3, 1, 2, 4, 5).reshape(wide, 4, 2, -1, 256))[0])
            return [p[:, k].transpose(1, 0, 2).reshape(-1, 1024) for k in range(2)]

        def taps(g, start):
            p = g[:, start : start + 288].reshape(16, 9, finer, 32 // finer, 256)
            return f32(summed(p.transpose(0, 2, 1, 3, 4).reshape(wide, 9, -1, 256))[0]).reshape(-1, 256)

        ga, gb1, gc, gd, ge = (jnp.concatenate(g) for g in (ga, gb1, gc, gd, ge))
        e2 = ga[:, 0:128].reshape(16, 128, 2, finer, 128 // finer).transpose(0, 3, 1, 2, 4)
        e2 = summed(e2.reshape(wide, 1, -1)).reshape(128, 2, -1)
        expand2 = f32(e2.transpose(1, 0, 2).reshape(256, -1))
        spatial2 = taps(ga, 128)
        reduce2 = blocks(gb1, 0, 4, 32)
        squeeze2, excite2 = both(gb1, 128)
        expand1, project1 = blocks(gc, 0, 4, 32), blocks(gc, 128, 4, 64)
        squeeze1, excite1 = both(gc, 384)
        spatial1, reduce1 = taps(gd, 0), blocks(ge, 0, 1, 64)
    return (
        result.reshape(B, 7, 8, 1024).transpose(0, 2, 1, 3),
        dimg.reshape(B, 14, 8, 1024).transpose(0, 2, 1, 3),
        reduce1, dgain1, dbias1,
        spatial1.reshape(3, 3, -1, 256), dgain2, dbias2,
        expand1, dgain3, dbias3,
        project1, dgainp, dbiasp,
        squeeze1.T, dsbias1, excite1, debias1,
        reduce2.T, dgain4, dbias4,
        spatial2.reshape(3, 3, -1, 256), dgain5, dbias5,
        expand2, dgain6, dbias6,
        squeeze2.T, dsbias2, excite2, debias2,
        norms,
    )


def solution(mesh):
    rep, nar = P(), P("narrow")
    return jax.shard_map(
        local,
        mesh=mesh,
        in_specs=(P("wide", "narrow", None, None),) + (rep,) * 18 + (
            P("narrow", None), rep, rep,
            P(None, None, None, "narrow"), nar, nar,
            P("narrow", None), nar, nar,
            P("narrow", None), rep, P(None, "narrow"), nar,
            P("wide", None, None, "narrow"),
        ),
        out_specs=(
            P("wide", None, None, "narrow"), P("wide", "narrow", None, None),
            P("wide", "narrow"), rep, rep,
            P(None, None, "wide", "narrow"), rep, rep,
            P("wide", "narrow"), rep, rep,
            P("wide", "narrow"), rep, rep,
            P("narrow", "wide"), rep, P("wide", "narrow"), rep,
            P("narrow", "wide"), rep, rep,
            P(None, None, "wide", "narrow"), nar, nar,
            P("narrow", "wide"), nar, nar,
            P("narrow", "wide"), rep, P("wide", "narrow"), nar,
            rep,
        ),
        check_vma=False,
    )
```

```python
import functools

import numpy as np
import jax
import jax.numpy as jnp
from jax import lax
from jax.experimental import pallas as pl
from jax.experimental.pallas import tpu as pltpu
from jax.sharding import PartitionSpec as P

EPSILON = 1e-05
BF = jnp.bfloat16
F32 = jnp.float32
B = 4
POS = 56
LIMIT = 14
SCALE = 0.01
UNROLL = 2
M = B * POS
HALF = 112
HROWS = B * HALF
VMEM = pl.BlockSpec(memory_space=pltpu.VMEM)
SMEM = pl.BlockSpec(memory_space=pltpu.SMEM)
ANY = pl.BlockSpec(memory_space=pl.ANY)
INV_IN, INV_OUT, CELLS, MICRO, INV_ALL = 0, 2, 4, 8, 12
NARROW, CORE, DEST = 0, 1, 2
W6_AT, EX_AT, SQ_AT, VEC_AT, PACK_ROWS = 0, 1024, 1280, 1536, 1552


def mm(a, b):
    return lax.dot_general(a, b, (((1,), (0,)), ((), ())), preferred_element_type=F32)


def mm_nt(a, b):
    return lax.dot_general(a, b, (((1,), (1,)), ((), ())), preferred_element_type=F32)


def mm_tn(a, b):
    return lax.dot_general(a, b, (((0,), (0,)), ((), ())), preferred_element_type=F32)


def f32(v):
    return v.astype(F32)


def low(v):
    return v.astype(BF)


def split2(v):
    a = low(v)
    return a, low(v - f32(a))


def split3(v):
    a = low(v)
    r = v - f32(a)
    b = low(r)
    return a, b, low(r - f32(b))


def dot3(v, w):
    return sum(mm(p, w) for p in split3(v))


def dot3_nt(v, w):
    return sum(mm_nt(p, w) for p in split3(v))


def outer(a, b):
    a1, a2 = split2(a)
    b1, b2 = split2(b)
    return mm_tn(a1, b1) + mm_tn(a1, b2) + mm_tn(a2, b1)


def sigmoid(v):
    return 1.0 / (1.0 + jnp.exp(-v))


def slope(v):
    s = sigmoid(v)
    return s * (1.0 + v * (1.0 - s))


def cols(c, size=256):
    return pl.ds(pl.multiple_of(c * size, size), size)


def expand(rows):
    return jnp.concatenate([jnp.broadcast_to(r, (POS, r.shape[1])) for r in rows], axis=0)


def pick(r0, r1, fs):
    return expand([r0 * (1.0 - fs[MICRO + b]) + r1 * fs[MICRO + b] for b in range(B)])


def image_sums(v):
    return [jnp.sum(v[b * POS : (b + 1) * POS], axis=0, keepdims=True) for b in range(B)]


def grouped(sums, fs, reps=1):
    zero = one = 0.0
    for b in range(B):
        zero = zero + sums[b] * (1.0 - fs[MICRO + b])
        one = one + sums[b] * fs[MICRO + b]
    return [zero, one]


def group_sums(v, fs):
    return grouped(image_sums(v), fs)


def put(ref, at, rows, sl):
    for k, r in enumerate(rows):
        ref[at + k : at + k + 1, sl] = r


def add_parts(parts, tot):
    t = parts[0]
    for k in range(1, parts.shape[0]):
        t = t + parts[k]
    tot[...] = t


def coefs(tot, at, sl, fs, inv):
    i0, i1 = fs[inv], fs[inv + 1]
    m0, m1 = tot[at : at + 1, sl] * i0, tot[at + 1 : at + 2, sl] * i1
    q0 = lax.rsqrt(tot[at + 2 : at + 3, sl] * i0 - m0 * m0 + EPSILON)
    q1 = lax.rsqrt(tot[at + 3 : at + 4, sl] * i1 - m1 * m1 + EPSILON)
    return pick(m0, m1, fs), pick(q0, q1, fs)


def means(tot, at, sl, fs, inv):
    i0, i1 = fs[inv], fs[inv + 1]
    a = pick(tot[at : at + 1, sl] * i0, tot[at + 1 : at + 2, sl] * i1, fs)
    b = pick(tot[at + 2 : at + 3, sl] * i0, tot[at + 3 : at + 4, sl] * i1, fs)
    return a, b


def stat_rows(v, keep, fs):
    kept = v * keep
    return group_sums(kept, fs) + group_sums(kept * v, fs)


def back_rows(d, x, fs):
    return group_sums(d, fs) + group_sums(d * x, fs)


def loop(count, body):
    lax.fori_loop(0, count, lambda c, _: (body(c), 0)[1], 0, unroll=UNROLL)


def loop_from(first, last, body):
    for c in range(first, last):
        body(c)


def copy_all(pairs, sems):
    copies = [pltpu.make_async_copy(s, d, sems.at[k]) for k, (s, d) in enumerate(pairs)]
    for c in copies:
        c.start()
    return copies


def wait_all(copies):
    for c in copies:
        c.wait()


def at_rows(start, size):
    return pl.ds(pl.multiple_of(start, 16), size)


def flip(p):
    return (p & 1) * 8 + (p & 2) * 2 + (p & 4) // 2 + (p & 8) // 8


def setup_kernel(exact, crop, micro, fs, isc, keep, keep1, keep_half, sh, perm):
    n = lax.axis_index("narrow").astype(jnp.int32)
    w = lax.axis_index("wide").astype(jnp.int32)
    isc[NARROW] = n
    isc[CORE] = w & 1
    for p in range(16):
        isc[DEST + p] = (w ^ flip(p)) if exact else jnp.int32(p)

    def count(k, sums):
        c, one = crop[k], micro[k]
        a, b = (c >> 4) * (c >> 4), (c >> 5) * (c >> 5)
        return (
            sums[0] + a * (1 - one), sums[1] + a * one, sums[2] + b * (1 - one), sums[3] + b * one,
        )

    zero = jnp.int32(0)
    sums = lax.fori_loop(0, crop.shape[0], count, (zero, zero, zero, zero))
    for k in range(4):
        fs[k] = 1.0 / sums[k].astype(F32)
    fs[INV_ALL] = 1.0 / ((sums[2] + sums[3]).astype(F32) * 2048.0)
    at = lax.broadcasted_iota(jnp.int32, (POS, 1), 0)
    i8, j7 = at & 7, at >> 3
    at = lax.broadcasted_iota(jnp.int32, (HALF, 1), 0)
    r8, c14 = n * 8 + (at & 7), at >> 3

    def inside(r, c, side):
        return jnp.where((r < side) & (c < side), 1.0, 0.0).astype(F32)

    for b in range(B):
        c = crop[w * B + b]
        side_in, side_out = c >> 4, c >> 5
        fs[CELLS + b] = 1.0 / (side_out * side_out).astype(F32)
        fs[MICRO + b] = micro[w * B + b].astype(F32)
        keep[b * POS : (b + 1) * POS, :] = inside(i8, j7, side_out)
        for k in range(4):
            keep1[k, b * POS : (b + 1) * POS, :] = inside(2 * i8 + k // 2, 2 * j7 + k % 2, side_in)
        keep_half[b * HALF : (b + 1) * HALF, :] = inside(r8, c14, side_in)
    place = lax.broadcasted_iota(jnp.int32, (POS, M), 1)
    it = lax.broadcasted_iota(jnp.int32, (POS, M), 0)
    for t in range(9):
        di, dj = t // 3 - 1, t % 3 - 1
        i, j = (it & 7) + di, (it >> 3) + dj
        fits = (i >= 0) & (i < 8) & (j >= 0) & (j < 7)
        sh[t] = low(jnp.concatenate([
            jnp.where(fits & (place == b * POS + j * 8 + i), 1.0, 0.0) for b in range(B)
        ], axis=0))
    place = lax.broadcasted_iota(jnp.int32, (POS, HALF), 1)
    it = lax.broadcasted_iota(jnp.int32, (POS, HALF), 0)
    for half in range(2):
        planes = []
        for k in range(4):
            r, c = 2 * (it & 7) + k // 2, 2 * (it >> 3) + k % 2
            planes.append(
                jnp.where(((r >> 3) == half) & (place == c * 8 + (r & 7)), 1.0, 0.0)
            )
        perm[half] = low(jnp.concatenate(planes, axis=0))


def one_half_kernel(fs, px, keep, w1_far, st, x, w1, flat, sems):
    copies = copy_all([(px, x), (w1_far, w1)], sems)
    copies[0].wait()
    for b in range(B):
        flat[b * HALF : (b + 1) * HALF, :] = x[b]
    copies[1].wait()

    def body(c):
        sl = cols(c)
        v = mm(flat[...], w1[:, sl]) * keep[...]
        sums = [jnp.sum(v[b * HALF : (b + 1) * HALF], axis=0, keepdims=True) for b in range(B)]
        v2 = v * v
        sq = [jnp.sum(v2[b * HALF : (b + 1) * HALF], axis=0, keepdims=True) for b in range(B)]
        put(st, 0, grouped(sums, fs) + grouped(sq, fs), sl)

    loop(2, body)


TAPS = [(p, q) for p in range(3) for q in range(3)]


def stage_two_kernel(
    fs, isc, own, other, part, part_other, perm, keep1, keep, w1, ws, gb, sh,
    xp, strided, x1, col, pre2, st, tot1, tmp, hid, tot,
):
    n = isc[NARROW]
    tot[...] = part[...] + part_other[...]
    tot1[...] = tot[...]

    def permute(c):
        sl = cols(c)
        for b in range(B):
            r = mm(perm[n], own[b, :, sl]) + mm(perm[1 - n], other[b, :, sl])
            for k in range(4):
                tmp[k, b * POS : (b + 1) * POS, :] = r[k * POS : (k + 1) * POS]
        for k in range(4):
            xp[k, :, sl] = low(tmp[k] * keep1[k])
        strided[:, sl] = xp[0, :, sl]

    loop(4, permute)

    def first(c):
        k, sl = c // 2, cols(c % 2)
        v = mm(xp[k], w1[:, sl])
        mean, scale = coefs(tot, 0, sl, fs, INV_IN)
        x = (v - mean) * scale
        x1[k, :, sl] = x
        o = x * gb[0:1, sl] + gb[1:2, sl]
        hid[k, :, sl] = low(o * sigmoid(o) * keep1[k])

    loop(8, first)
    for t, (p, q) in enumerate(TAPS):
        h = hid[2 * (p != 1) + (q != 1)]
        if p == 0 or q == 0:
            h = low(mm(sh[3 * (0 if p == 0 else 1) + (0 if q == 0 else 1)], h))
        col[t] = h

    def second(c):
        sl = cols(c)
        v = mm(col[0], ws[0, :, sl])
        for t in range(1, 9):
            v = v + mm(col[t], ws[t, :, sl])
        pre2[:, sl] = v
        put(st, 0, stat_rows(v, keep[...], fs), sl)

    loop(2, second)


def project_kernel(fs, x, keep, wp_far, w3_far, prep, st, w3, wp, sems):
    copies = []
    for c in range(4):
        sl = slice(c * 512, (c + 1) * 512)
        copies.append(pltpu.make_async_copy(wp_far.at[:, sl], wp.at[:, sl], sems.at[c]))
    copies.append(pltpu.make_async_copy(w3_far, w3, sems.at[4]))
    for c in copies:
        c.start()

    def body(c):
        sl = cols(c)
        v = mm(x[...], wp[:, sl])
        prep[:, sl] = v
        put(st, 0, stat_rows(v, keep[...], fs), sl)

    for c in range(4):
        copies[c].wait()
        loop_from(2 * c, 2 * c + 2, body)
    copies[4].wait()


def stage_three_kernel(fs, parts, pre2, stp, keep, w3, gb, h2, pre3, st, tot2, tot):
    add_parts(parts, tot)
    tot2[...] = tot[...]
    sl = slice(0, 512)
    mean, scale = coefs(tot, 0, sl, fs, INV_OUT)
    o = (pre2[...] - mean) * scale * gb[2:3, :] + gb[3:4, :]
    h2[...] = low(o * sigmoid(o) * keep[...])
    st[4:8, :] = stp[...]

    def body(c):
        sl = cols(c)
        v = mm(h2[...], w3[:, sl])
        pre3[:, sl] = v
        put(st, 0, stat_rows(v, keep[...], fs), sl)

    loop(8, body)


def fetch_four_kernel(isc, own, r1, r2, w4, sems):
    n, core = isc[NARROW], isc[CORE]
    away = (1 - n) * 1024
    wait_all(copy_all(
        [
            (own, w4.at[at_rows(n * 1024, 1024)]),
            (r1, w4.at[at_rows(away + core * 512, 512)]),
            (r2, w4.at[at_rows(away + (1 - core) * 512, 512)]),
        ],
        sems,
    ))


def stage_four_kernel(
    fs, parts, pre3, prep, keep, vec, sqb, sq_far, ex_far, w4,
    lows, pre4, st, tot3, gate, sp, pooled, squares, unit, short, acc, tot, sq, ex, sems,
):
    copies = copy_all([(sq_far, sq), (ex_far, ex)], sems)
    add_parts(parts, tot)
    tot3[...] = tot[...]
    pooled[...] = jnp.zeros((8, 2048), F32)

    def units(c):
        sl = cols(c)
        mean, scale = coefs(tot, 0, sl, fs, INV_OUT)
        u = ((pre3[:, sl] - mean) * scale * vec[0:1, sl] + vec[1:2, sl]) * keep[...]
        unit[:, sl] = u
        for b, r in enumerate(image_sums(u)):
            pooled[b : b + 1, sl] = r * fs[CELLS + b]
        mean, scale = coefs(tot, 4, sl, fs, INV_OUT)
        s = ((prep[:, sl] - mean) * scale * vec[2:3, sl] + vec[3:4, sl]) * keep[...]
        short[:, sl] = s

    loop(8, units)
    wait_all(copies)
    sp[...] = dot3(pooled[...], sq[...]) + sqb[0:1, :]
    squeezed = sp[...] * sigmoid(sp[...])
    gate[...] = sigmoid(dot3(squeezed, ex[...]) + vec[4:5, :])
    squares[...] = jnp.zeros((8, 256), F32)
    acc[...] = jnp.zeros((M, 512), F32)

    def streams(c):
        sl = cols(c)
        branch = unit[:, sl] * expand([gate[b : b + 1, sl] for b in range(B)])
        s = short[:, sl]
        join = branch + s
        stream = join * sigmoid(join) * keep[...]
        for k, v in enumerate((stream, branch, s)):
            squares[k : k + 1, :] += jnp.sum(v * v, axis=0, keepdims=True)
        lo = low(stream)
        lows[:, sl] = lo
        acc[...] += mm(lo, w4[cols(c), :])

    loop(8, streams)
    pre4[...] = acc[...]
    put(st, 0, stat_rows(acc[...], keep[...], fs), slice(0, 512))


def fetch_five_kernel(isc, own, r1, r2, w5, sems):
    n, core = isc[NARROW], isc[CORE]
    wait_all(copy_all([
        (own, w5.at[n]),
        (r1, w5.at[1 - n, at_rows(core * 2304, 2304)]),
        (r2, w5.at[1 - n, at_rows((1 - core) * 2304, 2304)]),
    ], sems))


def stage_five_kernel(
    fs, parts, pre4, keep, gb, sh, w5, col, pre5, st, tot4, tot
):
    add_parts(parts, tot)
    tot4[...] = tot[...]
    mean, scale = coefs(tot, 0, slice(0, 512), fs, INV_OUT)
    o = (pre4[...] - mean) * scale * gb[4:5, :] + gb[5:6, :]
    h = low(o * sigmoid(o) * keep[...])
    for t in range(9):
        col[t] = h if t == 4 else low(mm(sh[t], h))
    def body(c):
        v = 0.0
        for t in range(9):
            v = v + mm(col[t], w5[c, t * 512 : (t + 1) * 512, :])
        pre5[:, cols(c)] = v
        put(st, 0, stat_rows(v, keep[...], fs), cols(c))

    loop(2, body)


def fetch_six_kernel(isc, own, r1, r2, vown, w6, gain5, vec2, vaway, sems):
    n, core = isc[NARROW], isc[CORE]
    pairs = [(r1.at[VEC_AT:PACK_ROWS], vaway), (own, w6.at[at_rows(n * 256, 256)])]
    for r, h in ((r1, core), (r2, 1 - core)):
        for c in range(8):
            pairs.append(
                (
                    r.at[W6_AT + c * 128 : W6_AT + (c + 1) * 128],
                    w6.at[at_rows((1 - n) * 256 + h * 128, 128), c * 256 : (c + 1) * 256],
                )
            )
    copies = copy_all(pairs, sems)
    copies[0].wait()
    for side, v in ((n, f32(vown[...])), (1 - n, f32(vaway[...]))):
        for k in range(2):
            gain5[k : k + 1, cols(side)] = v[k : k + 1]
        for k in range(3):
            for c in range(4):
                at = 2 + 4 * k + c
                vec2[k : k + 1, cols(side * 4 + c)] = v[at : at + 1]
    wait_all(copies[1:])


def stage_six_kernel(
    fs, parts, pre5, keep, gain5, w6, h5, pre6, st, tot5, tot
):
    add_parts(parts, tot)
    tot5[...] = tot[...]
    mean, scale = coefs(tot, 0, slice(0, 512), fs, INV_OUT)
    o = (pre5[...] - mean) * scale * gain5[0:1, :] + gain5[1:2, :]
    h5[...] = low(o * sigmoid(o) * keep[...])

    def body(c):
        sl = cols(c)
        v = mm(h5[...], w6[:, sl])
        pre6[:, sl] = v
        put(st, 0, stat_rows(v, keep[...], fs), sl)

    loop(8, body)


def fetch_turn_kernel(isc, sqown, exown, r1, r2, ogown, ogother, sq, ex, og, sems):
    n, core = isc[NARROW], isc[CORE]
    pairs = [
        (sqown, sq.at[at_rows(n * 1024, 1024)]),
        (exown, ex.at[n]),
        (ogown, og.at[n]),
        (ogother, og.at[1 - n]),
    ]
    for r, h in ((r1, core), (r2, 1 - core)):
        for k in range(2):
            pairs.append(
                (
                    r.at[SQ_AT : SQ_AT + 256, k * 128 : (k + 1) * 128],
                    sq.at[at_rows((1 - n) * 1024 + h * 512 + k * 256, 256)],
                )
            )
        for c in range(4):
            pairs.append(
                (
                    r.at[EX_AT + c * 64 : EX_AT + (c + 1) * 64],
                    ex.at[1 - n, at_rows(h * 64, 64), c * 256 : (c + 1) * 256],
                )
            )
    wait_all(copy_all(pairs, sems))


def turn_kernel(
    fs, isc, parts, pre6, keep, lows, vec, sqb, sq1s, sq, ex, og,
    result, dj2, pay, extra, tot6, gate, dp, pooled, de, ds, squeezed, unit, res, tot, sp,
):
    n = isc[NARROW]
    add_parts(parts, tot)
    tot6[...] = tot[...]
    pooled[...] = jnp.zeros((8, 2048), F32)
    de[...] = jnp.zeros((8, 2048), F32)

    def units(c):
        sl = cols(c)
        mean, scale = coefs(tot, 0, sl, fs, INV_OUT)
        u = ((pre6[:, sl] - mean) * scale * vec[0:1, sl] + vec[1:2, sl]) * keep[...]
        unit[:, sl] = u
        for b, r in enumerate(image_sums(u)):
            pooled[b : b + 1, sl] = r * fs[CELLS + b]

    loop(8, units)
    sp[...] = dot3(pooled[...], sq[...]) + sqb[1:2, :]
    squeezed[...] = sp[...] * sigmoid(sp[...])
    for h in range(2):
        sl = slice(h * 1024, (h + 1) * 1024)
        gate[:, sl] = sigmoid(dot3(squeezed[...], ex[h]) + vec[2:3, sl])
    extra[...] = jnp.zeros((8, 512), F32)
    for k in range(3):
        extra[5 + k // 2 : 6 + k // 2, (k % 2) * 256 : (k % 2) * 256 + 256] = sq1s[k : k + 1, :]

    def streams(c):
        sl = cols(c)
        h, part = c // 4, cols(c % 4)
        u = unit[:, sl]
        branch = u * expand([gate[b : b + 1, sl] for b in range(B)])
        join = branch + f32(lows[:, sl])
        s = sigmoid(join)
        stream = join * s * keep[...]
        res[h, :, part] = low(stream)
        d = f32(og[h, :, part]) * keep[...] * (s * (1.0 + join * (1.0 - s)))
        dj2[:, sl] = d
        for b, r in enumerate(image_sums(d * u)):
            de[b : b + 1, sl] = r
        extra[6:7, 256:512] += jnp.sum(branch * branch, axis=0, keepdims=True)
        extra[7:8, 0:256] += jnp.sum(stream * stream, axis=0, keepdims=True)

    loop(8, streams)
    result[...] = res[n]
    de[...] = de[...] * gate[...] * (1.0 - gate[...])
    back = 0.0
    for h in range(2):
        back = back + dot3_nt(de[:, h * 1024 : (h + 1) * 1024], ex[h])
    ds[...] = back * slope(sp[...])
    dp[...] = dot3_nt(ds[...], sq[...])
    for b in range(B):
        dp[b : b + 1, :] = dp[b : b + 1, :] * fs[CELLS + b]
    total = jnp.sum(de[...], axis=0, keepdims=True)
    for k in range(4):
        extra[k : k + 1, :] = total[:, k * 512 : (k + 1) * 512]
    extra[4:5, 0:128] = jnp.sum(ds[...], axis=0, keepdims=True)

    def tops(c):
        sl = cols(c)
        mean, scale = coefs(tot, 0, sl, fs, INV_OUT)
        x = (pre6[:, sl] - mean) * scale
        du = (
            dj2[:, sl] * expand([gate[b : b + 1, sl] for b in range(B)])
            + expand([dp[b : b + 1, sl] for b in range(B)])
        ) * keep[...]
        put(pay, 0, back_rows(du, x, fs), sl)

    loop(8, tops)


def whole_gain(tot, at, gain, bias):
    gain[...] = (tot[at + 2 : at + 3, :] + tot[at + 3 : at + 4, :]).reshape(gain.shape)
    bias[...] = (tot[at : at + 1, :] + tot[at + 1 : at + 2, :]).reshape(bias.shape)


def half_gain(tot, n, gain, bias):
    sl = cols(n, gain.shape[0])
    gain[...] = (tot[2:3, sl] + tot[3:4, sl]).reshape(gain.shape)
    bias[...] = (tot[0:1, sl] + tot[1:2, sl]).reshape(bias.shape)


def back_six_kernel(
    fs, isc, parts, tot6, pre6, dj2, gate, dp, pre5, tot5, extra, keep, vec, gain5, w6,
    d6, do5, st, dgain, dbias, tot, acc,
):
    add_parts(parts, tot)
    half_gain(tot, isc[NARROW], dgain, dbias)
    acc[...] = jnp.zeros((M, 512), F32)

    def body(c):
        sl = cols(c)
        mean, scale = coefs(tot6, 0, sl, fs, INV_OUT)
        x = (pre6[:, sl] - mean) * scale
        du = (
            dj2[:, sl] * expand([gate[b : b + 1, sl] for b in range(B)])
            + expand([dp[b : b + 1, sl] for b in range(B)])
        ) * keep[...]
        a, bb = means(tot, 0, sl, fs, INV_OUT)
        d = low((du - a - x * bb) * (scale * vec[0:1, sl]) * keep[...])
        d6[:, sl] = d
        acc[...] += mm_nt(d, w6[:, sl])

    loop(8, body)
    mean, scale = coefs(tot5, 0, slice(0, 512), fs, INV_OUT)
    x = (pre5[...] - mean) * scale
    o = x * gain5[0:1, :] + gain5[1:2, :]
    d = acc[...] * keep[...] * slope(o)
    do5[...] = d
    put(st, 0, back_rows(d, x, fs), slice(0, 512))
    st[4:12, :] = extra[...]


def back_five_kernel(
    fs, isc, parts, tot5, pre5, do5, pre4, tot4, keep, gb, gain5, sh, w5,
    d5, do4, st, dgain, dbias, debias, dsbias, norms, tot,
):
    n = isc[NARROW]
    add_parts(parts, tot)
    half_gain(tot, n, dgain, dbias)
    excite = jnp.concatenate([tot[pl.ds(4 + 2 * n, 1), :], tot[pl.ds(5 + 2 * n, 1), :]], axis=1)
    debias[...] = excite.reshape(1024)
    dsbias[...] = tot[8:9, 0:128].reshape(128)
    for k in range(5):
        v = tot[9 + k // 2 : 10 + k // 2, (k % 2) * 256 : (k % 2) * 256 + 256]
        norms[k] = jnp.sqrt(jnp.sum(v, axis=1, keepdims=True) * fs[INV_ALL])[0, 0]
    sl = slice(0, 512)
    mean, scale = coefs(tot5, 0, sl, fs, INV_OUT)
    x = (pre5[...] - mean) * scale
    a, bb = means(tot, 0, sl, fs, INV_OUT)
    d = low((do5[...] - a - x * bb) * (scale * gain5[0:1, :]) * keep[...])
    d5[...] = d
    acc = 0.0
    for t in range(9):
        dc = d if t == 4 else low(mm(sh[8 - t], d))
        for h in range(2):
            acc = acc + mm_nt(dc[:, h * 256 : (h + 1) * 256], w5[h, t * 512 : (t + 1) * 512, :])
    mean, scale = coefs(tot4, 0, sl, fs, INV_OUT)
    x = (pre4[...] - mean) * scale
    o = x * gb[4:5, :] + gb[5:6, :]
    d = acc * keep[...] * slope(o)
    do4[...] = d
    put(st, 0, back_rows(d, x, fs), sl)


def back_four_kernel(
    fs, parts, tot4, pre4, do4, dj2, tot3, pre3, prep, gate, sp, keep, gb, vec, sq_far, ex_far, w4,
    d4, dj1, st, dgain, dbias, dp, de, ds, bias, tot, sq, ex, sems,
):
    copies = copy_all([(sq_far, sq), (ex_far, ex)], sems)
    add_parts(parts, tot)
    whole_gain(tot, 0, dgain, dbias)
    de[...] = jnp.zeros((8, 2048), F32)
    mean, scale = coefs(tot4, 0, slice(0, 512), fs, INV_OUT)
    x = (pre4[...] - mean) * scale
    a, bb = means(tot, 0, slice(0, 512), fs, INV_OUT)
    d4[...] = low((do4[...] - a - x * bb) * (scale * gb[4:5, :]) * keep[...])

    def joins(c):
        sl = cols(c)
        back = dj2[:, sl] + mm_nt(d4[...], w4[cols(c), :])
        mean, scale = coefs(tot3, 0, sl, fs, INV_OUT)
        u = ((pre3[:, sl] - mean) * scale * vec[0:1, sl] + vec[1:2, sl]) * keep[...]
        mean, scale = coefs(tot3, 4, sl, fs, INV_OUT)
        s = ((prep[:, sl] - mean) * scale * vec[2:3, sl] + vec[3:4, sl]) * keep[...]
        join = u * expand([gate[b : b + 1, sl] for b in range(B)]) + s
        d = f32(low(back)) * keep[...] * slope(join)
        dj1[:, sl] = d
        for b, r in enumerate(image_sums(d * u)):
            de[b : b + 1, sl] = r

    loop(8, joins)
    wait_all(copies)
    de[...] = de[...] * gate[...] * (1.0 - gate[...])
    ds[...] = dot3_nt(de[...], ex[...]) * slope(sp[...])
    dp[...] = dot3_nt(ds[...], sq[...])
    for b in range(B):
        dp[b : b + 1, :] = dp[b : b + 1, :] * fs[CELLS + b]
    total = jnp.sum(de[...], axis=0, keepdims=True)
    bias[...] = jnp.zeros((8, 512), F32)
    for k in range(4):
        bias[k : k + 1, :] = total[:, k * 512 : (k + 1) * 512]
    bias[4:5, 0:128] = jnp.sum(ds[...], axis=0, keepdims=True)

    def tops(c):
        sl = cols(c)
        d = dj1[:, sl]
        mean, scale = coefs(tot3, 0, sl, fs, INV_OUT)
        x = (pre3[:, sl] - mean) * scale
        du = (
            d * expand([gate[b : b + 1, sl] for b in range(B)])
            + expand([dp[b : b + 1, sl] for b in range(B)])
        ) * keep[...]
        put(st, 0, back_rows(du, x, fs), sl)
        mean, scale = coefs(tot3, 4, sl, fs, INV_OUT)
        put(st, 4, back_rows(d, (prep[:, sl] - mean) * scale, fs), sl)

    loop(8, tops)


def back_three_kernel(
    fs, parts, tot3, pre3, prep, dj1, gate, dp, bias, pre2, tot2, keep, vec, gb, w3,
    d3, dproj, do2, st, dgain, dbias, dgainp, dbiasp, tot, acc,
):
    add_parts(parts, tot)
    whole_gain(tot, 0, dgain, dbias)
    whole_gain(tot, 4, dgainp, dbiasp)
    acc[...] = jnp.zeros((M, 512), F32)

    def body(c):
        sl = cols(c)
        mean, scale = coefs(tot3, 0, sl, fs, INV_OUT)
        x = (pre3[:, sl] - mean) * scale
        dj = dj1[:, sl]
        du = (
            dj * expand([gate[b : b + 1, sl] for b in range(B)])
            + expand([dp[b : b + 1, sl] for b in range(B)])
        ) * keep[...]
        a, bb = means(tot, 0, sl, fs, INV_OUT)
        d = low((du - a - x * bb) * (scale * vec[0:1, sl]) * keep[...])
        d3[:, sl] = d
        acc[...] += mm_nt(d, w3[:, sl])
        mean, scale = coefs(tot3, 4, sl, fs, INV_OUT)
        x = (prep[:, sl] - mean) * scale
        a, bb = means(tot, 4, sl, fs, INV_OUT)
        dproj[:, sl] = low((dj - a - x * bb) * (scale * vec[2:3, sl]) * keep[...])

    loop(8, body)
    sl = slice(0, 512)
    mean, scale = coefs(tot2, 0, sl, fs, INV_OUT)
    x = (pre2[...] - mean) * scale
    o = x * gb[2:3, :] + gb[3:4, :]
    d = acc[...] * keep[...] * slope(o)
    do2[...] = d
    put(st, 0, back_rows(d, x, fs), sl)
    st[4:12, :] = bias[...]


def fetch_two_kernel(far, ws, sems):
    wait_all(copy_all([(far.at[3 * k : 3 * k + 3], ws.at[3 * k : 3 * k + 3]) for k in range(3)], sems))


def back_two_kernel(
    fs, parts, tot2, pre2, do2, x1, keep1, keep, gb, sh, ws,
    d2, do1, st, dgain, dbias, debias, dsbias, tot, dcol,
):
    add_parts(parts, tot)
    whole_gain(tot, 0, dgain, dbias)
    debias[...] = jnp.concatenate([tot[k : k + 1, :] for k in range(4, 8)], axis=1).reshape(2048)
    dsbias[...] = tot[8:9, 0:128].reshape(128)
    sl = slice(0, 512)
    mean, scale = coefs(tot2, 0, sl, fs, INV_OUT)
    x = (pre2[...] - mean) * scale
    a, bb = means(tot, 0, sl, fs, INV_OUT)
    d = low((do2[...] - a - x * bb) * (scale * gb[2:3, :]) * keep[...])
    d2[...] = d
    dcol[0] = d
    dcol[1] = low(mm(sh[5], d))
    dcol[2] = low(mm(sh[7], d))
    dcol[3] = low(mm(sh[8], d))
    terms = (
        ((0, 4),),
        ((0, 5), (1, 3)),
        ((0, 7), (2, 1)),
        ((0, 8), (1, 6), (2, 2), (3, 0)),
    )
    st[...] = jnp.zeros((4, 512), F32)
    for k in range(4):
        acc = 0.0
        for which, t in terms[k]:
            acc = acc + mm_nt(dcol[which], ws[t])
        x = x1[k]
        o = x * gb[0:1, :] + gb[1:2, :]
        d = acc * keep1[k] * slope(o)
        do1[k] = d
        rows = back_rows(d, x, fs)
        for r in range(4):
            st[r : r + 1, :] += rows[r]


def deal(isc, full, rows, keep, send, at):
    for p in range(16):
        tile = full[pl.ds(pl.multiple_of(isc[DEST + p] * rows, rows), rows), :]
        (keep if p < 8 else send)[p % 8, at_rows(at, rows), :] = tile


def back_one_kernel(
    fs, isc, parts, tot1, x1, do1, xp, keep1, gb, d1, gkeep, gsend, dgain, dbias, tot, dn, full
):
    n = isc[NARROW]
    add_parts(parts, tot)
    whole_gain(tot, 0, dgain, dbias)
    sl = slice(0, 512)
    scale = coefs(tot1, 0, sl, fs, INV_IN)[1] * gb[0:1, :]
    a, bb = means(tot, 0, sl, fs, INV_IN)
    planes = []
    for k in range(4):
        d = (do1[k] - a - x1[k] * bb) * scale * keep1[k]
        planes.append(d)
        dn[k] = low(d)
    for b in range(B):
        d1[b] = low(jnp.concatenate([d[b * POS : (b + 1) * POS] for d in planes], axis=0))

    def body(c):
        g = 0.0
        for k in range(4):
            g = g + mm_tn(xp[k, :, cols(c)], dn[k, :, cols(n)])
        full[cols(c), :] = low(g)

    loop(4, body)
    deal(isc, full, 64, gkeep, gsend, 0)


def placed_kernel(isc, dproj, wp_far, out, cc, pick_own, spread, wp, sems):
    n = isc[NARROW]
    copies = [
        pltpu.make_async_copy(wp_far.at[cut], wp.at[cut], sems.at[k])
        for k, cut in enumerate(slice(256 * k, 256 * (k + 1)) for k in range(4))
    ]
    for c in copies:
        c.start()
    for b in range(B):
        place = lax.broadcasted_iota(jnp.int32, (32, M), 1)
        it = lax.broadcasted_iota(jnp.int32, (32, M), 0)
        pick_own[b * 32 : (b + 1) * 32, :] = low(jnp.where(
            (place == b * POS + (it >> 2) * 8 + n * 4 + (it & 3)) & (it < 28), 1.0, 0.0
        ))
        place = lax.broadcasted_iota(jnp.int32, (HALF, 128), 1)
        it = lax.broadcasted_iota(jnp.int32, (HALF, 128), 0)
        spread[b * HALF : (b + 1) * HALF, :] = low(jnp.where(
            ((it & 9) == 0) & (place == b * 32 + (it >> 4) * 4 + ((it & 7) >> 1)), 1.0, 0.0
        ))
    cc[...] = low(mm(pick_own[...], dproj[...]))
    for c in range(4):
        sl = cols(c)
        copies[c].wait()
        hi, lo = split2(mm_nt(cc[...], wp[sl, :]))
        out[:, sl] = mm(spread[...], hi) + mm(spread[...], lo)


def image_kernel(isc, perm, d1, placed, keep, w1, out, dc):
    n = isc[NARROW]
    for b in range(B):
        dc[b * HALF : (b + 1) * HALF, :] = low(mm_tn(perm[n], d1[b]))
    for c in range(4):
        sl = cols(c)
        out[:, sl] = (mm_nt(dc[...], w1[sl, :]) + placed[:, sl]) * keep[...]


def grads_a_kernel(isc, h5, d6, col4, d5, gkeep, gsend, wider, full):
    n = isc[NARROW]

    def expand2(c):
        wider[:, cols(c)] = low(mm_tn(h5[:, cols(n)], d6[:, cols(c)]))

    loop(8, expand2)
    for p in range(16):
        sl = cols(isc[DEST + p], 128)
        for k in range(2):
            (gkeep if p < 8 else gsend)[p % 8, 0:128, k * 128 : (k + 1) * 128] = wider[
                k * 128 : (k + 1) * 128, sl
            ]

    def spatial(t):
        full[...] = low(mm_tn(col4[t], d5[:, cols(n)]))
        deal(isc, full, 32, gkeep, gsend, 128 + t * 32)

    loop(9, spatial)


def gate_grads(isc, n, c, at, squeezed, pooled, de, ds, gkeep, gsend, q, e):
    sl = cols(n * 4 + c)
    q[...] = outer(ds[...], pooled[:, sl])
    e[...] = outer(squeezed[...], de[:, sl])
    for p in range(16):
        rows = pl.ds(pl.multiple_of(isc[DEST + p] * 8, 8), 8)
        both = jnp.concatenate([q[rows, :], e[rows, :]], axis=0)
        (gkeep if p < 8 else gsend)[p % 8, at_rows(at + c * 16, 16), :] = low(both)


def grads_b_kernel(
    isc, d4, lows, sq2, pooled2, de2, ds2, sp1, pooled1, de1, ds1, gkeep, gsend, full, q, e, sq1
):
    n = isc[NARROW]
    sq1[...] = sp1[...] * sigmoid(sp1[...])

    def body(c):
        full[...] = low(mm_tn(d4[...], lows[:, cols(n * 4 + c)]))
        deal(isc, full, 32, gkeep, gsend, c * 32)
        gate_grads(isc, n, c, 128, sq2, pooled2, de2, ds2, gkeep, gsend, q, e)
        gate_grads(isc, n, c, 192, sq1, pooled1, de1, ds1, gkeep, gsend, q, e)

    loop(4, body)


def grads_c_kernel(isc, h2, d3, strided, dproj, gkeep, gsend, full, taller):
    n = isc[NARROW]

    def body(c):
        sl = cols(n * 4 + c)
        full[...] = low(mm_tn(h2[...], d3[:, sl]))
        deal(isc, full, 32, gkeep, gsend, c * 32)
        taller[...] = low(mm_tn(strided[...], dproj[:, sl]))
        deal(isc, taller, 64, gkeep, gsend, 128 + c * 64)

    loop(4, body)


def grads_d_kernel(isc, col1, d2, gkeep, gsend, full):
    n = isc[NARROW]

    def spatial(t):
        full[...] = low(mm_tn(col1[t], d2[:, cols(n)]))
        deal(isc, full, 32, gkeep, gsend, t * 32)

    loop(9, spatial)


def joined(v, out, at, rows):
    for c in range(4):
        out[:, c * 256 : (c + 1) * 256] = v[at + c * rows : at + (c + 1) * rows, :]


def unpack_gates(v, at, squeeze, excite):
    for c in range(4):
        part = v[at + c * 16 : at + (c + 1) * 16, :]
        squeeze[:, c * 256 : (c + 1) * 256] = part[0:8]
        excite[:, c * 256 : (c + 1) * 256] = part[8:16]


def unpack_a_kernel(a, b, expand2, spatial2):
    v = f32(a[0]) + f32(b[0])
    expand2[0:128, :] = v[0:128, 0:128]
    expand2[128:256, :] = v[0:128, 128:256]
    spatial2[...] = v[128:416, :]


def unpack_b_kernel(a, b, reduce2, squeeze2, excite2, squeeze1, excite1):
    v = f32(a[0]) + f32(b[0])
    joined(v, reduce2, 0, 32)
    unpack_gates(v, 128, squeeze2, excite2)
    unpack_gates(v, 192, squeeze1, excite1)


def unpack_c_kernel(a, b, expand1, project1):
    v = f32(a[0]) + f32(b[0])
    joined(v, expand1, 0, 32)
    joined(v, project1, 128, 64)


def unpack_d_kernel(a, b, spatial1):
    spatial1[...] = f32(a[0]) + f32(b[0])


VECTORS = (512,) * 6 + (2048,) * 5 + (128,) * 2 + (256,) * 2 + (1024,) * 3


def pack_kernel(isc, w5, w4, w6, ex, sq, ws_far, *refs):
    far, refs = refs[:18], refs[18:]
    out, w5_half, w4_half, gb, vec1, sqb, vown, ws, w6v, exv, sqv, rows = refs[:12]
    vecs, sems = refs[12:30], refs[30]
    core = isc[CORE]
    pairs = [(f, v) for f, v in zip(far, vecs)] + [
        (w6.at[at_rows(core * 128, 128)], w6v),
        (ex.at[at_rows(core * 64, 64)], exv),
        (sq.at[at_rows(core * 512, 512)], sqv),
        (w4.at[at_rows(core * 512, 512)], w4_half),
        (w5.at[at_rows(core * 2304, 2304)], w5_half),
        (ws_far, ws),
    ]
    copies = copy_all(pairs, sems)
    wait_all(copies[:21])

    def row(v):
        return f32(v[...]).reshape(1, v.shape[0])

    for k in range(6):
        gb[k : k + 1, :] = row(vecs[k])
    for k in range(5):
        vec1[k : k + 1, :] = row(vecs[6 + k])
    for k in range(2):
        sqb[k : k + 1, :] = row(vecs[11 + k])
    rows[...] = jnp.zeros((16, 256), F32)
    at = 0
    for v in vecs[13:18]:
        r = row(v)
        for c in range(v.shape[0] // 256):
            rows[at : at + 1, :] = r[:, c * 256 : (c + 1) * 256]
            at += 1
    vown[...] = low(rows[...])
    for c in range(8):
        out[W6_AT + c * 128 : W6_AT + (c + 1) * 128, :] = w6v[:, c * 256 : (c + 1) * 256]
    for c in range(4):
        out[EX_AT + c * 64 : EX_AT + (c + 1) * 64, :] = exv[:, c * 256 : (c + 1) * 256]
    for k in range(2):
        out[SQ_AT : SQ_AT + 256, k * 128 : (k + 1) * 128] = sqv[k * 256 : (k + 1) * 256, :]
    out[VEC_AT:PACK_ROWS, :] = vown[...]
    wait_all(copies[21:])


def call(body, outs, args, scratch=(), flops=1e8, size=5e6, name=None, vmem=LIMIT):
    specs, values = [], []
    for a in args:
        kind, v = a if isinstance(a, tuple) else (VMEM, a)
        specs.append(kind)
        values.append(v)
    return pl.pallas_call(
        body,
        out_shape=tuple(o if hasattr(o, "memory_space") else jax.ShapeDtypeStruct(o[0], o[1]) for o in outs),
        in_specs=specs,
        out_specs=tuple(o[2] if isinstance(o, tuple) and len(o) > 2 else pl.BlockSpec(memory_space=getattr(o, "memory_space", pltpu.VMEM)) for o in outs),
        scratch_shapes=list(scratch),
        compiler_params=pltpu.CompilerParams(vmem_limit_bytes=vmem * 2**20),
        cost_estimate=pl.CostEstimate(
            flops=int(flops * SCALE), bytes_accessed=int(size * SCALE), transcendentals=0
        ),
        name=name,
    )(*values)


def swap(v, axis, pairs):
    return lax.ppermute(v, axis, pairs)


def after(v, *others):
    return lax.optimization_barrier((v,) + others)[0]


def local(
    images, crop, micro,
    first_reduce, first_reduce_gain, first_reduce_bias,
    first_spatial, first_spatial_gain, first_spatial_bias,
    first_expand, first_expand_gain, first_expand_bias,
    first_project, first_project_gain, first_project_bias,
    first_squeeze, first_squeeze_bias, first_excite, first_excite_bias,
    second_reduce, second_reduce_gain, second_reduce_bias,
    second_spatial, second_spatial_gain, second_spatial_bias,
    second_expand, second_expand_gain, second_expand_bias,
    second_squeeze, second_squeeze_bias, second_excite, second_excite_bias,
    out_grad,
):
    wide = lax.axis_size("wide")
    exact = wide == 16
    near = [(i, i ^ 1) for i in range(wide)]
    pair = [(0, 1), (1, 0)]
    V = pltpu.VMEM
    D = pltpu.SemaphoreType.DMA
    out = lambda *shape: (shape, F32)
    f = lambda *shape: V(shape, F32)
    h = lambda *shape: V(shape, BF)
    far = lambda v: (ANY, pltpu.with_memory_space_constraint(v, pltpu.HBM))

    def steps(x, *first, before=None):
        results, step = [], 1
        x = after(x, *first)
        while step < wide:
            y = after(x, *(before or {}).get(len(results), ()))
            x = x + swap(y, "wide", [(i, i ^ step) for i in range(wide)])
            results.append(x)
            step *= 2
        return x[None], results

    own_px = images.transpose(0, 2, 1, 3).reshape(B, HALF, 1024)
    other_px = swap(own_px, "narrow", pair)
    ws_far = first_spatial.reshape(9, 512, 512)

    fs_, isc_, keep, keep1, keep_half, sh, perm = call(
        functools.partial(setup_kernel, exact),
        [
            pltpu.SMEM((13,), F32), pltpu.SMEM((18,), jnp.int32), f(M, 1), f(4, M, 1), f(HROWS, 1),
            h(9, M, M), h(2, M, HALF),
        ],
        [(SMEM, far(crop)[1]), (SMEM, far(micro)[1])], name="setup",
    )
    fs, isc = (SMEM, fs_), (SMEM, isc_)
    st1, xown, w1 = call(
        one_half_kernel, [f(4, 512), h(B, HALF, 1024), h(1024, 512)],
        [fs, far(own_px), keep_half, far(first_reduce)],
        [V((HROWS, 1024), BF), D((2,))], flops=5e8, name="one_half",
    )
    part = steps(st1)[0][0]

    w5_own = second_spatial.reshape(9 * 512, 256)
    vectors = [
        first_reduce_gain, first_reduce_bias, first_spatial_gain, first_spatial_bias,
        second_reduce_gain, second_reduce_bias, first_expand_gain, first_expand_bias,
        first_project_gain, first_project_bias, first_excite_bias,
        first_squeeze_bias, second_squeeze_bias,
        second_spatial_gain, second_spatial_bias, second_expand_gain, second_expand_bias, second_excite_bias,
    ]
    pack, w5_half, w4_half, gb, vec1, sqb, vown, ws = call(
        pack_kernel,
        [
            ((PACK_ROWS, 256), BF), ((2304, 256), BF), ((512, 512), BF), f(8, 512), f(8, 2048), f(8, 128), h(16, 256),
            h(9, 512, 512),
        ],
        [
            (SMEM, after(isc_, st1)), far(w5_own), far(second_reduce), far(second_expand), far(second_excite),
            far(second_squeeze), far(ws_far),
        ] + [far(v) for v in vectors],
        [V((128, 2048), BF), V((64, 1024), BF), V((512, 128), BF), V((16, 256), F32)]
        + [V((size,), BF) for size in VECTORS] + [D((24,))],
        size=2e7, name="pack",
    )
    part = after(part, gb)
    part_other = swap(part, "narrow", pair)
    w4_r1 = swap(after(w4_half, other_px, part_other), "narrow", pair)
    og_own = out_grad.transpose(0, 2, 1, 3).reshape(M, 1024)

    xp, strided, x1, col1, pre2, st2, tot1 = call(
        stage_two_kernel,
        [h(4, M, 1024), h(M, 1024), f(4, M, 512), h(9, M, 512), f(M, 512), f(4, 512), f(4, 512)],
        [fs, isc, xown, other_px, part, part_other, perm, keep1, keep, w1, ws, gb, sh],
        [V((4, M, 256), F32), V((4, M, 512), BF), V((4, 512), F32)],
        flops=4e9, size=2e7, name="stage_two",
    )
    parts2, sent2 = steps(st2, before={3: (w4_r1,)})
    w4_r2 = swap(after(w4_r1, sent2[1]), "wide", near)
    w5_r1 = swap(after(w5_half, w4_r1, sent2[1]), "narrow", pair)
    prep, stp, w3 = call(
        project_kernel, [f(M, 2048), f(4, 2048), h(512, 2048)],
        [fs, strided, keep, far(first_project), far(first_expand)],
        [V((1024, 2048), BF), D((5,))], flops=1e9, size=8e6, name="project",
    )
    h2, pre3, st3, tot2 = call(
        stage_three_kernel, [h(M, 512), f(M, 2048), f(8, 2048), f(4, 512)],
        [fs, parts2, pre2, stp, keep, w3, gb], [V((4, 512), F32)],
        flops=1e9, size=6e6, name="stage_three",
    )
    parts3, _ = steps(st3, before={3: (w4_r2,)})
    w5_r2 = swap(after(w5_r1, parts3), "wide", near)
    pk1 = swap(after(pack, w5_r1, parts3), "narrow", pair)
    w4 = call(
        fetch_four_kernel, [h(2048, 512)],
        [(SMEM, after(isc_, st3)), far(second_reduce), (ANY, w4_r1), (ANY, w4_r2)], [D((3,))],
        size=4e6, name="fetch_four",
    )[0]
    lows, pre4, st4, tot3, gate1, sp1, pooled1, squares = call(
        stage_four_kernel,
        [
            h(M, 2048), f(M, 512), f(4, 512), f(8, 2048), f(8, 2048), f(8, 128), f(8, 2048), f(8, 256),
        ],
        [fs, parts3, pre3, prep, keep, vec1, sqb, far(first_squeeze), far(first_excite), w4],
        [
            V((M, 2048), F32), V((M, 2048), F32), V((M, 512), F32), V((8, 2048), F32),
            V((2048, 128), BF), V((128, 2048), BF), D((2,)),
        ],
        flops=1e9, size=1e7, name="stage_four",
    )
    parts4, _ = steps(st4, before={3: (w5_r2,)})
    w5 = call(
        fetch_five_kernel, [h(2, 4608, 256)],
        [(SMEM, after(isc_, st4)), far(w5_own), (ANY, w5_r1), (ANY, w5_r2)], [D((3,))],
        size=8e6, name="fetch_five",
    )[0]
    col4, pre5, st5, tot4 = call(
        stage_five_kernel, [h(9, M, 512), f(M, 512), f(4, 512), f(4, 512)],
        [fs, parts4, pre4, keep, gb, sh, w5], [V((4, 512), F32)],
        flops=2e9, size=1e7, name="stage_five",
    )
    pk2 = swap(after(pk1, st5), "wide", near)
    parts5, _ = steps(st5, before={3: (pk2,)})
    og_other = swap(after(og_own, pk1, st5), "narrow", pair)
    pk1, pk2 = (ANY, pk1), (ANY, pk2)
    w6, gain5, vec2 = call(
        fetch_six_kernel, [h(512, 2048), f(2, 512), f(3, 2048)],
        [(SMEM, after(isc_, st5)), far(second_expand), pk1, pk2, vown],
        [V((16, 256), BF), D((18,))], size=4e6, name="fetch_six",
    )
    h5, pre6, st6, tot5 = call(
        stage_six_kernel, [h(M, 512), f(M, 2048), f(4, 2048), f(4, 512)],
        [fs, parts5, pre5, keep, gain5, w6], [V((4, 512), F32)],
        flops=1e9, size=6e6, name="stage_six",
    )
    parts6, _ = steps(st6)
    sq, ex, og = call(
        fetch_turn_kernel, [h(2048, 128), h(2, 128, 1024), h(2, M, 1024)],
        [
            (SMEM, after(isc_, st6)), far(second_squeeze), far(second_excite), pk1, pk2,
            far(og_own), (ANY, og_other),
        ],
        [D((16,))], size=4e6, name="fetch_turn",
    )
    result, dj2, pay6, extra6, tot6, gate2, dp2, pooled2, de2, ds2, sq2 = call(
        turn_kernel,
        [
            ((M, 1024), BF), f(M, 2048), f(4, 2048), f(8, 512), f(4, 2048), f(8, 2048),
            f(8, 2048), f(8, 2048), f(8, 2048), f(8, 128), f(8, 128),
        ],
        [fs, isc, parts6, pre6, keep, lows, vec2, sqb, squares, sq, ex, og],
        [V((M, 2048), F32), V((2, M, 1024), BF), V((4, 2048), F32), V((8, 128), F32)],
        flops=1e9, size=1e7, name="turn",
    )
    back6, _ = steps(pay6)
    d6, do5, bt5, dgain6, dbias6 = call(
        back_six_kernel, [h(M, 2048), f(M, 512), f(12, 512), out(1024), out(1024)],
        [fs, isc, back6, tot6, pre6, dj2, gate2, dp2, pre5, tot5, extra6, keep, vec2, gain5, w6],
        [V((4, 2048), F32), V((M, 512), F32)],
        flops=1e9, size=1e7, name="back_six",
    )
    back5, _ = steps(bt5)
    d5, do4, bt4, dgain5, dbias5, debias2, dsbias2, norms = call(
        back_five_kernel,
        [h(M, 512), f(M, 512), f(4, 512), out(256), out(256), out(1024), out(128), ((5,), F32, SMEM)],
        [fs, isc, back5, tot5, pre5, do5, pre4, tot4, keep, gb, gain5, sh, w5],
        [V((12, 512), F32)],
        flops=2e9, size=1e7, name="back_five",
    )

    def step(g, k, *ties):
        if not exact:
            return g, ()
        kept, sent = g
        got = swap(after(sent, *ties), "wide", [(i, i ^ (1 << k)) for i in range(wide)])
        if k == 3:
            return (kept, got), (got,)
        half = kept.shape[0] // 2
        return (kept[:half] + got[:half], kept[half:] + got[half:]), (got,)

    ga = call(
        grads_a_kernel, [h(8, 416, 256)] * 2, [isc, h5, d6, col4, d5],
        [V((256, 2048), BF), V((512, 256), BF)], flops=2e9, size=1e7, name="grads_a",
    )
    back4, sent4 = steps(bt4, *ga)
    ga, _ = step(ga, 0, sent4[0])
    back4 = after(back4, *ga)
    ga, xa = step(ga, 1, sent4[1])
    d4, dj1, bt3, dgain4, dbias4, dp1, de1, ds1, bias1 = call(
        back_four_kernel,
        [
            h(M, 512), f(M, 2048), f(8, 2048), out(512), out(512), f(8, 2048),
            f(8, 2048), f(8, 128), f(8, 512),
        ],
        [
            fs, back4, tot4, pre4, do4, dj2, tot3, pre3, prep, gate1, sp1, keep, gb, vec1,
            far(first_squeeze), far(first_excite), w4,
        ],
        [V((4, 512), F32), V((2048, 128), BF), V((128, 2048), BF), D((2,))],
        flops=1e9, size=1e7, name="back_four",
    )
    gb1 = call(
        grads_b_kernel, [h(8, 256, 256)] * 2,
        [isc, d4, lows, sq2, pooled2, de2, ds2, sp1, pooled1, de1, ds1],
        [V((512, 256), BF), V((128, 256), F32), V((128, 256), F32), V((8, 128), F32)],
        flops=1e9, size=4e6, name="grads_b",
    )
    back3, sent3 = steps(bt3, *gb1, before={1: xa})
    gb1, _ = step(gb1, 0, sent3[0])
    back3 = after(back3, *gb1)
    ga, za = step(ga, 2, sent3[3])
    d3, dproj, do2, bt2, dgain3, dbias3, dgainp, dbiasp = call(
        back_three_kernel,
        [h(M, 2048), h(M, 2048), f(M, 512), f(12, 512), out(2048), out(2048), out(2048), out(2048)],
        [fs, back3, tot3, pre3, prep, dj1, gate1, dp1, bias1, pre2, tot2, keep, vec1, gb, w3],
        [V((8, 2048), F32), V((M, 512), F32)],
        flops=1e9, size=1e7, name="back_three",
    )
    gc = call(
        grads_c_kernel, [h(8, 384, 256)] * 2, [isc, h2, d3, strided, dproj],
        [V((512, 256), BF), V((1024, 256), BF)],
        flops=3e9, size=1e7, name="grads_c",
    )
    back2, sent2 = steps(bt2, *gc, *za)
    gc, _ = step(gc, 0, sent2[0])
    back2 = after(back2, *gc)
    gc, xc = step(gc, 1, sent2[1])
    ws_back = call(
        fetch_two_kernel, [h(9, 512, 512)], [far(after(ws_far, bt2))], [D((3,))], size=9e6, name="fetch_two",
    )[0]
    d2, do1, bt1, dgain2, dbias2, debias1, dsbias1 = call(
        back_two_kernel,
        [h(M, 512), f(4, M, 512), f(4, 512), out(512), out(512), out(2048), out(128)],
        [fs, back2, tot2, pre2, do2, x1, keep1, keep, gb, sh, ws_back],
        [V((12, 512), F32), V((4, M, 512), BF)],
        flops=2e9, size=1e7, name="back_two",
    )
    gd = call(
        grads_d_kernel, [h(8, 288, 256)] * 2, [isc, col1, d2], [V((512, 256), BF)],
        flops=2e9, size=6e6, name="grads_d",
    )
    back1, sent1 = steps(bt1, *gd, before={1: xc})
    gd, _ = step(gd, 0)
    gd0 = gd
    gd, xd = step(gd, 1, sent1[2])
    gb1, _ = step(gb1, 1, sent1[2])
    gc, _ = step(gc, 2, sent1[3])
    ga, _ = step(ga, 3, sent1[3])
    back1 = after(back1, *gd0)
    placed = call(
        placed_kernel, [f(HROWS, 1024)], [(SMEM, after(isc_, sent1[2])), dproj, far(first_project)],
        [V((128, 2048), BF), V((128, M), BF), V((HROWS, 128), BF), V((1024, 2048), BF), D((4,))],
        flops=1e9, size=1e7, name="placed",
    )[0]
    back1, placed = lax.optimization_barrier((back1, placed))
    d1, ge_keep, ge_send, dgain1, dbias1 = call(
        back_one_kernel, [h(B, M, 512), h(8, 64, 256), h(8, 64, 256), out(512), out(512)],
        [fs, isc, back1, tot1, x1, do1, xp, keep1, gb],
        [V((4, 512), F32), V((4, M, 512), BF), V((1024, 256), BF)],
        flops=1e9, size=6e6, name="back_one",
    )
    ge = (ge_keep, ge_send)
    dimg = call(
        image_kernel, [out(HROWS, 1024)], [isc, perm, d1, placed, keep_half, w1],
        [V((HROWS, 512), BF)], flops=1e9, size=1e7, name="image",
    )[0]

    if exact:
        ge, _ = step(ge, 0)
        dimg, *ge = lax.optimization_barrier((dimg,) + ge)
        gb1, _ = step(gb1, 2)
        gd, _ = step(gd, 2)
        gc, _ = step(gc, 3)
        gb1, _ = step(gb1, 3)
        ge, _ = step(ge, 1)
        ge, _ = step(ge, 2)
        gd, _ = step(gd, 3)
        ge, _ = step(ge, 3)
        expand2, spatial2 = call(
            unpack_a_kernel, [out(256, 128), out(288, 256)], list(ga), name="unpack_a"
        )
        reduce2, squeeze2, excite2, squeeze1, excite1 = call(
            unpack_b_kernel, [out(32, 1024)] + [out(8, 1024)] * 4, list(gb1), name="unpack_b"
        )
        expand1, project1 = call(
            unpack_c_kernel, [out(32, 1024), out(64, 1024)], list(gc), name="unpack_c"
        )
        spatial1 = call(unpack_d_kernel, [out(288, 256)], list(gd), name="unpack_d")[0]
        reduce1 = call(unpack_d_kernel, [out(64, 256)], list(ge), name="unpack_e")[0]
    else:
        finer = wide // 16

        def summed(g):
            return lax.psum_scatter(g, "wide", scatter_dimension=0, tiled=True)

        def blocks(g, start, count, rows):
            p = g[:, start : start + count * rows].reshape(16, count, finer, rows // finer, 256)
            p = summed(p.transpose(0, 2, 1, 3, 4).reshape(wide, count, rows // finer, 256))[0]
            return f32(p).transpose(1, 0, 2).reshape(rows // finer, count * 256)

        def both(g, start):
            p = g[:, start : start + 64].reshape(16, 4, 2, finer, 8 // finer, 256)
            p = f32(summed(p.transpose(0, 3, 1, 2, 4, 5).reshape(wide, 4, 2, -1, 256))[0])
            return [p[:, k].transpose(1, 0, 2).reshape(-1, 1024) for k in range(2)]

        def taps(g, start):
            p = g[:, start : start + 288].reshape(16, 9, finer, 32 // finer, 256)
            return f32(summed(p.transpose(0, 2, 1, 3, 4).reshape(wide, 9, -1, 256))[0]).reshape(-1, 256)

        ga, gb1, gc, gd, ge = (jnp.concatenate(g) for g in (ga, gb1, gc, gd, ge))
        e2 = ga[:, 0:128].reshape(16, 128, 2, finer, 128 // finer).transpose(0, 3, 1, 2, 4)
        e2 = summed(e2.reshape(wide, 1, -1)).reshape(128, 2, -1)
        expand2 = f32(e2.transpose(1, 0, 2).reshape(256, -1))
        spatial2 = taps(ga, 128)
        reduce2 = blocks(gb1, 0, 4, 32)
        squeeze2, excite2 = both(gb1, 128)
        expand1, project1 = blocks(gc, 0, 4, 32), blocks(gc, 128, 4, 64)
        squeeze1, excite1 = both(gb1, 192)
        spatial1, reduce1 = taps(gd, 0), blocks(ge, 0, 1, 64)
    return (
        result.reshape(B, 7, 8, 1024).transpose(0, 2, 1, 3),
        dimg.reshape(B, 14, 8, 1024).transpose(0, 2, 1, 3),
        reduce1, dgain1, dbias1,
        spatial1.reshape(3, 3, -1, 256), dgain2, dbias2,
        expand1, dgain3, dbias3,
        project1, dgainp, dbiasp,
        squeeze1.T, dsbias1, excite1, debias1,
        reduce2.T, dgain4, dbias4,
        spatial2.reshape(3, 3, -1, 256), dgain5, dbias5,
        expand2, dgain6, dbias6,
        squeeze2.T, dsbias2, excite2, debias2,
        norms,
    )


def solution(mesh):
    rep, nar = P(), P("narrow")
    return jax.shard_map(
        local,
        mesh=mesh,
        in_specs=(P("wide", "narrow", None, None),) + (rep,) * 18 + (
            P("narrow", None), rep, rep,
            P(None, None, None, "narrow"), nar, nar,
            P("narrow", None), nar, nar,
            P("narrow", None), rep, P(None, "narrow"), nar,
            P("wide", None, None, "narrow"),
        ),
        out_specs=(
            P("wide", None, None, "narrow"), P("wide", "narrow", None, None),
            P("wide", "narrow"), rep, rep,
            P(None, None, "wide", "narrow"), rep, rep,
            P("wide", "narrow"), rep, rep,
            P("wide", "narrow"), rep, rep,
            P("narrow", "wide"), rep, P("wide", "narrow"), rep,
            P("narrow", "wide"), rep, rep,
            P(None, None, "wide", "narrow"), nar, nar,
            P("narrow", "wide"), nar, nar,
            P("narrow", "wide"), rep, P("wide", "narrow"), nar,
            rep,
        ),
        check_vma=False,
    )
```

```python
import functools

import numpy as np
import jax
import jax.numpy as jnp
from jax import lax
from jax.experimental import pallas as pl
from jax.experimental.pallas import tpu as pltpu
from jax.sharding import PartitionSpec as P

EPSILON = 1e-05
BF = jnp.bfloat16
F32 = jnp.float32
B = 4
POS = 56
LIMIT = 14
SCALE = 0.01
UNROLL = 2
M = B * POS
HALF = 112
HROWS = B * HALF
VMEM = pl.BlockSpec(memory_space=pltpu.VMEM)
SMEM = pl.BlockSpec(memory_space=pltpu.SMEM)
ANY = pl.BlockSpec(memory_space=pl.ANY)
INV_IN, INV_OUT, CELLS, MICRO, INV_ALL = 0, 2, 4, 8, 12
NARROW, CORE, DEST = 0, 1, 2
W6_AT, EX_AT, SQ_AT, VE2, PACK_ROWS = 0, 1024, 1280, 1536, 1552


def mm(a, b):
    return lax.dot_general(a, b, (((1,), (0,)), ((), ())), preferred_element_type=F32)


def mm_nt(a, b):
    return lax.dot_general(a, b, (((1,), (1,)), ((), ())), preferred_element_type=F32)


def mm_tn(a, b):
    return lax.dot_general(a, b, (((0,), (0,)), ((), ())), preferred_element_type=F32)


def f32(v):
    return v.astype(F32)


def low(v):
    return v.astype(BF)


def split2(v):
    a = low(v)
    return a, low(v - f32(a))


def split3(v):
    a = low(v)
    r = v - f32(a)
    b = low(r)
    return a, b, low(r - f32(b))


def dot3(v, w):
    return sum(mm(p, w) for p in split3(v))


def dot3_nt(v, w):
    return sum(mm_nt(p, w) for p in split3(v))


def outer(a, b):
    a1, a2 = split2(a)
    b1, b2 = split2(b)
    return mm_tn(a1, b1) + mm_tn(a1, b2) + mm_tn(a2, b1)


def sigmoid(v):
    return 1.0 / (1.0 + jnp.exp(-v))


def slope(v):
    s = sigmoid(v)
    return s * (1.0 + v * (1.0 - s))


def cols(c, size=256):
    return pl.ds(pl.multiple_of(c * size, size), size)


def expand(rows):
    return jnp.concatenate([jnp.broadcast_to(r, (POS, r.shape[1])) for r in rows], axis=0)


def pick(r0, r1, fs):
    return expand([r0 * (1.0 - fs[MICRO + b]) + r1 * fs[MICRO + b] for b in range(B)])


def image_sums(v):
    return [jnp.sum(v[b * POS : (b + 1) * POS], axis=0, keepdims=True) for b in range(B)]


def grouped(sums, fs, reps=1):
    zero = one = 0.0
    for b in range(B):
        zero = zero + sums[b] * (1.0 - fs[MICRO + b])
        one = one + sums[b] * fs[MICRO + b]
    return [zero, one]


def group_sums(v, fs):
    return grouped(image_sums(v), fs)


def put(ref, at, rows, sl):
    for k, r in enumerate(rows):
        ref[at + k : at + k + 1, sl] = r


def add_parts(parts, tot):
    t = parts[0]
    for k in range(1, parts.shape[0]):
        t = t + parts[k]
    tot[...] = t


def coefs(tot, at, sl, fs, inv):
    i0, i1 = fs[inv], fs[inv + 1]
    m0, m1 = tot[at : at + 1, sl] * i0, tot[at + 1 : at + 2, sl] * i1
    q0 = lax.rsqrt(tot[at + 2 : at + 3, sl] * i0 - m0 * m0 + EPSILON)
    q1 = lax.rsqrt(tot[at + 3 : at + 4, sl] * i1 - m1 * m1 + EPSILON)
    return pick(m0, m1, fs), pick(q0, q1, fs)


def means(tot, at, sl, fs, inv):
    i0, i1 = fs[inv], fs[inv + 1]
    a = pick(tot[at : at + 1, sl] * i0, tot[at + 1 : at + 2, sl] * i1, fs)
    b = pick(tot[at + 2 : at + 3, sl] * i0, tot[at + 3 : at + 4, sl] * i1, fs)
    return a, b


def stat_rows(v, keep, fs):
    kept = v * keep
    return group_sums(kept, fs) + group_sums(kept * v, fs)


def back_rows(d, x, fs):
    return group_sums(d, fs) + group_sums(d * x, fs)


def loop(count, body):
    lax.fori_loop(0, count, lambda c, _: (body(c), 0)[1], 0, unroll=UNROLL)


def loop_from(first, last, body):
    for c in range(first, last):
        body(c)


def copy_all(pairs, sems):
    copies = [pltpu.make_async_copy(s, d, sems.at[k]) for k, (s, d) in enumerate(pairs)]
    for c in copies:
        c.start()
    return copies


def wait_all(copies):
    for c in copies:
        c.wait()


def at_rows(start, size):
    return pl.ds(pl.multiple_of(start, 16), size)


def flip(p):
    return (p & 1) * 8 + (p & 2) * 2 + (p & 4) // 2 + (p & 8) // 8


def setup_kernel(exact, crop, micro, fs, isc, keep, keep1, keep_half, sh, perm):
    n = lax.axis_index("narrow").astype(jnp.int32)
    w = lax.axis_index("wide").astype(jnp.int32)
    isc[NARROW] = n
    isc[CORE] = w & 1
    for p in range(16):
        isc[DEST + p] = (w ^ flip(p)) if exact else jnp.int32(p)

    def count(k, sums):
        c, one = crop[k], micro[k]
        a, b = (c >> 4) * (c >> 4), (c >> 5) * (c >> 5)
        return (
            sums[0] + a * (1 - one), sums[1] + a * one, sums[2] + b * (1 - one), sums[3] + b * one,
        )

    zero = jnp.int32(0)
    sums = lax.fori_loop(0, crop.shape[0], count, (zero, zero, zero, zero))
    for k in range(4):
        fs[k] = 1.0 / sums[k].astype(F32)
    fs[INV_ALL] = 1.0 / ((sums[2] + sums[3]).astype(F32) * 2048.0)
    at = lax.broadcasted_iota(jnp.int32, (POS, 1), 0)
    i8, j7 = at & 7, at >> 3
    at = lax.broadcasted_iota(jnp.int32, (HALF, 1), 0)
    r8, c14 = n * 8 + (at & 7), at >> 3

    def inside(r, c, side):
        return jnp.where((r < side) & (c < side), 1.0, 0.0).astype(F32)

    for b in range(B):
        c = crop[w * B + b]
        side_in, side_out = c >> 4, c >> 5
        fs[CELLS + b] = 1.0 / (side_out * side_out).astype(F32)
        fs[MICRO + b] = micro[w * B + b].astype(F32)
        keep[b * POS : (b + 1) * POS, :] = inside(i8, j7, side_out)
        for k in range(4):
            keep1[k, b * POS : (b + 1) * POS, :] = inside(2 * i8 + k // 2, 2 * j7 + k % 2, side_in)
        keep_half[b * HALF : (b + 1) * HALF, :] = inside(r8, c14, side_in)
    place = lax.broadcasted_iota(jnp.int32, (POS, M), 1)
    it = lax.broadcasted_iota(jnp.int32, (POS, M), 0)
    for t in range(9):
        di, dj = t // 3 - 1, t % 3 - 1
        i, j = (it & 7) + di, (it >> 3) + dj
        fits = (i >= 0) & (i < 8) & (j >= 0) & (j < 7)
        sh[t] = low(jnp.concatenate([
            jnp.where(fits & (place == b * POS + j * 8 + i), 1.0, 0.0) for b in range(B)
        ], axis=0))
    place = lax.broadcasted_iota(jnp.int32, (POS, HALF), 1)
    it = lax.broadcasted_iota(jnp.int32, (POS, HALF), 0)
    for half in range(2):
        planes = []
        for k in range(4):
            r, c = 2 * (it & 7) + k // 2, 2 * (it >> 3) + k % 2
            planes.append(
                jnp.where(((r >> 3) == half) & (place == c * 8 + (r & 7)), 1.0, 0.0)
            )
        perm[half] = low(jnp.concatenate(planes, axis=0))


def one_half_kernel(fs, px, keep, w1_far, st, x, w1, flat, sems):
    copies = copy_all([(px, x), (w1_far, w1)], sems)
    copies[0].wait()
    for b in range(B):
        flat[b * HALF : (b + 1) * HALF, :] = x[b]
    copies[1].wait()

    def body(c):
        sl = cols(c)
        v = mm(flat[...], w1[:, sl]) * keep[...]
        sums = [jnp.sum(v[b * HALF : (b + 1) * HALF], axis=0, keepdims=True) for b in range(B)]
        v2 = v * v
        sq = [jnp.sum(v2[b * HALF : (b + 1) * HALF], axis=0, keepdims=True) for b in range(B)]
        put(st, 0, grouped(sums, fs) + grouped(sq, fs), sl)

    loop(2, body)


TAPS = [(p, q) for p in range(3) for q in range(3)]


def stage_two_kernel(
    fs, isc, own, other, part, part_other, perm, keep1, keep, w1, ws, gb, sh,
    xp, strided, x1, col, pre2, st, tot1, tmp, hid, tot,
):
    n = isc[NARROW]
    tot[...] = part[...] + part_other[...]
    tot1[...] = tot[...]

    def permute(c):
        sl = cols(c)
        for b in range(B):
            r = mm(perm[n], own[b, :, sl]) + mm(perm[1 - n], other[b, :, sl])
            for k in range(4):
                tmp[k, b * POS : (b + 1) * POS, :] = r[k * POS : (k + 1) * POS]
        for k in range(4):
            xp[k, :, sl] = low(tmp[k] * keep1[k])
        strided[:, sl] = xp[0, :, sl]

    loop(4, permute)

    def first(c):
        k, sl = c // 2, cols(c % 2)
        v = mm(xp[k], w1[:, sl])
        mean, scale = coefs(tot, 0, sl, fs, INV_IN)
        x = (v - mean) * scale
        x1[k, :, sl] = x
        o = x * gb[0:1, sl] + gb[1:2, sl]
        hid[k, :, sl] = low(o * sigmoid(o) * keep1[k])

    loop(8, first)
    for t, (p, q) in enumerate(TAPS):
        h = hid[2 * (p != 1) + (q != 1)]
        if p == 0 or q == 0:
            h = low(mm(sh[3 * (0 if p == 0 else 1) + (0 if q == 0 else 1)], h))
        col[t] = h

    def second(c):
        sl = cols(c)
        v = mm(col[0], ws[0, :, sl])
        for t in range(1, 9):
            v = v + mm(col[t], ws[t, :, sl])
        pre2[:, sl] = v
        put(st, 0, stat_rows(v, keep[...], fs), sl)

    loop(2, second)


def project_kernel(fs, x, keep, wp_far, w3_far, prep, st, w3, wp, sems):
    copies = []
    for c in range(4):
        sl = slice(c * 512, (c + 1) * 512)
        copies.append(pltpu.make_async_copy(wp_far.at[:, sl], wp.at[:, sl], sems.at[c]))
    copies.append(pltpu.make_async_copy(w3_far, w3, sems.at[4]))
    for c in copies:
        c.start()

    def body(c):
        sl = cols(c)
        v = mm(x[...], wp[:, sl])
        prep[:, sl] = v
        put(st, 0, stat_rows(v, keep[...], fs), sl)

    for c in range(4):
        copies[c].wait()
        loop_from(2 * c, 2 * c + 2, body)
    copies[4].wait()


def stage_three_kernel(fs, parts, pre2, stp, keep, w3, gb, h2, pre3, st, tot2, tot):
    add_parts(parts, tot)
    tot2[...] = tot[...]
    sl = slice(0, 512)
    mean, scale = coefs(tot, 0, sl, fs, INV_OUT)
    o = (pre2[...] - mean) * scale * gb[2:3, :] + gb[3:4, :]
    h2[...] = low(o * sigmoid(o) * keep[...])
    st[4:8, :] = stp[...]

    def body(c):
        sl = cols(c)
        v = mm(h2[...], w3[:, sl])
        pre3[:, sl] = v
        put(st, 0, stat_rows(v, keep[...], fs), sl)

    loop(8, body)


def fetch_four_kernel(isc, own, r1, r2, w4, sems):
    n, core = isc[NARROW], isc[CORE]
    away = (1 - n) * 1024
    wait_all(copy_all(
        [
            (own, w4.at[at_rows(n * 1024, 1024)]),
            (r1, w4.at[at_rows(away + core * 512, 512)]),
            (r2, w4.at[at_rows(away + (1 - core) * 512, 512)]),
        ],
        sems,
    ))


def stage_four_kernel(
    fs, parts, pre3, prep, keep, vec, sqb, sq_far, ex_far, w4,
    lows, pre4, st, tot3, gate, sp, pooled, squares, unit, short, acc, tot, sq, ex, sems,
):
    copies = copy_all([(sq_far, sq), (ex_far, ex)], sems)
    add_parts(parts, tot)
    tot3[...] = tot[...]
    pooled[...] = jnp.zeros((8, 2048), F32)

    def units(c):
        sl = cols(c)
        mean, scale = coefs(tot, 0, sl, fs, INV_OUT)
        u = ((pre3[:, sl] - mean) * scale * vec[0:1, sl] + vec[1:2, sl]) * keep[...]
        unit[:, sl] = u
        for b, r in enumerate(image_sums(u)):
            pooled[b : b + 1, sl] = r * fs[CELLS + b]
        mean, scale = coefs(tot, 4, sl, fs, INV_OUT)
        s = ((prep[:, sl] - mean) * scale * vec[2:3, sl] + vec[3:4, sl]) * keep[...]
        short[:, sl] = s

    loop(8, units)
    wait_all(copies)
    sp[...] = dot3(pooled[...], sq[...]) + sqb[0:1, :]
    squeezed = sp[...] * sigmoid(sp[...])
    gate[...] = sigmoid(dot3(squeezed, ex[...]) + vec[4:5, :])
    squares[...] = jnp.zeros((8, 256), F32)
    acc[...] = jnp.zeros((M, 512), F32)

    def streams(c):
        sl = cols(c)
        branch = unit[:, sl] * expand([gate[b : b + 1, sl] for b in range(B)])
        s = short[:, sl]
        join = branch + s
        stream = join * sigmoid(join) * keep[...]
        for k, v in enumerate((stream, branch, s)):
            squares[k : k + 1, :] += jnp.sum(v * v, axis=0, keepdims=True)
        lo = low(stream)
        lows[:, sl] = lo
        acc[...] += mm(lo, w4[cols(c), :])

    loop(8, streams)
    pre4[...] = acc[...]
    put(st, 0, stat_rows(acc[...], keep[...], fs), slice(0, 512))


def fetch_five_kernel(isc, own, r1, r2, w5, sems):
    n, core = isc[NARROW], isc[CORE]
    wait_all(copy_all([
        (own, w5.at[n]),
        (r1, w5.at[1 - n, at_rows(core * 2304, 2304)]),
        (r2, w5.at[1 - n, at_rows((1 - core) * 2304, 2304)]),
    ], sems))


def stage_five_kernel(
    fs, parts, pre4, keep, gb, sh, w5, col, pre5, st, tot4, tot
):
    add_parts(parts, tot)
    tot4[...] = tot[...]
    mean, scale = coefs(tot, 0, slice(0, 512), fs, INV_OUT)
    o = (pre4[...] - mean) * scale * gb[4:5, :] + gb[5:6, :]
    h = low(o * sigmoid(o) * keep[...])
    for t in range(9):
        col[t] = h if t == 4 else low(mm(sh[t], h))
    def body(c):
        v = 0.0
        for t in range(9):
            v = v + mm(col[t], w5[c, t * 512 : (t + 1) * 512, :])
        pre5[:, cols(c)] = v
        put(st, 0, stat_rows(v, keep[...], fs), cols(c))

    loop(2, body)


def fetch_six_kernel(isc, own, r1, r2, vown, w6, gain5, vec2, vaway, sems):
    n, core = isc[NARROW], isc[CORE]
    pairs = [(r1.at[VE2:PACK_ROWS], vaway), (own, w6.at[at_rows(n * 256, 256)])]
    for r, h in ((r1, core), (r2, 1 - core)):
        for c in range(8):
            pairs.append(
                (
                    r.at[W6_AT + c * 128 : W6_AT + (c + 1) * 128],
                    w6.at[at_rows((1 - n) * 256 + h * 128, 128), c * 256 : (c + 1) * 256],
                )
            )
    copies = copy_all(pairs, sems)
    copies[0].wait()
    for side, v in ((n, f32(vown[...])), (1 - n, f32(vaway[...]))):
        for k in range(2):
            gain5[k : k + 1, cols(side)] = v[k : k + 1]
        for k in range(3):
            for c in range(4):
                at = 2 + 4 * k + c
                vec2[k : k + 1, cols(side * 4 + c)] = v[at : at + 1]
    wait_all(copies[1:])


def stage_six_kernel(
    fs, parts, pre5, keep, gain5, w6, h5, pre6, st, tot5, tot
):
    add_parts(parts, tot)
    tot5[...] = tot[...]
    mean, scale = coefs(tot, 0, slice(0, 512), fs, INV_OUT)
    o = (pre5[...] - mean) * scale * gain5[0:1, :] + gain5[1:2, :]
    h5[...] = low(o * sigmoid(o) * keep[...])

    def body(c):
        sl = cols(c)
        v = mm(h5[...], w6[:, sl])
        pre6[:, sl] = v
        put(st, 0, stat_rows(v, keep[...], fs), sl)

    loop(8, body)


def fetch_turn_kernel(isc, sqown, exown, r1, r2, ogown, ogother, sq, ex, og, sems):
    n, core = isc[NARROW], isc[CORE]
    pairs = [
        (sqown, sq.at[at_rows(n * 1024, 1024)]),
        (exown, ex.at[n]),
        (ogown, og.at[n]),
        (ogother, og.at[1 - n]),
    ]
    for r, h in ((r1, core), (r2, 1 - core)):
        for k in range(2):
            pairs.append(
                (
                    r.at[SQ_AT : SQ_AT + 256, k * 128 : (k + 1) * 128],
                    sq.at[at_rows((1 - n) * 1024 + h * 512 + k * 256, 256)],
                )
            )
        for c in range(4):
            pairs.append(
                (
                    r.at[EX_AT + c * 64 : EX_AT + (c + 1) * 64],
                    ex.at[1 - n, at_rows(h * 64, 64), c * 256 : (c + 1) * 256],
                )
            )
    wait_all(copy_all(pairs, sems))


def turn_kernel(
    fs, isc, parts, pre6, keep, lows, vec, sqb, sq1s, sq, ex, og,
    result, dj2, pay, extra, tot6, gate, dp, pooled, de, ds, squeezed, unit, res, tot, sp,
):
    n = isc[NARROW]
    add_parts(parts, tot)
    tot6[...] = tot[...]
    pooled[...] = jnp.zeros((8, 2048), F32)
    de[...] = jnp.zeros((8, 2048), F32)

    def units(c):
        sl = cols(c)
        mean, scale = coefs(tot, 0, sl, fs, INV_OUT)
        u = ((pre6[:, sl] - mean) * scale * vec[0:1, sl] + vec[1:2, sl]) * keep[...]
        unit[:, sl] = u
        for b, r in enumerate(image_sums(u)):
            pooled[b : b + 1, sl] = r * fs[CELLS + b]

    loop(8, units)
    sp[...] = dot3(pooled[...], sq[...]) + sqb[1:2, :]
    squeezed[...] = sp[...] * sigmoid(sp[...])
    for h in range(2):
        sl = slice(h * 1024, (h + 1) * 1024)
        gate[:, sl] = sigmoid(dot3(squeezed[...], ex[h]) + vec[2:3, sl])
    extra[...] = jnp.zeros((8, 512), F32)
    for k in range(3):
        extra[5 + k // 2 : 6 + k // 2, (k % 2) * 256 : (k % 2) * 256 + 256] = sq1s[k : k + 1, :]

    def streams(c):
        sl = cols(c)
        h, part = c // 4, cols(c % 4)
        u = unit[:, sl]
        branch = u * expand([gate[b : b + 1, sl] for b in range(B)])
        join = branch + f32(lows[:, sl])
        s = sigmoid(join)
        stream = join * s * keep[...]
        res[h, :, part] = low(stream)
        d = f32(og[h, :, part]) * keep[...] * (s * (1.0 + join * (1.0 - s)))
        dj2[:, sl] = d
        for b, r in enumerate(image_sums(d * u)):
            de[b : b + 1, sl] = r
        extra[6:7, 256:512] += jnp.sum(branch * branch, axis=0, keepdims=True)
        extra[7:8, 0:256] += jnp.sum(stream * stream, axis=0, keepdims=True)

    loop(8, streams)
    result[...] = res[n]
    de[...] = de[...] * gate[...] * (1.0 - gate[...])
    back = 0.0
    for h in range(2):
        back = back + dot3_nt(de[:, h * 1024 : (h + 1) * 1024], ex[h])
    ds[...] = back * slope(sp[...])
    dp[...] = dot3_nt(ds[...], sq[...])
    for b in range(B):
        dp[b : b + 1, :] = dp[b : b + 1, :] * fs[CELLS + b]
    total = jnp.sum(de[...], axis=0, keepdims=True)
    for k in range(4):
        extra[k : k + 1, :] = total[:, k * 512 : (k + 1) * 512]
    extra[4:5, 0:128] = jnp.sum(ds[...], axis=0, keepdims=True)

    def tops(c):
        sl = cols(c)
        mean, scale = coefs(tot, 0, sl, fs, INV_OUT)
        x = (pre6[:, sl] - mean) * scale
        du = (
            dj2[:, sl] * expand([gate[b : b + 1, sl] for b in range(B)])
            + expand([dp[b : b + 1, sl] for b in range(B)])
        ) * keep[...]
        put(pay, 0, back_rows(du, x, fs), sl)

    loop(8, tops)


def whole_gain(tot, at, gain, bias):
    gain[...] = (tot[at + 2 : at + 3, :] + tot[at + 3 : at + 4, :]).reshape(gain.shape)
    bias[...] = (tot[at : at + 1, :] + tot[at + 1 : at + 2, :]).reshape(bias.shape)


def half_gain(tot, n, gain, bias):
    sl = cols(n, gain.shape[0])
    gain[...] = (tot[2:3, sl] + tot[3:4, sl]).reshape(gain.shape)
    bias[...] = (tot[0:1, sl] + tot[1:2, sl]).reshape(bias.shape)


def back_six_kernel(
    fs, isc, parts, tot6, pre6, dj2, gate, dp, pre5, tot5, extra, keep, vec, gain5, w6,
    d6, do5, st, dgain, dbias, tot, acc,
):
    add_parts(parts, tot)
    half_gain(tot, isc[NARROW], dgain, dbias)
    acc[...] = jnp.zeros((M, 512), F32)

    def body(c):
        sl = cols(c)
        mean, scale = coefs(tot6, 0, sl, fs, INV_OUT)
        x = (pre6[:, sl] - mean) * scale
        du = (
            dj2[:, sl] * expand([gate[b : b + 1, sl] for b in range(B)])
            + expand([dp[b : b + 1, sl] for b in range(B)])
        ) * keep[...]
        a, bb = means(tot, 0, sl, fs, INV_OUT)
        d = low((du - a - x * bb) * (scale * vec[0:1, sl]) * keep[...])
        d6[:, sl] = d
        acc[...] += mm_nt(d, w6[:, sl])

    loop(8, body)
    mean, scale = coefs(tot5, 0, slice(0, 512), fs, INV_OUT)
    x = (pre5[...] - mean) * scale
    o = x * gain5[0:1, :] + gain5[1:2, :]
    d = acc[...] * keep[...] * slope(o)
    do5[...] = d
    put(st, 0, back_rows(d, x, fs), slice(0, 512))
    st[4:12, :] = extra[...]


def back_five_kernel(
    fs, isc, parts, tot5, pre5, do5, pre4, tot4, keep, gb, gain5, sh, w5,
    d5, do4, st, dgain, dbias, debias, dsbias, norms, tot,
):
    n = isc[NARROW]
    add_parts(parts, tot)
    half_gain(tot, n, dgain, dbias)
    excite = jnp.concatenate([tot[pl.ds(4 + 2 * n, 1), :], tot[pl.ds(5 + 2 * n, 1), :]], axis=1)
    debias[...] = excite.reshape(1024)
    dsbias[...] = tot[8:9, 0:128].reshape(128)
    for k in range(5):
        v = tot[9 + k // 2 : 10 + k // 2, (k % 2) * 256 : (k % 2) * 256 + 256]
        norms[k] = jnp.sqrt(jnp.sum(v, axis=1, keepdims=True) * fs[INV_ALL])[0, 0]
    sl = slice(0, 512)
    mean, scale = coefs(tot5, 0, sl, fs, INV_OUT)
    x = (pre5[...] - mean) * scale
    a, bb = means(tot, 0, sl, fs, INV_OUT)
    d = low((do5[...] - a - x * bb) * (scale * gain5[0:1, :]) * keep[...])
    d5[...] = d
    acc = 0.0
    for t in range(9):
        dc = d if t == 4 else low(mm(sh[8 - t], d))
        for h in range(2):
            acc = acc + mm_nt(dc[:, h * 256 : (h + 1) * 256], w5[h, t * 512 : (t + 1) * 512, :])
    mean, scale = coefs(tot4, 0, sl, fs, INV_OUT)
    x = (pre4[...] - mean) * scale
    o = x * gb[4:5, :] + gb[5:6, :]
    d = acc * keep[...] * slope(o)
    do4[...] = d
    put(st, 0, back_rows(d, x, fs), sl)


def back_four_kernel(
    fs, parts, tot4, pre4, do4, dj2, tot3, pre3, prep, gate, sp, keep, gb, vec, sq_far, ex_far, w4,
    d4, dj1, st, dgain, dbias, dp, de, ds, bias, tot, sq, ex, sems,
):
    copies = copy_all([(sq_far, sq), (ex_far, ex)], sems)
    add_parts(parts, tot)
    whole_gain(tot, 0, dgain, dbias)
    de[...] = jnp.zeros((8, 2048), F32)
    mean, scale = coefs(tot4, 0, slice(0, 512), fs, INV_OUT)
    x = (pre4[...] - mean) * scale
    a, bb = means(tot, 0, slice(0, 512), fs, INV_OUT)
    d4[...] = low((do4[...] - a - x * bb) * (scale * gb[4:5, :]) * keep[...])

    def joins(c):
        sl = cols(c)
        back = dj2[:, sl] + mm_nt(d4[...], w4[cols(c), :])
        mean, scale = coefs(tot3, 0, sl, fs, INV_OUT)
        u = ((pre3[:, sl] - mean) * scale * vec[0:1, sl] + vec[1:2, sl]) * keep[...]
        mean, scale = coefs(tot3, 4, sl, fs, INV_OUT)
        s = ((prep[:, sl] - mean) * scale * vec[2:3, sl] + vec[3:4, sl]) * keep[...]
        join = u * expand([gate[b : b + 1, sl] for b in range(B)]) + s
        d = f32(low(back)) * keep[...] * slope(join)
        dj1[:, sl] = d
        for b, r in enumerate(image_sums(d * u)):
            de[b : b + 1, sl] = r

    loop(8, joins)
    wait_all(copies)
    de[...] = de[...] * gate[...] * (1.0 - gate[...])
    ds[...] = dot3_nt(de[...], ex[...]) * slope(sp[...])
    dp[...] = dot3_nt(ds[...], sq[...])
    for b in range(B):
        dp[b : b + 1, :] = dp[b : b + 1, :] * fs[CELLS + b]
    total = jnp.sum(de[...], axis=0, keepdims=True)
    bias[...] = jnp.zeros((8, 512), F32)
    for k in range(4):
        bias[k : k + 1, :] = total[:, k * 512 : (k + 1) * 512]
    bias[4:5, 0:128] = jnp.sum(ds[...], axis=0, keepdims=True)

    def tops(c):
        sl = cols(c)
        d = dj1[:, sl]
        mean, scale = coefs(tot3, 0, sl, fs, INV_OUT)
        x = (pre3[:, sl] - mean) * scale
        du = (
            d * expand([gate[b : b + 1, sl] for b in range(B)])
            + expand([dp[b : b + 1, sl] for b in range(B)])
        ) * keep[...]
        put(st, 0, back_rows(du, x, fs), sl)
        mean, scale = coefs(tot3, 4, sl, fs, INV_OUT)
        put(st, 4, back_rows(d, (prep[:, sl] - mean) * scale, fs), sl)

    loop(8, tops)


def back_three_kernel(
    fs, parts, tot3, pre3, prep, dj1, gate, dp, bias, pre2, tot2, keep, vec, gb, w3,
    d3, dproj, do2, st, dgain, dbias, dgainp, dbiasp, tot, acc,
):
    add_parts(parts, tot)
    whole_gain(tot, 0, dgain, dbias)
    whole_gain(tot, 4, dgainp, dbiasp)
    acc[...] = jnp.zeros((M, 512), F32)

    def body(c):
        sl = cols(c)
        mean, scale = coefs(tot3, 0, sl, fs, INV_OUT)
        x = (pre3[:, sl] - mean) * scale
        dj = dj1[:, sl]
        du = (
            dj * expand([gate[b : b + 1, sl] for b in range(B)])
            + expand([dp[b : b + 1, sl] for b in range(B)])
        ) * keep[...]
        a, bb = means(tot, 0, sl, fs, INV_OUT)
        d = low((du - a - x * bb) * (scale * vec[0:1, sl]) * keep[...])
        d3[:, sl] = d
        acc[...] += mm_nt(d, w3[:, sl])
        mean, scale = coefs(tot3, 4, sl, fs, INV_OUT)
        x = (prep[:, sl] - mean) * scale
        a, bb = means(tot, 4, sl, fs, INV_OUT)
        dproj[:, sl] = low((dj - a - x * bb) * (scale * vec[2:3, sl]) * keep[...])

    loop(8, body)
    sl = slice(0, 512)
    mean, scale = coefs(tot2, 0, sl, fs, INV_OUT)
    x = (pre2[...] - mean) * scale
    o = x * gb[2:3, :] + gb[3:4, :]
    d = acc[...] * keep[...] * slope(o)
    do2[...] = d
    put(st, 0, back_rows(d, x, fs), sl)
    st[4:12, :] = bias[...]


def fetch_two_kernel(far, ws, sems):
    wait_all(copy_all([(far.at[3 * k : 3 * k + 3], ws.at[3 * k : 3 * k + 3]) for k in range(3)], sems))


def back_two_kernel(
    fs, parts, tot2, pre2, do2, x1, keep1, keep, gb, sh, ws,
    d2, do1, st, dgain, dbias, debias, dsbias, tot, dcol,
):
    add_parts(parts, tot)
    whole_gain(tot, 0, dgain, dbias)
    debias[...] = jnp.concatenate([tot[k : k + 1, :] for k in range(4, 8)], axis=1).reshape(2048)
    dsbias[...] = tot[8:9, 0:128].reshape(128)
    sl = slice(0, 512)
    mean, scale = coefs(tot2, 0, sl, fs, INV_OUT)
    x = (pre2[...] - mean) * scale
    a, bb = means(tot, 0, sl, fs, INV_OUT)
    d = low((do2[...] - a - x * bb) * (scale * gb[2:3, :]) * keep[...])
    d2[...] = d
    dcol[0] = d
    dcol[1] = low(mm(sh[5], d))
    dcol[2] = low(mm(sh[7], d))
    dcol[3] = low(mm(sh[8], d))
    terms = (
        ((0, 4),),
        ((0, 5), (1, 3)),
        ((0, 7), (2, 1)),
        ((0, 8), (1, 6), (2, 2), (3, 0)),
    )
    st[...] = jnp.zeros((4, 512), F32)
    for k in range(4):
        acc = 0.0
        for which, t in terms[k]:
            acc = acc + mm_nt(dcol[which], ws[t])
        x = x1[k]
        o = x * gb[0:1, :] + gb[1:2, :]
        d = acc * keep1[k] * slope(o)
        do1[k] = d
        rows = back_rows(d, x, fs)
        for r in range(4):
            st[r : r + 1, :] += rows[r]


def deal(isc, full, rows, keep, send, at):
    for p in range(16):
        tile = full[pl.ds(pl.multiple_of(isc[DEST + p] * rows, rows), rows), :]
        (keep if p < 8 else send)[p % 8, at_rows(at, rows), :] = tile


def back_one_kernel(
    fs, isc, parts, tot1, x1, do1, xp, keep1, gb, d1, gkeep, gsend, dgain, dbias, tot, dn, full
):
    n = isc[NARROW]
    add_parts(parts, tot)
    whole_gain(tot, 0, dgain, dbias)
    sl = slice(0, 512)
    scale = coefs(tot1, 0, sl, fs, INV_IN)[1] * gb[0:1, :]
    a, bb = means(tot, 0, sl, fs, INV_IN)
    planes = []
    for k in range(4):
        d = (do1[k] - a - x1[k] * bb) * scale * keep1[k]
        planes.append(d)
        dn[k] = low(d)
    for b in range(B):
        d1[b] = low(jnp.concatenate([d[b * POS : (b + 1) * POS] for d in planes], axis=0))

    def body(c):
        g = 0.0
        for k in range(4):
            g = g + mm_tn(xp[k, :, cols(c)], dn[k, :, cols(n)])
        full[cols(c), :] = low(g)

    loop(4, body)
    deal(isc, full, 64, gkeep, gsend, 0)


def placed_kernel(isc, dproj, wp_far, out, cc, pick_own, spread, wp, sems):
    n = isc[NARROW]
    copies = [
        pltpu.make_async_copy(wp_far.at[cut], wp.at[cut], sems.at[k])
        for k, cut in enumerate(slice(256 * k, 256 * (k + 1)) for k in range(4))
    ]
    for c in copies:
        c.start()
    for b in range(B):
        place = lax.broadcasted_iota(jnp.int32, (32, M), 1)
        it = lax.broadcasted_iota(jnp.int32, (32, M), 0)
        pick_own[b * 32 : (b + 1) * 32, :] = low(jnp.where(
            (place == b * POS + (it >> 2) * 8 + n * 4 + (it & 3)) & (it < 28), 1.0, 0.0
        ))
        place = lax.broadcasted_iota(jnp.int32, (HALF, 128), 1)
        it = lax.broadcasted_iota(jnp.int32, (HALF, 128), 0)
        spread[b * HALF : (b + 1) * HALF, :] = low(jnp.where(
            ((it & 9) == 0) & (place == b * 32 + (it >> 4) * 4 + ((it & 7) >> 1)), 1.0, 0.0
        ))
    cc[...] = low(mm(pick_own[...], dproj[...]))
    for c in range(4):
        sl = cols(c)
        copies[c].wait()
        hi, lo = split2(mm_nt(cc[...], wp[sl, :]))
        out[:, sl] = mm(spread[...], hi) + mm(spread[...], lo)


def image_kernel(isc, perm, d1, placed, keep, w1, out, dc):
    n = isc[NARROW]
    for b in range(B):
        dc[b * HALF : (b + 1) * HALF, :] = low(mm_tn(perm[n], d1[b]))
    for c in range(4):
        sl = cols(c)
        out[:, sl] = (mm_nt(dc[...], w1[sl, :]) + placed[:, sl]) * keep[...]


def grads_a_kernel(isc, h5, d6, col4, d5, gkeep, gsend, wider, full):
    n = isc[NARROW]

    def expand2(c):
        wider[:, cols(c)] = low(mm_tn(h5[:, cols(n)], d6[:, cols(c)]))

    loop(8, expand2)
    for p in range(16):
        sl = cols(isc[DEST + p], 128)
        for k in range(2):
            (gkeep if p < 8 else gsend)[p % 8, 0:128, k * 128 : (k + 1) * 128] = wider[
                k * 128 : (k + 1) * 128, sl
            ]

    def spatial(t):
        full[...] = low(mm_tn(col4[t], d5[:, cols(n)]))
        deal(isc, full, 32, gkeep, gsend, 128 + t * 32)

    loop(9, spatial)


def gate_grads(isc, n, c, at, squeezed, pooled, de, ds, gkeep, gsend, q, e):
    sl = cols(n * 4 + c)
    q[...] = outer(ds[...], pooled[:, sl])
    e[...] = outer(squeezed[...], de[:, sl])
    for p in range(16):
        rows = pl.ds(pl.multiple_of(isc[DEST + p] * 8, 8), 8)
        both = jnp.concatenate([q[rows, :], e[rows, :]], axis=0)
        (gkeep if p < 8 else gsend)[p % 8, at_rows(at + c * 16, 16), :] = low(both)


def grads_b_kernel(
    isc, d4, lows, sq2, pooled2, de2, ds2, sp1, pooled1, de1, ds1, gkeep, gsend, full, q, e, sq1
):
    n = isc[NARROW]
    sq1[...] = sp1[...] * sigmoid(sp1[...])

    def body(c):
        full[...] = low(mm_tn(d4[...], lows[:, cols(n * 4 + c)]))
        deal(isc, full, 32, gkeep, gsend, c * 32)
        gate_grads(isc, n, c, 128, sq2, pooled2, de2, ds2, gkeep, gsend, q, e)
        gate_grads(isc, n, c, 192, sq1, pooled1, de1, ds1, gkeep, gsend, q, e)

    loop(4, body)


def grads_c_kernel(isc, h2, d3, strided, dproj, gkeep, gsend, full, taller):
    n = isc[NARROW]

    def body(c):
        sl = cols(n * 4 + c)
        full[...] = low(mm_tn(h2[...], d3[:, sl]))
        deal(isc, full, 32, gkeep, gsend, c * 32)
        taller[...] = low(mm_tn(strided[...], dproj[:, sl]))
        deal(isc, taller, 64, gkeep, gsend, 128 + c * 64)

    loop(4, body)


def grads_d_kernel(isc, col1, d2, gkeep, gsend, full):
    n = isc[NARROW]

    def spatial(t):
        full[...] = low(mm_tn(col1[t], d2[:, cols(n)]))
        deal(isc, full, 32, gkeep, gsend, t * 32)

    loop(9, spatial)


def joined(v, out, at, rows):
    for c in range(4):
        out[:, c * 256 : (c + 1) * 256] = v[at + c * rows : at + (c + 1) * rows, :]


def unpack_gates(v, at, squeeze, excite):
    for c in range(4):
        part = v[at + c * 16 : at + (c + 1) * 16, :]
        squeeze[:, c * 256 : (c + 1) * 256] = part[0:8]
        excite[:, c * 256 : (c + 1) * 256] = part[8:16]


def unpack_kernel(
    a, b, c, d, expand2, spatial2, reduce2, squeeze2, excite2, squeeze1, excite1, expand1, project1
):
    v = f32(a[0]) + f32(b[0])
    expand2[0:128, :] = v[0:128, 0:128]
    expand2[128:256, :] = v[0:128, 128:256]
    spatial2[...] = v[128:416, :]
    joined(v, reduce2, 416, 32)
    unpack_gates(v, 544, squeeze2, excite2)
    unpack_gates(v, 608, squeeze1, excite1)
    v = f32(c[0]) + f32(d[0])
    joined(v, expand1, 0, 32)
    joined(v, project1, 128, 64)


def unpack_last_kernel(a, b, c, d, spatial1, reduce1):
    spatial1[...] = f32(a[0]) + f32(b[0])
    reduce1[...] = f32(c[0]) + f32(d[0])


VECTORS = (512,) * 6 + (2048,) * 5 + (128,) * 2 + (256,) * 2 + (1024,) * 3


def pack_kernel(isc, w5, w4, w6, ex, sq, ws_far, *refs):
    far, refs = refs[:18], refs[18:]
    out, w5_half, w4_half, gb, vec1, sqb, vown, ws, w6v, exv, sqv, rows = refs[:12]
    vecs, sems = refs[12:30], refs[30]
    core = isc[CORE]
    pairs = [(f, v) for f, v in zip(far, vecs)] + [
        (w6.at[at_rows(core * 128, 128)], w6v),
        (ex.at[at_rows(core * 64, 64)], exv),
        (sq.at[at_rows(core * 512, 512)], sqv),
        (w4.at[at_rows(core * 512, 512)], w4_half),
        (w5.at[at_rows(core * 2304, 2304)], w5_half),
        (ws_far, ws),
    ]
    copies = copy_all(pairs, sems)
    wait_all(copies[:21])

    def row(v):
        return f32(v[...]).reshape(1, v.shape[0])

    for k in range(6):
        gb[k : k + 1, :] = row(vecs[k])
    for k in range(5):
        vec1[k : k + 1, :] = row(vecs[6 + k])
    for k in range(2):
        sqb[k : k + 1, :] = row(vecs[11 + k])
    rows[...] = jnp.zeros((16, 256), F32)
    at = 0
    for v in vecs[13:18]:
        r = row(v)
        for c in range(v.shape[0] // 256):
            rows[at : at + 1, :] = r[:, c * 256 : (c + 1) * 256]
            at += 1
    vown[...] = low(rows[...])
    for c in range(8):
        out[W6_AT + c * 128 : W6_AT + (c + 1) * 128, :] = w6v[:, c * 256 : (c + 1) * 256]
    for c in range(4):
        out[EX_AT + c * 64 : EX_AT + (c + 1) * 64, :] = exv[:, c * 256 : (c + 1) * 256]
    for k in range(2):
        out[SQ_AT : SQ_AT + 256, k * 128 : (k + 1) * 128] = sqv[k * 256 : (k + 1) * 256, :]
    out[VE2:PACK_ROWS, :] = vown[...]
    wait_all(copies[21:])


def call(body, outs, args, scratch=(), flops=1e8, size=5e6, name=None, vmem=LIMIT):
    specs, values = [], []
    for a in args:
        kind, v = a if isinstance(a, tuple) else (VMEM, a)
        specs.append(kind)
        values.append(v)
    return pl.pallas_call(
        body,
        out_shape=tuple(o if hasattr(o, "memory_space") else jax.ShapeDtypeStruct(o[0], o[1]) for o in outs),
        in_specs=specs,
        out_specs=tuple(o[2] if isinstance(o, tuple) and len(o) > 2 else pl.BlockSpec(memory_space=getattr(o, "memory_space", pltpu.VMEM)) for o in outs),
        scratch_shapes=list(scratch),
        compiler_params=pltpu.CompilerParams(vmem_limit_bytes=vmem * 2**20),
        cost_estimate=pl.CostEstimate(
            flops=int(flops * SCALE), bytes_accessed=int(size * SCALE), transcendentals=0
        ),
        name=name,
    )(*values)


def swap(v, axis, pairs):
    return lax.ppermute(v, axis, pairs)


def after(v, *others):
    return lax.optimization_barrier((v,) + others)[0]


def local(
    images, crop, micro,
    first_reduce, first_reduce_gain, first_reduce_bias,
    first_spatial, first_spatial_gain, first_spatial_bias,
    first_expand, first_expand_gain, first_expand_bias,
    first_project, first_project_gain, first_project_bias,
    first_squeeze, first_squeeze_bias, first_excite, first_excite_bias,
    second_reduce, second_reduce_gain, second_reduce_bias,
    second_spatial, second_spatial_gain, second_spatial_bias,
    second_expand, second_expand_gain, second_expand_bias,
    second_squeeze, second_squeeze_bias, second_excite, second_excite_bias,
    out_grad,
):
    wide = lax.axis_size("wide")
    exact = wide == 16
    near = [(i, i ^ 1) for i in range(wide)]
    pair = [(0, 1), (1, 0)]
    V = pltpu.VMEM
    D = pltpu.SemaphoreType.DMA
    out = lambda *shape: (shape, F32)
    f = lambda *shape: V(shape, F32)
    h = lambda *shape: V(shape, BF)
    far = lambda v: (ANY, pltpu.with_memory_space_constraint(v, pltpu.HBM))

    def steps(x, *first, before=None):
        results, step = [], 1
        x = after(x, *first)
        while step < wide:
            due = (before or {}).get(len(results), ())
            y = after(x, *(due(results) if callable(due) else due))
            x = x + swap(y, "wide", [(i, i ^ step) for i in range(wide)])
            results.append(x)
            step *= 2
        return x[None], results

    own_px = images.transpose(0, 2, 1, 3).reshape(B, HALF, 1024)
    other_px = swap(own_px, "narrow", pair)
    ws_far = first_spatial.reshape(9, 512, 512)

    fs_, isc_, keep, keep1, keep_half, sh, perm = call(
        functools.partial(setup_kernel, exact),
        [
            pltpu.SMEM((13,), F32), pltpu.SMEM((18,), jnp.int32), f(M, 1), f(4, M, 1), f(HROWS, 1),
            h(9, M, M), h(2, M, HALF),
        ],
        [(SMEM, far(crop)[1]), (SMEM, far(micro)[1])], name="setup",
    )
    fs, isc = (SMEM, fs_), (SMEM, isc_)
    st1, xown, w1 = call(
        one_half_kernel, [f(4, 512), h(B, HALF, 1024), h(1024, 512)],
        [fs, far(own_px), keep_half, far(first_reduce)],
        [V((HROWS, 1024), BF), D((2,))], flops=5e8, name="one_half",
    )
    part = steps(st1)[0][0]

    w5_own = second_spatial.reshape(9 * 512, 256)
    vectors = [
        first_reduce_gain, first_reduce_bias, first_spatial_gain, first_spatial_bias,
        second_reduce_gain, second_reduce_bias, first_expand_gain, first_expand_bias,
        first_project_gain, first_project_bias, first_excite_bias,
        first_squeeze_bias, second_squeeze_bias,
        second_spatial_gain, second_spatial_bias, second_expand_gain, second_expand_bias, second_excite_bias,
    ]
    pack, w5_half, w4_half, gb, vec1, sqb, vown, ws = call(
        pack_kernel,
        [
            ((PACK_ROWS, 256), BF), ((2304, 256), BF), ((512, 512), BF), f(8, 512), f(8, 2048), f(8, 128), h(16, 256),
            h(9, 512, 512),
        ],
        [
            (SMEM, after(isc_, st1)), far(w5_own), far(second_reduce), far(second_expand), far(second_excite),
            far(second_squeeze), far(ws_far),
        ] + [far(v) for v in vectors],
        [V((128, 2048), BF), V((64, 1024), BF), V((512, 128), BF), V((16, 256), F32)]
        + [V((size,), BF) for size in VECTORS] + [D((24,))],
        size=2e7, name="pack",
    )
    part = after(part, gb)
    part_other = swap(part, "narrow", pair)
    w4_r1 = swap(after(w4_half, other_px, part_other), "narrow", pair)
    og_own = out_grad.transpose(0, 2, 1, 3).reshape(M, 1024)

    xp, strided, x1, col1, pre2, st2, tot1 = call(
        stage_two_kernel,
        [h(4, M, 1024), h(M, 1024), f(4, M, 512), h(9, M, 512), f(M, 512), f(4, 512), f(4, 512)],
        [fs, isc, xown, other_px, part, part_other, perm, keep1, keep, w1, ws, gb, sh],
        [V((4, M, 256), F32), V((4, M, 512), BF), V((4, 512), F32)],
        flops=4e9, size=2e7, name="stage_two",
    )
    parts2, sent2 = steps(st2, before={3: (w4_r1,)})
    w4_r2 = swap(after(w4_r1, sent2[1]), "wide", near)
    w5_r1 = swap(after(w5_half, w4_r1, sent2[1]), "narrow", pair)
    prep, stp, w3 = call(
        project_kernel, [f(M, 2048), f(4, 2048), h(512, 2048)],
        [fs, strided, keep, far(first_project), far(first_expand)],
        [V((1024, 2048), BF), D((5,))], flops=1e9, size=8e6, name="project",
    )
    h2, pre3, st3, tot2 = call(
        stage_three_kernel, [h(M, 512), f(M, 2048), f(8, 2048), f(4, 512)],
        [fs, parts2, pre2, stp, keep, w3, gb], [V((4, 512), F32)],
        flops=1e9, size=6e6, name="stage_three",
    )
    parts3, _ = steps(st3, before={3: (w4_r2,)})
    w5_r2 = swap(after(w5_r1, parts3), "wide", near)
    pk1 = swap(after(pack, w5_r1, parts3), "narrow", pair)
    w4 = call(
        fetch_four_kernel, [h(2048, 512)],
        [(SMEM, after(isc_, st3)), far(second_reduce), (ANY, w4_r1), (ANY, w4_r2)], [D((3,))],
        size=4e6, name="fetch_four",
    )[0]
    lows, pre4, st4, tot3, gate1, sp1, pooled1, squares = call(
        stage_four_kernel,
        [
            h(M, 2048), f(M, 512), f(4, 512), f(8, 2048), f(8, 2048), f(8, 128), f(8, 2048), f(8, 256),
        ],
        [fs, parts3, pre3, prep, keep, vec1, sqb, far(first_squeeze), far(first_excite), w4],
        [
            V((M, 2048), F32), V((M, 2048), F32), V((M, 512), F32), V((8, 2048), F32),
            V((2048, 128), BF), V((128, 2048), BF), D((2,)),
        ],
        flops=1e9, size=1e7, name="stage_four",
    )
    parts4, _ = steps(st4, before={3: (w5_r2,)})
    w5 = call(
        fetch_five_kernel, [h(2, 4608, 256)],
        [(SMEM, after(isc_, st4)), far(w5_own), (ANY, w5_r1), (ANY, w5_r2)], [D((3,))],
        size=8e6, name="fetch_five",
    )[0]
    col4, pre5, st5, tot4 = call(
        stage_five_kernel, [h(9, M, 512), f(M, 512), f(4, 512), f(4, 512)],
        [fs, parts4, pre4, keep, gb, sh, w5], [V((4, 512), F32)],
        flops=2e9, size=1e7, name="stage_five",
    )
    pk2 = swap(after(pk1, st5), "wide", near)
    parts5, _ = steps(st5, before={3: (pk2,)})
    og_other = swap(after(og_own, pk1, st5), "narrow", pair)
    pk1, pk2 = (ANY, pk1), (ANY, pk2)
    w6, gain5, vec2 = call(
        fetch_six_kernel, [h(512, 2048), f(2, 512), f(3, 2048)],
        [(SMEM, after(isc_, st5)), far(second_expand), pk1, pk2, vown],
        [V((16, 256), BF), D((18,))], size=4e6, name="fetch_six",
    )
    h5, pre6, st6, tot5 = call(
        stage_six_kernel, [h(M, 512), f(M, 2048), f(4, 2048), f(4, 512)],
        [fs, parts5, pre5, keep, gain5, w6], [V((4, 512), F32)],
        flops=1e9, size=6e6, name="stage_six",
    )
    parts6, _ = steps(st6)
    sq, ex, og = call(
        fetch_turn_kernel, [h(2048, 128), h(2, 128, 1024), h(2, M, 1024)],
        [
            (SMEM, after(isc_, st6)), far(second_squeeze), far(second_excite), pk1, pk2,
            far(og_own), (ANY, og_other),
        ],
        [D((16,))], size=4e6, name="fetch_turn",
    )
    result, dj2, pay6, extra6, tot6, gate2, dp2, pooled2, de2, ds2, sq2 = call(
        turn_kernel,
        [
            ((M, 1024), BF), f(M, 2048), f(4, 2048), f(8, 512), f(4, 2048), f(8, 2048),
            f(8, 2048), f(8, 2048), f(8, 2048), f(8, 128), f(8, 128),
        ],
        [fs, isc, parts6, pre6, keep, lows, vec2, sqb, squares, sq, ex, og],
        [V((M, 2048), F32), V((2, M, 1024), BF), V((4, 2048), F32), V((8, 128), F32)],
        flops=1e9, size=1e7, name="turn",
    )
    back6, _ = steps(pay6)
    d6, do5, bt5, dgain6, dbias6 = call(
        back_six_kernel, [h(M, 2048), f(M, 512), f(12, 512), out(1024), out(1024)],
        [fs, isc, back6, tot6, pre6, dj2, gate2, dp2, pre5, tot5, extra6, keep, vec2, gain5, w6],
        [V((4, 2048), F32), V((M, 512), F32)],
        flops=1e9, size=1e7, name="back_six",
    )
    back5, _ = steps(bt5)
    d5, do4, bt4, dgain5, dbias5, debias2, dsbias2, norms = call(
        back_five_kernel,
        [h(M, 512), f(M, 512), f(4, 512), out(256), out(256), out(1024), out(128), ((5,), F32, SMEM)],
        [fs, isc, back5, tot5, pre5, do5, pre4, tot4, keep, gb, gain5, sh, w5],
        [V((12, 512), F32)],
        flops=2e9, size=1e7, name="back_five",
    )

    def step(g, k, *ties):
        if not exact:
            return g, ()
        kept, sent = g
        got = swap(after(sent, *ties), "wide", [(i, i ^ (1 << k)) for i in range(wide)])
        if k == 3:
            return (kept, got), (got,)
        half = kept.shape[0] // 2
        return (kept[:half] + got[:half], kept[half:] + got[half:]), (got,)

    ga = call(
        grads_a_kernel, [h(8, 416, 256)] * 2, [isc, h5, d6, col4, d5],
        [V((256, 2048), BF), V((512, 256), BF)], flops=2e9, size=1e7, name="grads_a",
    )
    held = {}

    def core_step(name, g, tied=True):
        def due(results):
            held[name], _ = step(g, 0, *(results[:1] if tied else ()))
            return held[name] if exact else ()

        return due

    back4, sent4 = steps(bt4, *ga, before={2: core_step("a", ga)})
    ga, xa = step(held["a"], 1, sent4[1])
    d4, dj1, bt3, dgain4, dbias4, dp1, de1, ds1, bias1 = call(
        back_four_kernel,
        [
            h(M, 512), f(M, 2048), f(8, 2048), out(512), out(512), f(8, 2048),
            f(8, 2048), f(8, 128), f(8, 512),
        ],
        [
            fs, back4, tot4, pre4, do4, dj2, tot3, pre3, prep, gate1, sp1, keep, gb, vec1,
            far(first_squeeze), far(first_excite), w4,
        ],
        [V((4, 512), F32), V((2048, 128), BF), V((128, 2048), BF), D((2,))],
        flops=1e9, size=1e7, name="back_four",
    )
    gb1 = call(
        grads_b_kernel, [h(8, 256, 256)] * 2,
        [isc, d4, lows, sq2, pooled2, de2, ds2, sp1, pooled1, de1, ds1],
        [V((512, 256), BF), V((128, 256), F32), V((128, 256), F32), V((8, 128), F32)],
        flops=1e9, size=4e6, name="grads_b",
    )
    ws_back = call(
        fetch_two_kernel, [h(9, 512, 512)], [far(after(ws_far, bt4))], [D((3,))], size=9e6, name="fetch_two",
    )[0]
    back3, sent3 = steps(bt3, *gb1, *xa, ws_back, before={3: core_step("b", gb1, True)})
    gb1 = held["b"]
    gb1, xb = step(gb1, 1, sent3[3])
    ga, za = step(ga, 2, sent3[3])
    d3, dproj, do2, bt2, dgain3, dbias3, dgainp, dbiasp = call(
        back_three_kernel,
        [h(M, 2048), h(M, 2048), f(M, 512), f(12, 512), out(2048), out(2048), out(2048), out(2048)],
        [fs, back3, tot3, pre3, prep, dj1, gate1, dp1, bias1, pre2, tot2, keep, vec1, gb, w3],
        [V((8, 2048), F32), V((M, 512), F32)],
        flops=1e9, size=1e7, name="back_three",
    )
    gc = call(
        grads_c_kernel, [h(8, 384, 256)] * 2, [isc, h2, d3, strided, dproj],
        [V((512, 256), BF), V((1024, 256), BF)],
        flops=3e9, size=1e7, name="grads_c",
    )
    back2, sent2 = steps(bt2, *gc, *za, *xb, before={2: core_step("c", gc)})
    gc, xc = step(held["c"], 1, sent2[1])
    d2, do1, bt1, dgain2, dbias2, debias1, dsbias1 = call(
        back_two_kernel,
        [h(M, 512), f(4, M, 512), f(4, 512), out(512), out(512), out(2048), out(128)],
        [fs, back2, tot2, pre2, do2, x1, keep1, keep, gb, sh, ws_back],
        [V((12, 512), F32), V((4, M, 512), BF)],
        flops=2e9, size=1e7, name="back_two",
    )
    gd = call(
        grads_d_kernel, [h(8, 288, 256)] * 2, [isc, col1, d2], [V((512, 256), BF)],
        flops=2e9, size=6e6, name="grads_d",
    )
    placed = call(
        placed_kernel, [f(HROWS, 1024)], [(SMEM, after(isc_, bt2)), dproj, far(first_project)],
        [V((128, 2048), BF), V((128, M), BF), V((HROWS, 128), BF), V((1024, 2048), BF), D((4,))],
        flops=1e9, size=1e7, name="placed",
    )[0]
    back1, sent1 = steps(bt1, *gd, *xc, placed)
    gd, _ = step(gd, 0, sent1[0])
    gd0 = gd
    gd, xd = step(gd, 1, sent1[2])
    gc, _ = step(gc, 2, sent1[3])
    back1 = after(back1, *gd0)
    d1, ge_keep, ge_send, dgain1, dbias1 = call(
        back_one_kernel, [h(B, M, 512), h(8, 64, 256), h(8, 64, 256), out(512), out(512)],
        [fs, isc, back1, tot1, x1, do1, xp, keep1, gb],
        [V((4, 512), F32), V((4, M, 512), BF), V((1024, 256), BF)],
        flops=1e9, size=6e6, name="back_one",
    )
    ge = (ge_keep, ge_send)
    dimg = call(
        image_kernel, [out(HROWS, 1024)], [isc, perm, d1, placed, keep_half, w1],
        [V((HROWS, 512), BF)], flops=1e9, size=1e7, name="image",
    )[0]

    if exact:
        ge, _ = step(ge, 0)
        dimg, *gd = lax.optimization_barrier((dimg,) + gd)
        gb1, _ = step(gb1, 2)
        gab = tuple(jnp.concatenate(p, axis=1) for p in zip(ga, gb1))
        gab, _ = step(gab, 3)
        gd, _ = step(gd, 2)
        gc, _ = step(gc, 3)
        ge, _ = step(ge, 1)
        ge, _ = step(ge, 2)
        gd, _ = step(gd, 3)
        ge, _ = step(ge, 3)
        (
            expand2, spatial2, reduce2, squeeze2, excite2, squeeze1, excite1, expand1, project1,
        ) = call(
            unpack_kernel,
            [out(256, 128), out(288, 256), out(32, 1024)] + [out(8, 1024)] * 4 + [out(32, 1024), out(64, 1024)],
            list(gab + gc), name="unpack",
        )
        spatial1, reduce1 = call(
            unpack_last_kernel, [out(288, 256), out(64, 256)], list(gd + ge), name="unpack_last"
        )
    else:
        finer = wide // 16

        def summed(g):
            return lax.psum_scatter(g, "wide", scatter_dimension=0, tiled=True)

        def blocks(g, start, count, rows):
            p = g[:, start : start + count * rows].reshape(16, count, finer, rows // finer, 256)
            p = summed(p.transpose(0, 2, 1, 3, 4).reshape(wide, count, rows // finer, 256))[0]
            return f32(p).transpose(1, 0, 2).reshape(rows // finer, count * 256)

        def both(g, start):
            p = g[:, start : start + 64].reshape(16, 4, 2, finer, 8 // finer, 256)
            p = f32(summed(p.transpose(0, 3, 1, 2, 4, 5).reshape(wide, 4, 2, -1, 256))[0])
            return [p[:, k].transpose(1, 0, 2).reshape(-1, 1024) for k in range(2)]

        def taps(g, start):
            p = g[:, start : start + 288].reshape(16, 9, finer, 32 // finer, 256)
            return f32(summed(p.transpose(0, 2, 1, 3, 4).reshape(wide, 9, -1, 256))[0]).reshape(-1, 256)

        ga, gb1, gc, gd, ge = (jnp.concatenate(g) for g in (ga, gb1, gc, gd, ge))
        e2 = ga[:, 0:128].reshape(16, 128, 2, finer, 128 // finer).transpose(0, 3, 1, 2, 4)
        e2 = summed(e2.reshape(wide, 1, -1)).reshape(128, 2, -1)
        expand2 = f32(e2.transpose(1, 0, 2).reshape(256, -1))
        spatial2 = taps(ga, 128)
        reduce2 = blocks(gb1, 0, 4, 32)
        squeeze2, excite2 = both(gb1, 128)
        expand1, project1 = blocks(gc, 0, 4, 32), blocks(gc, 128, 4, 64)
        squeeze1, excite1 = both(gb1, 192)
        spatial1, reduce1 = taps(gd, 0), blocks(ge, 0, 1, 64)
    return (
        result.reshape(B, 7, 8, 1024).transpose(0, 2, 1, 3),
        dimg.reshape(B, 14, 8, 1024).transpose(0, 2, 1, 3),
        reduce1, dgain1, dbias1,
        spatial1.reshape(3, 3, -1, 256), dgain2, dbias2,
        expand1, dgain3, dbias3,
        project1, dgainp, dbiasp,
        squeeze1.T, dsbias1, excite1, debias1,
        reduce2.T, dgain4, dbias4,
        spatial2.reshape(3, 3, -1, 256), dgain5, dbias5,
        expand2, dgain6, dbias6,
        squeeze2.T, dsbias2, excite2, debias2,
        norms,
    )


def solution(mesh):
    rep, nar = P(), P("narrow")
    return jax.shard_map(
        local,
        mesh=mesh,
        in_specs=(P("wide", "narrow", None, None),) + (rep,) * 18 + (
            P("narrow", None), rep, rep,
            P(None, None, None, "narrow"), nar, nar,
            P("narrow", None), nar, nar,
            P("narrow", None), rep, P(None, "narrow"), nar,
            P("wide", None, None, "narrow"),
        ),
        out_specs=(
            P("wide", None, None, "narrow"), P("wide", "narrow", None, None),
            P("wide", "narrow"), rep, rep,
            P(None, None, "wide", "narrow"), rep, rep,
            P("wide", "narrow"), rep, rep,
            P("wide", "narrow"), rep, rep,
            P("narrow", "wide"), rep, P("wide", "narrow"), rep,
            P("narrow", "wide"), rep, rep,
            P(None, None, "wide", "narrow"), nar, nar,
            P("narrow", "wide"), nar, nar,
            P("narrow", "wide"), rep, P("wide", "narrow"), nar,
            rep,
        ),
        check_vma=False,
    )
```

```python
import functools

import numpy as np
import jax
import jax.numpy as jnp
from jax import lax
from jax.experimental import pallas as pl
from jax.experimental.pallas import tpu as pltpu
from jax.sharding import PartitionSpec as P

EPSILON = 1e-05
BF = jnp.bfloat16
F32 = jnp.float32
B = 4
POS = 56
LIMIT = 14
SCALE = 0.01
UNROLL = 2
M = B * POS
HALF = 112
HROWS = B * HALF
VMEM = pl.BlockSpec(memory_space=pltpu.VMEM)
SMEM = pl.BlockSpec(memory_space=pltpu.SMEM)
ANY = pl.BlockSpec(memory_space=pl.ANY)
INV_IN, INV_OUT, CELLS, MICRO, INV_ALL = 0, 2, 4, 8, 12
NARROW, CORE, DEST = 0, 1, 2
W6_AT, EX_AT, SQ_AT, VE2, PACK_ROWS = 0, 1024, 1280, 1536, 1552


def mm(a, b):
    return lax.dot_general(a, b, (((1,), (0,)), ((), ())), preferred_element_type=F32)


def mm_nt(a, b):
    return lax.dot_general(a, b, (((1,), (1,)), ((), ())), preferred_element_type=F32)


def mm_tn(a, b):
    return lax.dot_general(a, b, (((0,), (0,)), ((), ())), preferred_element_type=F32)


def f32(v):
    return v.astype(F32)


def low(v):
    return v.astype(BF)


def split2(v):
    a = low(v)
    return a, low(v - f32(a))


def stack3(v):
    a = f32(low(v))
    r = v - a
    b = f32(low(r))
    return low(jnp.concatenate([a, b, r - b, jnp.zeros_like(v)], axis=0))


def sum3(p):
    return p[0:8] + p[8:16] + p[16:24]


def dot3(v, w):
    return sum3(mm(stack3(v), w))


def dot3_nt(v, w):
    return sum3(mm_nt(stack3(v), w))


def outer(a, b):
    a1, b1 = f32(low(a)), f32(low(b))
    zeros = jnp.zeros_like
    left = low(jnp.concatenate([a1, a1, a - a1, zeros(a)], axis=0))
    return mm_tn(left, low(jnp.concatenate([b1, b - b1, b1, zeros(b)], axis=0)))


def sigmoid(v):
    return 1.0 / (1.0 + jnp.exp(-v))


def slope(v):
    s = sigmoid(v)
    return s * (1.0 + v * (1.0 - s))


def cols(c, size=256):
    return pl.ds(pl.multiple_of(c * size, size), size)


def expand(rows):
    return jnp.concatenate([jnp.broadcast_to(r, (POS, r.shape[1])) for r in rows], axis=0)


def pick(r0, r1, fs):
    return expand([r0 * (1.0 - fs[MICRO + b]) + r1 * fs[MICRO + b] for b in range(B)])


def image_sums(v):
    return [jnp.sum(v[b * POS : (b + 1) * POS], axis=0, keepdims=True) for b in range(B)]


def grouped(sums, fs, reps=1):
    zero = one = 0.0
    for b in range(B):
        zero = zero + sums[b] * (1.0 - fs[MICRO + b])
        one = one + sums[b] * fs[MICRO + b]
    return [zero, one]


def group_sums(v, fs):
    return grouped(image_sums(v), fs)


def put(ref, at, rows, sl):
    for k, r in enumerate(rows):
        ref[at + k : at + k + 1, sl] = r


def add_parts(parts, tot):
    t = parts[0]
    for k in range(1, parts.shape[0]):
        t = t + parts[k]
    tot[...] = t


def coefs(tot, at, sl, fs, inv):
    i0, i1 = fs[inv], fs[inv + 1]
    m0, m1 = tot[at : at + 1, sl] * i0, tot[at + 1 : at + 2, sl] * i1
    q0 = lax.rsqrt(tot[at + 2 : at + 3, sl] * i0 - m0 * m0 + EPSILON)
    q1 = lax.rsqrt(tot[at + 3 : at + 4, sl] * i1 - m1 * m1 + EPSILON)
    return pick(m0, m1, fs), pick(q0, q1, fs)


def means(tot, at, sl, fs, inv):
    i0, i1 = fs[inv], fs[inv + 1]
    a = pick(tot[at : at + 1, sl] * i0, tot[at + 1 : at + 2, sl] * i1, fs)
    b = pick(tot[at + 2 : at + 3, sl] * i0, tot[at + 3 : at + 4, sl] * i1, fs)
    return a, b


def stat_rows(v, keep, fs):
    kept = v * keep
    return group_sums(kept, fs) + group_sums(kept * v, fs)


def back_rows(d, x, fs):
    return group_sums(d, fs) + group_sums(d * x, fs)


def loop(count, body):
    lax.fori_loop(0, count, lambda c, _: (body(c), 0)[1], 0, unroll=UNROLL)


def loop_from(first, last, body):
    for c in range(first, last):
        body(c)


def copy_all(pairs, sems):
    copies = [pltpu.make_async_copy(s, d, sems.at[k]) for k, (s, d) in enumerate(pairs)]
    for c in copies:
        c.start()
    return copies


def wait_all(copies):
    for c in copies:
        c.wait()


def at_rows(start, size):
    return pl.ds(pl.multiple_of(start, 16), size)


def flip(p):
    return (p & 1) * 8 + (p & 2) * 2 + (p & 4) // 2 + (p & 8) // 8


def setup_kernel(
    exact, crop, micro, px, w1_far, fs, isc, keep, keep1, keep_half, sh, perm, st, x, w1, flat, sems
):
    copies = copy_all([(px, x), (w1_far, w1)], sems)
    n = lax.axis_index("narrow").astype(jnp.int32)
    w = lax.axis_index("wide").astype(jnp.int32)
    isc[NARROW] = n
    isc[CORE] = w & 1
    for p in range(16):
        isc[DEST + p] = (w ^ flip(p)) if exact else jnp.int32(p)

    def count(k, sums):
        c, one = crop[k], micro[k]
        a, b = (c >> 4) * (c >> 4), (c >> 5) * (c >> 5)
        return (
            sums[0] + a * (1 - one), sums[1] + a * one, sums[2] + b * (1 - one), sums[3] + b * one,
        )

    zero = jnp.int32(0)
    sums = lax.fori_loop(0, crop.shape[0], count, (zero, zero, zero, zero))
    for k in range(4):
        fs[k] = 1.0 / sums[k].astype(F32)
    fs[INV_ALL] = 1.0 / ((sums[2] + sums[3]).astype(F32) * 2048.0)
    at = lax.broadcasted_iota(jnp.int32, (POS, 1), 0)
    i8, j7 = at & 7, at >> 3
    at = lax.broadcasted_iota(jnp.int32, (HALF, 1), 0)
    r8, c14 = n * 8 + (at & 7), at >> 3

    def inside(r, c, side):
        return jnp.where((r < side) & (c < side), 1.0, 0.0).astype(F32)

    for b in range(B):
        c = crop[w * B + b]
        side_in, side_out = c >> 4, c >> 5
        fs[CELLS + b] = 1.0 / (side_out * side_out).astype(F32)
        fs[MICRO + b] = micro[w * B + b].astype(F32)
        keep[b * POS : (b + 1) * POS, :] = inside(i8, j7, side_out)
        for k in range(4):
            keep1[k, b * POS : (b + 1) * POS, :] = inside(2 * i8 + k // 2, 2 * j7 + k % 2, side_in)
        keep_half[b * HALF : (b + 1) * HALF, :] = inside(r8, c14, side_in)
    place = lax.broadcasted_iota(jnp.int32, (POS, M), 1)
    it = lax.broadcasted_iota(jnp.int32, (POS, M), 0)
    for t in range(9):
        di, dj = t // 3 - 1, t % 3 - 1
        i, j = (it & 7) + di, (it >> 3) + dj
        fits = (i >= 0) & (i < 8) & (j >= 0) & (j < 7)
        sh[t] = low(jnp.concatenate([
            jnp.where(fits & (place == b * POS + j * 8 + i), 1.0, 0.0) for b in range(B)
        ], axis=0))
    place = lax.broadcasted_iota(jnp.int32, (POS, HALF), 1)
    it = lax.broadcasted_iota(jnp.int32, (POS, HALF), 0)
    for half in range(2):
        planes = []
        for k in range(4):
            r, c = 2 * (it & 7) + k // 2, 2 * (it >> 3) + k % 2
            planes.append(
                jnp.where(((r >> 3) == half) & (place == c * 8 + (r & 7)), 1.0, 0.0)
            )
        perm[half] = low(jnp.concatenate(planes, axis=0))
    copies[0].wait()
    for b in range(B):
        flat[b * HALF : (b + 1) * HALF, :] = x[b]
    copies[1].wait()

    def body(c):
        sl = cols(c)
        v = mm(flat[...], w1[:, sl]) * keep_half[...]
        sums = [jnp.sum(v[b * HALF : (b + 1) * HALF], axis=0, keepdims=True) for b in range(B)]
        v2 = v * v
        sq = [jnp.sum(v2[b * HALF : (b + 1) * HALF], axis=0, keepdims=True) for b in range(B)]
        put(st, 0, grouped(sums, fs) + grouped(sq, fs), sl)

    loop(2, body)


TAPS = [(p, q) for p in range(3) for q in range(3)]


def stage_two_kernel(
    fs, isc, own, other, part, part_other, perm, keep1, keep, w1, ws_far, gb, sh,
    xp, strided, x1, col, pre2, st, tot1, tmp, hid, tot, ws, sems,
):
    n = isc[NARROW]
    copies = copy_all([(ws_far.at[3 * k : 3 * k + 3], ws.at[3 * k : 3 * k + 3]) for k in range(3)], sems)
    tot[...] = part[...] + part_other[...]
    tot1[...] = tot[...]

    def permute(c):
        sl = cols(c)
        for b in range(B):
            r = mm(perm[n], own[b, :, sl]) + mm(perm[1 - n], other[b, :, sl])
            for k in range(4):
                tmp[k, b * POS : (b + 1) * POS, :] = r[k * POS : (k + 1) * POS]
        for k in range(4):
            xp[k, :, sl] = low(tmp[k] * keep1[k])
        strided[:, sl] = xp[0, :, sl]

    loop(4, permute)

    def first(c):
        k, sl = c // 2, cols(c % 2)
        v = mm(xp[k], w1[:, sl])
        mean, scale = coefs(tot, 0, sl, fs, INV_IN)
        x = (v - mean) * scale
        x1[k, :, sl] = x
        o = x * gb[0:1, sl] + gb[1:2, sl]
        hid[k, :, sl] = low(o * sigmoid(o) * keep1[k])

    loop(8, first)
    for t, (p, q) in enumerate(TAPS):
        h = hid[2 * (p != 1) + (q != 1)]
        if p == 0 or q == 0:
            h = low(mm(sh[3 * (0 if p == 0 else 1) + (0 if q == 0 else 1)], h))
        col[t] = h
    wait_all(copies)

    def second(c):
        sl = cols(c)
        v = mm(col[0], ws[0, :, sl])
        for t in range(1, 9):
            v = v + mm(col[t], ws[t, :, sl])
        pre2[:, sl] = v
        put(st, 0, stat_rows(v, keep[...], fs), sl)

    loop(2, second)


def project_kernel(fs, x, keep, wp_far, w3_far, prep, st, w3, wp, sems):
    copies = []
    for c in range(4):
        sl = slice(c * 512, (c + 1) * 512)
        copies.append(pltpu.make_async_copy(wp_far.at[:, sl], wp.at[:, sl], sems.at[c]))
    copies.append(pltpu.make_async_copy(w3_far, w3, sems.at[4]))
    for c in copies:
        c.start()

    def body(c):
        sl = cols(c)
        v = mm(x[...], wp[:, sl])
        prep[:, sl] = v
        put(st, 0, stat_rows(v, keep[...], fs), sl)

    for c in range(4):
        copies[c].wait()
        loop_from(2 * c, 2 * c + 2, body)
    copies[4].wait()


def stage_three_kernel(fs, parts, pre2, stp, keep, w3, gb, h2, pre3, st, tot2, tot):
    add_parts(parts, tot)
    tot2[...] = tot[...]
    sl = slice(0, 512)
    mean, scale = coefs(tot, 0, sl, fs, INV_OUT)
    o = (pre2[...] - mean) * scale * gb[2:3, :] + gb[3:4, :]
    h2[...] = low(o * sigmoid(o) * keep[...])
    st[4:8, :] = stp[...]

    def body(c):
        sl = cols(c)
        v = mm(h2[...], w3[:, sl])
        pre3[:, sl] = v
        put(st, 0, stat_rows(v, keep[...], fs), sl)

    loop(8, body)


def fetch_four_kernel(isc, own, r1, r2, w4, sems):
    n, core = isc[NARROW], isc[CORE]
    away = (1 - n) * 1024
    wait_all(copy_all(
        [
            (own, w4.at[at_rows(n * 1024, 1024)]),
            (r1, w4.at[at_rows(away + core * 512, 512)]),
            (r2, w4.at[at_rows(away + (1 - core) * 512, 512)]),
        ],
        sems,
    ))


def stage_four_kernel(
    fs, parts, pre3, prep, keep, vec, sqb, sq_far, ex_far, w4,
    lows, pre4, st, tot3, gate, sp, pooled, squares, unit, short, acc, tot, sq, ex, sems,
):
    copies = copy_all([(sq_far, sq), (ex_far, ex)], sems)
    add_parts(parts, tot)
    tot3[...] = tot[...]
    pooled[...] = jnp.zeros((8, 2048), F32)

    def units(c):
        sl = cols(c)
        mean, scale = coefs(tot, 0, sl, fs, INV_OUT)
        u = ((pre3[:, sl] - mean) * scale * vec[0:1, sl] + vec[1:2, sl]) * keep[...]
        unit[:, sl] = u
        for b, r in enumerate(image_sums(u)):
            pooled[b : b + 1, sl] = r * fs[CELLS + b]
        mean, scale = coefs(tot, 4, sl, fs, INV_OUT)
        s = ((prep[:, sl] - mean) * scale * vec[2:3, sl] + vec[3:4, sl]) * keep[...]
        short[:, sl] = s

    loop(8, units)
    wait_all(copies)
    sp[...] = dot3(pooled[...], sq[...]) + sqb[0:1, :]
    squeezed = sp[...] * sigmoid(sp[...])
    gate[...] = sigmoid(dot3(squeezed, ex[...]) + vec[4:5, :])
    squares[...] = jnp.zeros((8, 256), F32)
    acc[...] = jnp.zeros((M, 512), F32)

    def streams(c):
        sl = cols(c)
        branch = unit[:, sl] * expand([gate[b : b + 1, sl] for b in range(B)])
        s = short[:, sl]
        join = branch + s
        stream = join * sigmoid(join) * keep[...]
        for k, v in enumerate((stream, branch, s)):
            squares[k : k + 1, :] += jnp.sum(v * v, axis=0, keepdims=True)
        lo = low(stream)
        lows[:, sl] = lo
        acc[...] += mm(lo, w4[cols(c), :])

    loop(8, streams)
    pre4[...] = acc[...]
    put(st, 0, stat_rows(acc[...], keep[...], fs), slice(0, 512))


def fetch_five_kernel(isc, own, r1, r2, w5, sems):
    n, core = isc[NARROW], isc[CORE]
    wait_all(copy_all([
        (own, w5.at[n]),
        (r1, w5.at[1 - n, at_rows(core * 2304, 2304)]),
        (r2, w5.at[1 - n, at_rows((1 - core) * 2304, 2304)]),
    ], sems))


def stage_five_kernel(
    fs, parts, pre4, keep, gb, sh, w5, col, pre5, st, tot4, tot
):
    add_parts(parts, tot)
    tot4[...] = tot[...]
    mean, scale = coefs(tot, 0, slice(0, 512), fs, INV_OUT)
    o = (pre4[...] - mean) * scale * gb[4:5, :] + gb[5:6, :]
    h = low(o * sigmoid(o) * keep[...])
    for t in range(9):
        col[t] = h if t == 4 else low(mm(sh[t], h))
    def body(c):
        v = 0.0
        for t in range(9):
            v = v + mm(col[t], w5[c, t * 512 : (t + 1) * 512, :])
        pre5[:, cols(c)] = v
        put(st, 0, stat_rows(v, keep[...], fs), cols(c))

    loop(2, body)


def fetch_six_kernel(isc, own, r1, r2, vown, w6, gain5, vec2, vaway, sems):
    n, core = isc[NARROW], isc[CORE]
    pairs = [(r1.at[VE2:PACK_ROWS], vaway), (own, w6.at[at_rows(n * 256, 256)])]
    for r, h in ((r1, core), (r2, 1 - core)):
        for c in range(8):
            pairs.append(
                (
                    r.at[W6_AT + c * 128 : W6_AT + (c + 1) * 128],
                    w6.at[at_rows((1 - n) * 256 + h * 128, 128), c * 256 : (c + 1) * 256],
                )
            )
    copies = copy_all(pairs, sems)
    copies[0].wait()
    for side, v in ((n, f32(vown[...])), (1 - n, f32(vaway[...]))):
        for k in range(2):
            gain5[k : k + 1, cols(side)] = v[k : k + 1]
        for k in range(3):
            for c in range(4):
                at = 2 + 4 * k + c
                vec2[k : k + 1, cols(side * 4 + c)] = v[at : at + 1]
    wait_all(copies[1:])


def stage_six_kernel(
    fs, parts, pre5, keep, gain5, w6, h5, pre6, st, tot5, tot
):
    add_parts(parts, tot)
    tot5[...] = tot[...]
    mean, scale = coefs(tot, 0, slice(0, 512), fs, INV_OUT)
    o = (pre5[...] - mean) * scale * gain5[0:1, :] + gain5[1:2, :]
    h5[...] = low(o * sigmoid(o) * keep[...])

    def body(c):
        sl = cols(c)
        v = mm(h5[...], w6[:, sl])
        pre6[:, sl] = v
        put(st, 0, stat_rows(v, keep[...], fs), sl)

    loop(8, body)


def fetch_turn_kernel(isc, sqown, exown, r1, r2, ogown, ogother, sq, ex, og, sems):
    n, core = isc[NARROW], isc[CORE]
    pairs = [
        (sqown, sq.at[at_rows(n * 1024, 1024)]),
        (exown, ex.at[n]),
        (ogown, og.at[n]),
        (ogother, og.at[1 - n]),
    ]
    for r, h in ((r1, core), (r2, 1 - core)):
        for k in range(2):
            pairs.append(
                (
                    r.at[SQ_AT : SQ_AT + 256, k * 128 : (k + 1) * 128],
                    sq.at[at_rows((1 - n) * 1024 + h * 512 + k * 256, 256)],
                )
            )
        for c in range(4):
            pairs.append(
                (
                    r.at[EX_AT + c * 64 : EX_AT + (c + 1) * 64],
                    ex.at[1 - n, at_rows(h * 64, 64), c * 256 : (c + 1) * 256],
                )
            )
    wait_all(copy_all(pairs, sems))


def turn_kernel(
    fs, isc, parts, pre6, keep, lows, vec, sqb, sq1s, sq, ex, og,
    result, dj2, pay, extra, tot6, gate, dp, pooled, de, ds, squeezed, unit, res, tot, sp,
):
    n = isc[NARROW]
    add_parts(parts, tot)
    tot6[...] = tot[...]
    pooled[...] = jnp.zeros((8, 2048), F32)
    de[...] = jnp.zeros((8, 2048), F32)

    def units(c):
        sl = cols(c)
        mean, scale = coefs(tot, 0, sl, fs, INV_OUT)
        u = ((pre6[:, sl] - mean) * scale * vec[0:1, sl] + vec[1:2, sl]) * keep[...]
        unit[:, sl] = u
        for b, r in enumerate(image_sums(u)):
            pooled[b : b + 1, sl] = r * fs[CELLS + b]

    loop(8, units)
    sp[...] = dot3(pooled[...], sq[...]) + sqb[1:2, :]
    squeezed[...] = sp[...] * sigmoid(sp[...])
    for h in range(2):
        sl = slice(h * 1024, (h + 1) * 1024)
        gate[:, sl] = sigmoid(dot3(squeezed[...], ex[h]) + vec[2:3, sl])
    extra[...] = jnp.zeros((8, 512), F32)
    for k in range(3):
        extra[5 + k // 2 : 6 + k // 2, (k % 2) * 256 : (k % 2) * 256 + 256] = sq1s[k : k + 1, :]

    def streams(c):
        sl = cols(c)
        h, part = c // 4, cols(c % 4)
        u = unit[:, sl]
        branch = u * expand([gate[b : b + 1, sl] for b in range(B)])
        join = branch + f32(lows[:, sl])
        s = sigmoid(join)
        stream = join * s * keep[...]
        res[h, :, part] = low(stream)
        d = f32(og[h, :, part]) * keep[...] * (s * (1.0 + join * (1.0 - s)))
        dj2[:, sl] = d
        for b, r in enumerate(image_sums(d * u)):
            de[b : b + 1, sl] = r
        extra[6:7, 256:512] += jnp.sum(branch * branch, axis=0, keepdims=True)
        extra[7:8, 0:256] += jnp.sum(stream * stream, axis=0, keepdims=True)

    loop(8, streams)
    result[...] = res[n]
    de[...] = de[...] * gate[...] * (1.0 - gate[...])
    back = 0.0
    for h in range(2):
        back = back + dot3_nt(de[:, h * 1024 : (h + 1) * 1024], ex[h])
    ds[...] = back * slope(sp[...])
    dp[...] = dot3_nt(ds[...], sq[...])
    for b in range(B):
        dp[b : b + 1, :] = dp[b : b + 1, :] * fs[CELLS + b]
    total = jnp.sum(de[...], axis=0, keepdims=True)
    for k in range(4):
        extra[k : k + 1, :] = total[:, k * 512 : (k + 1) * 512]
    extra[4:5, 0:128] = jnp.sum(ds[...], axis=0, keepdims=True)

    def tops(c):
        sl = cols(c)
        mean, scale = coefs(tot, 0, sl, fs, INV_OUT)
        x = (pre6[:, sl] - mean) * scale
        du = (
            dj2[:, sl] * expand([gate[b : b + 1, sl] for b in range(B)])
            + expand([dp[b : b + 1, sl] for b in range(B)])
        ) * keep[...]
        put(pay, 0, back_rows(du, x, fs), sl)

    loop(8, tops)


def whole_gain(tot, at, gain, bias):
    gain[...] = (tot[at + 2 : at + 3, :] + tot[at + 3 : at + 4, :]).reshape(gain.shape)
    bias[...] = (tot[at : at + 1, :] + tot[at + 1 : at + 2, :]).reshape(bias.shape)


def half_gain(tot, n, gain, bias):
    sl = cols(n, gain.shape[0])
    gain[...] = (tot[2:3, sl] + tot[3:4, sl]).reshape(gain.shape)
    bias[...] = (tot[0:1, sl] + tot[1:2, sl]).reshape(bias.shape)


def back_six_kernel(
    fs, isc, parts, tot6, pre6, dj2, gate, dp, pre5, tot5, extra, keep, vec, gain5, w6,
    d6, do5, st, dgain, dbias, tot, acc,
):
    add_parts(parts, tot)
    half_gain(tot, isc[NARROW], dgain, dbias)
    acc[...] = jnp.zeros((M, 512), F32)

    def body(c):
        sl = cols(c)
        mean, scale = coefs(tot6, 0, sl, fs, INV_OUT)
        x = (pre6[:, sl] - mean) * scale
        du = (
            dj2[:, sl] * expand([gate[b : b + 1, sl] for b in range(B)])
            + expand([dp[b : b + 1, sl] for b in range(B)])
        ) * keep[...]
        a, bb = means(tot, 0, sl, fs, INV_OUT)
        d = low((du - a - x * bb) * (scale * vec[0:1, sl]) * keep[...])
        d6[:, sl] = d
        acc[...] += mm_nt(d, w6[:, sl])

    loop(8, body)
    mean, scale = coefs(tot5, 0, slice(0, 512), fs, INV_OUT)
    x = (pre5[...] - mean) * scale
    o = x * gain5[0:1, :] + gain5[1:2, :]
    d = acc[...] * keep[...] * slope(o)
    do5[...] = d
    put(st, 0, back_rows(d, x, fs), slice(0, 512))
    st[4:12, :] = extra[...]


def back_five_kernel(
    fs, isc, parts, tot5, pre5, do5, pre4, tot4, keep, gb, gain5, sh, w5,
    d5, do4, st, dgain, dbias, debias, dsbias, norms, tot,
):
    n = isc[NARROW]
    add_parts(parts, tot)
    half_gain(tot, n, dgain, dbias)
    excite = jnp.concatenate([tot[pl.ds(4 + 2 * n, 1), :], tot[pl.ds(5 + 2 * n, 1), :]], axis=1)
    debias[...] = excite.reshape(1024)
    dsbias[...] = tot[8:9, 0:128].reshape(128)
    for k in range(5):
        v = tot[9 + k // 2 : 10 + k // 2, (k % 2) * 256 : (k % 2) * 256 + 256]
        norms[k] = jnp.sqrt(jnp.sum(v, axis=1, keepdims=True) * fs[INV_ALL])[0, 0]
    sl = slice(0, 512)
    mean, scale = coefs(tot5, 0, sl, fs, INV_OUT)
    x = (pre5[...] - mean) * scale
    a, bb = means(tot, 0, sl, fs, INV_OUT)
    d = low((do5[...] - a - x * bb) * (scale * gain5[0:1, :]) * keep[...])
    d5[...] = d
    acc = 0.0
    for t in range(9):
        dc = d if t == 4 else low(mm(sh[8 - t], d))
        for h in range(2):
            acc = acc + mm_nt(dc[:, h * 256 : (h + 1) * 256], w5[h, t * 512 : (t + 1) * 512, :])
    mean, scale = coefs(tot4, 0, sl, fs, INV_OUT)
    x = (pre4[...] - mean) * scale
    o = x * gb[4:5, :] + gb[5:6, :]
    d = acc * keep[...] * slope(o)
    do4[...] = d
    put(st, 0, back_rows(d, x, fs), sl)


def back_four_kernel(
    fs, parts, tot4, pre4, do4, dj2, tot3, pre3, prep, gate, sp, keep, gb, vec, sq_far, ex_far, w4,
    d4, dj1, st, dgain, dbias, dp, de, ds, bias, tot, sq, ex, sems,
):
    copies = copy_all([(sq_far, sq), (ex_far, ex)], sems)
    add_parts(parts, tot)
    whole_gain(tot, 0, dgain, dbias)
    de[...] = jnp.zeros((8, 2048), F32)
    mean, scale = coefs(tot4, 0, slice(0, 512), fs, INV_OUT)
    x = (pre4[...] - mean) * scale
    a, bb = means(tot, 0, slice(0, 512), fs, INV_OUT)
    d4[...] = low((do4[...] - a - x * bb) * (scale * gb[4:5, :]) * keep[...])

    def joins(c):
        sl = cols(c)
        back = dj2[:, sl] + mm_nt(d4[...], w4[cols(c), :])
        mean, scale = coefs(tot3, 0, sl, fs, INV_OUT)
        u = ((pre3[:, sl] - mean) * scale * vec[0:1, sl] + vec[1:2, sl]) * keep[...]
        mean, scale = coefs(tot3, 4, sl, fs, INV_OUT)
        s = ((prep[:, sl] - mean) * scale * vec[2:3, sl] + vec[3:4, sl]) * keep[...]
        join = u * expand([gate[b : b + 1, sl] for b in range(B)]) + s
        d = f32(low(back)) * keep[...] * slope(join)
        dj1[:, sl] = d
        for b, r in enumerate(image_sums(d * u)):
            de[b : b + 1, sl] = r

    loop(8, joins)
    wait_all(copies)
    de[...] = de[...] * gate[...] * (1.0 - gate[...])
    ds[...] = dot3_nt(de[...], ex[...]) * slope(sp[...])
    dp[...] = dot3_nt(ds[...], sq[...])
    for b in range(B):
        dp[b : b + 1, :] = dp[b : b + 1, :] * fs[CELLS + b]
    total = jnp.sum(de[...], axis=0, keepdims=True)
    bias[...] = jnp.zeros((8, 512), F32)
    for k in range(4):
        bias[k : k + 1, :] = total[:, k * 512 : (k + 1) * 512]
    bias[4:5, 0:128] = jnp.sum(ds[...], axis=0, keepdims=True)

    def tops(c):
        sl = cols(c)
        d = dj1[:, sl]
        mean, scale = coefs(tot3, 0, sl, fs, INV_OUT)
        x = (pre3[:, sl] - mean) * scale
        du = (
            d * expand([gate[b : b + 1, sl] for b in range(B)])
            + expand([dp[b : b + 1, sl] for b in range(B)])
        ) * keep[...]
        put(st, 0, back_rows(du, x, fs), sl)
        mean, scale = coefs(tot3, 4, sl, fs, INV_OUT)
        put(st, 4, back_rows(d, (prep[:, sl] - mean) * scale, fs), sl)

    loop(8, tops)


def back_three_kernel(
    fs, parts, tot3, pre3, prep, dj1, gate, dp, bias, pre2, tot2, keep, vec, gb, w3,
    d3, dproj, do2, st, dgain, dbias, dgainp, dbiasp, tot, acc,
):
    add_parts(parts, tot)
    whole_gain(tot, 0, dgain, dbias)
    whole_gain(tot, 4, dgainp, dbiasp)
    acc[...] = jnp.zeros((M, 512), F32)

    def body(c):
        sl = cols(c)
        mean, scale = coefs(tot3, 0, sl, fs, INV_OUT)
        x = (pre3[:, sl] - mean) * scale
        dj = dj1[:, sl]
        du = (
            dj * expand([gate[b : b + 1, sl] for b in range(B)])
            + expand([dp[b : b + 1, sl] for b in range(B)])
        ) * keep[...]
        a, bb = means(tot, 0, sl, fs, INV_OUT)
        d = low((du - a - x * bb) * (scale * vec[0:1, sl]) * keep[...])
        d3[:, sl] = d
        acc[...] += mm_nt(d, w3[:, sl])
        mean, scale = coefs(tot3, 4, sl, fs, INV_OUT)
        x = (prep[:, sl] - mean) * scale
        a, bb = means(tot, 4, sl, fs, INV_OUT)
        dproj[:, sl] = low((dj - a - x * bb) * (scale * vec[2:3, sl]) * keep[...])

    loop(8, body)
    sl = slice(0, 512)
    mean, scale = coefs(tot2, 0, sl, fs, INV_OUT)
    x = (pre2[...] - mean) * scale
    o = x * gb[2:3, :] + gb[3:4, :]
    d = acc[...] * keep[...] * slope(o)
    do2[...] = d
    put(st, 0, back_rows(d, x, fs), sl)
    st[4:12, :] = bias[...]


def fetch_two_kernel(far, ws, sems):
    wait_all(copy_all([(far.at[3 * k : 3 * k + 3], ws.at[3 * k : 3 * k + 3]) for k in range(3)], sems))


def back_two_kernel(
    fs, parts, tot2, pre2, do2, x1, keep1, keep, gb, sh, ws,
    d2, do1, st, dgain, dbias, debias, dsbias, tot, dcol,
):
    add_parts(parts, tot)
    whole_gain(tot, 0, dgain, dbias)
    debias[...] = jnp.concatenate([tot[k : k + 1, :] for k in range(4, 8)], axis=1).reshape(2048)
    dsbias[...] = tot[8:9, 0:128].reshape(128)
    sl = slice(0, 512)
    mean, scale = coefs(tot2, 0, sl, fs, INV_OUT)
    x = (pre2[...] - mean) * scale
    a, bb = means(tot, 0, sl, fs, INV_OUT)
    d = low((do2[...] - a - x * bb) * (scale * gb[2:3, :]) * keep[...])
    d2[...] = d
    dcol[0] = d
    dcol[1] = low(mm(sh[5], d))
    dcol[2] = low(mm(sh[7], d))
    dcol[3] = low(mm(sh[8], d))
    terms = (
        ((0, 4),),
        ((0, 5), (1, 3)),
        ((0, 7), (2, 1)),
        ((0, 8), (1, 6), (2, 2), (3, 0)),
    )
    st[...] = jnp.zeros((4, 512), F32)
    for k in range(4):
        acc = 0.0
        for which, t in terms[k]:
            acc = acc + mm_nt(dcol[which], ws[t])
        x = x1[k]
        o = x * gb[0:1, :] + gb[1:2, :]
        d = acc * keep1[k] * slope(o)
        do1[k] = d
        rows = back_rows(d, x, fs)
        for r in range(4):
            st[r : r + 1, :] += rows[r]


def deal(isc, full, rows, keep, send, at):
    for p in range(16):
        tile = full[pl.ds(pl.multiple_of(isc[DEST + p] * rows, rows), rows), :]
        (keep if p < 8 else send)[p % 8, at_rows(at, rows), :] = tile


def back_one_kernel(
    fs, isc, parts, tot1, x1, do1, xp, keep1, gb, d1, gkeep, gsend, dgain, dbias, tot, dn, full
):
    n = isc[NARROW]
    add_parts(parts, tot)
    whole_gain(tot, 0, dgain, dbias)
    sl = slice(0, 512)
    scale = coefs(tot1, 0, sl, fs, INV_IN)[1] * gb[0:1, :]
    a, bb = means(tot, 0, sl, fs, INV_IN)
    planes = []
    for k in range(4):
        d = (do1[k] - a - x1[k] * bb) * scale * keep1[k]
        planes.append(d)
        dn[k] = low(d)
    for b in range(B):
        d1[b] = low(jnp.concatenate([d[b * POS : (b + 1) * POS] for d in planes], axis=0))

    def body(c):
        g = 0.0
        for k in range(4):
            g = g + mm_tn(xp[k, :, cols(c)], dn[k, :, cols(n)])
        full[cols(c), :] = low(g)

    loop(4, body)
    deal(isc, full, 64, gkeep, gsend, 0)


def placed_kernel(isc, dproj, wp_far, out, cc, pick_own, spread, wp, sems):
    n = isc[NARROW]
    copies = [
        pltpu.make_async_copy(wp_far.at[cut], wp.at[cut], sems.at[k])
        for k, cut in enumerate(slice(256 * k, 256 * (k + 1)) for k in range(4))
    ]
    for c in copies:
        c.start()
    for b in range(B):
        place = lax.broadcasted_iota(jnp.int32, (32, M), 1)
        it = lax.broadcasted_iota(jnp.int32, (32, M), 0)
        pick_own[b * 32 : (b + 1) * 32, :] = low(jnp.where(
            (place == b * POS + (it >> 2) * 8 + n * 4 + (it & 3)) & (it < 28), 1.0, 0.0
        ))
        place = lax.broadcasted_iota(jnp.int32, (HALF, 128), 1)
        it = lax.broadcasted_iota(jnp.int32, (HALF, 128), 0)
        spread[b * HALF : (b + 1) * HALF, :] = low(jnp.where(
            ((it & 9) == 0) & (place == b * 32 + (it >> 4) * 4 + ((it & 7) >> 1)), 1.0, 0.0
        ))
    cc[...] = low(mm(pick_own[...], dproj[...]))
    for c in range(4):
        sl = cols(c)
        copies[c].wait()
        hi, lo = split2(mm_nt(cc[...], wp[sl, :]))
        out[:, sl] = mm(spread[...], hi) + mm(spread[...], lo)


def image_kernel(isc, perm, d1, placed, keep, w1, out, dc):
    n = isc[NARROW]
    for b in range(B):
        dc[b * HALF : (b + 1) * HALF, :] = low(mm_tn(perm[n], d1[b]))
    for c in range(4):
        sl = cols(c)
        out[:, sl] = (mm_nt(dc[...], w1[sl, :]) + placed[:, sl]) * keep[...]


def grads_a_kernel(isc, h5, d6, col4, d5, gkeep, gsend, wider, full):
    n = isc[NARROW]

    def expand2(c):
        wider[:, cols(c)] = low(mm_tn(h5[:, cols(n)], d6[:, cols(c)]))

    loop(8, expand2)
    for p in range(16):
        sl = cols(isc[DEST + p], 128)
        for k in range(2):
            (gkeep if p < 8 else gsend)[p % 8, 0:128, k * 128 : (k + 1) * 128] = wider[
                k * 128 : (k + 1) * 128, sl
            ]

    def spatial(t):
        full[...] = low(mm_tn(col4[t], d5[:, cols(n)]))
        deal(isc, full, 32, gkeep, gsend, 128 + t * 32)

    loop(9, spatial)


def gate_grads(isc, n, c, at, squeezed, pooled, de, ds, gkeep, gsend, q, e):
    sl = cols(n * 4 + c)
    q[...] = outer(ds[...], pooled[:, sl])
    e[...] = outer(squeezed[...], de[:, sl])
    for p in range(16):
        rows = pl.ds(pl.multiple_of(isc[DEST + p] * 8, 8), 8)
        both = jnp.concatenate([q[rows, :], e[rows, :]], axis=0)
        (gkeep if p < 8 else gsend)[p % 8, at_rows(at + c * 16, 16), :] = low(both)


def grads_b_kernel(
    isc, d4, lows, sq2, pooled2, de2, ds2, sp1, pooled1, de1, ds1, gkeep, gsend, full, q, e, sq1
):
    n = isc[NARROW]
    sq1[...] = sp1[...] * sigmoid(sp1[...])

    def body(c):
        full[...] = low(mm_tn(d4[...], lows[:, cols(n * 4 + c)]))
        deal(isc, full, 32, gkeep, gsend, c * 32)
        gate_grads(isc, n, c, 128, sq2, pooled2, de2, ds2, gkeep, gsend, q, e)
        gate_grads(isc, n, c, 192, sq1, pooled1, de1, ds1, gkeep, gsend, q, e)

    loop(4, body)


def grads_c_kernel(isc, h2, d3, strided, dproj, gkeep, gsend, full, taller):
    n = isc[NARROW]

    def body(c):
        sl = cols(n * 4 + c)
        full[...] = low(mm_tn(h2[...], d3[:, sl]))
        deal(isc, full, 32, gkeep, gsend, c * 32)
        taller[...] = low(mm_tn(strided[...], dproj[:, sl]))
        deal(isc, taller, 64, gkeep, gsend, 128 + c * 64)

    loop(4, body)


def grads_d_kernel(isc, col1, d2, gkeep, gsend, full):
    n = isc[NARROW]

    def spatial(t):
        full[...] = low(mm_tn(col1[t], d2[:, cols(n)]))
        deal(isc, full, 32, gkeep, gsend, t * 32)

    loop(9, spatial)


def joined(v, out, at, rows):
    for c in range(4):
        out[:, c * 256 : (c + 1) * 256] = v[at + c * rows : at + (c + 1) * rows, :]


def unpack_gates(v, at, squeeze, excite):
    for c in range(4):
        part = v[at + c * 16 : at + (c + 1) * 16, :]
        squeeze[:, c * 256 : (c + 1) * 256] = part[0:8]
        excite[:, c * 256 : (c + 1) * 256] = part[8:16]


def unpack_kernel(
    a, b, c, d, expand2, spatial2, reduce2, squeeze2, excite2, squeeze1, excite1, expand1, project1
):
    v = f32(a[0]) + f32(b[0])
    expand2[0:128, :] = v[0:128, 0:128]
    expand2[128:256, :] = v[0:128, 128:256]
    spatial2[...] = v[128:416, :]
    joined(v, reduce2, 416, 32)
    unpack_gates(v, 544, squeeze2, excite2)
    unpack_gates(v, 608, squeeze1, excite1)
    v = f32(c[0]) + f32(d[0])
    joined(v, expand1, 0, 32)
    joined(v, project1, 128, 64)


def unpack_last_kernel(a, b, c, d, spatial1, reduce1):
    spatial1[...] = f32(a[0]) + f32(b[0])
    reduce1[...] = f32(c[0]) + f32(d[0])


VECTORS = (512,) * 6 + (2048,) * 5 + (128,) * 2 + (256,) * 2 + (1024,) * 3


def pack_kernel(isc, w5, w4, w6, ex, sq, *refs):
    far, refs = refs[:18], refs[18:]
    out, w5_half, w4_half, gb, vec1, sqb, vown, w6v, exv, sqv, rows = refs[:11]
    vecs, sems = refs[11:29], refs[29]
    core = isc[CORE]
    pairs = [(f, v) for f, v in zip(far, vecs)] + [
        (w6.at[at_rows(core * 128, 128)], w6v),
        (ex.at[at_rows(core * 64, 64)], exv),
        (sq.at[at_rows(core * 512, 512)], sqv),
        (w4.at[at_rows(core * 512, 512)], w4_half),
        (w5.at[at_rows(core * 2304, 2304)], w5_half),
    ]
    copies = copy_all(pairs, sems)
    wait_all(copies[:21])

    def row(v):
        return f32(v[...]).reshape(1, v.shape[0])

    for k in range(6):
        gb[k : k + 1, :] = row(vecs[k])
    for k in range(5):
        vec1[k : k + 1, :] = row(vecs[6 + k])
    for k in range(2):
        sqb[k : k + 1, :] = row(vecs[11 + k])
    rows[...] = jnp.zeros((16, 256), F32)
    at = 0
    for v in vecs[13:18]:
        r = row(v)
        for c in range(v.shape[0] // 256):
            rows[at : at + 1, :] = r[:, c * 256 : (c + 1) * 256]
            at += 1
    vown[...] = low(rows[...])
    for c in range(8):
        out[W6_AT + c * 128 : W6_AT + (c + 1) * 128, :] = w6v[:, c * 256 : (c + 1) * 256]
    for c in range(4):
        out[EX_AT + c * 64 : EX_AT + (c + 1) * 64, :] = exv[:, c * 256 : (c + 1) * 256]
    for k in range(2):
        out[SQ_AT : SQ_AT + 256, k * 128 : (k + 1) * 128] = sqv[k * 256 : (k + 1) * 256, :]
    out[VE2:PACK_ROWS, :] = vown[...]
    wait_all(copies[21:])


def call(body, outs, args, scratch=(), flops=1e8, size=5e6, name=None, vmem=LIMIT):
    specs, values = [], []
    for a in args:
        kind, v = a if isinstance(a, tuple) else (VMEM, a)
        specs.append(kind)
        values.append(v)
    return pl.pallas_call(
        body,
        out_shape=tuple(o if hasattr(o, "memory_space") else jax.ShapeDtypeStruct(o[0], o[1]) for o in outs),
        in_specs=specs,
        out_specs=tuple(o[2] if isinstance(o, tuple) and len(o) > 2 else pl.BlockSpec(memory_space=getattr(o, "memory_space", pltpu.VMEM)) for o in outs),
        scratch_shapes=list(scratch),
        compiler_params=pltpu.CompilerParams(vmem_limit_bytes=vmem * 2**20),
        cost_estimate=pl.CostEstimate(
            flops=int(flops * SCALE), bytes_accessed=int(size * SCALE), transcendentals=0
        ),
        name=name,
    )(*values)


def swap(v, axis, pairs):
    return lax.ppermute(v, axis, pairs)


def after(v, *others):
    return lax.optimization_barrier((v,) + others)[0]


def local(
    images, crop, micro,
    first_reduce, first_reduce_gain, first_reduce_bias,
    first_spatial, first_spatial_gain, first_spatial_bias,
    first_expand, first_expand_gain, first_expand_bias,
    first_project, first_project_gain, first_project_bias,
    first_squeeze, first_squeeze_bias, first_excite, first_excite_bias,
    second_reduce, second_reduce_gain, second_reduce_bias,
    second_spatial, second_spatial_gain, second_spatial_bias,
    second_expand, second_expand_gain, second_expand_bias,
    second_squeeze, second_squeeze_bias, second_excite, second_excite_bias,
    out_grad,
):
    wide = lax.axis_size("wide")
    exact = wide == 16
    near = [(i, i ^ 1) for i in range(wide)]
    pair = [(0, 1), (1, 0)]
    V = pltpu.VMEM
    D = pltpu.SemaphoreType.DMA
    out = lambda *shape: (shape, F32)
    f = lambda *shape: V(shape, F32)
    h = lambda *shape: V(shape, BF)
    far = lambda v: (ANY, pltpu.with_memory_space_constraint(v, pltpu.HBM))

    def steps(x, *first, before=None):
        results, step = [], 1
        x = after(x, *first)
        while step < wide:
            due = (before or {}).get(len(results), ())
            y = after(x, *(due(results) if callable(due) else due))
            x = x + swap(y, "wide", [(i, i ^ step) for i in range(wide)])
            results.append(x)
            step *= 2
        return x[None], results

    own_px = images.transpose(0, 2, 1, 3).reshape(B, HALF, 1024)
    other_px = swap(own_px, "narrow", pair)
    ws_far = first_spatial.reshape(9, 512, 512)

    fs_, isc_, keep, keep1, keep_half, sh, perm, st1, xown, w1 = call(
        functools.partial(setup_kernel, exact),
        [
            pltpu.SMEM((13,), F32), pltpu.SMEM((18,), jnp.int32), f(M, 1), f(4, M, 1), f(HROWS, 1), h(9, M, M), h(2, M, HALF),
            f(4, 512), h(B, HALF, 1024), h(1024, 512),
        ],
        [(SMEM, far(crop)[1]), (SMEM, far(micro)[1]), far(own_px), far(first_reduce)],
        [V((HROWS, 1024), BF), D((2,))], name="setup",
    )
    fs, isc = (SMEM, fs_), (SMEM, isc_)
    part = steps(st1)[0][0]

    w5_own = second_spatial.reshape(9 * 512, 256)
    vectors = [
        first_reduce_gain, first_reduce_bias, first_spatial_gain, first_spatial_bias,
        second_reduce_gain, second_reduce_bias, first_expand_gain, first_expand_bias,
        first_project_gain, first_project_bias, first_excite_bias,
        first_squeeze_bias, second_squeeze_bias,
        second_spatial_gain, second_spatial_bias, second_expand_gain, second_expand_bias, second_excite_bias,
    ]
    pack, w5_half, w4_half, gb, vec1, sqb, vown = call(
        pack_kernel,
        [
            ((PACK_ROWS, 256), BF), ((2304, 256), BF), ((512, 512), BF), f(8, 512), f(8, 2048), f(8, 128), h(16, 256),
        ],
        [
            (SMEM, after(isc_, st1)), far(w5_own), far(second_reduce), far(second_expand), far(second_excite),
            far(second_squeeze),
        ] + [far(v) for v in vectors],
        [V((128, 2048), BF), V((64, 1024), BF), V((512, 128), BF), V((16, 256), F32)]
        + [V((size,), BF) for size in VECTORS] + [D((24,))],
        size=2e7, name="pack",
    )
    part = after(part, gb)
    part_other = swap(part, "narrow", pair)
    w4_r1 = swap(after(w4_half, other_px, part_other), "narrow", pair)
    og_own = out_grad.transpose(0, 2, 1, 3).reshape(M, 1024)

    xp, strided, x1, col1, pre2, st2, tot1 = call(
        stage_two_kernel,
        [h(4, M, 1024), h(M, 1024), f(4, M, 512), h(9, M, 512), f(M, 512), f(4, 512), f(4, 512)],
        [fs, isc, xown, other_px, part, part_other, perm, keep1, keep, w1, far(ws_far), gb, sh],
        [
            V((4, M, 256), F32), V((4, M, 512), BF), V((4, 512), F32), V((9, 512, 512), BF), D((3,)),
        ],
        flops=4e9, size=2e7, name="stage_two",
    )
    parts2, sent2 = steps(st2, before={3: (w4_r1,)})
    w4_r2 = swap(after(w4_r1, sent2[1]), "wide", near)
    w5_r1 = swap(after(w5_half, w4_r1, sent2[1]), "narrow", pair)
    prep, stp, w3 = call(
        project_kernel, [f(M, 2048), f(4, 2048), h(512, 2048)],
        [fs, strided, keep, far(first_project), far(first_expand)],
        [V((1024, 2048), BF), D((5,))], flops=1e9, size=8e6, name="project",
    )
    h2, pre3, st3, tot2 = call(
        stage_three_kernel, [h(M, 512), f(M, 2048), f(8, 2048), f(4, 512)],
        [fs, parts2, pre2, stp, keep, w3, gb], [V((4, 512), F32)],
        flops=1e9, size=6e6, name="stage_three",
    )
    parts3, _ = steps(st3, before={3: (w4_r2,)})
    w5_r2 = swap(after(w5_r1, parts3), "wide", near)
    pk1 = swap(after(pack, w5_r1, parts3), "narrow", pair)
    w4 = call(
        fetch_four_kernel, [h(2048, 512)],
        [(SMEM, after(isc_, st3)), far(second_reduce), (ANY, w4_r1), (ANY, w4_r2)], [D((3,))],
        size=4e6, name="fetch_four",
    )[0]
    lows, pre4, st4, tot3, gate1, sp1, pooled1, squares = call(
        stage_four_kernel,
        [
            h(M, 2048), f(M, 512), f(4, 512), f(8, 2048), f(8, 2048), f(8, 128), f(8, 2048), f(8, 256),
        ],
        [fs, parts3, pre3, prep, keep, vec1, sqb, far(first_squeeze), far(first_excite), w4],
        [
            V((M, 2048), F32), V((M, 2048), F32), V((M, 512), F32), V((8, 2048), F32),
            V((2048, 128), BF), V((128, 2048), BF), D((2,)),
        ],
        flops=1e9, size=1e7, name="stage_four",
    )
    parts4, _ = steps(st4, before={3: (w5_r2,)})
    w5 = call(
        fetch_five_kernel, [h(2, 4608, 256)],
        [(SMEM, after(isc_, st4)), far(w5_own), (ANY, w5_r1), (ANY, w5_r2)], [D((3,))],
        size=8e6, name="fetch_five",
    )[0]
    col4, pre5, st5, tot4 = call(
        stage_five_kernel, [h(9, M, 512), f(M, 512), f(4, 512), f(4, 512)],
        [fs, parts4, pre4, keep, gb, sh, w5], [V((4, 512), F32)],
        flops=2e9, size=1e7, name="stage_five",
    )
    pk2 = swap(after(pk1, st5), "wide", near)
    parts5, _ = steps(st5, before={3: (pk2,)})
    og_other = swap(after(og_own, pk1, st5), "narrow", pair)
    pk1, pk2 = (ANY, pk1), (ANY, pk2)
    w6, gain5, vec2 = call(
        fetch_six_kernel, [h(512, 2048), f(2, 512), f(3, 2048)],
        [(SMEM, after(isc_, st5)), far(second_expand), pk1, pk2, vown],
        [V((16, 256), BF), D((18,))], size=4e6, name="fetch_six",
    )
    h5, pre6, st6, tot5 = call(
        stage_six_kernel, [h(M, 512), f(M, 2048), f(4, 2048), f(4, 512)],
        [fs, parts5, pre5, keep, gain5, w6], [V((4, 512), F32)],
        flops=1e9, size=6e6, name="stage_six",
    )
    parts6, _ = steps(st6)
    sq, ex, og = call(
        fetch_turn_kernel, [h(2048, 128), h(2, 128, 1024), h(2, M, 1024)],
        [
            (SMEM, after(isc_, st6)), far(second_squeeze), far(second_excite), pk1, pk2,
            far(og_own), (ANY, og_other),
        ],
        [D((16,))], size=4e6, name="fetch_turn",
    )
    result, dj2, pay6, extra6, tot6, gate2, dp2, pooled2, de2, ds2, sq2 = call(
        turn_kernel,
        [
            ((M, 1024), BF), f(M, 2048), f(4, 2048), f(8, 512), f(4, 2048), f(8, 2048),
            f(8, 2048), f(8, 2048), f(8, 2048), f(8, 128), f(8, 128),
        ],
        [fs, isc, parts6, pre6, keep, lows, vec2, sqb, squares, sq, ex, og],
        [V((M, 2048), F32), V((2, M, 1024), BF), V((4, 2048), F32), V((8, 128), F32)],
        flops=1e9, size=1e7, name="turn",
    )
    back6, _ = steps(pay6)
    d6, do5, bt5, dgain6, dbias6 = call(
        back_six_kernel, [h(M, 2048), f(M, 512), f(12, 512), out(1024), out(1024)],
        [fs, isc, back6, tot6, pre6, dj2, gate2, dp2, pre5, tot5, extra6, keep, vec2, gain5, w6],
        [V((4, 2048), F32), V((M, 512), F32)],
        flops=1e9, size=1e7, name="back_six",
    )
    back5, _ = steps(bt5)
    d5, do4, bt4, dgain5, dbias5, debias2, dsbias2, norms = call(
        back_five_kernel,
        [h(M, 512), f(M, 512), f(4, 512), out(256), out(256), out(1024), out(128), ((5,), F32, SMEM)],
        [fs, isc, back5, tot5, pre5, do5, pre4, tot4, keep, gb, gain5, sh, w5],
        [V((12, 512), F32)],
        flops=2e9, size=1e7, name="back_five",
    )

    def step(g, k, *ties):
        if not exact:
            return g, ()
        kept, sent = g
        got = swap(after(sent, *ties), "wide", [(i, i ^ (1 << k)) for i in range(wide)])
        if k == 3:
            return (kept, got), (got,)
        half = kept.shape[0] // 2
        return (kept[:half] + got[:half], kept[half:] + got[half:]), (got,)

    ga = call(
        grads_a_kernel, [h(8, 416, 256)] * 2, [isc, h5, d6, col4, d5],
        [V((256, 2048), BF), V((512, 256), BF)], flops=2e9, size=1e7, name="grads_a",
    )
    held = {}

    def core_step(name, g, tied=True):
        def due(results):
            held[name], _ = step(g, 0, *(results[:1] if tied else ()))
            return held[name] if exact else ()

        return due

    back4, sent4 = steps(bt4, *ga, before={2: core_step("a", ga)})
    ga, xa = step(held["a"], 1, sent4[1])
    d4, dj1, bt3, dgain4, dbias4, dp1, de1, ds1, bias1 = call(
        back_four_kernel,
        [
            h(M, 512), f(M, 2048), f(8, 2048), out(512), out(512), f(8, 2048),
            f(8, 2048), f(8, 128), f(8, 512),
        ],
        [
            fs, back4, tot4, pre4, do4, dj2, tot3, pre3, prep, gate1, sp1, keep, gb, vec1,
            far(first_squeeze), far(first_excite), w4,
        ],
        [V((4, 512), F32), V((2048, 128), BF), V((128, 2048), BF), D((2,))],
        flops=1e9, size=1e7, name="back_four",
    )
    gb1 = call(
        grads_b_kernel, [h(8, 256, 256)] * 2,
        [isc, d4, lows, sq2, pooled2, de2, ds2, sp1, pooled1, de1, ds1],
        [V((512, 256), BF), V((128, 256), F32), V((128, 256), F32), V((8, 128), F32)],
        flops=1e9, size=4e6, name="grads_b",
    )
    ws_back = call(
        fetch_two_kernel, [h(9, 512, 512)], [far(after(ws_far, bt4))], [D((3,))], size=9e6, name="fetch_two",
    )[0]
    back3, sent3 = steps(bt3, *gb1, *xa, ws_back, before={3: core_step("b", gb1, True)})
    gb1 = held["b"]
    gb1, xb = step(gb1, 1, sent3[3])
    ga, za = step(ga, 2, sent3[3])
    d3, dproj, do2, bt2, dgain3, dbias3, dgainp, dbiasp = call(
        back_three_kernel,
        [h(M, 2048), h(M, 2048), f(M, 512), f(12, 512), out(2048), out(2048), out(2048), out(2048)],
        [fs, back3, tot3, pre3, prep, dj1, gate1, dp1, bias1, pre2, tot2, keep, vec1, gb, w3],
        [V((8, 2048), F32), V((M, 512), F32)],
        flops=1e9, size=1e7, name="back_three",
    )
    gc = call(
        grads_c_kernel, [h(8, 384, 256)] * 2, [isc, h2, d3, strided, dproj],
        [V((512, 256), BF), V((1024, 256), BF)],
        flops=3e9, size=1e7, name="grads_c",
    )
    back2, sent2 = steps(bt2, *gc, *za, *xb, before={2: core_step("c", gc)})
    gc, xc = step(held["c"], 1, sent2[1])
    d2, do1, bt1, dgain2, dbias2, debias1, dsbias1 = call(
        back_two_kernel,
        [h(M, 512), f(4, M, 512), f(4, 512), out(512), out(512), out(2048), out(128)],
        [fs, back2, tot2, pre2, do2, x1, keep1, keep, gb, sh, ws_back],
        [V((12, 512), F32), V((4, M, 512), BF)],
        flops=2e9, size=1e7, name="back_two",
    )
    gd = call(
        grads_d_kernel, [h(8, 288, 256)] * 2, [isc, col1, d2], [V((512, 256), BF)],
        flops=2e9, size=6e6, name="grads_d",
    )
    placed = call(
        placed_kernel, [f(HROWS, 1024)], [(SMEM, after(isc_, bt2)), dproj, far(first_project)],
        [V((128, 2048), BF), V((128, M), BF), V((HROWS, 128), BF), V((1024, 2048), BF), D((4,))],
        flops=1e9, size=1e7, name="placed",
    )[0]
    back1, sent1 = steps(bt1, *gd, *xc, placed)
    gd, _ = step(gd, 0, sent1[0])
    gd0 = gd
    gd, xd = step(gd, 1, sent1[2])
    gc, _ = step(gc, 2, sent1[3])
    back1 = after(back1, *gd0)
    d1, ge_keep, ge_send, dgain1, dbias1 = call(
        back_one_kernel, [h(B, M, 512), h(8, 64, 256), h(8, 64, 256), out(512), out(512)],
        [fs, isc, back1, tot1, x1, do1, xp, keep1, gb],
        [V((4, 512), F32), V((4, M, 512), BF), V((1024, 256), BF)],
        flops=1e9, size=6e6, name="back_one",
    )
    ge = (ge_keep, ge_send)
    dimg = call(
        image_kernel, [out(HROWS, 1024)], [isc, perm, d1, placed, keep_half, w1],
        [V((HROWS, 512), BF)], flops=1e9, size=1e7, name="image",
    )[0]

    if exact:
        ge, _ = step(ge, 0)
        dimg, *gd = lax.optimization_barrier((dimg,) + gd)
        gb1, _ = step(gb1, 2)
        gab = tuple(jnp.concatenate(p, axis=1) for p in zip(ga, gb1))
        gab, _ = step(gab, 3)
        gd, _ = step(gd, 2)
        gc, _ = step(gc, 3)
        ge, _ = step(ge, 1)
        ge, _ = step(ge, 2)
        gd, _ = step(gd, 3)
        ge, _ = step(ge, 3)
        (
            expand2, spatial2, reduce2, squeeze2, excite2, squeeze1, excite1, expand1, project1,
        ) = call(
            unpack_kernel,
            [out(256, 128), out(288, 256), out(32, 1024)] + [out(8, 1024)] * 4 + [out(32, 1024), out(64, 1024)],
            list(gab + gc), name="unpack",
        )
        spatial1, reduce1 = call(
            unpack_last_kernel, [out(288, 256), out(64, 256)], list(gd + ge), name="unpack_last"
        )
    else:
        finer = wide // 16

        def summed(g):
            return lax.psum_scatter(g, "wide", scatter_dimension=0, tiled=True)

        def blocks(g, start, count, rows):
            p = g[:, start : start + count * rows].reshape(16, count, finer, rows // finer, 256)
            p = summed(p.transpose(0, 2, 1, 3, 4).reshape(wide, count, rows // finer, 256))[0]
            return f32(p).transpose(1, 0, 2).reshape(rows // finer, count * 256)

        def both(g, start):
            p = g[:, start : start + 64].reshape(16, 4, 2, finer, 8 // finer, 256)
            p = f32(summed(p.transpose(0, 3, 1, 2, 4, 5).reshape(wide, 4, 2, -1, 256))[0])
            return [p[:, k].transpose(1, 0, 2).reshape(-1, 1024) for k in range(2)]

        def taps(g, start):
            p = g[:, start : start + 288].reshape(16, 9, finer, 32 // finer, 256)
            return f32(summed(p.transpose(0, 2, 1, 3, 4).reshape(wide, 9, -1, 256))[0]).reshape(-1, 256)

        ga, gb1, gc, gd, ge = (jnp.concatenate(g) for g in (ga, gb1, gc, gd, ge))
        e2 = ga[:, 0:128].reshape(16, 128, 2, finer, 128 // finer).transpose(0, 3, 1, 2, 4)
        e2 = summed(e2.reshape(wide, 1, -1)).reshape(128, 2, -1)
        expand2 = f32(e2.transpose(1, 0, 2).reshape(256, -1))
        spatial2 = taps(ga, 128)
        reduce2 = blocks(gb1, 0, 4, 32)
        squeeze2, excite2 = both(gb1, 128)
        expand1, project1 = blocks(gc, 0, 4, 32), blocks(gc, 128, 4, 64)
        squeeze1, excite1 = both(gb1, 192)
        spatial1, reduce1 = taps(gd, 0), blocks(ge, 0, 1, 64)
    return (
        result.reshape(B, 7, 8, 1024).transpose(0, 2, 1, 3),
        dimg.reshape(B, 14, 8, 1024).transpose(0, 2, 1, 3),
        reduce1, dgain1, dbias1,
        spatial1.reshape(3, 3, -1, 256), dgain2, dbias2,
        expand1, dgain3, dbias3,
        project1, dgainp, dbiasp,
        squeeze1.T, dsbias1, excite1, debias1,
        reduce2.T, dgain4, dbias4,
        spatial2.reshape(3, 3, -1, 256), dgain5, dbias5,
        expand2, dgain6, dbias6,
        squeeze2.T, dsbias2, excite2, debias2,
        norms,
    )


def solution(mesh):
    rep, nar = P(), P("narrow")
    return jax.shard_map(
        local,
        mesh=mesh,
        in_specs=(P("wide", "narrow", None, None),) + (rep,) * 18 + (
            P("narrow", None), rep, rep,
            P(None, None, None, "narrow"), nar, nar,
            P("narrow", None), nar, nar,
            P("narrow", None), rep, P(None, "narrow"), nar,
            P("wide", None, None, "narrow"),
        ),
        out_specs=(
            P("wide", None, None, "narrow"), P("wide", "narrow", None, None),
            P("wide", "narrow"), rep, rep,
            P(None, None, "wide", "narrow"), rep, rep,
            P("wide", "narrow"), rep, rep,
            P("wide", "narrow"), rep, rep,
            P("narrow", "wide"), rep, P("wide", "narrow"), rep,
            P("narrow", "wide"), rep, rep,
            P(None, None, "wide", "narrow"), nar, nar,
            P("narrow", "wide"), nar, nar,
            P("narrow", "wide"), rep, P("wide", "narrow"), nar,
            rep,
        ),
        check_vma=False,
    )
```

```python
import functools

import numpy as np
import jax
import jax.numpy as jnp
from jax import lax
from jax.experimental import pallas as pl
from jax.experimental.pallas import tpu as pltpu
from jax.sharding import PartitionSpec as P

EPSILON = 1e-05
BF = jnp.bfloat16
F32 = jnp.float32
B = 4
POS = 56
LIMIT = 14
SCALE = 0.01
UNROLL = 2
M = B * POS
HALF = 112
HROWS = B * HALF
VMEM = pl.BlockSpec(memory_space=pltpu.VMEM)
SMEM = pl.BlockSpec(memory_space=pltpu.SMEM)
ANY = pl.BlockSpec(memory_space=pl.ANY)
INV_IN, INV_OUT, CELLS, MICRO, INV_ALL = 0, 2, 4, 8, 12
NARROW, CORE, DEST = 0, 1, 2
W6_AT, EX_AT, SQ_AT, VE2, PACK_ROWS = 0, 1024, 1280, 1536, 1552


def mm(a, b):
    return lax.dot_general(a, b, (((1,), (0,)), ((), ())), preferred_element_type=F32)


def mm_nt(a, b):
    return lax.dot_general(a, b, (((1,), (1,)), ((), ())), preferred_element_type=F32)


def mm_tn(a, b):
    return lax.dot_general(a, b, (((0,), (0,)), ((), ())), preferred_element_type=F32)


def f32(v):
    return v.astype(F32)


def low(v):
    return v.astype(BF)


def split2(v):
    a = low(v)
    return a, low(v - f32(a))


def stack3(v):
    a = f32(low(v))
    r = v - a
    b = f32(low(r))
    return low(jnp.concatenate([a, b, r - b, jnp.zeros_like(v)], axis=0))


def sum3(p):
    return p[0:8] + p[8:16] + p[16:24]


def dot3(v, w):
    return sum3(mm(stack3(v), w))


def dot3_nt(v, w):
    return sum3(mm_nt(stack3(v), w))


def outer(a, b):
    a1, b1 = f32(low(a)), f32(low(b))
    zeros = jnp.zeros_like
    left = low(jnp.concatenate([a1, a1, a - a1, zeros(a)], axis=0))
    return mm_tn(left, low(jnp.concatenate([b1, b - b1, b1, zeros(b)], axis=0)))


def sigmoid(v):
    return 1.0 / (1.0 + jnp.exp(-v))


def slope(v):
    s = sigmoid(v)
    return s * (1.0 + v * (1.0 - s))


def cols(c, size=256):
    return pl.ds(pl.multiple_of(c * size, size), size)


def expand(rows):
    return jnp.concatenate([jnp.broadcast_to(r, (POS, r.shape[1])) for r in rows], axis=0)


def pick(r0, r1, fs):
    return expand([r0 * (1.0 - fs[MICRO + b]) + r1 * fs[MICRO + b] for b in range(B)])


def image_sums(v):
    return [jnp.sum(v[b * POS : (b + 1) * POS], axis=0, keepdims=True) for b in range(B)]


def grouped(sums, fs, reps=1):
    zero = one = 0.0
    for b in range(B):
        zero = zero + sums[b] * (1.0 - fs[MICRO + b])
        one = one + sums[b] * fs[MICRO + b]
    return [zero, one]


def group_sums(v, fs):
    return grouped(image_sums(v), fs)


def put(ref, at, rows, sl):
    for k, r in enumerate(rows):
        ref[at + k : at + k + 1, sl] = r


def add_parts(parts, tot):
    t = parts[0]
    for k in range(1, parts.shape[0]):
        t = t + parts[k]
    tot[...] = t


def coefs(tot, at, sl, fs, inv):
    i0, i1 = fs[inv], fs[inv + 1]
    m0, m1 = tot[at : at + 1, sl] * i0, tot[at + 1 : at + 2, sl] * i1
    q0 = lax.rsqrt(tot[at + 2 : at + 3, sl] * i0 - m0 * m0 + EPSILON)
    q1 = lax.rsqrt(tot[at + 3 : at + 4, sl] * i1 - m1 * m1 + EPSILON)
    return pick(m0, m1, fs), pick(q0, q1, fs)


def means(tot, at, sl, fs, inv):
    i0, i1 = fs[inv], fs[inv + 1]
    a = pick(tot[at : at + 1, sl] * i0, tot[at + 1 : at + 2, sl] * i1, fs)
    b = pick(tot[at + 2 : at + 3, sl] * i0, tot[at + 3 : at + 4, sl] * i1, fs)
    return a, b


def stat_rows(v, keep, fs):
    kept = v * keep
    return group_sums(kept, fs) + group_sums(kept * v, fs)


def back_rows(d, x, fs):
    return group_sums(d, fs) + group_sums(d * x, fs)


def loop(count, body, unroll=UNROLL):
    lax.fori_loop(0, count, lambda c, _: (body(c), 0)[1], 0, unroll=unroll)


def copy_all(pairs, sems):
    copies = [pltpu.make_async_copy(s, d, sems.at[k]) for k, (s, d) in enumerate(pairs)]
    for c in copies:
        c.start()
    return copies


def wait_all(copies):
    for c in copies:
        c.wait()


def at_rows(start, size):
    return pl.ds(pl.multiple_of(start, 16), size)


def flip(p):
    return (p & 1) * 8 + (p & 2) * 2 + (p & 4) // 2 + (p & 8) // 8


def setup_kernel(
    exact, crop, micro, px, w1_far, fs, isc, keep, keep1, keep_half, sh, perm, st, x, w1, flat, sems
):
    copies = copy_all([(px, x), (w1_far, w1)], sems)
    n = lax.axis_index("narrow").astype(jnp.int32)
    w = lax.axis_index("wide").astype(jnp.int32)
    isc[NARROW] = n
    isc[CORE] = w & 1
    for p in range(16):
        isc[DEST + p] = (w ^ flip(p)) if exact else jnp.int32(p)

    def count(k, sums):
        c, one = crop[k], micro[k]
        a, b = (c >> 4) * (c >> 4), (c >> 5) * (c >> 5)
        return (
            sums[0] + a * (1 - one), sums[1] + a * one, sums[2] + b * (1 - one), sums[3] + b * one,
        )

    zero = jnp.int32(0)
    sums = lax.fori_loop(0, crop.shape[0], count, (zero, zero, zero, zero))
    for k in range(4):
        fs[k] = 1.0 / sums[k].astype(F32)
    fs[INV_ALL] = 1.0 / ((sums[2] + sums[3]).astype(F32) * 2048.0)
    at = lax.broadcasted_iota(jnp.int32, (POS, 1), 0)
    i8, j7 = at & 7, at >> 3
    at = lax.broadcasted_iota(jnp.int32, (HALF, 1), 0)
    r8, c14 = n * 8 + (at & 7), at >> 3

    def inside(r, c, side):
        return jnp.where((r < side) & (c < side), 1.0, 0.0).astype(F32)

    for b in range(B):
        c = crop[w * B + b]
        side_in, side_out = c >> 4, c >> 5
        fs[CELLS + b] = 1.0 / (side_out * side_out).astype(F32)
        fs[MICRO + b] = micro[w * B + b].astype(F32)
        keep[b * POS : (b + 1) * POS, :] = inside(i8, j7, side_out)
        for k in range(4):
            keep1[k, b * POS : (b + 1) * POS, :] = inside(2 * i8 + k // 2, 2 * j7 + k % 2, side_in)
        keep_half[b * HALF : (b + 1) * HALF, :] = inside(r8, c14, side_in)
    place = lax.broadcasted_iota(jnp.int32, (POS, M), 1)
    it = lax.broadcasted_iota(jnp.int32, (POS, M), 0)
    for t in range(9):
        di, dj = t // 3 - 1, t % 3 - 1
        i, j = (it & 7) + di, (it >> 3) + dj
        fits = (i >= 0) & (i < 8) & (j >= 0) & (j < 7)
        sh[t] = low(jnp.concatenate([
            jnp.where(fits & (place == b * POS + j * 8 + i), 1.0, 0.0) for b in range(B)
        ], axis=0))
    place = lax.broadcasted_iota(jnp.int32, (POS, HALF), 1)
    it = lax.broadcasted_iota(jnp.int32, (POS, HALF), 0)
    for half in range(2):
        planes = []
        for k in range(4):
            r, c = 2 * (it & 7) + k // 2, 2 * (it >> 3) + k % 2
            planes.append(
                jnp.where(((r >> 3) == half) & (place == c * 8 + (r & 7)), 1.0, 0.0)
            )
        perm[half] = low(jnp.concatenate(planes, axis=0))
    copies[0].wait()
    for b in range(B):
        flat[b * HALF : (b + 1) * HALF, :] = x[b]
    copies[1].wait()

    def body(c):
        sl = cols(c)
        v = mm(flat[...], w1[:, sl]) * keep_half[...]
        sums = [jnp.sum(v[b * HALF : (b + 1) * HALF], axis=0, keepdims=True) for b in range(B)]
        v2 = v * v
        sq = [jnp.sum(v2[b * HALF : (b + 1) * HALF], axis=0, keepdims=True) for b in range(B)]
        put(st, 0, grouped(sums, fs) + grouped(sq, fs), sl)

    loop(2, body)


TAPS = [(p, q) for p in range(3) for q in range(3)]


def stage_two_kernel(
    fs, isc, own, other, part, part_other, perm, keep1, keep, w1, ws_far, gb, sh,
    xp, strided, x1, col, pre2, st, tot1, tmp, hid, tot, ws, sems,
):
    n = isc[NARROW]
    copies = copy_all([(ws_far.at[3 * k : 3 * k + 3], ws.at[3 * k : 3 * k + 3]) for k in range(3)], sems)
    tot[...] = part[...] + part_other[...]
    tot1[...] = tot[...]

    def permute(c):
        sl = cols(c)
        for b in range(B):
            r = mm(perm[n], own[b, :, sl]) + mm(perm[1 - n], other[b, :, sl])
            for k in range(4):
                tmp[k, b * POS : (b + 1) * POS, :] = r[k * POS : (k + 1) * POS]
        for k in range(4):
            xp[k, :, sl] = low(tmp[k] * keep1[k])
        strided[:, sl] = xp[0, :, sl]

    loop(4, permute)

    def first(c):
        k, sl = c // 2, cols(c % 2)
        v = mm(xp[k], w1[:, sl])
        mean, scale = coefs(tot, 0, sl, fs, INV_IN)
        x = (v - mean) * scale
        x1[k, :, sl] = x
        o = x * gb[0:1, sl] + gb[1:2, sl]
        hid[k, :, sl] = low(o * sigmoid(o) * keep1[k])

    loop(8, first)
    for t, (p, q) in enumerate(TAPS):
        h = hid[2 * (p != 1) + (q != 1)]
        if p == 0 or q == 0:
            h = low(mm(sh[3 * (0 if p == 0 else 1) + (0 if q == 0 else 1)], h))
        col[t] = h
    wait_all(copies)

    def second(c):
        sl = cols(c)
        v = mm(col[0], ws[0, :, sl])
        for t in range(1, 9):
            v = v + mm(col[t], ws[t, :, sl])
        pre2[:, sl] = v
        put(st, 0, stat_rows(v, keep[...], fs), sl)

    loop(2, second)


def project_kernel(fs, x, keep, wp_far, w3_far, prep, st, w3, wp, sems):
    def part(k):
        sl = cols(k, 512)
        return pltpu.make_async_copy(wp_far.at[:, sl], wp.at[:, sl], sems.at[k])

    for k in range(4):
        part(k).start()
    w3_copy = pltpu.make_async_copy(w3_far, w3, sems.at[4])
    w3_copy.start()

    def body(c):
        sl = cols(c)
        v = mm(x[...], wp[:, sl])
        prep[:, sl] = v
        put(st, 0, stat_rows(v, keep[...], fs), sl)

    def pair(k):
        part(k).wait()
        body(2 * k)
        body(2 * k + 1)

    loop(4, pair, 1)
    w3_copy.wait()


def stage_three_kernel(fs, parts, pre2, stp, keep, w3, gb, h2, pre3, st, tot2, tot):
    add_parts(parts, tot)
    tot2[...] = tot[...]
    sl = slice(0, 512)
    mean, scale = coefs(tot, 0, sl, fs, INV_OUT)
    o = (pre2[...] - mean) * scale * gb[2:3, :] + gb[3:4, :]
    h2[...] = low(o * sigmoid(o) * keep[...])
    st[4:8, :] = stp[...]

    def body(c):
        sl = cols(c)
        v = mm(h2[...], w3[:, sl])
        pre3[:, sl] = v
        put(st, 0, stat_rows(v, keep[...], fs), sl)

    loop(8, body, 4)


def fetch_four_kernel(isc, own, r1, r2, w4, sems):
    n, core = isc[NARROW], isc[CORE]
    away = (1 - n) * 1024
    wait_all(copy_all(
        [
            (own, w4.at[at_rows(n * 1024, 1024)]),
            (r1, w4.at[at_rows(away + core * 512, 512)]),
            (r2, w4.at[at_rows(away + (1 - core) * 512, 512)]),
        ],
        sems,
    ))


def stage_four_kernel(
    fs, parts, pre3, prep, keep, vec, sqb, sq_far, ex_far, w4,
    lows, pre4, st, tot3, gate, sp, pooled, squares, unit, short, acc, tot, sq, ex, sems,
):
    copies = copy_all([(sq_far, sq), (ex_far, ex)], sems)
    add_parts(parts, tot)
    tot3[...] = tot[...]
    pooled[...] = jnp.zeros((8, 2048), F32)

    def units(c):
        sl = cols(c)
        mean, scale = coefs(tot, 0, sl, fs, INV_OUT)
        u = ((pre3[:, sl] - mean) * scale * vec[0:1, sl] + vec[1:2, sl]) * keep[...]
        unit[:, sl] = u
        for b, r in enumerate(image_sums(u)):
            pooled[b : b + 1, sl] = r * fs[CELLS + b]
        mean, scale = coefs(tot, 4, sl, fs, INV_OUT)
        s = ((prep[:, sl] - mean) * scale * vec[2:3, sl] + vec[3:4, sl]) * keep[...]
        short[:, sl] = s

    loop(8, units, 4)
    wait_all(copies)
    sp[...] = dot3(pooled[...], sq[...]) + sqb[0:1, :]
    squeezed = sp[...] * sigmoid(sp[...])
    gate[...] = sigmoid(dot3(squeezed, ex[...]) + vec[4:5, :])
    squares[...] = jnp.zeros((8, 256), F32)
    acc[...] = jnp.zeros((M, 512), F32)

    def streams(c):
        sl = cols(c)
        branch = unit[:, sl] * expand([gate[b : b + 1, sl] for b in range(B)])
        s = short[:, sl]
        join = branch + s
        stream = join * sigmoid(join) * keep[...]
        for k, v in enumerate((stream, branch, s)):
            squares[k : k + 1, :] += jnp.sum(v * v, axis=0, keepdims=True)
        lo = low(stream)
        lows[:, sl] = lo
        acc[...] += mm(lo, w4[cols(c), :])

    loop(8, streams, 4)
    pre4[...] = acc[...]
    put(st, 0, stat_rows(acc[...], keep[...], fs), slice(0, 512))


def fetch_five_kernel(isc, own, r1, r2, w5, sems):
    n, core = isc[NARROW], isc[CORE]
    wait_all(copy_all([
        (own, w5.at[n]),
        (r1, w5.at[1 - n, at_rows(core * 2304, 2304)]),
        (r2, w5.at[1 - n, at_rows((1 - core) * 2304, 2304)]),
    ], sems))


def stage_five_kernel(
    fs, parts, pre4, keep, gb, sh, w5, col, pre5, st, tot4, tot
):
    add_parts(parts, tot)
    tot4[...] = tot[...]
    mean, scale = coefs(tot, 0, slice(0, 512), fs, INV_OUT)
    o = (pre4[...] - mean) * scale * gb[4:5, :] + gb[5:6, :]
    h = low(o * sigmoid(o) * keep[...])
    for t in range(9):
        col[t] = h if t == 4 else low(mm(sh[t], h))
    def body(c):
        v = 0.0
        for t in range(9):
            v = v + mm(col[t], w5[c, t * 512 : (t + 1) * 512, :])
        pre5[:, cols(c)] = v
        put(st, 0, stat_rows(v, keep[...], fs), cols(c))

    loop(2, body)


def fetch_six_kernel(isc, own, r1, r2, vown, w6, gain5, vec2, vaway, sems):
    n, core = isc[NARROW], isc[CORE]
    pairs = [(r1.at[VE2:PACK_ROWS], vaway), (own, w6.at[at_rows(n * 256, 256)])]
    for r, h in ((r1, core), (r2, 1 - core)):
        for c in range(8):
            pairs.append(
                (
                    r.at[W6_AT + c * 128 : W6_AT + (c + 1) * 128],
                    w6.at[at_rows((1 - n) * 256 + h * 128, 128), c * 256 : (c + 1) * 256],
                )
            )
    copies = copy_all(pairs, sems)
    copies[0].wait()
    for side, v in ((n, f32(vown[...])), (1 - n, f32(vaway[...]))):
        for k in range(2):
            gain5[k : k + 1, cols(side)] = v[k : k + 1]
        for k in range(3):
            for c in range(4):
                at = 2 + 4 * k + c
                vec2[k : k + 1, cols(side * 4 + c)] = v[at : at + 1]
    wait_all(copies[1:])


def stage_six_kernel(
    fs, parts, pre5, keep, gain5, w6, h5, pre6, st, tot5, tot
):
    add_parts(parts, tot)
    tot5[...] = tot[...]
    mean, scale = coefs(tot, 0, slice(0, 512), fs, INV_OUT)
    o = (pre5[...] - mean) * scale * gain5[0:1, :] + gain5[1:2, :]
    h5[...] = low(o * sigmoid(o) * keep[...])

    def body(c):
        sl = cols(c)
        v = mm(h5[...], w6[:, sl])
        pre6[:, sl] = v
        put(st, 0, stat_rows(v, keep[...], fs), sl)

    loop(8, body)


def fetch_turn_kernel(isc, sqown, exown, r1, r2, ogown, ogother, sq, ex, og, sems):
    n, core = isc[NARROW], isc[CORE]
    pairs = [
        (sqown, sq.at[at_rows(n * 1024, 1024)]),
        (exown, ex.at[n]),
        (ogown, og.at[n]),
        (ogother, og.at[1 - n]),
    ]
    for r, h in ((r1, core), (r2, 1 - core)):
        for k in range(2):
            pairs.append(
                (
                    r.at[SQ_AT : SQ_AT + 256, k * 128 : (k + 1) * 128],
                    sq.at[at_rows((1 - n) * 1024 + h * 512 + k * 256, 256)],
                )
            )
        for c in range(4):
            pairs.append(
                (
                    r.at[EX_AT + c * 64 : EX_AT + (c + 1) * 64],
                    ex.at[1 - n, at_rows(h * 64, 64), c * 256 : (c + 1) * 256],
                )
            )
    wait_all(copy_all(pairs, sems))


def turn_kernel(
    fs, isc, parts, pre6, keep, lows, vec, sqb, sq1s, sq, ex, og,
    result, dj2, pay, extra, tot6, gate, dp, pooled, de, ds, squeezed, unit, res, tot, sp,
):
    n = isc[NARROW]
    add_parts(parts, tot)
    tot6[...] = tot[...]
    pooled[...] = jnp.zeros((8, 2048), F32)
    de[...] = jnp.zeros((8, 2048), F32)

    def units(c):
        sl = cols(c)
        mean, scale = coefs(tot, 0, sl, fs, INV_OUT)
        u = ((pre6[:, sl] - mean) * scale * vec[0:1, sl] + vec[1:2, sl]) * keep[...]
        unit[:, sl] = u
        for b, r in enumerate(image_sums(u)):
            pooled[b : b + 1, sl] = r * fs[CELLS + b]

    loop(8, units, 4)
    sp[...] = dot3(pooled[...], sq[...]) + sqb[1:2, :]
    squeezed[...] = sp[...] * sigmoid(sp[...])
    for h in range(2):
        sl = slice(h * 1024, (h + 1) * 1024)
        gate[:, sl] = sigmoid(dot3(squeezed[...], ex[h]) + vec[2:3, sl])
    extra[...] = jnp.zeros((8, 512), F32)
    for k in range(3):
        extra[5 + k // 2 : 6 + k // 2, (k % 2) * 256 : (k % 2) * 256 + 256] = sq1s[k : k + 1, :]

    def streams(c):
        sl = cols(c)
        h, part = c // 4, cols(c % 4)
        u = unit[:, sl]
        branch = u * expand([gate[b : b + 1, sl] for b in range(B)])
        join = branch + f32(lows[:, sl])
        s = sigmoid(join)
        stream = join * s * keep[...]
        res[h, :, part] = low(stream)
        d = f32(og[h, :, part]) * keep[...] * (s * (1.0 + join * (1.0 - s)))
        dj2[:, sl] = d
        for b, r in enumerate(image_sums(d * u)):
            de[b : b + 1, sl] = r
        extra[6:7, 256:512] += jnp.sum(branch * branch, axis=0, keepdims=True)
        extra[7:8, 0:256] += jnp.sum(stream * stream, axis=0, keepdims=True)

    loop(8, streams, 4)
    result[...] = res[n]
    de[...] = de[...] * gate[...] * (1.0 - gate[...])
    back = 0.0
    for h in range(2):
        back = back + dot3_nt(de[:, h * 1024 : (h + 1) * 1024], ex[h])
    ds[...] = back * slope(sp[...])
    dp[...] = dot3_nt(ds[...], sq[...])
    for b in range(B):
        dp[b : b + 1, :] = dp[b : b + 1, :] * fs[CELLS + b]
    total = jnp.sum(de[...], axis=0, keepdims=True)
    for k in range(4):
        extra[k : k + 1, :] = total[:, k * 512 : (k + 1) * 512]
    extra[4:5, 0:128] = jnp.sum(ds[...], axis=0, keepdims=True)

    def tops(c):
        sl = cols(c)
        mean, scale = coefs(tot, 0, sl, fs, INV_OUT)
        x = (pre6[:, sl] - mean) * scale
        du = (
            dj2[:, sl] * expand([gate[b : b + 1, sl] for b in range(B)])
            + expand([dp[b : b + 1, sl] for b in range(B)])
        ) * keep[...]
        put(pay, 0, back_rows(du, x, fs), sl)

    loop(8, tops, 4)


def whole_gain(tot, at, gain, bias):
    gain[...] = (tot[at + 2 : at + 3, :] + tot[at + 3 : at + 4, :]).reshape(gain.shape)
    bias[...] = (tot[at : at + 1, :] + tot[at + 1 : at + 2, :]).reshape(bias.shape)


def half_gain(tot, n, gain, bias):
    sl = cols(n, gain.shape[0])
    gain[...] = (tot[2:3, sl] + tot[3:4, sl]).reshape(gain.shape)
    bias[...] = (tot[0:1, sl] + tot[1:2, sl]).reshape(bias.shape)


def back_six_kernel(
    fs, isc, parts, tot6, pre6, dj2, gate, dp, pre5, tot5, extra, keep, vec, gain5, w6,
    d6, do5, st, dgain, dbias, tot, acc,
):
    add_parts(parts, tot)
    half_gain(tot, isc[NARROW], dgain, dbias)
    acc[...] = jnp.zeros((M, 512), F32)

    def body(c):
        sl = cols(c)
        mean, scale = coefs(tot6, 0, sl, fs, INV_OUT)
        x = (pre6[:, sl] - mean) * scale
        du = (
            dj2[:, sl] * expand([gate[b : b + 1, sl] for b in range(B)])
            + expand([dp[b : b + 1, sl] for b in range(B)])
        ) * keep[...]
        a, bb = means(tot, 0, sl, fs, INV_OUT)
        d = low((du - a - x * bb) * (scale * vec[0:1, sl]) * keep[...])
        d6[:, sl] = d
        acc[...] += mm_nt(d, w6[:, sl])

    loop(8, body, 4)
    mean, scale = coefs(tot5, 0, slice(0, 512), fs, INV_OUT)
    x = (pre5[...] - mean) * scale
    o = x * gain5[0:1, :] + gain5[1:2, :]
    d = acc[...] * keep[...] * slope(o)
    do5[...] = d
    put(st, 0, back_rows(d, x, fs), slice(0, 512))
    st[4:12, :] = extra[...]


def back_five_kernel(
    fs, isc, parts, tot5, pre5, do5, pre4, tot4, keep, gb, gain5, sh, w5,
    d5, do4, st, dgain, dbias, debias, dsbias, norms, tot,
):
    n = isc[NARROW]
    add_parts(parts, tot)
    half_gain(tot, n, dgain, dbias)
    excite = jnp.concatenate([tot[pl.ds(4 + 2 * n, 1), :], tot[pl.ds(5 + 2 * n, 1), :]], axis=1)
    debias[...] = excite.reshape(1024)
    dsbias[...] = tot[8:9, 0:128].reshape(128)
    for k in range(5):
        v = tot[9 + k // 2 : 10 + k // 2, (k % 2) * 256 : (k % 2) * 256 + 256]
        norms[k] = jnp.sqrt(jnp.sum(v, axis=1, keepdims=True) * fs[INV_ALL])[0, 0]
    sl = slice(0, 512)
    mean, scale = coefs(tot5, 0, sl, fs, INV_OUT)
    x = (pre5[...] - mean) * scale
    a, bb = means(tot, 0, sl, fs, INV_OUT)
    d = low((do5[...] - a - x * bb) * (scale * gain5[0:1, :]) * keep[...])
    d5[...] = d
    acc = 0.0
    for t in range(9):
        dc = d if t == 4 else low(mm(sh[8 - t], d))
        for h in range(2):
            acc = acc + mm_nt(dc[:, h * 256 : (h + 1) * 256], w5[h, t * 512 : (t + 1) * 512, :])
    mean, scale = coefs(tot4, 0, sl, fs, INV_OUT)
    x = (pre4[...] - mean) * scale
    o = x * gb[4:5, :] + gb[5:6, :]
    d = acc * keep[...] * slope(o)
    do4[...] = d
    put(st, 0, back_rows(d, x, fs), sl)


def back_four_kernel(
    fs, parts, tot4, pre4, do4, dj2, tot3, pre3, prep, gate, sp, keep, gb, vec, sq_far, ex_far, w4,
    d4, dj1, st, dgain, dbias, dp, de, ds, bias, tot, sq, ex, sems,
):
    copies = copy_all([(sq_far, sq), (ex_far, ex)], sems)
    add_parts(parts, tot)
    whole_gain(tot, 0, dgain, dbias)
    de[...] = jnp.zeros((8, 2048), F32)
    mean, scale = coefs(tot4, 0, slice(0, 512), fs, INV_OUT)
    x = (pre4[...] - mean) * scale
    a, bb = means(tot, 0, slice(0, 512), fs, INV_OUT)
    d4[...] = low((do4[...] - a - x * bb) * (scale * gb[4:5, :]) * keep[...])

    def joins(c):
        sl = cols(c)
        back = dj2[:, sl] + mm_nt(d4[...], w4[cols(c), :])
        mean, scale = coefs(tot3, 0, sl, fs, INV_OUT)
        u = ((pre3[:, sl] - mean) * scale * vec[0:1, sl] + vec[1:2, sl]) * keep[...]
        mean, scale = coefs(tot3, 4, sl, fs, INV_OUT)
        s = ((prep[:, sl] - mean) * scale * vec[2:3, sl] + vec[3:4, sl]) * keep[...]
        join = u * expand([gate[b : b + 1, sl] for b in range(B)]) + s
        d = f32(low(back)) * keep[...] * slope(join)
        dj1[:, sl] = d
        for b, r in enumerate(image_sums(d * u)):
            de[b : b + 1, sl] = r

    loop(8, joins)
    wait_all(copies)
    de[...] = de[...] * gate[...] * (1.0 - gate[...])
    ds[...] = dot3_nt(de[...], ex[...]) * slope(sp[...])
    dp[...] = dot3_nt(ds[...], sq[...])
    for b in range(B):
        dp[b : b + 1, :] = dp[b : b + 1, :] * fs[CELLS + b]
    total = jnp.sum(de[...], axis=0, keepdims=True)
    bias[...] = jnp.zeros((8, 512), F32)
    for k in range(4):
        bias[k : k + 1, :] = total[:, k * 512 : (k + 1) * 512]
    bias[4:5, 0:128] = jnp.sum(ds[...], axis=0, keepdims=True)

    def tops(c):
        sl = cols(c)
        d = dj1[:, sl]
        mean, scale = coefs(tot3, 0, sl, fs, INV_OUT)
        x = (pre3[:, sl] - mean) * scale
        du = (
            d * expand([gate[b : b + 1, sl] for b in range(B)])
            + expand([dp[b : b + 1, sl] for b in range(B)])
        ) * keep[...]
        put(st, 0, back_rows(du, x, fs), sl)
        mean, scale = coefs(tot3, 4, sl, fs, INV_OUT)
        put(st, 4, back_rows(d, (prep[:, sl] - mean) * scale, fs), sl)

    loop(8, tops)


def back_three_kernel(
    fs, parts, tot3, pre3, prep, dj1, gate, dp, bias, pre2, tot2, keep, vec, gb, w3,
    d3, dproj, do2, st, dgain, dbias, dgainp, dbiasp, tot, acc,
):
    add_parts(parts, tot)
    whole_gain(tot, 0, dgain, dbias)
    whole_gain(tot, 4, dgainp, dbiasp)
    acc[...] = jnp.zeros((M, 512), F32)

    def body(c):
        sl = cols(c)
        mean, scale = coefs(tot3, 0, sl, fs, INV_OUT)
        x = (pre3[:, sl] - mean) * scale
        dj = dj1[:, sl]
        du = (
            dj * expand([gate[b : b + 1, sl] for b in range(B)])
            + expand([dp[b : b + 1, sl] for b in range(B)])
        ) * keep[...]
        a, bb = means(tot, 0, sl, fs, INV_OUT)
        d = low((du - a - x * bb) * (scale * vec[0:1, sl]) * keep[...])
        d3[:, sl] = d
        acc[...] += mm_nt(d, w3[:, sl])
        mean, scale = coefs(tot3, 4, sl, fs, INV_OUT)
        x = (prep[:, sl] - mean) * scale
        a, bb = means(tot, 4, sl, fs, INV_OUT)
        dproj[:, sl] = low((dj - a - x * bb) * (scale * vec[2:3, sl]) * keep[...])

    loop(8, body)
    sl = slice(0, 512)
    mean, scale = coefs(tot2, 0, sl, fs, INV_OUT)
    x = (pre2[...] - mean) * scale
    o = x * gb[2:3, :] + gb[3:4, :]
    d = acc[...] * keep[...] * slope(o)
    do2[...] = d
    put(st, 0, back_rows(d, x, fs), sl)
    st[4:12, :] = bias[...]


def fetch_two_kernel(far, ws, sems):
    wait_all(copy_all([(far.at[3 * k : 3 * k + 3], ws.at[3 * k : 3 * k + 3]) for k in range(3)], sems))


def back_two_kernel(
    fs, parts, tot2, pre2, do2, x1, keep1, keep, gb, sh, ws,
    d2, do1, st, dgain, dbias, debias, dsbias, tot, dcol,
):
    add_parts(parts, tot)
    whole_gain(tot, 0, dgain, dbias)
    debias[...] = jnp.concatenate([tot[k : k + 1, :] for k in range(4, 8)], axis=1).reshape(2048)
    dsbias[...] = tot[8:9, 0:128].reshape(128)
    sl = slice(0, 512)
    mean, scale = coefs(tot2, 0, sl, fs, INV_OUT)
    x = (pre2[...] - mean) * scale
    a, bb = means(tot, 0, sl, fs, INV_OUT)
    d = low((do2[...] - a - x * bb) * (scale * gb[2:3, :]) * keep[...])
    d2[...] = d
    dcol[0] = d
    dcol[1] = low(mm(sh[5], d))
    dcol[2] = low(mm(sh[7], d))
    dcol[3] = low(mm(sh[8], d))
    terms = (
        ((0, 4),),
        ((0, 5), (1, 3)),
        ((0, 7), (2, 1)),
        ((0, 8), (1, 6), (2, 2), (3, 0)),
    )
    st[...] = jnp.zeros((4, 512), F32)
    for k in range(4):
        acc = 0.0
        for which, t in terms[k]:
            acc = acc + mm_nt(dcol[which], ws[t])
        x = x1[k]
        o = x * gb[0:1, :] + gb[1:2, :]
        d = acc * keep1[k] * slope(o)
        do1[k] = d
        rows = back_rows(d, x, fs)
        for r in range(4):
            st[r : r + 1, :] += rows[r]


def deal(isc, full, rows, keep, send, at):
    for p in range(16):
        tile = full[pl.ds(pl.multiple_of(isc[DEST + p] * rows, rows), rows), :]
        (keep if p < 8 else send)[p % 8, at_rows(at, rows), :] = tile


def back_one_kernel(
    fs, isc, parts, tot1, x1, do1, xp, keep1, gb, d1, gkeep, gsend, dgain, dbias, tot, dn, full
):
    n = isc[NARROW]
    add_parts(parts, tot)
    whole_gain(tot, 0, dgain, dbias)
    sl = slice(0, 512)
    scale = coefs(tot1, 0, sl, fs, INV_IN)[1] * gb[0:1, :]
    a, bb = means(tot, 0, sl, fs, INV_IN)
    planes = []
    for k in range(4):
        d = (do1[k] - a - x1[k] * bb) * scale * keep1[k]
        planes.append(d)
        dn[k] = low(d)
    for b in range(B):
        d1[b] = low(jnp.concatenate([d[b * POS : (b + 1) * POS] for d in planes], axis=0))

    def body(c):
        g = 0.0
        for k in range(4):
            g = g + mm_tn(xp[k, :, cols(c)], dn[k, :, cols(n)])
        full[cols(c), :] = low(g)

    loop(4, body, 4)
    deal(isc, full, 64, gkeep, gsend, 0)


def placed_kernel(isc, dproj, wp_far, out, cc, pick_own, spread, wp, sems):
    n = isc[NARROW]

    def part(k):
        return pltpu.make_async_copy(wp_far.at[cols(k), :], wp.at[cols(k), :], sems.at[k])

    for k in range(4):
        part(k).start()
    for b in range(B):
        place = lax.broadcasted_iota(jnp.int32, (32, M), 1)
        it = lax.broadcasted_iota(jnp.int32, (32, M), 0)
        pick_own[b * 32 : (b + 1) * 32, :] = low(jnp.where(
            (place == b * POS + (it >> 2) * 8 + n * 4 + (it & 3)) & (it < 28), 1.0, 0.0
        ))
        place = lax.broadcasted_iota(jnp.int32, (HALF, 128), 1)
        it = lax.broadcasted_iota(jnp.int32, (HALF, 128), 0)
        spread[b * HALF : (b + 1) * HALF, :] = low(jnp.where(
            ((it & 9) == 0) & (place == b * 32 + (it >> 4) * 4 + ((it & 7) >> 1)), 1.0, 0.0
        ))
    cc[...] = low(mm(pick_own[...], dproj[...]))

    def body(c):
        sl = cols(c)
        part(c).wait()
        hi, lo = split2(mm_nt(cc[...], wp[sl, :]))
        out[:, sl] = mm(spread[...], hi) + mm(spread[...], lo)

    loop(4, body, 1)


def image_kernel(isc, perm, d1, placed, keep, w1, out, dc):
    n = isc[NARROW]
    for b in range(B):
        dc[b * HALF : (b + 1) * HALF, :] = low(mm_tn(perm[n], d1[b]))
    for c in range(4):
        sl = cols(c)
        out[:, sl] = (mm_nt(dc[...], w1[sl, :]) + placed[:, sl]) * keep[...]


def grads_a_kernel(isc, h5, d6, col4, d5, gkeep, gsend, wider, full):
    n = isc[NARROW]

    def expand2(c):
        wider[:, cols(c)] = low(mm_tn(h5[:, cols(n)], d6[:, cols(c)]))

    loop(8, expand2, 4)
    for p in range(16):
        sl = cols(isc[DEST + p], 128)
        for k in range(2):
            (gkeep if p < 8 else gsend)[p % 8, 0:128, k * 128 : (k + 1) * 128] = wider[
                k * 128 : (k + 1) * 128, sl
            ]

    def spatial(t):
        full[...] = low(mm_tn(col4[t], d5[:, cols(n)]))
        deal(isc, full, 32, gkeep, gsend, 128 + t * 32)

    loop(9, spatial, 3)


def gate_grads(isc, n, c, at, squeezed, pooled, de, ds, gkeep, gsend, q, e):
    sl = cols(n * 4 + c)
    q[...] = outer(ds[...], pooled[:, sl])
    e[...] = outer(squeezed[...], de[:, sl])
    for p in range(16):
        rows = pl.ds(pl.multiple_of(isc[DEST + p] * 8, 8), 8)
        both = jnp.concatenate([q[rows, :], e[rows, :]], axis=0)
        (gkeep if p < 8 else gsend)[p % 8, at_rows(at + c * 16, 16), :] = low(both)


def grads_b_kernel(
    isc, d4, lows, sq2, pooled2, de2, ds2, sp1, pooled1, de1, ds1, gkeep, gsend, full, q, e, sq1
):
    n = isc[NARROW]
    sq1[...] = sp1[...] * sigmoid(sp1[...])

    def body(c):
        full[...] = low(mm_tn(d4[...], lows[:, cols(n * 4 + c)]))
        deal(isc, full, 32, gkeep, gsend, c * 32)
        gate_grads(isc, n, c, 128, sq2, pooled2, de2, ds2, gkeep, gsend, q, e)
        gate_grads(isc, n, c, 192, sq1, pooled1, de1, ds1, gkeep, gsend, q, e)

    loop(4, body, 4)


def grads_c_kernel(isc, h2, d3, strided, dproj, gkeep, gsend, full, taller):
    n = isc[NARROW]

    def body(c):
        sl = cols(n * 4 + c)
        full[...] = low(mm_tn(h2[...], d3[:, sl]))
        deal(isc, full, 32, gkeep, gsend, c * 32)
        taller[...] = low(mm_tn(strided[...], dproj[:, sl]))
        deal(isc, taller, 64, gkeep, gsend, 128 + c * 64)

    loop(4, body, 4)


def grads_d_kernel(isc, col1, d2, gkeep, gsend, full):
    n = isc[NARROW]

    def spatial(t):
        full[...] = low(mm_tn(col1[t], d2[:, cols(n)]))
        deal(isc, full, 32, gkeep, gsend, t * 32)

    loop(9, spatial)


def joined(v, out, at, rows):
    for c in range(4):
        out[:, c * 256 : (c + 1) * 256] = v[at + c * rows : at + (c + 1) * rows, :]


def unpack_gates(v, at, squeeze, excite):
    for c in range(4):
        part = v[at + c * 16 : at + (c + 1) * 16, :]
        squeeze[:, c * 256 : (c + 1) * 256] = part[0:8]
        excite[:, c * 256 : (c + 1) * 256] = part[8:16]


def unpack_kernel(
    a, b, c, d, expand2, spatial2, reduce2, squeeze2, excite2, squeeze1, excite1, expand1, project1
):
    v = f32(a[0]) + f32(b[0])
    expand2[0:128, :] = v[0:128, 0:128]
    expand2[128:256, :] = v[0:128, 128:256]
    spatial2[...] = v[128:416, :]
    joined(v, reduce2, 416, 32)
    unpack_gates(v, 544, squeeze2, excite2)
    unpack_gates(v, 608, squeeze1, excite1)
    v = f32(c[0]) + f32(d[0])
    joined(v, expand1, 0, 32)
    joined(v, project1, 128, 64)


def unpack_last_kernel(a, b, c, d, spatial1, reduce1):
    spatial1[...] = f32(a[0]) + f32(b[0])
    reduce1[...] = f32(c[0]) + f32(d[0])


VECTORS = (512,) * 6 + (2048,) * 5 + (128,) * 2 + (256,) * 2 + (1024,) * 3


def pack_kernel(isc, w5, w4, w6, ex, sq, *refs):
    far, refs = refs[:18], refs[18:]
    out, w5_half, w4_half, gb, vec1, sqb, vown, w6v, exv, sqv, rows = refs[:11]
    vecs, sems = refs[11:29], refs[29]
    core = isc[CORE]
    pairs = [(f, v) for f, v in zip(far, vecs)] + [
        (w6.at[at_rows(core * 128, 128)], w6v),
        (ex.at[at_rows(core * 64, 64)], exv),
        (sq.at[at_rows(core * 512, 512)], sqv),
        (w4.at[at_rows(core * 512, 512)], w4_half),
        (w5.at[at_rows(core * 2304, 2304)], w5_half),
    ]
    copies = copy_all(pairs, sems)
    wait_all(copies[:21])

    def row(v):
        return f32(v[...]).reshape(1, v.shape[0])

    for k in range(6):
        gb[k : k + 1, :] = row(vecs[k])
    for k in range(5):
        vec1[k : k + 1, :] = row(vecs[6 + k])
    for k in range(2):
        sqb[k : k + 1, :] = row(vecs[11 + k])
    rows[...] = jnp.zeros((16, 256), F32)
    at = 0
    for v in vecs[13:18]:
        r = row(v)
        for c in range(v.shape[0] // 256):
            rows[at : at + 1, :] = r[:, c * 256 : (c + 1) * 256]
            at += 1
    vown[...] = low(rows[...])
    for c in range(8):
        out[W6_AT + c * 128 : W6_AT + (c + 1) * 128, :] = w6v[:, c * 256 : (c + 1) * 256]
    for c in range(4):
        out[EX_AT + c * 64 : EX_AT + (c + 1) * 64, :] = exv[:, c * 256 : (c + 1) * 256]
    for k in range(2):
        out[SQ_AT : SQ_AT + 256, k * 128 : (k + 1) * 128] = sqv[k * 256 : (k + 1) * 256, :]
    out[VE2:PACK_ROWS, :] = vown[...]
    wait_all(copies[21:])


def call(body, outs, args, scratch=(), flops=1e8, size=5e6, name=None, vmem=LIMIT):
    specs, values = [], []
    for a in args:
        kind, v = a if isinstance(a, tuple) else (VMEM, a)
        specs.append(kind)
        values.append(v)
    return pl.pallas_call(
        body,
        out_shape=tuple(o if hasattr(o, "memory_space") else jax.ShapeDtypeStruct(o[0], o[1]) for o in outs),
        in_specs=specs,
        out_specs=tuple(o[2] if isinstance(o, tuple) and len(o) > 2 else pl.BlockSpec(memory_space=getattr(o, "memory_space", pltpu.VMEM)) for o in outs),
        scratch_shapes=list(scratch),
        compiler_params=pltpu.CompilerParams(vmem_limit_bytes=vmem * 2**20),
        cost_estimate=pl.CostEstimate(
            flops=int(flops * SCALE), bytes_accessed=int(size * SCALE), transcendentals=0
        ),
        name=name,
    )(*values)


def swap(v, axis, pairs):
    return lax.ppermute(v, axis, pairs)


def after(v, *others):
    return lax.optimization_barrier((v,) + others)[0]


def local(
    images, crop, micro,
    first_reduce, first_reduce_gain, first_reduce_bias,
    first_spatial, first_spatial_gain, first_spatial_bias,
    first_expand, first_expand_gain, first_expand_bias,
    first_project, first_project_gain, first_project_bias,
    first_squeeze, first_squeeze_bias, first_excite, first_excite_bias,
    second_reduce, second_reduce_gain, second_reduce_bias,
    second_spatial, second_spatial_gain, second_spatial_bias,
    second_expand, second_expand_gain, second_expand_bias,
    second_squeeze, second_squeeze_bias, second_excite, second_excite_bias,
    out_grad,
):
    wide = lax.axis_size("wide")
    exact = wide == 16
    near = [(i, i ^ 1) for i in range(wide)]
    pair = [(0, 1), (1, 0)]
    V = pltpu.VMEM
    D = pltpu.SemaphoreType.DMA
    out = lambda *shape: (shape, F32)
    f = lambda *shape: V(shape, F32)
    h = lambda *shape: V(shape, BF)
    far = lambda v: (ANY, pltpu.with_memory_space_constraint(v, pltpu.HBM))

    def steps(x, *first, before=None):
        results, step = [], 1
        x = after(x, *first)
        while step < wide:
            due = (before or {}).get(len(results), ())
            y = after(x, *(due(results) if callable(due) else due))
            x = x + swap(y, "wide", [(i, i ^ step) for i in range(wide)])
            results.append(x)
            step *= 2
        return x[None], results

    own_px = images.transpose(0, 2, 1, 3).reshape(B, HALF, 1024)
    other_px = swap(own_px, "narrow", pair)
    ws_far = first_spatial.reshape(9, 512, 512)

    fs_, isc_, keep, keep1, keep_half, sh, perm, st1, xown, w1 = call(
        functools.partial(setup_kernel, exact),
        [
            pltpu.SMEM((13,), F32), pltpu.SMEM((18,), jnp.int32), f(M, 1), f(4, M, 1), f(HROWS, 1), h(9, M, M), h(2, M, HALF),
            f(4, 512), h(B, HALF, 1024), h(1024, 512),
        ],
        [(SMEM, far(crop)[1]), (SMEM, far(micro)[1]), far(own_px), far(first_reduce)],
        [V((HROWS, 1024), BF), D((2,))], name="setup",
    )
    fs, isc = (SMEM, fs_), (SMEM, isc_)
    part = steps(st1)[0][0]

    w5_own = second_spatial.reshape(9 * 512, 256)
    vectors = [
        first_reduce_gain, first_reduce_bias, first_spatial_gain, first_spatial_bias,
        second_reduce_gain, second_reduce_bias, first_expand_gain, first_expand_bias,
        first_project_gain, first_project_bias, first_excite_bias,
        first_squeeze_bias, second_squeeze_bias,
        second_spatial_gain, second_spatial_bias, second_expand_gain, second_expand_bias, second_excite_bias,
    ]
    pack, w5_half, w4_half, gb, vec1, sqb, vown = call(
        pack_kernel,
        [
            ((PACK_ROWS, 256), BF), ((2304, 256), BF), ((512, 512), BF), f(8, 512), f(8, 2048), f(8, 128), h(16, 256),
        ],
        [
            (SMEM, after(isc_, st1)), far(w5_own), far(second_reduce), far(second_expand), far(second_excite),
            far(second_squeeze),
        ] + [far(v) for v in vectors],
        [V((128, 2048), BF), V((64, 1024), BF), V((512, 128), BF), V((16, 256), F32)]
        + [V((size,), BF) for size in VECTORS] + [D((24,))],
        size=2e7, name="pack",
    )
    part = after(part, gb)
    part_other = swap(part, "narrow", pair)
    w4_r1 = swap(after(w4_half, other_px, part_other), "narrow", pair)
    og_own = out_grad.transpose(0, 2, 1, 3).reshape(M, 1024)

    xp, strided, x1, col1, pre2, st2, tot1 = call(
        stage_two_kernel,
        [h(4, M, 1024), h(M, 1024), f(4, M, 512), h(9, M, 512), f(M, 512), f(4, 512), f(4, 512)],
        [fs, isc, xown, other_px, part, part_other, perm, keep1, keep, w1, far(ws_far), gb, sh],
        [
            V((4, M, 256), F32), V((4, M, 512), BF), V((4, 512), F32), V((9, 512, 512), BF), D((3,)),
        ],
        flops=4e9, size=2e7, name="stage_two",
    )
    parts2, sent2 = steps(st2, before={3: (w4_r1,)})
    w4_r2 = swap(after(w4_r1, sent2[1]), "wide", near)
    w5_r1 = swap(after(w5_half, w4_r1, sent2[1]), "narrow", pair)
    prep, stp, w3 = call(
        project_kernel, [f(M, 2048), f(4, 2048), h(512, 2048)],
        [fs, strided, keep, far(first_project), far(first_expand)],
        [V((1024, 2048), BF), D((5,))], flops=1e9, size=8e6, name="project",
    )
    h2, pre3, st3, tot2 = call(
        stage_three_kernel, [h(M, 512), f(M, 2048), f(8, 2048), f(4, 512)],
        [fs, parts2, pre2, stp, keep, w3, gb], [V((4, 512), F32)],
        flops=1e9, size=6e6, name="stage_three",
    )
    parts3, _ = steps(st3, before={3: (w4_r2,)})
    w5_r2 = swap(after(w5_r1, parts3), "wide", near)
    pk1 = swap(after(pack, w5_r1, parts3), "narrow", pair)
    w4 = call(
        fetch_four_kernel, [h(2048, 512)],
        [(SMEM, after(isc_, st3)), far(second_reduce), (ANY, w4_r1), (ANY, w4_r2)], [D((3,))],
        size=4e6, name="fetch_four",
    )[0]
    lows, pre4, st4, tot3, gate1, sp1, pooled1, squares = call(
        stage_four_kernel,
        [
            h(M, 2048), f(M, 512), f(4, 512), f(8, 2048), f(8, 2048), f(8, 128), f(8, 2048), f(8, 256),
        ],
        [fs, parts3, pre3, prep, keep, vec1, sqb, far(first_squeeze), far(first_excite), w4],
        [
            V((M, 2048), F32), V((M, 2048), F32), V((M, 512), F32), V((8, 2048), F32),
            V((2048, 128), BF), V((128, 2048), BF), D((2,)),
        ],
        flops=1e9, size=1e7, name="stage_four",
    )
    parts4, _ = steps(st4, before={3: (w5_r2,)})
    w5 = call(
        fetch_five_kernel, [h(2, 4608, 256)],
        [(SMEM, after(isc_, st4)), far(w5_own), (ANY, w5_r1), (ANY, w5_r2)], [D((3,))],
        size=8e6, name="fetch_five",
    )[0]
    col4, pre5, st5, tot4 = call(
        stage_five_kernel, [h(9, M, 512), f(M, 512), f(4, 512), f(4, 512)],
        [fs, parts4, pre4, keep, gb, sh, w5], [V((4, 512), F32)],
        flops=2e9, size=1e7, name="stage_five",
    )
    pk2 = swap(after(pk1, st5), "wide", near)
    parts5, _ = steps(st5, before={3: (pk2,)})
    og_other = swap(after(og_own, pk1, st5), "narrow", pair)
    pk1, pk2 = (ANY, pk1), (ANY, pk2)
    w6, gain5, vec2 = call(
        fetch_six_kernel, [h(512, 2048), f(2, 512), f(3, 2048)],
        [(SMEM, after(isc_, st5)), far(second_expand), pk1, pk2, vown],
        [V((16, 256), BF), D((18,))], size=4e6, name="fetch_six",
    )
    h5, pre6, st6, tot5 = call(
        stage_six_kernel, [h(M, 512), f(M, 2048), f(4, 2048), f(4, 512)],
        [fs, parts5, pre5, keep, gain5, w6], [V((4, 512), F32)],
        flops=1e9, size=6e6, name="stage_six",
    )
    parts6, _ = steps(st6)
    sq, ex, og = call(
        fetch_turn_kernel, [h(2048, 128), h(2, 128, 1024), h(2, M, 1024)],
        [
            (SMEM, after(isc_, st6)), far(second_squeeze), far(second_excite), pk1, pk2,
            far(og_own), (ANY, og_other),
        ],
        [D((16,))], size=4e6, name="fetch_turn",
    )
    result, dj2, pay6, extra6, tot6, gate2, dp2, pooled2, de2, ds2, sq2 = call(
        turn_kernel,
        [
            ((M, 1024), BF), f(M, 2048), f(4, 2048), f(8, 512), f(4, 2048), f(8, 2048),
            f(8, 2048), f(8, 2048), f(8, 2048), f(8, 128), f(8, 128),
        ],
        [fs, isc, parts6, pre6, keep, lows, vec2, sqb, squares, sq, ex, og],
        [V((M, 2048), F32), V((2, M, 1024), BF), V((4, 2048), F32), V((8, 128), F32)],
        flops=1e9, size=1e7, name="turn",
    )
    back6, _ = steps(pay6)
    d6, do5, bt5, dgain6, dbias6 = call(
        back_six_kernel, [h(M, 2048), f(M, 512), f(12, 512), out(1024), out(1024)],
        [fs, isc, back6, tot6, pre6, dj2, gate2, dp2, pre5, tot5, extra6, keep, vec2, gain5, w6],
        [V((4, 2048), F32), V((M, 512), F32)],
        flops=1e9, size=1e7, name="back_six",
    )
    back5, _ = steps(bt5)
    d5, do4, bt4, dgain5, dbias5, debias2, dsbias2, norms = call(
        back_five_kernel,
        [h(M, 512), f(M, 512), f(4, 512), out(256), out(256), out(1024), out(128), ((5,), F32, SMEM)],
        [fs, isc, back5, tot5, pre5, do5, pre4, tot4, keep, gb, gain5, sh, w5],
        [V((12, 512), F32)],
        flops=2e9, size=1e7, name="back_five",
    )

    def step(g, k, *ties):
        if not exact:
            return g, ()
        kept, sent = g
        got = swap(after(sent, *ties), "wide", [(i, i ^ (1 << k)) for i in range(wide)])
        if k == 3:
            return (kept, got), (got,)
        half = kept.shape[0] // 2
        return (kept[:half] + got[:half], kept[half:] + got[half:]), (got,)

    ga = call(
        grads_a_kernel, [h(8, 416, 256)] * 2, [isc, h5, d6, col4, d5],
        [V((256, 2048), BF), V((512, 256), BF)], flops=2e9, size=1e7, name="grads_a",
    )
    held = {}

    def core_step(name, g, tied=True):
        def due(results):
            held[name], _ = step(g, 0, *(results[:1] if tied else ()))
            return held[name] if exact else ()

        return due

    back4, sent4 = steps(bt4, *ga, before={2: core_step("a", ga)})
    ga, xa = step(held["a"], 1, sent4[1])
    d4, dj1, bt3, dgain4, dbias4, dp1, de1, ds1, bias1 = call(
        back_four_kernel,
        [
            h(M, 512), f(M, 2048), f(8, 2048), out(512), out(512), f(8, 2048),
            f(8, 2048), f(8, 128), f(8, 512),
        ],
        [
            fs, back4, tot4, pre4, do4, dj2, tot3, pre3, prep, gate1, sp1, keep, gb, vec1,
            far(first_squeeze), far(first_excite), w4,
        ],
        [V((4, 512), F32), V((2048, 128), BF), V((128, 2048), BF), D((2,))],
        flops=1e9, size=1e7, name="back_four",
    )
    gb1 = call(
        grads_b_kernel, [h(8, 256, 256)] * 2,
        [isc, d4, lows, sq2, pooled2, de2, ds2, sp1, pooled1, de1, ds1],
        [V((512, 256), BF), V((128, 256), F32), V((128, 256), F32), V((8, 128), F32)],
        flops=1e9, size=4e6, name="grads_b",
    )
    ws_back = call(
        fetch_two_kernel, [h(9, 512, 512)], [far(after(ws_far, bt4))], [D((3,))], size=9e6, name="fetch_two",
    )[0]
    back3, sent3 = steps(bt3, *gb1, *xa, ws_back, before={3: core_step("b", gb1, True)})
    gb1 = held["b"]
    gb1, xb = step(gb1, 1, sent3[3])
    ga, za = step(ga, 2, sent3[3])
    d3, dproj, do2, bt2, dgain3, dbias3, dgainp, dbiasp = call(
        back_three_kernel,
        [h(M, 2048), h(M, 2048), f(M, 512), f(12, 512), out(2048), out(2048), out(2048), out(2048)],
        [fs, back3, tot3, pre3, prep, dj1, gate1, dp1, bias1, pre2, tot2, keep, vec1, gb, w3],
        [V((8, 2048), F32), V((M, 512), F32)],
        flops=1e9, size=1e7, name="back_three",
    )
    gc = call(
        grads_c_kernel, [h(8, 384, 256)] * 2, [isc, h2, d3, strided, dproj],
        [V((512, 256), BF), V((1024, 256), BF)],
        flops=3e9, size=1e7, name="grads_c",
    )
    back2, sent2 = steps(bt2, *gc, *za, *xb, before={2: core_step("c", gc)})
    gc, xc = step(held["c"], 1, sent2[1])
    d2, do1, bt1, dgain2, dbias2, debias1, dsbias1 = call(
        back_two_kernel,
        [h(M, 512), f(4, M, 512), f(4, 512), out(512), out(512), out(2048), out(128)],
        [fs, back2, tot2, pre2, do2, x1, keep1, keep, gb, sh, ws_back],
        [V((12, 512), F32), V((4, M, 512), BF)],
        flops=2e9, size=1e7, name="back_two",
    )
    gd = call(
        grads_d_kernel, [h(8, 288, 256)] * 2, [isc, col1, d2], [V((512, 256), BF)],
        flops=2e9, size=6e6, name="grads_d",
    )
    placed = call(
        placed_kernel, [f(HROWS, 1024)], [(SMEM, after(isc_, bt2)), dproj, far(first_project)],
        [V((128, 2048), BF), V((128, M), BF), V((HROWS, 128), BF), V((1024, 2048), BF), D((4,))],
        flops=1e9, size=1e7, name="placed",
    )[0]
    back1, sent1 = steps(bt1, *gd, *xc, placed)
    gd, _ = step(gd, 0, sent1[0])
    gd0 = gd
    gd, xd = step(gd, 1, sent1[2])
    gc, _ = step(gc, 2, sent1[3])
    back1 = after(back1, *gd0)
    d1, ge_keep, ge_send, dgain1, dbias1 = call(
        back_one_kernel, [h(B, M, 512), h(8, 64, 256), h(8, 64, 256), out(512), out(512)],
        [fs, isc, back1, tot1, x1, do1, xp, keep1, gb],
        [V((4, 512), F32), V((4, M, 512), BF), V((1024, 256), BF)],
        flops=1e9, size=6e6, name="back_one",
    )
    ge = (ge_keep, ge_send)
    dimg = call(
        image_kernel, [out(HROWS, 1024)], [isc, perm, d1, placed, keep_half, w1],
        [V((HROWS, 512), BF)], flops=1e9, size=1e7, name="image",
    )[0]

    if exact:
        ge, _ = step(ge, 0)
        dimg, *gd = lax.optimization_barrier((dimg,) + gd)
        gb1, _ = step(gb1, 2)
        gab = tuple(jnp.concatenate(p, axis=1) for p in zip(ga, gb1))
        gab, _ = step(gab, 3)
        gd, _ = step(gd, 2)
        gc, _ = step(gc, 3)
        ge, _ = step(ge, 1)
        ge, _ = step(ge, 2)
        gd, _ = step(gd, 3)
        ge, _ = step(ge, 3)
        (
            expand2, spatial2, reduce2, squeeze2, excite2, squeeze1, excite1, expand1, project1,
        ) = call(
            unpack_kernel,
            [out(256, 128), out(288, 256), out(32, 1024)] + [out(8, 1024)] * 4 + [out(32, 1024), out(64, 1024)],
            list(gab + gc), name="unpack",
        )
        spatial1, reduce1 = call(
            unpack_last_kernel, [out(288, 256), out(64, 256)], list(gd + ge), name="unpack_last"
        )
    else:
        finer = wide // 16

        def summed(g):
            return lax.psum_scatter(g, "wide", scatter_dimension=0, tiled=True)

        def blocks(g, start, count, rows):
            p = g[:, start : start + count * rows].reshape(16, count, finer, rows // finer, 256)
            p = summed(p.transpose(0, 2, 1, 3, 4).reshape(wide, count, rows // finer, 256))[0]
            return f32(p).transpose(1, 0, 2).reshape(rows // finer, count * 256)

        def both(g, start):
            p = g[:, start : start + 64].reshape(16, 4, 2, finer, 8 // finer, 256)
            p = f32(summed(p.transpose(0, 3, 1, 2, 4, 5).reshape(wide, 4, 2, -1, 256))[0])
            return [p[:, k].transpose(1, 0, 2).reshape(-1, 1024) for k in range(2)]

        def taps(g, start):
            p = g[:, start : start + 288].reshape(16, 9, finer, 32 // finer, 256)
            return f32(summed(p.transpose(0, 2, 1, 3, 4).reshape(wide, 9, -1, 256))[0]).reshape(-1, 256)

        ga, gb1, gc, gd, ge = (jnp.concatenate(g) for g in (ga, gb1, gc, gd, ge))
        e2 = ga[:, 0:128].reshape(16, 128, 2, finer, 128 // finer).transpose(0, 3, 1, 2, 4)
        e2 = summed(e2.reshape(wide, 1, -1)).reshape(128, 2, -1)
        expand2 = f32(e2.transpose(1, 0, 2).reshape(256, -1))
        spatial2 = taps(ga, 128)
        reduce2 = blocks(gb1, 0, 4, 32)
        squeeze2, excite2 = both(gb1, 128)
        expand1, project1 = blocks(gc, 0, 4, 32), blocks(gc, 128, 4, 64)
        squeeze1, excite1 = both(gb1, 192)
        spatial1, reduce1 = taps(gd, 0), blocks(ge, 0, 1, 64)
    return (
        result.reshape(B, 7, 8, 1024).transpose(0, 2, 1, 3),
        dimg.reshape(B, 14, 8, 1024).transpose(0, 2, 1, 3),
        reduce1, dgain1, dbias1,
        spatial1.reshape(3, 3, -1, 256), dgain2, dbias2,
        expand1, dgain3, dbias3,
        project1, dgainp, dbiasp,
        squeeze1.T, dsbias1, excite1, debias1,
        reduce2.T, dgain4, dbias4,
        spatial2.reshape(3, 3, -1, 256), dgain5, dbias5,
        expand2, dgain6, dbias6,
        squeeze2.T, dsbias2, excite2, debias2,
        norms,
    )


def solution(mesh):
    rep, nar = P(), P("narrow")
    return jax.shard_map(
        local,
        mesh=mesh,
        in_specs=(P("wide", "narrow", None, None),) + (rep,) * 18 + (
            P("narrow", None), rep, rep,
            P(None, None, None, "narrow"), nar, nar,
            P("narrow", None), nar, nar,
            P("narrow", None), rep, P(None, "narrow"), nar,
            P("wide", None, None, "narrow"),
        ),
        out_specs=(
            P("wide", None, None, "narrow"), P("wide", "narrow", None, None),
            P("wide", "narrow"), rep, rep,
            P(None, None, "wide", "narrow"), rep, rep,
            P("wide", "narrow"), rep, rep,
            P("wide", "narrow"), rep, rep,
            P("narrow", "wide"), rep, P("wide", "narrow"), rep,
            P("narrow", "wide"), rep, rep,
            P(None, None, "wide", "narrow"), nar, nar,
            P("narrow", "wide"), nar, nar,
            P("narrow", "wide"), rep, P("wide", "narrow"), nar,
            rep,
        ),
        check_vma=False,
    )
```

```python
import functools

import numpy as np
import jax
import jax.numpy as jnp
from jax import lax
from jax.experimental import pallas as pl
from jax.experimental.pallas import tpu as pltpu
from jax.sharding import PartitionSpec as P

EPSILON = 1e-05
BF = jnp.bfloat16
F32 = jnp.float32
B = 4
POS = 56
LIMIT = 14
SCALE = 0.01
UNROLL = 2
M = B * POS
HALF = 112
HROWS = B * HALF
VMEM = pl.BlockSpec(memory_space=pltpu.VMEM)
SMEM = pl.BlockSpec(memory_space=pltpu.SMEM)
ANY = pl.BlockSpec(memory_space=pl.ANY)
INV_IN, INV_OUT, CELLS, MICRO, INV_ALL = 0, 2, 4, 8, 12
NARROW, CORE, DEST = 0, 1, 2
W6_AT, EX_AT, SQ_AT, VE2, PACK_ROWS = 0, 1024, 1280, 1536, 1552


def mm(a, b):
    return lax.dot_general(a, b, (((1,), (0,)), ((), ())), preferred_element_type=F32)


def mm_nt(a, b):
    return lax.dot_general(a, b, (((1,), (1,)), ((), ())), preferred_element_type=F32)


def mm_tn(a, b):
    return lax.dot_general(a, b, (((0,), (0,)), ((), ())), preferred_element_type=F32)


def f32(v):
    return v.astype(F32)


def low(v):
    return v.astype(BF)


def split2(v):
    a = low(v)
    return a, low(v - f32(a))


def stack3(v):
    a = f32(low(v))
    r = v - a
    b = f32(low(r))
    return low(jnp.concatenate([a, b, r - b, jnp.zeros_like(v)], axis=0))


def sum3(p):
    return p[0:8] + p[8:16] + p[16:24]


def dot3(v, w):
    return sum3(mm(stack3(v), w))


def dot3_nt(v, w):
    return sum3(mm_nt(stack3(v), w))


def outer(a, b):
    a1, b1 = f32(low(a)), f32(low(b))
    zeros = jnp.zeros_like
    left = low(jnp.concatenate([a1, a1, a - a1, zeros(a)], axis=0))
    return mm_tn(left, low(jnp.concatenate([b1, b - b1, b1, zeros(b)], axis=0)))


def sigmoid(v):
    return 1.0 / (1.0 + jnp.exp(-v))


def slope(v):
    s = sigmoid(v)
    return s * (1.0 + v * (1.0 - s))


def cols(c, size=256):
    return pl.ds(pl.multiple_of(c * size, size), size)


def expand(rows):
    return jnp.concatenate([jnp.broadcast_to(r, (POS, r.shape[1])) for r in rows], axis=0)


def pick(r0, r1, fs):
    return expand([r0 * (1.0 - fs[MICRO + b]) + r1 * fs[MICRO + b] for b in range(B)])


def image_sums(v):
    return [jnp.sum(v[b * POS : (b + 1) * POS], axis=0, keepdims=True) for b in range(B)]


def grouped(sums, fs, reps=1):
    zero = one = 0.0
    for b in range(B):
        zero = zero + sums[b] * (1.0 - fs[MICRO + b])
        one = one + sums[b] * fs[MICRO + b]
    return [zero, one]


def group_sums(v, fs):
    return grouped(image_sums(v), fs)


def put(ref, at, rows, sl):
    for k, r in enumerate(rows):
        ref[at + k : at + k + 1, sl] = r


def add_parts(parts, tot):
    t = parts[0]
    for k in range(1, parts.shape[0]):
        t = t + parts[k]
    tot[...] = t


def coefs(tot, at, sl, fs, inv):
    i0, i1 = fs[inv], fs[inv + 1]
    m0, m1 = tot[at : at + 1, sl] * i0, tot[at + 1 : at + 2, sl] * i1
    q0 = lax.rsqrt(tot[at + 2 : at + 3, sl] * i0 - m0 * m0 + EPSILON)
    q1 = lax.rsqrt(tot[at + 3 : at + 4, sl] * i1 - m1 * m1 + EPSILON)
    return pick(m0, m1, fs), pick(q0, q1, fs)


def means(tot, at, sl, fs, inv):
    i0, i1 = fs[inv], fs[inv + 1]
    a = pick(tot[at : at + 1, sl] * i0, tot[at + 1 : at + 2, sl] * i1, fs)
    b = pick(tot[at + 2 : at + 3, sl] * i0, tot[at + 3 : at + 4, sl] * i1, fs)
    return a, b


def stat_rows(v, keep, fs):
    kept = v * keep
    return group_sums(kept, fs) + group_sums(kept * v, fs)


def back_rows(d, x, fs):
    return group_sums(d, fs) + group_sums(d * x, fs)


def loop(count, body, unroll=UNROLL):
    lax.fori_loop(0, count, lambda c, _: (body(c), 0)[1], 0, unroll=unroll)


def copy_all(pairs, sems):
    copies = [pltpu.make_async_copy(s, d, sems.at[k]) for k, (s, d) in enumerate(pairs)]
    for c in copies:
        c.start()
    return copies


def wait_all(copies):
    for c in copies:
        c.wait()


def at_rows(start, size):
    return pl.ds(pl.multiple_of(start, 16), size)


def flip(p):
    return (p & 1) * 8 + (p & 2) * 2 + (p & 4) // 2 + (p & 8) // 8


def setup_kernel(
    exact, crop, micro, px, w1_far, fs, isc, keep, keep1, keep_half, sh, perm, st, x, w1, flat, sems
):
    copies = copy_all([(px, x), (w1_far, w1)], sems)
    n = lax.axis_index("narrow").astype(jnp.int32)
    w = lax.axis_index("wide").astype(jnp.int32)
    isc[NARROW] = n
    isc[CORE] = w & 1
    for p in range(16):
        isc[DEST + p] = (w ^ flip(p)) if exact else jnp.int32(p)

    def count(k, sums):
        c, one = crop[k], micro[k]
        a, b = (c >> 4) * (c >> 4), (c >> 5) * (c >> 5)
        return (
            sums[0] + a * (1 - one), sums[1] + a * one, sums[2] + b * (1 - one), sums[3] + b * one,
        )

    zero = jnp.int32(0)
    sums = lax.fori_loop(0, crop.shape[0], count, (zero, zero, zero, zero))
    for k in range(4):
        fs[k] = 1.0 / sums[k].astype(F32)
    fs[INV_ALL] = 1.0 / ((sums[2] + sums[3]).astype(F32) * 2048.0)
    at = lax.broadcasted_iota(jnp.int32, (POS, 1), 0)
    i8, j7 = at & 7, at >> 3
    at = lax.broadcasted_iota(jnp.int32, (HALF, 1), 0)
    r8, c14 = n * 8 + (at & 7), at >> 3

    def inside(r, c, side):
        return jnp.where((r < side) & (c < side), 1.0, 0.0).astype(F32)

    for b in range(B):
        c = crop[w * B + b]
        side_in, side_out = c >> 4, c >> 5
        fs[CELLS + b] = 1.0 / (side_out * side_out).astype(F32)
        fs[MICRO + b] = micro[w * B + b].astype(F32)
        keep[b * POS : (b + 1) * POS, :] = inside(i8, j7, side_out)
        for k in range(4):
            keep1[k, b * POS : (b + 1) * POS, :] = inside(2 * i8 + k // 2, 2 * j7 + k % 2, side_in)
        keep_half[b * HALF : (b + 1) * HALF, :] = inside(r8, c14, side_in)
    place = lax.broadcasted_iota(jnp.int32, (POS, M), 1)
    it = lax.broadcasted_iota(jnp.int32, (POS, M), 0)
    for t in range(9):
        di, dj = t // 3 - 1, t % 3 - 1
        i, j = (it & 7) + di, (it >> 3) + dj
        fits = (i >= 0) & (i < 8) & (j >= 0) & (j < 7)
        sh[t] = low(jnp.concatenate([
            jnp.where(fits & (place == b * POS + j * 8 + i), 1.0, 0.0) for b in range(B)
        ], axis=0))
    place = lax.broadcasted_iota(jnp.int32, (POS, HALF), 1)
    it = lax.broadcasted_iota(jnp.int32, (POS, HALF), 0)
    for half in range(2):
        planes = []
        for k in range(4):
            r, c = 2 * (it & 7) + k // 2, 2 * (it >> 3) + k % 2
            planes.append(
                jnp.where(((r >> 3) == half) & (place == c * 8 + (r & 7)), 1.0, 0.0)
            )
        perm[half] = low(jnp.concatenate(planes, axis=0))
    copies[0].wait()
    for b in range(B):
        flat[b * HALF : (b + 1) * HALF, :] = x[b]
    copies[1].wait()

    def body(c):
        sl = cols(c)
        v = mm(flat[...], w1[:, sl]) * keep_half[...]
        sums = [jnp.sum(v[b * HALF : (b + 1) * HALF], axis=0, keepdims=True) for b in range(B)]
        v2 = v * v
        sq = [jnp.sum(v2[b * HALF : (b + 1) * HALF], axis=0, keepdims=True) for b in range(B)]
        put(st, 0, grouped(sums, fs) + grouped(sq, fs), sl)

    loop(2, body)


TAPS = [(p, q) for p in range(3) for q in range(3)]


def stage_two_kernel(
    fs, isc, own, other, part, part_other, perm, keep1, keep, w1, ws_far, gb, sh,
    xp, strided, x1, col, pre2, st, tot1, tmp, hid, tot, ws, sems,
):
    n = isc[NARROW]
    copies = copy_all([(ws_far.at[3 * k : 3 * k + 3], ws.at[3 * k : 3 * k + 3]) for k in range(3)], sems)
    tot[...] = part[...] + part_other[...]
    tot1[...] = tot[...]

    def permute(c):
        sl = cols(c)
        for b in range(B):
            r = mm(perm[n], own[b, :, sl]) + mm(perm[1 - n], other[b, :, sl])
            for k in range(4):
                tmp[k, b * POS : (b + 1) * POS, :] = r[k * POS : (k + 1) * POS]
        for k in range(4):
            xp[k, :, sl] = low(tmp[k] * keep1[k])
        strided[:, sl] = xp[0, :, sl]

    loop(4, permute)

    def first(c):
        k, sl = c // 2, cols(c % 2)
        v = mm(xp[k], w1[:, sl])
        mean, scale = coefs(tot, 0, sl, fs, INV_IN)
        x = (v - mean) * scale
        x1[k, :, sl] = x
        o = x * gb[0:1, sl] + gb[1:2, sl]
        hid[k, :, sl] = low(o * sigmoid(o) * keep1[k])

    loop(8, first)
    for t, (p, q) in enumerate(TAPS):
        h = hid[2 * (p != 1) + (q != 1)]
        if p == 0 or q == 0:
            h = low(mm(sh[3 * (0 if p == 0 else 1) + (0 if q == 0 else 1)], h))
        col[t] = h
    wait_all(copies)

    def second(c):
        sl = cols(c)
        v = mm(col[0], ws[0, :, sl])
        for t in range(1, 9):
            v = v + mm(col[t], ws[t, :, sl])
        pre2[:, sl] = v
        put(st, 0, stat_rows(v, keep[...], fs), sl)

    loop(2, second)


def project_kernel(fs, x, keep, wp_far, w3_far, prep, st, w3, wp, sems):
    def part(k):
        sl = cols(k, 512)
        return pltpu.make_async_copy(wp_far.at[:, sl], wp.at[:, sl], sems.at[k])

    for k in range(4):
        part(k).start()
    w3_copy = pltpu.make_async_copy(w3_far, w3, sems.at[4])
    w3_copy.start()

    def body(c):
        sl = cols(c)
        v = mm(x[...], wp[:, sl])
        prep[:, sl] = v
        put(st, 0, stat_rows(v, keep[...], fs), sl)

    def pair(k):
        part(k).wait()
        body(2 * k)
        body(2 * k + 1)

    loop(4, pair, 1)
    w3_copy.wait()


def stage_three_kernel(fs, parts, pre2, stp, keep, w3, gb, h2, pre3, st, tot2, tot):
    add_parts(parts, tot)
    tot2[...] = tot[...]
    sl = slice(0, 512)
    mean, scale = coefs(tot, 0, sl, fs, INV_OUT)
    o = (pre2[...] - mean) * scale * gb[2:3, :] + gb[3:4, :]
    h2[...] = low(o * sigmoid(o) * keep[...])
    st[4:8, :] = stp[...]

    def body(c):
        sl = cols(c)
        v = mm(h2[...], w3[:, sl])
        pre3[:, sl] = v
        put(st, 0, stat_rows(v, keep[...], fs), sl)

    loop(8, body, 4)


def fetch_four_kernel(isc, own, r1, r2, w4, sems):
    n, core = isc[NARROW], isc[CORE]
    away = (1 - n) * 1024
    wait_all(copy_all(
        [
            (own, w4.at[at_rows(n * 1024, 1024)]),
            (r1, w4.at[at_rows(away + core * 512, 512)]),
            (r2, w4.at[at_rows(away + (1 - core) * 512, 512)]),
        ],
        sems,
    ))


def stage_four_kernel(
    fs, parts, pre3, prep, keep, vec, sqb, sq_far, ex_far, w4,
    lows, pre4, st, tot3, gate, sp, pooled, squares, unit, short, acc, tot, sq, ex, sems,
):
    copies = copy_all([(sq_far, sq), (ex_far, ex)], sems)
    add_parts(parts, tot)
    tot3[...] = tot[...]
    pooled[...] = jnp.zeros((8, 2048), F32)

    def units(c):
        sl = cols(c)
        mean, scale = coefs(tot, 0, sl, fs, INV_OUT)
        u = ((pre3[:, sl] - mean) * scale * vec[0:1, sl] + vec[1:2, sl]) * keep[...]
        unit[:, sl] = u
        for b, r in enumerate(image_sums(u)):
            pooled[b : b + 1, sl] = r * fs[CELLS + b]
        mean, scale = coefs(tot, 4, sl, fs, INV_OUT)
        s = ((prep[:, sl] - mean) * scale * vec[2:3, sl] + vec[3:4, sl]) * keep[...]
        short[:, sl] = s

    loop(8, units, 4)
    wait_all(copies)
    sp[...] = dot3(pooled[...], sq[...]) + sqb[0:1, :]
    squeezed = sp[...] * sigmoid(sp[...])
    gate[...] = sigmoid(dot3(squeezed, ex[...]) + vec[4:5, :])
    squares[...] = jnp.zeros((8, 256), F32)
    acc[...] = jnp.zeros((M, 512), F32)

    def streams(c):
        sl = cols(c)
        branch = unit[:, sl] * expand([gate[b : b + 1, sl] for b in range(B)])
        s = short[:, sl]
        join = branch + s
        stream = join * sigmoid(join) * keep[...]
        for k, v in enumerate((stream, branch, s)):
            squares[k : k + 1, :] += jnp.sum(v * v, axis=0, keepdims=True)
        lo = low(stream)
        lows[:, sl] = lo
        acc[...] += mm(lo, w4[cols(c), :])

    loop(8, streams, 4)
    pre4[...] = acc[...]
    put(st, 0, stat_rows(acc[...], keep[...], fs), slice(0, 512))


def fetch_five_kernel(isc, own, r1, r2, w5, sems):
    n, core = isc[NARROW], isc[CORE]
    wait_all(copy_all([
        (own, w5.at[n]),
        (r1, w5.at[1 - n, at_rows(core * 2304, 2304)]),
        (r2, w5.at[1 - n, at_rows((1 - core) * 2304, 2304)]),
    ], sems))


def stage_five_kernel(
    fs, parts, pre4, keep, gb, sh, w5, col, pre5, st, tot4, tot
):
    add_parts(parts, tot)
    tot4[...] = tot[...]
    mean, scale = coefs(tot, 0, slice(0, 512), fs, INV_OUT)
    o = (pre4[...] - mean) * scale * gb[4:5, :] + gb[5:6, :]
    h = low(o * sigmoid(o) * keep[...])
    for t in range(9):
        col[t] = h if t == 4 else low(mm(sh[t], h))
    def body(c):
        v = 0.0
        for t in range(9):
            v = v + mm(col[t], w5[c, t * 512 : (t + 1) * 512, :])
        pre5[:, cols(c)] = v
        put(st, 0, stat_rows(v, keep[...], fs), cols(c))

    loop(2, body)


def fetch_six_kernel(isc, own, r1, r2, vown, w6, gain5, vec2, vaway, sems):
    n, core = isc[NARROW], isc[CORE]
    pairs = [(r1.at[VE2:PACK_ROWS], vaway), (own, w6.at[at_rows(n * 256, 256)])]
    for r, h in ((r1, core), (r2, 1 - core)):
        for c in range(8):
            pairs.append(
                (
                    r.at[W6_AT + c * 128 : W6_AT + (c + 1) * 128],
                    w6.at[at_rows((1 - n) * 256 + h * 128, 128), c * 256 : (c + 1) * 256],
                )
            )
    copies = copy_all(pairs, sems)
    copies[0].wait()
    for side, v in ((n, f32(vown[...])), (1 - n, f32(vaway[...]))):
        for k in range(2):
            gain5[k : k + 1, cols(side)] = v[k : k + 1]
        for k in range(3):
            for c in range(4):
                at = 2 + 4 * k + c
                vec2[k : k + 1, cols(side * 4 + c)] = v[at : at + 1]
    wait_all(copies[1:])


def stage_six_kernel(
    fs, parts, pre5, keep, gain5, w6, h5, pre6, st, tot5, tot
):
    add_parts(parts, tot)
    tot5[...] = tot[...]
    mean, scale = coefs(tot, 0, slice(0, 512), fs, INV_OUT)
    o = (pre5[...] - mean) * scale * gain5[0:1, :] + gain5[1:2, :]
    h5[...] = low(o * sigmoid(o) * keep[...])

    def body(c):
        sl = cols(c)
        v = mm(h5[...], w6[:, sl])
        pre6[:, sl] = v
        put(st, 0, stat_rows(v, keep[...], fs), sl)

    loop(8, body)


def fetch_turn_kernel(isc, sqown, exown, r1, r2, ogown, ogother, sq, ex, og, sems):
    n, core = isc[NARROW], isc[CORE]
    pairs = [
        (sqown, sq.at[at_rows(n * 1024, 1024)]),
        (exown, ex.at[n]),
        (ogown, og.at[n]),
        (ogother, og.at[1 - n]),
    ]
    for r, h in ((r1, core), (r2, 1 - core)):
        for k in range(2):
            pairs.append(
                (
                    r.at[SQ_AT : SQ_AT + 256, k * 128 : (k + 1) * 128],
                    sq.at[at_rows((1 - n) * 1024 + h * 512 + k * 256, 256)],
                )
            )
        for c in range(4):
            pairs.append(
                (
                    r.at[EX_AT + c * 64 : EX_AT + (c + 1) * 64],
                    ex.at[1 - n, at_rows(h * 64, 64), c * 256 : (c + 1) * 256],
                )
            )
    wait_all(copy_all(pairs, sems))


def turn_kernel(
    fs, isc, parts, pre6, keep, lows, vec, sqb, sq1s, sq, ex, og,
    result, dj2, pay, extra, tot6, gate, dp, pooled, de, ds, squeezed, unit, res, tot, sp,
):
    n = isc[NARROW]
    add_parts(parts, tot)
    tot6[...] = tot[...]
    pooled[...] = jnp.zeros((8, 2048), F32)
    de[...] = jnp.zeros((8, 2048), F32)

    def units(c):
        sl = cols(c)
        mean, scale = coefs(tot, 0, sl, fs, INV_OUT)
        u = ((pre6[:, sl] - mean) * scale * vec[0:1, sl] + vec[1:2, sl]) * keep[...]
        unit[:, sl] = u
        for b, r in enumerate(image_sums(u)):
            pooled[b : b + 1, sl] = r * fs[CELLS + b]

    loop(8, units, 4)
    sp[...] = dot3(pooled[...], sq[...]) + sqb[1:2, :]
    squeezed[...] = sp[...] * sigmoid(sp[...])
    for h in range(2):
        sl = slice(h * 1024, (h + 1) * 1024)
        gate[:, sl] = sigmoid(dot3(squeezed[...], ex[h]) + vec[2:3, sl])
    extra[...] = jnp.zeros((8, 512), F32)
    for k in range(3):
        extra[5 + k // 2 : 6 + k // 2, (k % 2) * 256 : (k % 2) * 256 + 256] = sq1s[k : k + 1, :]

    def streams(c):
        sl = cols(c)
        h, part = c // 4, cols(c % 4)
        u = unit[:, sl]
        branch = u * expand([gate[b : b + 1, sl] for b in range(B)])
        join = branch + f32(lows[:, sl])
        s = sigmoid(join)
        stream = join * s * keep[...]
        res[h, :, part] = low(stream)
        d = f32(og[h, :, part]) * keep[...] * (s * (1.0 + join * (1.0 - s)))
        dj2[:, sl] = d
        for b, r in enumerate(image_sums(d * u)):
            de[b : b + 1, sl] = r
        extra[6:7, 256:512] += jnp.sum(branch * branch, axis=0, keepdims=True)
        extra[7:8, 0:256] += jnp.sum(stream * stream, axis=0, keepdims=True)

    loop(8, streams, 4)
    result[...] = res[n]
    de[...] = de[...] * gate[...] * (1.0 - gate[...])
    back = 0.0
    for h in range(2):
        back = back + dot3_nt(de[:, h * 1024 : (h + 1) * 1024], ex[h])
    ds[...] = back * slope(sp[...])
    dp[...] = dot3_nt(ds[...], sq[...])
    for b in range(B):
        dp[b : b + 1, :] = dp[b : b + 1, :] * fs[CELLS + b]
    total = jnp.sum(de[...], axis=0, keepdims=True)
    for k in range(4):
        extra[k : k + 1, :] = total[:, k * 512 : (k + 1) * 512]
    extra[4:5, 0:128] = jnp.sum(ds[...], axis=0, keepdims=True)

    def tops(c):
        sl = cols(c)
        mean, scale = coefs(tot, 0, sl, fs, INV_OUT)
        x = (pre6[:, sl] - mean) * scale
        du = (
            dj2[:, sl] * expand([gate[b : b + 1, sl] for b in range(B)])
            + expand([dp[b : b + 1, sl] for b in range(B)])
        ) * keep[...]
        put(pay, 0, back_rows(du, x, fs), sl)

    loop(8, tops, 4)


def whole_gain(tot, at, gain, bias):
    gain[...] = (tot[at + 2 : at + 3, :] + tot[at + 3 : at + 4, :]).reshape(gain.shape)
    bias[...] = (tot[at : at + 1, :] + tot[at + 1 : at + 2, :]).reshape(bias.shape)


def half_gain(tot, n, gain, bias):
    sl = cols(n, gain.shape[0])
    gain[...] = (tot[2:3, sl] + tot[3:4, sl]).reshape(gain.shape)
    bias[...] = (tot[0:1, sl] + tot[1:2, sl]).reshape(bias.shape)


def back_six_kernel(
    fs, isc, parts, tot6, pre6, dj2, gate, dp, pre5, tot5, extra, keep, vec, gain5, w6,
    d6, do5, st, dgain, dbias, tot, acc,
):
    add_parts(parts, tot)
    half_gain(tot, isc[NARROW], dgain, dbias)
    acc[...] = jnp.zeros((M, 512), F32)

    def body(c):
        sl = cols(c)
        mean, scale = coefs(tot6, 0, sl, fs, INV_OUT)
        x = (pre6[:, sl] - mean) * scale
        du = (
            dj2[:, sl] * expand([gate[b : b + 1, sl] for b in range(B)])
            + expand([dp[b : b + 1, sl] for b in range(B)])
        ) * keep[...]
        a, bb = means(tot, 0, sl, fs, INV_OUT)
        d = low((du - a - x * bb) * (scale * vec[0:1, sl]) * keep[...])
        d6[:, sl] = d
        acc[...] += mm_nt(d, w6[:, sl])

    loop(8, body, 4)
    mean, scale = coefs(tot5, 0, slice(0, 512), fs, INV_OUT)
    x = (pre5[...] - mean) * scale
    o = x * gain5[0:1, :] + gain5[1:2, :]
    d = acc[...] * keep[...] * slope(o)
    do5[...] = d
    put(st, 0, back_rows(d, x, fs), slice(0, 512))
    st[4:12, :] = extra[...]


def back_five_kernel(
    fs, isc, parts, tot5, pre5, do5, pre4, tot4, keep, gb, gain5, sh, w5,
    d5, do4, st, dgain, dbias, debias, dsbias, norms, tot,
):
    n = isc[NARROW]
    add_parts(parts, tot)
    half_gain(tot, n, dgain, dbias)
    excite = jnp.concatenate([tot[pl.ds(4 + 2 * n, 1), :], tot[pl.ds(5 + 2 * n, 1), :]], axis=1)
    debias[...] = excite.reshape(1024)
    dsbias[...] = tot[8:9, 0:128].reshape(128)
    for k in range(5):
        v = tot[9 + k // 2 : 10 + k // 2, (k % 2) * 256 : (k % 2) * 256 + 256]
        norms[k] = jnp.sqrt(jnp.sum(v, axis=1, keepdims=True) * fs[INV_ALL])[0, 0]
    sl = slice(0, 512)
    mean, scale = coefs(tot5, 0, sl, fs, INV_OUT)
    x = (pre5[...] - mean) * scale
    a, bb = means(tot, 0, sl, fs, INV_OUT)
    d = low((do5[...] - a - x * bb) * (scale * gain5[0:1, :]) * keep[...])
    d5[...] = d
    acc = 0.0
    for t in range(9):
        dc = d if t == 4 else low(mm(sh[8 - t], d))
        for h in range(2):
            acc = acc + mm_nt(dc[:, h * 256 : (h + 1) * 256], w5[h, t * 512 : (t + 1) * 512, :])
    mean, scale = coefs(tot4, 0, sl, fs, INV_OUT)
    x = (pre4[...] - mean) * scale
    o = x * gb[4:5, :] + gb[5:6, :]
    d = acc * keep[...] * slope(o)
    do4[...] = d
    put(st, 0, back_rows(d, x, fs), sl)


def back_four_kernel(
    fs, parts, tot4, pre4, do4, dj2, tot3, pre3, prep, gate, sp, keep, gb, vec, sq_far, ex_far, w4,
    d4, dj1, st, dgain, dbias, dp, de, ds, bias, tot, sq, ex, sems,
):
    copies = copy_all([(sq_far, sq), (ex_far, ex)], sems)
    add_parts(parts, tot)
    whole_gain(tot, 0, dgain, dbias)
    de[...] = jnp.zeros((8, 2048), F32)
    mean, scale = coefs(tot4, 0, slice(0, 512), fs, INV_OUT)
    x = (pre4[...] - mean) * scale
    a, bb = means(tot, 0, slice(0, 512), fs, INV_OUT)
    d4[...] = low((do4[...] - a - x * bb) * (scale * gb[4:5, :]) * keep[...])

    def joins(c):
        sl = cols(c)
        back = dj2[:, sl] + mm_nt(d4[...], w4[cols(c), :])
        mean, scale = coefs(tot3, 0, sl, fs, INV_OUT)
        u = ((pre3[:, sl] - mean) * scale * vec[0:1, sl] + vec[1:2, sl]) * keep[...]
        mean, scale = coefs(tot3, 4, sl, fs, INV_OUT)
        s = ((prep[:, sl] - mean) * scale * vec[2:3, sl] + vec[3:4, sl]) * keep[...]
        join = u * expand([gate[b : b + 1, sl] for b in range(B)]) + s
        d = f32(low(back)) * keep[...] * slope(join)
        dj1[:, sl] = d
        for b, r in enumerate(image_sums(d * u)):
            de[b : b + 1, sl] = r

    loop(8, joins)
    wait_all(copies)
    de[...] = de[...] * gate[...] * (1.0 - gate[...])
    ds[...] = dot3_nt(de[...], ex[...]) * slope(sp[...])
    dp[...] = dot3_nt(ds[...], sq[...])
    for b in range(B):
        dp[b : b + 1, :] = dp[b : b + 1, :] * fs[CELLS + b]
    total = jnp.sum(de[...], axis=0, keepdims=True)
    bias[...] = jnp.zeros((8, 512), F32)
    for k in range(4):
        bias[k : k + 1, :] = total[:, k * 512 : (k + 1) * 512]
    bias[4:5, 0:128] = jnp.sum(ds[...], axis=0, keepdims=True)

    def tops(c):
        sl = cols(c)
        d = dj1[:, sl]
        mean, scale = coefs(tot3, 0, sl, fs, INV_OUT)
        x = (pre3[:, sl] - mean) * scale
        du = (
            d * expand([gate[b : b + 1, sl] for b in range(B)])
            + expand([dp[b : b + 1, sl] for b in range(B)])
        ) * keep[...]
        put(st, 0, back_rows(du, x, fs), sl)
        mean, scale = coefs(tot3, 4, sl, fs, INV_OUT)
        put(st, 4, back_rows(d, (prep[:, sl] - mean) * scale, fs), sl)

    loop(8, tops)


def back_three_kernel(
    fs, parts, tot3, pre3, prep, dj1, gate, dp, bias, pre2, tot2, keep, vec, gb, w3,
    d3, dproj, do2, st, dgain, dbias, dgainp, dbiasp, tot, acc,
):
    add_parts(parts, tot)
    whole_gain(tot, 0, dgain, dbias)
    whole_gain(tot, 4, dgainp, dbiasp)
    acc[...] = jnp.zeros((M, 512), F32)

    def body(c):
        sl = cols(c)
        mean, scale = coefs(tot3, 0, sl, fs, INV_OUT)
        x = (pre3[:, sl] - mean) * scale
        dj = dj1[:, sl]
        du = (
            dj * expand([gate[b : b + 1, sl] for b in range(B)])
            + expand([dp[b : b + 1, sl] for b in range(B)])
        ) * keep[...]
        a, bb = means(tot, 0, sl, fs, INV_OUT)
        d = low((du - a - x * bb) * (scale * vec[0:1, sl]) * keep[...])
        d3[:, sl] = d
        acc[...] += mm_nt(d, w3[:, sl])
        mean, scale = coefs(tot3, 4, sl, fs, INV_OUT)
        x = (prep[:, sl] - mean) * scale
        a, bb = means(tot, 4, sl, fs, INV_OUT)
        dproj[:, sl] = low((dj - a - x * bb) * (scale * vec[2:3, sl]) * keep[...])

    loop(8, body)
    sl = slice(0, 512)
    mean, scale = coefs(tot2, 0, sl, fs, INV_OUT)
    x = (pre2[...] - mean) * scale
    o = x * gb[2:3, :] + gb[3:4, :]
    d = acc[...] * keep[...] * slope(o)
    do2[...] = d
    put(st, 0, back_rows(d, x, fs), sl)
    st[4:12, :] = bias[...]


def fetch_two_kernel(far, ws, sems):
    wait_all(copy_all([(far.at[3 * k : 3 * k + 3], ws.at[3 * k : 3 * k + 3]) for k in range(3)], sems))


def back_two_kernel(
    fs, parts, tot2, pre2, do2, x1, keep1, keep, gb, sh, ws,
    d2, do1, st, dgain, dbias, debias, dsbias, tot, dcol,
):
    add_parts(parts, tot)
    whole_gain(tot, 0, dgain, dbias)
    debias[...] = jnp.concatenate([tot[k : k + 1, :] for k in range(4, 8)], axis=1).reshape(2048)
    dsbias[...] = tot[8:9, 0:128].reshape(128)
    sl = slice(0, 512)
    mean, scale = coefs(tot2, 0, sl, fs, INV_OUT)
    x = (pre2[...] - mean) * scale
    a, bb = means(tot, 0, sl, fs, INV_OUT)
    d = low((do2[...] - a - x * bb) * (scale * gb[2:3, :]) * keep[...])
    d2[...] = d
    dcol[0] = d
    dcol[1] = low(mm(sh[5], d))
    dcol[2] = low(mm(sh[7], d))
    dcol[3] = low(mm(sh[8], d))
    terms = (
        ((0, 4),),
        ((0, 5), (1, 3)),
        ((0, 7), (2, 1)),
        ((0, 8), (1, 6), (2, 2), (3, 0)),
    )
    st[...] = jnp.zeros((4, 512), F32)
    for k in range(4):
        acc = 0.0
        for which, t in terms[k]:
            acc = acc + mm_nt(dcol[which], ws[t])
        x = x1[k]
        o = x * gb[0:1, :] + gb[1:2, :]
        d = acc * keep1[k] * slope(o)
        do1[k] = d
        rows = back_rows(d, x, fs)
        for r in range(4):
            st[r : r + 1, :] += rows[r]


def deal(isc, full, rows, keep, send, at):
    for p in range(16):
        tile = full[pl.ds(pl.multiple_of(isc[DEST + p] * rows, rows), rows), :]
        (keep if p < 8 else send)[p % 8, at_rows(at, rows), :] = tile


def back_one_kernel(
    fs, isc, parts, tot1, x1, do1, xp, keep1, gb, d1, gkeep, gsend, dgain, dbias, tot, dn, full
):
    n = isc[NARROW]
    add_parts(parts, tot)
    whole_gain(tot, 0, dgain, dbias)
    sl = slice(0, 512)
    scale = coefs(tot1, 0, sl, fs, INV_IN)[1] * gb[0:1, :]
    a, bb = means(tot, 0, sl, fs, INV_IN)
    planes = []
    for k in range(4):
        d = (do1[k] - a - x1[k] * bb) * scale * keep1[k]
        planes.append(d)
        dn[k] = low(d)
    for b in range(B):
        d1[b] = low(jnp.concatenate([d[b * POS : (b + 1) * POS] for d in planes], axis=0))

    def body(c):
        g = 0.0
        for k in range(4):
            g = g + mm_tn(xp[k, :, cols(c)], dn[k, :, cols(n)])
        full[cols(c), :] = low(g)

    loop(4, body, 4)
    deal(isc, full, 64, gkeep, gsend, 0)


def placed_kernel(isc, dproj, wp_far, out, cc, pick_own, spread, wp, sems):
    n = isc[NARROW]

    def part(k):
        return pltpu.make_async_copy(wp_far.at[cols(k), :], wp.at[cols(k), :], sems.at[k])

    for k in range(4):
        part(k).start()
    for b in range(B):
        place = lax.broadcasted_iota(jnp.int32, (32, M), 1)
        it = lax.broadcasted_iota(jnp.int32, (32, M), 0)
        pick_own[b * 32 : (b + 1) * 32, :] = low(jnp.where(
            (place == b * POS + (it >> 2) * 8 + n * 4 + (it & 3)) & (it < 28), 1.0, 0.0
        ))
        place = lax.broadcasted_iota(jnp.int32, (HALF, 128), 1)
        it = lax.broadcasted_iota(jnp.int32, (HALF, 128), 0)
        spread[b * HALF : (b + 1) * HALF, :] = low(jnp.where(
            ((it & 9) == 0) & (place == b * 32 + (it >> 4) * 4 + ((it & 7) >> 1)), 1.0, 0.0
        ))
    cc[...] = low(mm(pick_own[...], dproj[...]))

    def body(c):
        sl = cols(c)
        part(c).wait()
        hi, lo = split2(mm_nt(cc[...], wp[sl, :]))
        out[:, sl] = mm(spread[...], hi) + mm(spread[...], lo)

    loop(4, body, 1)


def image_kernel(isc, perm, d1, placed, keep, w1, out, dc):
    n = isc[NARROW]
    for b in range(B):
        dc[b * HALF : (b + 1) * HALF, :] = low(mm_tn(perm[n], d1[b]))
    for c in range(4):
        sl = cols(c)
        out[:, sl] = (mm_nt(dc[...], w1[sl, :]) + placed[:, sl]) * keep[...]


def grads_a_kernel(isc, h5, d6, col4, d5, gkeep, gsend, wider, full):
    n = isc[NARROW]

    def expand2(c):
        wider[:, cols(c)] = low(mm_tn(h5[:, cols(n)], d6[:, cols(c)]))

    loop(8, expand2, 4)
    for p in range(16):
        sl = cols(isc[DEST + p], 128)
        for k in range(2):
            (gkeep if p < 8 else gsend)[p % 8, 0:128, k * 128 : (k + 1) * 128] = wider[
                k * 128 : (k + 1) * 128, sl
            ]

    def spatial(t):
        full[...] = low(mm_tn(col4[t], d5[:, cols(n)]))
        deal(isc, full, 32, gkeep, gsend, 128 + t * 32)

    loop(9, spatial, 3)


def gate_grads(isc, n, c, at, squeezed, pooled, de, ds, gkeep, gsend, q, e):
    sl = cols(n * 4 + c)
    q[...] = outer(ds[...], pooled[:, sl])
    e[...] = outer(squeezed[...], de[:, sl])
    for p in range(16):
        rows = pl.ds(pl.multiple_of(isc[DEST + p] * 8, 8), 8)
        both = jnp.concatenate([q[rows, :], e[rows, :]], axis=0)
        (gkeep if p < 8 else gsend)[p % 8, at_rows(at + c * 16, 16), :] = low(both)


def grads_b_kernel(
    isc, d4, lows, sq2, pooled2, de2, ds2, sp1, pooled1, de1, ds1, gkeep, gsend, full, q, e, sq1
):
    n = isc[NARROW]
    sq1[...] = sp1[...] * sigmoid(sp1[...])

    def body(c):
        full[...] = low(mm_tn(d4[...], lows[:, cols(n * 4 + c)]))
        deal(isc, full, 32, gkeep, gsend, c * 32)
        gate_grads(isc, n, c, 128, sq2, pooled2, de2, ds2, gkeep, gsend, q, e)
        gate_grads(isc, n, c, 192, sq1, pooled1, de1, ds1, gkeep, gsend, q, e)

    loop(4, body, 4)


def grads_c_kernel(isc, h2, d3, strided, dproj, gkeep, gsend, full, taller):
    n = isc[NARROW]

    def body(c):
        sl = cols(n * 4 + c)
        full[...] = low(mm_tn(h2[...], d3[:, sl]))
        deal(isc, full, 32, gkeep, gsend, c * 32)
        taller[...] = low(mm_tn(strided[...], dproj[:, sl]))
        deal(isc, taller, 64, gkeep, gsend, 128 + c * 64)

    loop(4, body, 4)


def grads_d_kernel(isc, col1, d2, gkeep, gsend, full):
    n = isc[NARROW]

    def spatial(t):
        full[...] = low(mm_tn(col1[t], d2[:, cols(n)]))
        deal(isc, full, 32, gkeep, gsend, t * 32)

    loop(9, spatial)


def joined(v, out, at, rows):
    for c in range(4):
        out[:, c * 256 : (c + 1) * 256] = v[at + c * rows : at + (c + 1) * rows, :]


def unpack_gates(v, at, squeeze, excite):
    for c in range(4):
        part = v[at + c * 16 : at + (c + 1) * 16, :]
        squeeze[:, c * 256 : (c + 1) * 256] = part[0:8]
        excite[:, c * 256 : (c + 1) * 256] = part[8:16]


def unpack_kernel(
    a, b, c, d, expand2, spatial2, reduce2, squeeze2, excite2, squeeze1, excite1, expand1, project1
):
    v = f32(a[0]) + f32(b[0])
    expand2[0:128, :] = v[0:128, 0:128]
    expand2[128:256, :] = v[0:128, 128:256]
    spatial2[...] = v[128:416, :]
    joined(v, reduce2, 416, 32)
    unpack_gates(v, 544, squeeze2, excite2)
    unpack_gates(v, 608, squeeze1, excite1)
    v = f32(c[0]) + f32(d[0])
    joined(v, expand1, 0, 32)
    joined(v, project1, 128, 64)


def unpack_last_kernel(a, b, c, d, spatial1, reduce1):
    spatial1[...] = f32(a[0]) + f32(b[0])
    reduce1[...] = f32(c[0]) + f32(d[0])


VECTORS = (512,) * 6 + (2048,) * 5 + (128,) * 2 + (256,) * 2 + (1024,) * 3


def pack_kernel(isc, w5, w4, w6, ex, sq, *refs):
    far, refs = refs[:18], refs[18:]
    out, w5_half, w4_half, gb, vec1, sqb, vown, w6v, exv, sqv, rows = refs[:11]
    vecs, sems = refs[11:29], refs[29]
    core = isc[CORE]
    pairs = [(f, v) for f, v in zip(far, vecs)] + [
        (w6.at[at_rows(core * 128, 128)], w6v),
        (ex.at[at_rows(core * 64, 64)], exv),
        (sq.at[at_rows(core * 512, 512)], sqv),
        (w4.at[at_rows(core * 512, 512)], w4_half),
        (w5.at[at_rows(core * 2304, 2304)], w5_half),
    ]
    copies = copy_all(pairs, sems)
    wait_all(copies[:21])

    def row(v):
        return f32(v[...]).reshape(1, v.shape[0])

    for k in range(6):
        gb[k : k + 1, :] = row(vecs[k])
    for k in range(5):
        vec1[k : k + 1, :] = row(vecs[6 + k])
    for k in range(2):
        sqb[k : k + 1, :] = row(vecs[11 + k])
    rows[...] = jnp.zeros((16, 256), F32)
    at = 0
    for v in vecs[13:18]:
        r = row(v)
        for c in range(v.shape[0] // 256):
            rows[at : at + 1, :] = r[:, c * 256 : (c + 1) * 256]
            at += 1
    vown[...] = low(rows[...])
    for c in range(8):
        out[W6_AT + c * 128 : W6_AT + (c + 1) * 128, :] = w6v[:, c * 256 : (c + 1) * 256]
    for c in range(4):
        out[EX_AT + c * 64 : EX_AT + (c + 1) * 64, :] = exv[:, c * 256 : (c + 1) * 256]
    for k in range(2):
        out[SQ_AT : SQ_AT + 256, k * 128 : (k + 1) * 128] = sqv[k * 256 : (k + 1) * 256, :]
    out[VE2:PACK_ROWS, :] = vown[...]
    wait_all(copies[21:])


def call(body, outs, args, scratch=(), flops=1e8, size=5e6, name=None, vmem=LIMIT):
    specs, values = [], []
    for a in args:
        kind, v = a if isinstance(a, tuple) else (VMEM, a)
        specs.append(kind)
        values.append(v)
    return pl.pallas_call(
        body,
        out_shape=tuple(o if hasattr(o, "memory_space") else jax.ShapeDtypeStruct(o[0], o[1]) for o in outs),
        in_specs=specs,
        out_specs=tuple(o[2] if isinstance(o, tuple) and len(o) > 2 else pl.BlockSpec(memory_space=getattr(o, "memory_space", pltpu.VMEM)) for o in outs),
        scratch_shapes=list(scratch),
        compiler_params=pltpu.CompilerParams(vmem_limit_bytes=vmem * 2**20),
        cost_estimate=pl.CostEstimate(
            flops=int(flops * SCALE), bytes_accessed=int(size * SCALE), transcendentals=0
        ),
        name=name,
    )(*values)


def swap(v, axis, pairs):
    return lax.ppermute(v, axis, pairs)


def after(v, *others):
    return lax.optimization_barrier((v,) + others)[0]


def local(
    images, crop, micro,
    first_reduce, first_reduce_gain, first_reduce_bias,
    first_spatial, first_spatial_gain, first_spatial_bias,
    first_expand, first_expand_gain, first_expand_bias,
    first_project, first_project_gain, first_project_bias,
    first_squeeze, first_squeeze_bias, first_excite, first_excite_bias,
    second_reduce, second_reduce_gain, second_reduce_bias,
    second_spatial, second_spatial_gain, second_spatial_bias,
    second_expand, second_expand_gain, second_expand_bias,
    second_squeeze, second_squeeze_bias, second_excite, second_excite_bias,
    out_grad,
):
    wide = lax.axis_size("wide")
    exact = wide == 16
    near = [(i, i ^ 1) for i in range(wide)]
    pair = [(0, 1), (1, 0)]
    V = pltpu.VMEM
    D = pltpu.SemaphoreType.DMA
    out = lambda *shape: (shape, F32)
    f = lambda *shape: V(shape, F32)
    h = lambda *shape: V(shape, BF)
    far = lambda v: (ANY, pltpu.with_memory_space_constraint(v, pltpu.HBM))

    def steps(x, *first, before=None):
        results, step = [], 1
        x = after(x, *first)
        while step < wide:
            due = (before or {}).get(len(results), ())
            y = after(x, *(due(results) if callable(due) else due))
            x = x + swap(y, "wide", [(i, i ^ step) for i in range(wide)])
            results.append(x)
            step *= 2
        return x[None], results

    own_px = images.transpose(0, 2, 1, 3).reshape(B, HALF, 1024)
    other_px = swap(own_px, "narrow", pair)
    ws_far = first_spatial.reshape(9, 512, 512)

    fs_, isc_, keep, keep1, keep_half, sh, perm, st1, xown, w1 = call(
        functools.partial(setup_kernel, exact),
        [
            pltpu.SMEM((13,), F32), pltpu.SMEM((18,), jnp.int32), f(M, 1), f(4, M, 1), f(HROWS, 1), h(9, M, M), h(2, M, HALF),
            f(4, 512), h(B, HALF, 1024), h(1024, 512),
        ],
        [(SMEM, far(crop)[1]), (SMEM, far(micro)[1]), far(own_px), far(first_reduce)],
        [V((HROWS, 1024), BF), D((2,))], name="setup",
    )
    fs, isc = (SMEM, fs_), (SMEM, isc_)
    part = steps(st1)[0][0]

    w5_own = second_spatial.reshape(9 * 512, 256)
    vectors = [
        first_reduce_gain, first_reduce_bias, first_spatial_gain, first_spatial_bias,
        second_reduce_gain, second_reduce_bias, first_expand_gain, first_expand_bias,
        first_project_gain, first_project_bias, first_excite_bias,
        first_squeeze_bias, second_squeeze_bias,
        second_spatial_gain, second_spatial_bias, second_expand_gain, second_expand_bias, second_excite_bias,
    ]
    pack, w5_half, w4_half, gb, vec1, sqb, vown = call(
        pack_kernel,
        [
            ((PACK_ROWS, 256), BF), ((2304, 256), BF), ((512, 512), BF), f(8, 512), f(8, 2048), f(8, 128), h(16, 256),
        ],
        [
            (SMEM, after(isc_, st1)), far(w5_own), far(second_reduce), far(second_expand), far(second_excite),
            far(second_squeeze),
        ] + [far(v) for v in vectors],
        [V((128, 2048), BF), V((64, 1024), BF), V((512, 128), BF), V((16, 256), F32)]
        + [V((size,), BF) for size in VECTORS] + [D((24,))],
        size=2e7, name="pack",
    )
    part = after(part, gb)
    part_other = swap(part, "narrow", pair)
    w4_r1 = swap(after(w4_half, other_px, part_other), "narrow", pair)
    og_own = out_grad.transpose(0, 2, 1, 3).reshape(M, 1024)

    xp, strided, x1, col1, pre2, st2, tot1 = call(
        stage_two_kernel,
        [h(4, M, 1024), h(M, 1024), f(4, M, 512), h(9, M, 512), f(M, 512), f(4, 512), f(4, 512)],
        [fs, isc, xown, other_px, part, part_other, perm, keep1, keep, w1, far(ws_far), gb, sh],
        [
            V((4, M, 256), F32), V((4, M, 512), BF), V((4, 512), F32), V((9, 512, 512), BF), D((3,)),
        ],
        flops=4e9, size=2e7, name="stage_two",
    )
    parts2, sent2 = steps(st2, before={3: (w4_r1,)})
    w4_r2 = swap(after(w4_r1, sent2[1]), "wide", near)
    w5_r1 = swap(after(w5_half, w4_r1, sent2[1]), "narrow", pair)
    prep, stp, w3 = call(
        project_kernel, [f(M, 2048), f(4, 2048), h(512, 2048)],
        [fs, strided, keep, far(first_project), far(first_expand)],
        [V((1024, 2048), BF), D((5,))], flops=1e9, size=8e6, name="project",
    )
    h2, pre3, st3, tot2 = call(
        stage_three_kernel, [h(M, 512), f(M, 2048), f(8, 2048), f(4, 512)],
        [fs, parts2, pre2, stp, keep, w3, gb], [V((4, 512), F32)],
        flops=1e9, size=6e6, name="stage_three",
    )
    parts3, _ = steps(st3, before={3: (w4_r2,)})
    w4 = call(
        fetch_four_kernel, [h(2048, 512)],
        [(SMEM, after(isc_, st3)), far(second_reduce), (ANY, w4_r1), (ANY, w4_r2)], [D((3,))],
        size=4e6, name="fetch_four",
    )[0]
    lows, pre4, st4, tot3, gate1, sp1, pooled1, squares = call(
        stage_four_kernel,
        [
            h(M, 2048), f(M, 512), f(4, 512), f(8, 2048), f(8, 2048), f(8, 128), f(8, 2048), f(8, 256),
        ],
        [fs, parts3, pre3, prep, keep, vec1, sqb, far(first_squeeze), far(first_excite), w4],
        [
            V((M, 2048), F32), V((M, 2048), F32), V((M, 512), F32), V((8, 2048), F32),
            V((2048, 128), BF), V((128, 2048), BF), D((2,)),
        ],
        flops=1e9, size=1e7, name="stage_four",
    )
    held = {}

    def core_half(results):
        held["w5"] = swap(after(w5_r1, results[0]), "wide", near)
        return (held["w5"],)

    parts4, _ = steps(st4, before={3: core_half})
    w5_r2 = held["w5"]
    pk1 = swap(after(pack, w5_r1, st4), "narrow", pair)
    w5 = call(
        fetch_five_kernel, [h(2, 4608, 256)],
        [(SMEM, after(isc_, st4)), far(w5_own), (ANY, w5_r1), (ANY, w5_r2)], [D((3,))],
        size=8e6, name="fetch_five",
    )[0]
    col4, pre5, st5, tot4 = call(
        stage_five_kernel, [h(9, M, 512), f(M, 512), f(4, 512), f(4, 512)],
        [fs, parts4, pre4, keep, gb, sh, w5], [V((4, 512), F32)],
        flops=2e9, size=1e7, name="stage_five",
    )

    def core_rest(results):
        held["rest"] = swap(after(pk1, results[1]), "wide", near)
        return (held["rest"],)

    parts5, _ = steps(st5, before={3: core_rest})
    pk2 = held["rest"]
    og_other = swap(after(og_own, pk1, st5), "narrow", pair)
    pk1, pk2 = (ANY, pk1), (ANY, pk2)
    w6, gain5, vec2 = call(
        fetch_six_kernel, [h(512, 2048), f(2, 512), f(3, 2048)],
        [(SMEM, after(isc_, st5)), far(second_expand), pk1, pk2, vown],
        [V((16, 256), BF), D((18,))], size=4e6, name="fetch_six",
    )
    h5, pre6, st6, tot5 = call(
        stage_six_kernel, [h(M, 512), f(M, 2048), f(4, 2048), f(4, 512)],
        [fs, parts5, pre5, keep, gain5, w6], [V((4, 512), F32)],
        flops=1e9, size=6e6, name="stage_six",
    )
    parts6, _ = steps(st6)
    sq, ex, og = call(
        fetch_turn_kernel, [h(2048, 128), h(2, 128, 1024), h(2, M, 1024)],
        [
            (SMEM, after(isc_, st6)), far(second_squeeze), far(second_excite), pk1, pk2,
            far(og_own), (ANY, og_other),
        ],
        [D((16,))], size=4e6, name="fetch_turn",
    )
    result, dj2, pay6, extra6, tot6, gate2, dp2, pooled2, de2, ds2, sq2 = call(
        turn_kernel,
        [
            ((M, 1024), BF), f(M, 2048), f(4, 2048), f(8, 512), f(4, 2048), f(8, 2048),
            f(8, 2048), f(8, 2048), f(8, 2048), f(8, 128), f(8, 128),
        ],
        [fs, isc, parts6, pre6, keep, lows, vec2, sqb, squares, sq, ex, og],
        [V((M, 2048), F32), V((2, M, 1024), BF), V((4, 2048), F32), V((8, 128), F32)],
        flops=1e9, size=1e7, name="turn",
    )
    back6, _ = steps(pay6)
    d6, do5, bt5, dgain6, dbias6 = call(
        back_six_kernel, [h(M, 2048), f(M, 512), f(12, 512), out(1024), out(1024)],
        [fs, isc, back6, tot6, pre6, dj2, gate2, dp2, pre5, tot5, extra6, keep, vec2, gain5, w6],
        [V((4, 2048), F32), V((M, 512), F32)],
        flops=1e9, size=1e7, name="back_six",
    )
    back5, _ = steps(bt5)
    d5, do4, bt4, dgain5, dbias5, debias2, dsbias2, norms = call(
        back_five_kernel,
        [h(M, 512), f(M, 512), f(4, 512), out(256), out(256), out(1024), out(128), ((5,), F32, SMEM)],
        [fs, isc, back5, tot5, pre5, do5, pre4, tot4, keep, gb, gain5, sh, w5],
        [V((12, 512), F32)],
        flops=2e9, size=1e7, name="back_five",
    )

    def step(g, k, *ties):
        if not exact:
            return g, ()
        kept, sent = g
        got = swap(after(sent, *ties), "wide", [(i, i ^ (1 << k)) for i in range(wide)])
        if k == 3:
            return (kept, got), (got,)
        half = kept.shape[0] // 2
        return (kept[:half] + got[:half], kept[half:] + got[half:]), (got,)

    ga = call(
        grads_a_kernel, [h(8, 416, 256)] * 2, [isc, h5, d6, col4, d5],
        [V((256, 2048), BF), V((512, 256), BF)], flops=2e9, size=1e7, name="grads_a",
    )
    def core_step(name, g, tied=True):
        def due(results):
            held[name], _ = step(g, 0, *(results[:1] if tied else ()))
            return held[name] if exact else ()

        return due

    back4, sent4 = steps(bt4, *ga, before={2: core_step("a", ga)})
    ga, xa = step(held["a"], 1, sent4[1])
    d4, dj1, bt3, dgain4, dbias4, dp1, de1, ds1, bias1 = call(
        back_four_kernel,
        [
            h(M, 512), f(M, 2048), f(8, 2048), out(512), out(512), f(8, 2048),
            f(8, 2048), f(8, 128), f(8, 512),
        ],
        [
            fs, back4, tot4, pre4, do4, dj2, tot3, pre3, prep, gate1, sp1, keep, gb, vec1,
            far(first_squeeze), far(first_excite), w4,
        ],
        [V((4, 512), F32), V((2048, 128), BF), V((128, 2048), BF), D((2,))],
        flops=1e9, size=1e7, name="back_four",
    )
    gb1 = call(
        grads_b_kernel, [h(8, 256, 256)] * 2,
        [isc, d4, lows, sq2, pooled2, de2, ds2, sp1, pooled1, de1, ds1],
        [V((512, 256), BF), V((128, 256), F32), V((128, 256), F32), V((8, 128), F32)],
        flops=1e9, size=4e6, name="grads_b",
    )
    ws_back = call(
        fetch_two_kernel, [h(9, 512, 512)], [far(after(ws_far, bt4))], [D((3,))], size=9e6, name="fetch_two",
    )[0]
    back3, sent3 = steps(bt3, *gb1, *xa, ws_back, before={3: core_step("b", gb1, True)})
    gb1 = held["b"]
    gb1, xb = step(gb1, 1, sent3[3])
    ga, za = step(ga, 2, sent3[3])
    d3, dproj, do2, bt2, dgain3, dbias3, dgainp, dbiasp = call(
        back_three_kernel,
        [h(M, 2048), h(M, 2048), f(M, 512), f(12, 512), out(2048), out(2048), out(2048), out(2048)],
        [fs, back3, tot3, pre3, prep, dj1, gate1, dp1, bias1, pre2, tot2, keep, vec1, gb, w3],
        [V((8, 2048), F32), V((M, 512), F32)],
        flops=1e9, size=1e7, name="back_three",
    )
    gc = call(
        grads_c_kernel, [h(8, 384, 256)] * 2, [isc, h2, d3, strided, dproj],
        [V((512, 256), BF), V((1024, 256), BF)],
        flops=3e9, size=1e7, name="grads_c",
    )
    back2, sent2 = steps(bt2, *gc, *za, *xb, before={2: core_step("c", gc)})
    gc, xc = step(held["c"], 1, sent2[1])
    d2, do1, bt1, dgain2, dbias2, debias1, dsbias1 = call(
        back_two_kernel,
        [h(M, 512), f(4, M, 512), f(4, 512), out(512), out(512), out(2048), out(128)],
        [fs, back2, tot2, pre2, do2, x1, keep1, keep, gb, sh, ws_back],
        [V((12, 512), F32), V((4, M, 512), BF)],
        flops=2e9, size=1e7, name="back_two",
    )
    gd = call(
        grads_d_kernel, [h(8, 288, 256)] * 2, [isc, col1, d2], [V((512, 256), BF)],
        flops=2e9, size=6e6, name="grads_d",
    )
    placed = call(
        placed_kernel, [f(HROWS, 1024)], [(SMEM, after(isc_, bt2)), dproj, far(first_project)],
        [V((128, 2048), BF), V((128, M), BF), V((HROWS, 128), BF), V((1024, 2048), BF), D((4,))],
        flops=1e9, size=1e7, name="placed",
    )[0]
    back1, sent1 = steps(bt1, *gd, *xc, placed)
    gd, _ = step(gd, 0, sent1[0])
    gd0 = gd
    gd, xd = step(gd, 1, sent1[2])
    gc, _ = step(gc, 2, sent1[3])
    back1 = after(back1, *gd0)
    d1, ge_keep, ge_send, dgain1, dbias1 = call(
        back_one_kernel, [h(B, M, 512), h(8, 64, 256), h(8, 64, 256), out(512), out(512)],
        [fs, isc, back1, tot1, x1, do1, xp, keep1, gb],
        [V((4, 512), F32), V((4, M, 512), BF), V((1024, 256), BF)],
        flops=1e9, size=6e6, name="back_one",
    )
    ge = (ge_keep, ge_send)
    dimg = call(
        image_kernel, [out(HROWS, 1024)], [isc, perm, d1, placed, keep_half, w1],
        [V((HROWS, 512), BF)], flops=1e9, size=1e7, name="image",
    )[0]

    if exact:
        ge, _ = step(ge, 0)
        dimg, *gd = lax.optimization_barrier((dimg,) + gd)
        gb1, _ = step(gb1, 2)
        gab = tuple(jnp.concatenate(p, axis=1) for p in zip(ga, gb1))
        gab, _ = step(gab, 3)
        gd, _ = step(gd, 2)
        gc, _ = step(gc, 3)
        ge, _ = step(ge, 1)
        ge, _ = step(ge, 2)
        gd, _ = step(gd, 3)
        ge, _ = step(ge, 3)
        (
            expand2, spatial2, reduce2, squeeze2, excite2, squeeze1, excite1, expand1, project1,
        ) = call(
            unpack_kernel,
            [out(256, 128), out(288, 256), out(32, 1024)] + [out(8, 1024)] * 4 + [out(32, 1024), out(64, 1024)],
            list(gab + gc), name="unpack",
        )
        spatial1, reduce1 = call(
            unpack_last_kernel, [out(288, 256), out(64, 256)], list(gd + ge), name="unpack_last"
        )
    else:
        finer = wide // 16

        def summed(g):
            return lax.psum_scatter(g, "wide", scatter_dimension=0, tiled=True)

        def blocks(g, start, count, rows):
            p = g[:, start : start + count * rows].reshape(16, count, finer, rows // finer, 256)
            p = summed(p.transpose(0, 2, 1, 3, 4).reshape(wide, count, rows // finer, 256))[0]
            return f32(p).transpose(1, 0, 2).reshape(rows // finer, count * 256)

        def both(g, start):
            p = g[:, start : start + 64].reshape(16, 4, 2, finer, 8 // finer, 256)
            p = f32(summed(p.transpose(0, 3, 1, 2, 4, 5).reshape(wide, 4, 2, -1, 256))[0])
            return [p[:, k].transpose(1, 0, 2).reshape(-1, 1024) for k in range(2)]

        def taps(g, start):
            p = g[:, start : start + 288].reshape(16, 9, finer, 32 // finer, 256)
            return f32(summed(p.transpose(0, 2, 1, 3, 4).reshape(wide, 9, -1, 256))[0]).reshape(-1, 256)

        ga, gb1, gc, gd, ge = (jnp.concatenate(g) for g in (ga, gb1, gc, gd, ge))
        e2 = ga[:, 0:128].reshape(16, 128, 2, finer, 128 // finer).transpose(0, 3, 1, 2, 4)
        e2 = summed(e2.reshape(wide, 1, -1)).reshape(128, 2, -1)
        expand2 = f32(e2.transpose(1, 0, 2).reshape(256, -1))
        spatial2 = taps(ga, 128)
        reduce2 = blocks(gb1, 0, 4, 32)
        squeeze2, excite2 = both(gb1, 128)
        expand1, project1 = blocks(gc, 0, 4, 32), blocks(gc, 128, 4, 64)
        squeeze1, excite1 = both(gb1, 192)
        spatial1, reduce1 = taps(gd, 0), blocks(ge, 0, 1, 64)
    return (
        result.reshape(B, 7, 8, 1024).transpose(0, 2, 1, 3),
        dimg.reshape(B, 14, 8, 1024).transpose(0, 2, 1, 3),
        reduce1, dgain1, dbias1,
        spatial1.reshape(3, 3, -1, 256), dgain2, dbias2,
        expand1, dgain3, dbias3,
        project1, dgainp, dbiasp,
        squeeze1.T, dsbias1, excite1, debias1,
        reduce2.T, dgain4, dbias4,
        spatial2.reshape(3, 3, -1, 256), dgain5, dbias5,
        expand2, dgain6, dbias6,
        squeeze2.T, dsbias2, excite2, debias2,
        norms,
    )


def solution(mesh):
    rep, nar = P(), P("narrow")
    return jax.shard_map(
        local,
        mesh=mesh,
        in_specs=(P("wide", "narrow", None, None),) + (rep,) * 18 + (
            P("narrow", None), rep, rep,
            P(None, None, None, "narrow"), nar, nar,
            P("narrow", None), nar, nar,
            P("narrow", None), rep, P(None, "narrow"), nar,
            P("wide", None, None, "narrow"),
        ),
        out_specs=(
            P("wide", None, None, "narrow"), P("wide", "narrow", None, None),
            P("wide", "narrow"), rep, rep,
            P(None, None, "wide", "narrow"), rep, rep,
            P("wide", "narrow"), rep, rep,
            P("wide", "narrow"), rep, rep,
            P("narrow", "wide"), rep, P("wide", "narrow"), rep,
            P("narrow", "wide"), rep, rep,
            P(None, None, "wide", "narrow"), nar, nar,
            P("narrow", "wide"), nar, nar,
            P("narrow", "wide"), rep, P("wide", "narrow"), nar,
            rep,
        ),
        check_vma=False,
    )
```
